32 devices in a mesh: groups: 2 (over y), row: 4 (over x, core), col: 4 (over z).
Axes of the slice: x: 2, y: 2, z: 4, core: 2. Of those that a mesh axis runs over, the one named last changes fastest.
Arguments:
- tiles: float32 [512, 128, 128], P(('groups', 'row', 'col')), parts along dimension 0, may hold values from 0 to 9
- tile_index: int32 [512, 2], P(('groups', 'row', 'col')), parts along dimension 0, may hold values from 0 to 3, as said below
- tile_count: int32 [32], P(('groups', 'row', 'col')), parts along dimension 0, may hold values from 4 to 16, as said below
- sources: int32 [16], P('groups'), parts along dimension 0, may hold values from 0 to 2047
Outputs:
- distance: float32 [16, 2048], P('groups', ('row', 'col')), parts along dimension 0
- path_counts: float32 [16, 2048], P('groups', ('row', 'col')), parts along dimension 0
- centrality: float32 [4096], P(('groups', 'row', 'col')), parts along dimension 0
The draws below stay inside these ranges and needn't reach their ends.
There are 2 independent parts, one for each index of `groups`. The reference program is written for one: setup_inputs(seed, part) draws one part's arguments, and reference() takes and returns one part's arrays. A program takes and returns all parts, laid end to end along the dimension named above; each array names one. Nothing has to cross between parts.
Inputs may be any that keep to these rules, and one draw needn't show every extreme that they name: `tile_index`: entry (r, c) of a slot has r below 4 and c below 4; the 16 slots of one device name distinct pairs. `tile_count`: one entry per device; slots of a device from its count on hold only zeros; some device has all 16 slots live.
All inputs are finite; a program needn't handle non-finite values.
Results may differ from the reference program's by a relative error of at most 0.0003.
Values sent between devices are 32-bit elements; how exact they have to be, the bound alone decides.
No kernel may reach another device: no remote copies, remote signals or barrier semaphores. Data moves between devices by JAX's collectives and lax.ppermute only.
A program may use at most 64 MiB of HBM per device.

```python
import jax
import jax.numpy as jnp
from jax import lax

TILE = 128
SLOTS = 16
SOURCES = 8
WMAX = 8
LEVELS = 3
BACK = 2
DEVS = 16
VERTICES = 2048
SLOT_ALL = 256
N_ROW = 4
N_COL = 4


def tile_layout(key):
    layout_key = jax.random.fold_in(key, 101)
    perm_key, count_key, pick_key, weight_key, keep_key, level_key = jax.random.split(layout_key, 6)
    placed = jax.vmap(lambda one_key: jax.random.permutation(one_key, N_ROW * N_COL)[:SLOTS])(jax.random.split(perm_key, DEVS))
    live_counts = jax.random.randint(count_key, (DEVS,), SLOTS // 4, SLOTS + 1)
    fullest = jax.random.randint(pick_key, (), 0, DEVS)
    live_counts = jnp.where(jnp.arange(DEVS) == fullest, SLOTS, live_counts).astype(jnp.int32)
    whole_parts = jax.random.randint(weight_key, (DEVS, SLOTS, TILE, TILE), 1, WMAX + 1).astype(jnp.float32)
    kept_edges = jax.random.randint(keep_key, (DEVS, SLOTS, TILE, TILE), 0, TILE) < 2
    live_slots = jnp.arange(SLOTS)[None, :] < live_counts[:, None]
    vertex_level = jax.random.randint(level_key, (VERTICES,), 0, 2 ** 17).astype(jnp.float32) * 2.0 ** (-18)
    row_tile = placed // N_ROW
    col_tile = placed % N_ROW
    dev_ids = jnp.arange(DEVS)
    row_base = (dev_ids[:, None] // N_COL * N_COL + row_tile) * TILE
    col_base = (col_tile * N_COL + dev_ids[:, None] % N_COL) * TILE
    offsets = jnp.arange(TILE)
    row_level = vertex_level[row_base[:, :, None] + offsets[None, None, :]]
    col_level = vertex_level[col_base[:, :, None] + offsets[None, None, :]]
    weights = whole_parts + col_level[:, :, None, :] - row_level[:, :, :, None]
    tile_values = jnp.where(kept_edges & live_slots[:, :, None, None], weights, 0.0).reshape(DEVS * SLOTS, TILE, TILE).astype(jnp.float32)
    positions = jnp.stack([row_tile, col_tile], axis=-1).reshape(DEVS * SLOTS, 2).astype(jnp.int32)
    return (tile_values, positions, live_counts)


def draw_tiles(key, part):
    return tile_layout(key)[0]


def draw_tile_index(key, part):
    return tile_layout(key)[1]


def draw_tile_count(key, part):
    return tile_layout(key)[2]


def place_ends(drawn, own_key, low, high):
    longest = drawn.shape.index(max(drawn.shape))
    spots = []
    for shift in (0, 1):
        where = [jax.random.randint(jax.random.fold_in(own_key, axis), (), 0, length) for axis, length in enumerate(drawn.shape)]
        where[longest] = (where[longest] + shift) % drawn.shape[longest]
        spots.append(tuple(where))
    return drawn.at[spots[0]].set(low).at[spots[1]].set(high)


def setup_inputs(seed: int = 0, part: int = 0) -> dict:
    seeds = jax.random.split(jax.random.key(seed), 5)
    part_splits = jax.random.split(jax.random.fold_in(seeds[4], part), 5)
    tiles = draw_tiles(jax.random.fold_in(jax.random.fold_in(seeds[4], part), 71), part)
    tile_index = draw_tile_index(jax.random.fold_in(jax.random.fold_in(seeds[4], part), 71), part)
    tile_count = draw_tile_count(jax.random.fold_in(jax.random.fold_in(seeds[4], part), 71), part)
    sources = place_ends(jax.random.randint(part_splits[3], (SOURCES,), 0, VERTICES), jax.random.fold_in(part_splits[3], 1), 0, VERTICES - 1).astype(jnp.int32)
    return {"tiles": tiles, "tile_index": tile_index, "tile_count": tile_count, "sources": sources}


far_value = 1.0e6
no_edge = 2.0e6


def combine_pair(left_pair, right_pair):
    best_dist = jnp.minimum(left_pair[0], right_pair[0])
    total_count = jnp.where(left_pair[0] == best_dist, left_pair[1], 0.0) + jnp.where(right_pair[0] == best_dist, right_pair[1], 0.0)
    return best_dist, total_count


def edge_weights(raw_tile):
    return jnp.where(raw_tile > 0, raw_tile.astype(jnp.float32), no_edge)


def relax_tile(near_dist, near_count, weight_tile):
    source_rows = near_dist.shape[0]
    tile_side = weight_tile.shape[0]
    block_size = min(16, tile_side)
    blocks = tile_side // block_size
    dist_blocks = near_dist.reshape(source_rows, blocks, block_size).transpose(1, 0, 2)
    count_blocks = near_count.reshape(source_rows, blocks, block_size).transpose(1, 0, 2)
    weight_blocks = weight_tile.reshape(blocks, block_size, tile_side)

    def advance(carried, pieces):
        dist_part, count_part, weight_part = pieces
        reached = dist_part[:, :, None] + weight_part[None, :, :]
        best_dist = jnp.min(reached, axis=1)
        total_count = jnp.sum(jnp.where(reached == best_dist[:, None, :], count_part[:, :, None], 0.0), axis=1)
        return combine_pair(carried, (best_dist, total_count)), None

    initial = (jnp.full((source_rows, tile_side), far_value, near_dist.dtype), jnp.zeros((source_rows, tile_side), near_dist.dtype))
    result, unused = lax.scan(advance, initial, (dist_blocks, count_blocks, weight_blocks))
    return result


def depend_tile(upper_dist, lower_dist, lower_coef, weight_tile):
    source_rows = upper_dist.shape[0]
    tile_side = weight_tile.shape[0]
    block_size = min(16, tile_side)
    blocks = tile_side // block_size
    upper_blocks = upper_dist.reshape(source_rows, blocks, block_size).transpose(1, 0, 2)
    weight_blocks = weight_tile.reshape(blocks, block_size, tile_side)

    def dependency_rows(pieces):
        upper_part, weight_part = pieces
        reached = upper_part[:, :, None] + weight_part[None, :, :]
        return jnp.sum(jnp.where(reached == lower_dist[:, None, :], lower_coef[:, None, :], 0.0), axis=2)

    row_parts = lax.map(dependency_rows, (upper_blocks, weight_blocks))
    return row_parts.transpose(1, 0, 2).reshape(source_rows, tile_side)


def reference(tiles, tile_index, tile_count, sources):
    source_rows = sources.shape[0]
    vertex_ids = jnp.arange(VERTICES, dtype=jnp.int32)
    is_source = vertex_ids[None, :] == sources[:, None]
    start_dist = jnp.where(is_source, 0.0, far_value).astype(jnp.float32)
    source_ones = jnp.where(is_source, 1.0, 0.0).astype(jnp.float32)
    distance = start_dist
    path_counts = source_ones
    slot_ids = jnp.arange(SLOT_ALL, dtype=jnp.int32)

    def place(slot_id):
        owner_dev = slot_id // SLOTS
        local_slot = slot_id % SLOTS
        row_block = owner_dev // N_COL
        col_block = owner_dev % N_COL
        row_start = ((row_block * N_COL + tile_index[slot_id, 0]) * TILE).astype(jnp.int32)
        col_start = ((tile_index[slot_id, 1] * N_COL + col_block) * TILE).astype(jnp.int32)
        return row_start, col_start, local_slot < tile_count[owner_dev]

    for level_no in range(LEVELS):
        def forward_step(carried, slot_id, distance=distance, path_counts=path_counts):
            row_start, col_start, is_live = place(slot_id)
            weight_tile = edge_weights(tiles[slot_id])

            def active(current):
                near_dist = lax.dynamic_slice_in_dim(distance, row_start, TILE, 1)
                near_count = lax.dynamic_slice_in_dim(path_counts, row_start, TILE, 1)
                found = relax_tile(near_dist, near_count, weight_tile)
                previous = (lax.dynamic_slice_in_dim(current[0], col_start, TILE, 1), lax.dynamic_slice_in_dim(current[1], col_start, TILE, 1))
                merged = combine_pair(previous, found)
                return (lax.dynamic_update_slice_in_dim(current[0], merged[0], col_start, 1), lax.dynamic_update_slice_in_dim(current[1], merged[1], col_start, 1))

            return lax.cond(is_live, active, lambda unchanged: unchanged, carried), None

        initial = (jnp.full((source_rows, VERTICES), far_value, jnp.float32), jnp.zeros((source_rows, VERTICES), jnp.float32))
        (cand_dist, cand_count), unused = lax.scan(forward_step, initial, slot_ids)
        distance = jnp.minimum(start_dist, cand_dist)
        path_counts = source_ones + jnp.where(cand_dist == distance, cand_count, 0.0)

    dependency = jnp.zeros((source_rows, VERTICES), jnp.float32)
    for back_no in range(BACK):
        coefficient = jnp.where(path_counts > 0.5, (1.0 + dependency) / jnp.maximum(path_counts, 1.0), 0.0)

        def backward_step(carried, slot_id, coefficient=coefficient):
            row_start, col_start, is_live = place(slot_id)
            weight_tile = edge_weights(tiles[slot_id])

            def active(current):
                upper_dist = lax.dynamic_slice_in_dim(distance, row_start, TILE, 1)
                lower_dist = lax.dynamic_slice_in_dim(distance, col_start, TILE, 1)
                lower_coef = lax.dynamic_slice_in_dim(coefficient, col_start, TILE, 1)
                dep_term = depend_tile(upper_dist, lower_dist, lower_coef, weight_tile)
                previous = lax.dynamic_slice_in_dim(current, row_start, TILE, 1)
                return lax.dynamic_update_slice_in_dim(current, previous + dep_term, row_start, 1)

            return lax.cond(is_live, active, lambda unchanged: unchanged, carried), None

        accumulated, unused = lax.scan(backward_step, jnp.zeros((source_rows, VERTICES), jnp.float32), slot_ids)
        dependency = path_counts * accumulated

    centrality = jnp.sum(jnp.where(is_source, 0.0, dependency), axis=0) / source_rows
    shown = jnp.where(distance < 0.5 * far_value, distance, -1.0)
    return shown, path_counts, centrality
```

```python
import functools

import jax
import jax.numpy as jnp
from jax import lax
from jax.experimental import pallas as pl
from jax.experimental.pallas import tpu as pltpu
from jax.sharding import PartitionSpec as P

LEVELS = 3
BACK = 2
LANES = 128
SUB = 8

far_value = 1000000.0
no_edge = 2000000.0
vmem_limit = 48 * 1024 * 1024


def in_vmem():
    return pl.BlockSpec(memory_space=pltpu.VMEM)


def in_smem():
    return pl.BlockSpec(memory_space=pltpu.SMEM)


def piece(*shape):
    return jax.ShapeDtypeStruct(shape, jnp.float32)


def params():
    return pltpu.CompilerParams(vmem_limit_bytes=vmem_limit)


def edges(raw):
    return jnp.where(raw > 0, raw, no_edge)


def fold(block):
    return block.reshape(block.shape[0] // SUB, SUB, LANES)


def source_ids(sources_ref, rows):
    lane_row = lax.broadcasted_iota(jnp.int32, (rows, LANES), 0)
    ids = jnp.zeros((rows, LANES), jnp.int32)
    for s in range(rows):
        ids = jnp.where(lane_row == s, sources_ref[s], ids)
    return ids


def is_source(ids, block):
    lane = lax.broadcasted_iota(jnp.int32, ids.shape, 1)
    return ids == block * LANES + lane


def settle(found_dist, found_count, at_source):
    dist = jnp.where(at_source, 0.0, jnp.minimum(found_dist, far_value))
    count = jnp.where(found_dist == dist, found_count, 0.0)
    return dist, jnp.where(at_source, 1.0, 0.0) + count


def merge(pairs):
    best = functools.reduce(jnp.minimum, [p[0] for p in pairs])
    total = functools.reduce(jnp.add, [jnp.where(p[0] == best, p[1], 0.0) for p in pairs])
    return best, total


def spread(block):
    rows = block.shape[0]
    turned = block.T
    return [jnp.broadcast_to(turned[:, s : s + 1], (LANES, LANES)) for s in range(rows)]


def first_kernel(dims, tile_index, sources, tiles, *rest):
    n_row, n_col, slots, rows = dims
    outs, slot_of = rest[:n_row], rest[n_row]
    my_row = lax.axis_index("row")
    for out in outs:
        out[...] = jnp.full(out.shape, far_value, jnp.float32)

    def clear(at, _):
        slot_of[at] = -1
        return 0

    lax.fori_loop(0, n_row * n_col, clear, 0)
    for g in range(slots):
        slot_of[tile_index[g, 0] * n_row + tile_index[g, 1]] = g
    for s in range(rows):
        vertex = sources[s]
        block, place = vertex // LANES, lax.rem(vertex, LANES)
        r = lax.rem(block, n_col)

        @pl.when(block // n_col == my_row)
        def _():
            for di in range(n_row):
                c = lax.rem(my_row + di, n_row)
                g = slot_of[r * n_row + c]

                @pl.when(g >= 0)
                def _():
                    row = tiles[g, pl.ds(place, 1), :]
                    outs[di][pl.ds(s, 1), :] = jnp.where(row > 0, row, far_value)


def first_level(dims, tile_index, sources, tiles):
    n_row, n_col, slots, rows = dims
    return pl.pallas_call(
        functools.partial(first_kernel, dims),
        out_shape=[piece(rows, LANES)] * n_row,
        in_specs=[in_smem(), in_smem(), in_vmem()],
        out_specs=[in_vmem()] * n_row,
        scratch_shapes=[pltpu.SMEM((n_row * n_col,), jnp.int32)],
        compiler_params=params(),
        name="first_level",
    )(tile_index, sources, tiles)


def relax_kernel(dims, ways, counted, whole, *refs):
    n_row, n_col, slots, rows = dims
    tile_index, tile_count, sources, tiles = refs[:4]
    came = refs[4 : 4 + n_col * ways]
    rest = refs[4 + n_col * ways :]
    outs, rest = rest[:n_row], rest[n_row:]
    if whole:
        full, rest = rest[0], rest[1:]
    wide_dist, wide_count, acc, best_of = rest
    my_row = lax.axis_index("row")
    my_col = lax.axis_index("col")
    ids = source_ids(sources, rows)
    for dj in range(n_col):
        r = lax.rem(my_col + n_col - dj, n_col)
        at_source = is_source(ids, my_row * n_col + r)
        pairs = []
        for part in came[dj * ways : (dj + 1) * ways]:
            if counted:
                pairs.append((part[0], part[1]))
            else:
                found = part[...]
                pairs.append((found, jnp.where(found < far_value, 1.0, 0.0)))
        dist, count = settle(*merge(pairs), at_source)
        for s, block in enumerate(spread(dist)):
            wide_dist[r * rows + s] = block
        for s, block in enumerate(spread(count)):
            wide_count[r * rows + s] = block
    acc[...] = jnp.full(acc.shape, far_value, jnp.float32)
    live = tile_count[0]

    def lowest(g, _):
        r, c = tile_index[g, 0], tile_index[g, 1]
        weight = edges(tiles[g])
        for s in range(rows):
            reached = wide_dist[r * rows + s] + weight
            at = c * rows + s
            acc[at] = jnp.minimum(acc[at], jnp.min(fold(reached), axis=0))
        return 0

    lax.fori_loop(0, live, lowest, 0)
    for at in range(n_row * rows):
        best = jnp.min(acc[at], axis=0, keepdims=True)
        best_of[at] = jnp.broadcast_to(best, (SUB, LANES))
    acc[...] = jnp.zeros(acc.shape, jnp.float32)

    def tally(g, _):
        r, c = tile_index[g, 0], tile_index[g, 1]
        weight = edges(tiles[g])
        for s in range(rows):
            reached = wide_dist[r * rows + s] + weight
            at = c * rows + s
            hit = fold(reached) == best_of[at][None]
            acc[at] += jnp.sum(jnp.where(hit, fold(wide_count[r * rows + s]), 0.0), axis=0)
        return 0

    lax.fori_loop(0, live, tally, 0)
    for di in range(n_row):
        c = lax.rem(my_row + di, n_row)
        for s in range(rows):
            at = c * rows + s
            outs[di][0, pl.ds(s, 1), :] = best_of[at, 0:1, :]
            outs[di][1, pl.ds(s, 1), :] = jnp.sum(acc[at], axis=0, keepdims=True)
        if whole:
            full[c] = outs[di][...]


def relax_level(dims, ways, counted, whole, tile_index, tile_count, sources, tiles, came):
    n_row, n_col, slots, rows = dims
    out_shape = [piece(2, rows, LANES)] * n_row
    if whole:
        out_shape = out_shape + [piece(n_row, 2, rows, LANES)]
    return pl.pallas_call(
        functools.partial(relax_kernel, dims, ways, counted, whole),
        out_shape=out_shape,
        in_specs=[in_smem()] * 3 + [in_vmem()] * (1 + len(came)),
        out_specs=[in_vmem()] * len(out_shape),
        scratch_shapes=[
            pltpu.VMEM((n_col * rows, LANES, LANES), jnp.float32),
            pltpu.VMEM((n_col * rows, LANES, LANES), jnp.float32),
            pltpu.VMEM((n_row * rows, SUB, LANES), jnp.float32),
            pltpu.VMEM((n_row * rows, SUB, LANES), jnp.float32),
        ],
        compiler_params=params(),
        name="relax_level",
    )(tile_index, tile_count, sources, tiles, *came)


def sum_dependency(dims, tile_index, live, tiles, low_dist, coef, wide_dist, acc):
    n_row, n_col, slots, rows = dims
    acc[...] = jnp.zeros(acc.shape, jnp.float32)

    def gather(g, _):
        r, c = tile_index[g, 0], tile_index[g, 1]
        weight = edges(tiles[g])
        for s in range(rows):
            reached = wide_dist[r * rows + s] + weight
            hit = reached == low_dist[c, pl.ds(s, 1), :]
            acc[r * rows + s] += jnp.where(hit, coef[c, pl.ds(s, 1), :], 0.0)
        return 0

    lax.fori_loop(0, live, gather, 0)


def dependency_rows(acc, r, rows):
    lane = lax.broadcasted_iota(jnp.int32, (LANES, LANES), 1)
    turned = jnp.zeros((LANES, LANES), jnp.float32)
    for s in range(rows):
        turned = jnp.where(lane == s, jnp.sum(acc[r * rows + s], axis=1, keepdims=True), turned)
    return turned.T[:rows]


def lower_kernel(dims, ways, *refs):
    n_row, n_col, slots, rows = dims
    tile_index, tile_count, sources, tiles = refs[:4]
    side = refs[4 : 4 + (n_col - 1) * ways]
    rest = refs[4 + (n_col - 1) * ways :]
    wholes, rest = rest[:ways], rest[ways:]
    outs, rest = rest[:n_col], rest[n_col:]
    shown, own_paths, row_dist, row_paths, low_dist, low_paths, wide_dist, acc, coef = rest
    my_row = lax.axis_index("row")
    my_col = lax.axis_index("col")
    ids = source_ids(sources, rows)
    for c in range(n_row):
        at_source = is_source(ids, c * n_col + my_col)
        dist, count = settle(*merge([(part[c, 0], part[c, 1]) for part in wholes]), at_source)
        low_dist[c] = dist
        low_paths[c] = count
        coef[c] = jnp.where(count > 0.5, 1.0 / jnp.maximum(count, 1.0), 0.0)
    for dj in range(n_col):
        r = lax.rem(my_col + n_col - dj, n_col)
        if dj == 0:
            dist, count = low_dist[my_row], low_paths[my_row]
            shown[...] = jnp.where(dist < 0.5 * far_value, dist, -1.0)
            own_paths[...] = count
        else:
            at_source = is_source(ids, my_row * n_col + r)
            parts = side[(dj - 1) * ways : dj * ways]
            dist, count = settle(*merge([(part[0], part[1]) for part in parts]), at_source)
        row_dist[r] = dist
        row_paths[r] = count
        for s, block in enumerate(spread(dist)):
            wide_dist[r * rows + s] = block
    sum_dependency(dims, tile_index, tile_count[0], tiles, low_dist, coef, wide_dist, acc)
    for dj in range(n_col):
        r = lax.rem(my_col + dj, n_col)
        outs[dj][...] = dependency_rows(acc, r, rows)


def lower_level(dims, ways, tile_index, tile_count, sources, tiles, side, wholes):
    n_row, n_col, slots, rows = dims
    out_shape = [piece(rows, LANES)] * n_col + [
        piece(rows, LANES),
        piece(rows, LANES),
        piece(n_col, rows, LANES),
        piece(n_col, rows, LANES),
        piece(n_row, rows, LANES),
        piece(n_row, rows, LANES),
    ]
    return pl.pallas_call(
        functools.partial(lower_kernel, dims, ways),
        out_shape=out_shape,
        in_specs=[in_smem()] * 3 + [in_vmem()] * (1 + len(side) + len(wholes)),
        out_specs=[in_vmem()] * len(out_shape),
        scratch_shapes=[
            pltpu.VMEM((n_col * rows, LANES, LANES), jnp.float32),
            pltpu.VMEM((n_col * rows, LANES, LANES), jnp.float32),
            pltpu.VMEM((n_row, rows, LANES), jnp.float32),
        ],
        compiler_params=params(),
        name="lower_level",
    )(tile_index, tile_count, sources, tiles, *side, *wholes)


def upper_kernel(dims, ways, *refs):
    n_row, n_col, slots, rows = dims
    tile_index, tile_count, sources, tiles, row_dist, row_paths, low_dist, low_paths = refs[:8]
    came = refs[8 : 8 + n_row * ways]
    rest = refs[8 + n_row * ways :]
    outs, rest = rest[:n_col], rest[n_col:]
    wide_dist, acc, coef = rest
    my_row = lax.axis_index("row")
    my_col = lax.axis_index("col")
    ids = source_ids(sources, rows)
    for di in range(n_row):
        c = lax.rem(my_row + n_row - di, n_row)
        parts = came[di * ways : (di + 1) * ways]
        summed = functools.reduce(jnp.add, [part[...] for part in parts])
        count = low_paths[c]
        coef[c] = jnp.where(count > 0.5, (1.0 + count * summed) / jnp.maximum(count, 1.0), 0.0)
    for r in range(n_col):
        for s, block in enumerate(spread(row_dist[r])):
            wide_dist[r * rows + s] = block
    sum_dependency(dims, tile_index, tile_count[0], tiles, low_dist, coef, wide_dist, acc)
    for dj in range(n_col):
        r = lax.rem(my_col + dj, n_col)
        term = row_paths[r] * dependency_rows(acc, r, rows)
        at_source = is_source(ids, my_row * n_col + r)
        outs[dj][...] = jnp.sum(jnp.where(at_source, 0.0, term), axis=0, keepdims=True)


def upper_level(dims, ways, tile_index, tile_count, sources, tiles, bands, came):
    n_row, n_col, slots, rows = dims
    return pl.pallas_call(
        functools.partial(upper_kernel, dims, ways),
        out_shape=[piece(1, LANES)] * n_col,
        in_specs=[in_smem()] * 3 + [in_vmem()] * (1 + len(bands) + len(came)),
        out_specs=[in_vmem()] * n_col,
        scratch_shapes=[
            pltpu.VMEM((n_col * rows, LANES, LANES), jnp.float32),
            pltpu.VMEM((n_col * rows, LANES, LANES), jnp.float32),
            pltpu.VMEM((n_row, rows, LANES), jnp.float32),
        ],
        compiler_params=params(),
        name="upper_level",
    )(tile_index, tile_count, sources, tiles, *bands, *came)


def shifted(value, n_row, n_col, di, dj):
    if di == 0 and dj == 0:
        return value
    pairs = []
    for i in range(n_row):
        for j in range(n_col):
            target = (i + di) % n_row * n_col + (j + dj) % n_col
            pairs.append((i * n_col + j, target))
    return lax.ppermute(value, ("row", "col"), pairs)


def merge_arrays(parts):
    best, total = merge([(part[0], part[1]) for part in parts])
    return jnp.stack([best, total])


def per_device(tiles, tile_index, tile_count, sources):
    slots = tiles.shape[0]
    rows = sources.shape[0]
    n_row = lax.axis_size("row")
    n_col = lax.axis_size("col")
    dims = (n_row, n_col, slots, rows)
    direct = n_row * n_col <= 16
    ways = n_row if direct else 1
    move = functools.partial(shifted, n_row=n_row, n_col=n_col)

    def to_row_band(parts, join):
        if direct:
            return [move(parts[di], di=di, dj=dj) for dj in range(n_col) for di in range(n_row)]
        own = join([move(parts[di], di=di, dj=0) for di in range(n_row)])
        return [move(own, di=0, dj=dj) for dj in range(n_col)]

    firsts = first_level(dims, tile_index, sources, tiles)
    came = to_row_band(firsts, lambda parts: functools.reduce(jnp.minimum, parts))
    for level_no in range(1, LEVELS):
        last = level_no == LEVELS - 1
        outs = relax_level(
            dims, ways, level_no > 1, last, tile_index, tile_count, sources, tiles, came
        )
        if not last:
            came = to_row_band(outs, merge_arrays)
    parts, full = outs[:n_row], outs[n_row]
    wholes = [move(full, di=di, dj=0) for di in range(n_row)]
    if direct:
        side = [move(parts[di], di=di, dj=dj) for dj in range(1, n_col) for di in range(n_row)]
    else:
        wholes = [jax.vmap(lambda *given: merge_arrays(given))(*wholes)]
        own = lax.dynamic_index_in_dim(wholes[0], lax.axis_index("row"), 0, keepdims=False)
        side = [move(own, di=0, dj=dj) for dj in range(1, n_col)]
    lower = lower_level(dims, ways, tile_index, tile_count, sources, tiles, side, wholes)
    sums, rest = lower[:n_col], lower[n_col:]
    shown, own_paths, bands = rest[0], rest[1], rest[2:]
    if direct:
        came = [move(sums[dj], di=di, dj=dj) for di in range(n_row) for dj in range(n_col)]
        sum_ways = n_col
    else:
        own = functools.reduce(jnp.add, [move(sums[dj], di=0, dj=dj) for dj in range(n_col)])
        came = [move(own, di=di, dj=0) for di in range(n_row)]
        sum_ways = 1
    terms = upper_level(dims, sum_ways, tile_index, tile_count, sources, tiles, bands, came)
    total = functools.reduce(jnp.add, [move(terms[dj], di=0, dj=dj) for dj in range(n_col)])
    return shown, own_paths, total.reshape(LANES) / rows


def solution(mesh):
    in_specs = (
        P(("groups", "row", "col"), None, None),
        P(("groups", "row", "col"), None),
        P(("groups", "row", "col")),
        P("groups"),
    )
    out_specs = (
        P("groups", ("row", "col")),
        P("groups", ("row", "col")),
        P(("groups", "row", "col")),
    )
    return jax.shard_map(
        per_device, mesh=mesh, in_specs=in_specs, out_specs=out_specs, check_vma=False
    )
```

```python
import functools

import jax
import jax.numpy as jnp
from jax import lax
from jax.experimental import pallas as pl
from jax.experimental.pallas import tpu as pltpu
from jax.sharding import PartitionSpec as P

LEVELS = 3
BACK = 2
LANES = 128
SUB = 8

far_value = 1000000.0
no_edge = 2000000.0
vmem_limit = 48 * 1024 * 1024


def in_vmem():
    return pl.BlockSpec(memory_space=pltpu.VMEM)


def in_smem():
    return pl.BlockSpec(memory_space=pltpu.SMEM)


def piece(*shape):
    return jax.ShapeDtypeStruct(shape, jnp.float32)


def params():
    return pltpu.CompilerParams(vmem_limit_bytes=vmem_limit)


def edges(raw):
    return jnp.where(raw > 0, raw, no_edge)


def fold(block):
    return block.reshape(block.shape[0] // SUB, SUB, LANES)


def source_ids(sources_ref, rows):
    lane_row = lax.broadcasted_iota(jnp.int32, (rows, LANES), 0)
    ids = jnp.zeros((rows, LANES), jnp.int32)
    for s in range(rows):
        ids = jnp.where(lane_row == s, sources_ref[s], ids)
    return ids


def is_source(ids, block):
    lane = lax.broadcasted_iota(jnp.int32, ids.shape, 1)
    return ids == block * LANES + lane


def settle(found_dist, found_count, at_source):
    dist = jnp.where(at_source, 0.0, jnp.minimum(found_dist, far_value))
    count = jnp.where(found_dist == dist, found_count, 0.0)
    return dist, jnp.where(at_source, 1.0, 0.0) + count


def merge(pairs):
    best = functools.reduce(jnp.minimum, [p[0] for p in pairs])
    total = functools.reduce(jnp.add, [jnp.where(p[0] == best, p[1], 0.0) for p in pairs])
    return best, total


def spread(block):
    rows = block.shape[0]
    turned = block.T
    return [jnp.broadcast_to(turned[:, s : s + 1], (LANES, LANES)) for s in range(rows)]


def first_kernel(dims, tile_index, sources, tiles, out, slot_of):
    n_row, n_col, slots, rows = dims
    my_row = lax.axis_index("row")
    out[...] = jnp.full(out.shape, far_value, jnp.float32)

    def clear(at, _):
        slot_of[at] = -1
        return 0

    lax.fori_loop(0, n_row * n_col, clear, 0)
    for g in range(slots):
        slot_of[tile_index[g, 0] * n_row + tile_index[g, 1]] = g
    for s in range(rows):
        vertex = sources[s]
        block, place = vertex // LANES, lax.rem(vertex, LANES)
        r = lax.rem(block, n_col)

        @pl.when(block // n_col == my_row)
        def _():
            for c in range(n_row):
                g = slot_of[r * n_row + c]

                @pl.when(g >= 0)
                def _():
                    row = tiles[g, pl.ds(place, 1), :]
                    out[c, pl.ds(s, 1), :] = jnp.where(row > 0, row, far_value)


def first_level(dims, tile_index, sources, tiles):
    n_row, n_col, slots, rows = dims
    return pl.pallas_call(
        functools.partial(first_kernel, dims),
        out_shape=piece(n_row, rows, LANES),
        in_specs=[in_smem(), in_smem(), in_vmem()],
        out_specs=in_vmem(),
        scratch_shapes=[pltpu.SMEM((n_row * n_col,), jnp.int32)],
        compiler_params=params(),
        name="first_level",
    )(tile_index, sources, tiles)


def shares(came, ways, stride, at, share):
    parts = []
    for way in range(ways):
        part = came.at[way * stride + at] if stride else came.at[at * ways + way]
        parts.append(part if share is None else part.at[share])
    return parts


def relax_kernel(dims, ways, counted, picked, copies, *refs):
    n_row, n_col, slots, rows = dims
    tile_index, tile_count, sources, tiles, came, out, wide_dist, wide_count, acc, best_of = refs
    my_row = lax.axis_index("row")
    ids = source_ids(sources, rows)
    for r in range(n_col):
        at_source = is_source(ids, my_row * n_col + r)
        pairs = []
        for part in shares(came, ways, n_col, r, my_row if picked else None):
            if counted:
                pairs.append((part[0], part[1]))
            else:
                found = part[...]
                pairs.append((found, jnp.where(found < far_value, 1.0, 0.0)))
        dist, count = settle(*merge(pairs), at_source)
        for s, block in enumerate(spread(dist)):
            wide_dist[r * rows + s] = block
        for s, block in enumerate(spread(count)):
            wide_count[r * rows + s] = block
    acc[...] = jnp.full(acc.shape, far_value, jnp.float32)
    live = tile_count[0]

    def lowest(g, _):
        r, c = tile_index[g, 0], tile_index[g, 1]
        weight = edges(tiles[g])
        for s in range(rows):
            reached = wide_dist[r * rows + s] + weight
            at = c * rows + s
            acc[at] = jnp.minimum(acc[at], jnp.min(fold(reached), axis=0))
        return 0

    lax.fori_loop(0, live, lowest, 0)
    for at in range(n_row * rows):
        best = jnp.min(acc[at], axis=0, keepdims=True)
        best_of[at] = jnp.broadcast_to(best, (SUB, LANES))
    acc[...] = jnp.zeros(acc.shape, jnp.float32)

    def tally(g, _):
        r, c = tile_index[g, 0], tile_index[g, 1]
        weight = edges(tiles[g])
        for s in range(rows):
            reached = wide_dist[r * rows + s] + weight
            at = c * rows + s
            hit = fold(reached) == best_of[at][None]
            acc[at] += jnp.sum(jnp.where(hit, fold(wide_count[r * rows + s]), 0.0), axis=0)
        return 0

    lax.fori_loop(0, live, tally, 0)
    for c in range(n_row):
        for s in range(rows):
            at = c * rows + s
            out[c * copies, 0, pl.ds(s, 1), :] = best_of[at, 0:1, :]
            out[c * copies, 1, pl.ds(s, 1), :] = jnp.sum(acc[at], axis=0, keepdims=True)
        for copy in range(1, copies):
            out[c * copies + copy] = out[c * copies]


def relax_level(dims, ways, counted, picked, copies, tile_index, tile_count, sources, tiles, came):
    n_row, n_col, slots, rows = dims
    return pl.pallas_call(
        functools.partial(relax_kernel, dims, ways, counted, picked, copies),
        out_shape=piece(n_row * copies, 2, rows, LANES),
        in_specs=[in_smem()] * 3 + [in_vmem()] * 2,
        out_specs=in_vmem(),
        scratch_shapes=[
            pltpu.VMEM((n_col * rows, LANES, LANES), jnp.float32),
            pltpu.VMEM((n_col * rows, LANES, LANES), jnp.float32),
            pltpu.VMEM((n_row * rows, SUB, LANES), jnp.float32),
            pltpu.VMEM((n_row * rows, SUB, LANES), jnp.float32),
        ],
        compiler_params=params(),
        name="relax_level",
    )(tile_index, tile_count, sources, tiles, came)


def sum_dependency(dims, tile_index, live, tiles, low_dist, coef, wide_dist, acc):
    n_row, n_col, slots, rows = dims
    acc[...] = jnp.zeros(acc.shape, jnp.float32)

    def gather(g, _):
        r, c = tile_index[g, 0], tile_index[g, 1]
        weight = edges(tiles[g])
        for s in range(rows):
            reached = wide_dist[r * rows + s] + weight
            hit = reached == low_dist[c, pl.ds(s, 1), :]
            acc[r * rows + s] += jnp.where(hit, coef[c, pl.ds(s, 1), :], 0.0)
        return 0

    lax.fori_loop(0, live, gather, 0)


def dependency_rows(acc, r, rows):
    lane = lax.broadcasted_iota(jnp.int32, (LANES, LANES), 1)
    turned = jnp.zeros((LANES, LANES), jnp.float32)
    for s in range(rows):
        turned = jnp.where(lane == s, jnp.sum(acc[r * rows + s], axis=1, keepdims=True), turned)
    return turned.T[:rows]


def lower_kernel(dims, ways, picked, copies, *refs):
    n_row, n_col, slots, rows = dims
    tile_index, tile_count, sources, tiles, row_came, low_came = refs[:6]
    out, shown, own_paths, row_dist, row_paths, low_dist, low_paths = refs[6:13]
    wide_dist, acc, coef = refs[13:]
    my_row = lax.axis_index("row")
    my_col = lax.axis_index("col")
    ids = source_ids(sources, rows)
    for c in range(n_row):
        at_source = is_source(ids, c * n_col + my_col)
        if picked:
            parts = [low_came.at[way * n_col + my_col, c] for way in range(n_row)]
        else:
            parts = [low_came.at[c]]
        dist, count = settle(*merge([(part[0], part[1]) for part in parts]), at_source)
        low_dist[c] = dist
        low_paths[c] = count
        coef[c] = jnp.where(count > 0.5, 1.0 / jnp.maximum(count, 1.0), 0.0)
    for r in range(n_col):
        at_source = is_source(ids, my_row * n_col + r)
        parts = shares(row_came, ways, n_col, r, my_row if picked else None)
        dist, count = settle(*merge([(part[0], part[1]) for part in parts]), at_source)
        row_dist[r] = dist
        row_paths[r] = count
        for s, block in enumerate(spread(dist)):
            wide_dist[r * rows + s] = block
    dist = low_dist[my_row]
    shown[...] = jnp.where(dist < 0.5 * far_value, dist, -1.0)
    own_paths[...] = low_paths[my_row]
    sum_dependency(dims, tile_index, tile_count[0], tiles, low_dist, coef, wide_dist, acc)
    for r in range(n_col):
        block = dependency_rows(acc, r, rows)
        for copy in range(copies):
            out[copy * n_col + r] = block


def lower_level(dims, ways, picked, copies, tile_index, tile_count, sources, tiles, row_came, low_came):
    n_row, n_col, slots, rows = dims
    out_shape = [
        piece(copies * n_col, rows, LANES),
        piece(rows, LANES),
        piece(rows, LANES),
        piece(n_col, rows, LANES),
        piece(n_col, rows, LANES),
        piece(n_row, rows, LANES),
        piece(n_row, rows, LANES),
    ]
    return pl.pallas_call(
        functools.partial(lower_kernel, dims, ways, picked, copies),
        out_shape=out_shape,
        in_specs=[in_smem()] * 3 + [in_vmem()] * 3,
        out_specs=[in_vmem()] * len(out_shape),
        scratch_shapes=[
            pltpu.VMEM((n_col * rows, LANES, LANES), jnp.float32),
            pltpu.VMEM((n_col * rows, LANES, LANES), jnp.float32),
            pltpu.VMEM((n_row, rows, LANES), jnp.float32),
        ],
        compiler_params=params(),
        name="lower_level",
    )(tile_index, tile_count, sources, tiles, row_came, low_came)


def upper_kernel(dims, ways, picked, *refs):
    n_row, n_col, slots, rows = dims
    tile_index, tile_count, sources, tiles, row_dist, row_paths, low_dist, low_paths = refs[:8]
    came, out, wide_dist, acc, coef = refs[8:]
    my_row = lax.axis_index("row")
    my_col = lax.axis_index("col")
    ids = source_ids(sources, rows)
    for c in range(n_row):
        parts = shares(came, ways, 0, c, my_col if picked else None)
        summed = functools.reduce(jnp.add, [part[...] for part in parts])
        count = low_paths[c]
        coef[c] = jnp.where(count > 0.5, (1.0 + count * summed) / jnp.maximum(count, 1.0), 0.0)
    for r in range(n_col):
        for s, block in enumerate(spread(row_dist[r])):
            wide_dist[r * rows + s] = block
    sum_dependency(dims, tile_index, tile_count[0], tiles, low_dist, coef, wide_dist, acc)
    for r in range(n_col):
        term = row_paths[r] * dependency_rows(acc, r, rows)
        at_source = is_source(ids, my_row * n_col + r)
        out[r] = jnp.sum(jnp.where(at_source, 0.0, term), axis=0, keepdims=True)


def upper_level(dims, ways, picked, tile_index, tile_count, sources, tiles, bands, came):
    n_row, n_col, slots, rows = dims
    return pl.pallas_call(
        functools.partial(upper_kernel, dims, ways, picked),
        out_shape=piece(n_col, 1, LANES),
        in_specs=[in_smem()] * 3 + [in_vmem()] * (2 + len(bands)),
        out_specs=in_vmem(),
        scratch_shapes=[
            pltpu.VMEM((n_col * rows, LANES, LANES), jnp.float32),
            pltpu.VMEM((n_col * rows, LANES, LANES), jnp.float32),
            pltpu.VMEM((n_row, rows, LANES), jnp.float32),
        ],
        compiler_params=params(),
        name="upper_level",
    )(tile_index, tile_count, sources, tiles, *bands, came)


def merge_arrays(parts):
    best = jnp.min(parts[:, ..., 0, :, :], axis=0)
    hit = parts[..., 0, :, :] == best[None]
    return jnp.stack([best, jnp.sum(jnp.where(hit, parts[..., 1, :, :], 0.0), axis=0)], axis=-3)


def mine(parts, axis, at):
    return lax.dynamic_index_in_dim(parts, lax.axis_index(axis), at, keepdims=False)


def all_to_all(value, axes):
    return lax.all_to_all(value, axes, split_axis=0, concat_axis=0, tiled=True)


def per_device(tiles, tile_index, tile_count, sources):
    slots = tiles.shape[0]
    rows = sources.shape[0]
    n_row = lax.axis_size("row")
    n_col = lax.axis_size("col")
    dims = (n_row, n_col, slots, rows)
    both = ("row", "col")
    direct = n_row * n_col <= 16
    given = (tile_index, tile_count, sources, tiles)
    row_ways, col_ways = (n_row, n_col) if direct else (1, 1)

    firsts = first_level(dims, tile_index, sources, tiles)
    if direct:
        came = lax.all_gather(firsts, both)
    else:
        own = jnp.min(mine(lax.all_gather(firsts, "row"), "row", 1), axis=0)
        came = lax.all_gather(own, "col")
    for level_no in range(1, LEVELS):
        last = level_no == LEVELS - 1
        copies = n_col if direct and not last else 1
        outs = relax_level(
            dims, row_ways, level_no > 1, direct and level_no == 1, copies, *given, came
        )
        if not last:
            if direct:
                came = all_to_all(outs, both)
            else:
                own = merge_arrays(mine(lax.all_gather(outs, "row"), "row", 1))
                came = lax.all_gather(own, "col")
    if direct:
        low_came = lax.all_gather(outs, both)
        row_came = low_came
    else:
        low_came = merge_arrays(lax.all_gather(outs, "row"))
        row_came = lax.all_gather(mine(low_came, "row", 0), "col")
    lower = lower_level(dims, row_ways, direct, n_row if direct else 1, *given, row_came, low_came)
    sums, shown, own_paths, bands = lower[0], lower[1], lower[2], lower[3:]
    if direct:
        came = all_to_all(sums, both)
    else:
        own = jnp.sum(mine(lax.all_gather(sums, "col"), "col", 1), axis=0)
        came = lax.all_gather(own, "row")
    terms = upper_level(dims, col_ways, False, *given, bands, came)
    total = jnp.sum(all_to_all(terms, "col"), axis=(0, 1))
    return shown, own_paths, total / rows


def solution(mesh):
    in_specs = (
        P(("groups", "row", "col"), None, None),
        P(("groups", "row", "col"), None),
        P(("groups", "row", "col")),
        P("groups"),
    )
    out_specs = (
        P("groups", ("row", "col")),
        P("groups", ("row", "col")),
        P(("groups", "row", "col")),
    )
    return jax.shard_map(
        per_device, mesh=mesh, in_specs=in_specs, out_specs=out_specs, check_vma=False
    )
```

```python
import functools

import jax
import jax.numpy as jnp
from jax import lax
from jax.experimental import pallas as pl
from jax.experimental.pallas import tpu as pltpu
from jax.sharding import PartitionSpec as P

LEVELS = 3
BACK = 2
LANES = 128
SUB = 8

far_value = 1000000.0
no_edge = 2000000.0
vmem_limit = 48 * 1024 * 1024


def in_vmem():
    return pl.BlockSpec(memory_space=pltpu.VMEM)


def in_smem():
    return pl.BlockSpec(memory_space=pltpu.SMEM)


def piece(*shape):
    return jax.ShapeDtypeStruct(shape, jnp.float32)


def params():
    return pltpu.CompilerParams(vmem_limit_bytes=vmem_limit)


def edges(raw):
    return jnp.where(raw > 0, raw, no_edge)


def fold(block):
    return block.reshape(block.shape[0] // SUB, SUB, LANES)


def source_ids(sources_ref, rows):
    lane_row = lax.broadcasted_iota(jnp.int32, (rows, LANES), 0)
    ids = jnp.zeros((rows, LANES), jnp.int32)
    for s in range(rows):
        ids = jnp.where(lane_row == s, sources_ref[s], ids)
    return ids


def is_source(ids, block):
    lane = lax.broadcasted_iota(jnp.int32, ids.shape, 1)
    return ids == block * LANES + lane


def settle(found_dist, found_count, at_source):
    dist = jnp.where(at_source, 0.0, jnp.minimum(found_dist, far_value))
    count = jnp.where(found_dist == dist, found_count, 0.0)
    return dist, jnp.where(at_source, 1.0, 0.0) + count


def merge(pairs):
    best = functools.reduce(jnp.minimum, [p[0] for p in pairs])
    total = functools.reduce(jnp.add, [jnp.where(p[0] == best, p[1], 0.0) for p in pairs])
    return best, total


def spread(block):
    rows = block.shape[0]
    turned = block.T
    return [jnp.broadcast_to(turned[:, s : s + 1], (LANES, LANES)) for s in range(rows)]


def partner(at, step, size):
    if size & (size - 1) == 0:
        return at ^ step
    return (step + size - at) % size if isinstance(at, int) else lax.rem(step + size - at, size)


def first_kernel(dims, tile_index, sources, tiles, *rest):
    n_row, n_col, slots, rows = dims
    outs, slot_of, lines, sem = rest[:n_row], rest[n_row], rest[n_row + 1], rest[n_row + 2]
    my_row = lax.axis_index("row")

    def clear(at, _):
        slot_of[at] = -1
        return 0

    lax.fori_loop(0, n_row * n_col, clear, 0)
    for g in range(slots):
        slot_of[tile_index[0, g] * n_row + tile_index[1, g]] = g
    lines[...] = jnp.zeros(lines.shape, jnp.float32)

    def each(act):
        for s in range(rows):
            vertex = sources[s]
            block, place = vertex // LANES, lax.rem(vertex, LANES)
            r = lax.rem(block, n_col)

            @pl.when(block // n_col == my_row)
            def _():
                for step in range(n_row):
                    g = slot_of[r * n_row + partner(my_row, step, n_row)]

                    @pl.when(g >= 0)
                    def _():
                        source = tiles.at[g, pl.ds(place, 1), :]
                        line = lines.at[step, pl.ds(s, 1), :]
                        act(pltpu.make_async_copy(source, line, sem.at[step, s]))

    each(lambda copy: copy.start())
    each(lambda copy: copy.wait())
    for step in range(n_row):
        line = lines[step]
        outs[step][...] = jnp.where(line > 0, line, far_value)


def first_level(dims, tile_index, sources, tiles):
    n_row, n_col, slots, rows = dims
    return pl.pallas_call(
        functools.partial(first_kernel, dims),
        out_shape=[piece(rows, LANES)] * n_row,
        in_specs=[in_smem(), in_smem(), pl.BlockSpec(memory_space=pl.ANY)],
        out_specs=[in_vmem()] * n_row,
        scratch_shapes=[
            pltpu.SMEM((n_row * n_col,), jnp.int32),
            pltpu.VMEM((n_row, rows, LANES), jnp.float32),
            pltpu.SemaphoreType.DMA((n_row, rows)),
        ],
        compiler_params=params(),
        name="first_level",
    )(tile_index, sources, tiles)


def merge_kernel(ways, counted, *refs):
    parts, out = refs[:ways], refs[ways]
    if counted:
        best, total = merge([(part[0], part[1]) for part in parts])
        out[0] = best
        out[1] = total
    else:
        out[...] = functools.reduce(jnp.minimum, [part[...] for part in parts])


def merge_shares(parts, counted):
    return pl.pallas_call(
        functools.partial(merge_kernel, len(parts), counted),
        out_shape=piece(*parts[0].shape),
        in_specs=[in_vmem()] * len(parts),
        out_specs=in_vmem(),
        name="merge_shares",
    )(*parts)


def relax_kernel(dims, counted, whole, *refs):
    n_row, n_col, slots, rows = dims
    tile_index, tile_count, sources, tiles = refs[:4]
    came, refs = refs[4 : 4 + n_col], refs[4 + n_col :]
    outs, refs = (refs[:1], refs[1:]) if whole else (refs[:n_row], refs[n_row:])
    wide_dist, wide_count, acc, best_of = refs
    my_row = lax.axis_index("row")
    my_col = lax.axis_index("col")
    ids = source_ids(sources, rows)
    for step in range(n_col):
        r = partner(my_col, step, n_col)
        at_source = is_source(ids, my_row * n_col + r)
        if counted:
            found, count = came[step][0], came[step][1]
        else:
            found = came[step][...]
            count = jnp.where(found < far_value, 1.0, 0.0)
        dist, count = settle(found, count, at_source)
        for s, block in enumerate(spread(dist)):
            wide_dist[r * rows + s] = block
        for s, block in enumerate(spread(count)):
            wide_count[r * rows + s] = block
    acc[...] = jnp.full(acc.shape, far_value, jnp.float32)
    live = tile_count[0]

    def lowest(g, _):
        r, c = tile_index[0, g], tile_index[1, g]
        weight = edges(tiles[g])
        for s in range(rows):
            reached = wide_dist[r * rows + s] + weight
            at = c * rows + s
            acc[at] = jnp.minimum(acc[at], jnp.min(fold(reached), axis=0))
        return 0

    lax.fori_loop(0, live, lowest, 0)
    for at in range(n_row * rows):
        best = jnp.min(acc[at], axis=0, keepdims=True)
        best_of[at] = jnp.broadcast_to(best, (SUB, LANES))
    acc[...] = jnp.zeros(acc.shape, jnp.float32)

    def tally(g, _):
        r, c = tile_index[0, g], tile_index[1, g]
        weight = edges(tiles[g])
        for s in range(rows):
            reached = wide_dist[r * rows + s] + weight
            at = c * rows + s
            hit = fold(reached) == best_of[at][None]
            acc[at] += jnp.sum(jnp.where(hit, fold(wide_count[r * rows + s]), 0.0), axis=0)
        return 0

    lax.fori_loop(0, live, tally, 0)
    for step in range(n_row):
        c = step if whole else partner(my_row, step, n_row)
        out = outs[0].at[c] if whole else outs[step]
        for s in range(rows):
            at = c * rows + s
            out[0, pl.ds(s, 1), :] = best_of[at, 0:1, :]
            out[1, pl.ds(s, 1), :] = jnp.sum(acc[at], axis=0, keepdims=True)


def relax_level(dims, counted, whole, tile_index, tile_count, sources, tiles, came):
    n_row, n_col, slots, rows = dims
    if whole:
        out_shape = [piece(n_row, 2, rows, LANES)]
    else:
        out_shape = [piece(2, rows, LANES)] * n_row
    return pl.pallas_call(
        functools.partial(relax_kernel, dims, counted, whole),
        out_shape=out_shape,
        in_specs=[in_smem()] * 3 + [in_vmem()] * (1 + n_col),
        out_specs=[in_vmem()] * len(out_shape),
        scratch_shapes=[
            pltpu.VMEM((n_col * rows, LANES, LANES), jnp.float32),
            pltpu.VMEM((n_col * rows, LANES, LANES), jnp.float32),
            pltpu.VMEM((n_row * rows, SUB, LANES), jnp.float32),
            pltpu.VMEM((n_row * rows, SUB, LANES), jnp.float32),
        ],
        compiler_params=params(),
        name="relax_level",
    )(tile_index, tile_count, sources, tiles, *came)


def band_kernel(dims, *refs):
    n_row, n_col, slots, rows = dims
    sources, wholes = refs[0], refs[1 : 1 + n_row]
    own, shown, own_paths, low_dist, low_paths = refs[1 + n_row :]
    my_row = lax.axis_index("row")
    my_col = lax.axis_index("col")
    ids = source_ids(sources, rows)
    for c in range(n_row):
        at_source = is_source(ids, c * n_col + my_col)
        dist, count = settle(*merge([(part[c, 0], part[c, 1]) for part in wholes]), at_source)
        low_dist[c] = dist
        low_paths[c] = count
    dist, count = low_dist[my_row], low_paths[my_row]
    own[0] = dist
    own[1] = count
    shown[...] = jnp.where(dist < 0.5 * far_value, dist, -1.0)
    own_paths[...] = count


def settle_band(dims, sources, wholes):
    n_row, n_col, slots, rows = dims
    out_shape = [
        piece(2, rows, LANES),
        piece(rows, LANES),
        piece(rows, LANES),
        piece(n_row, rows, LANES),
        piece(n_row, rows, LANES),
    ]
    return pl.pallas_call(
        functools.partial(band_kernel, dims),
        out_shape=out_shape,
        in_specs=[in_smem()] + [in_vmem()] * n_row,
        out_specs=[in_vmem()] * len(out_shape),
        name="settle_band",
    )(sources, *wholes)


def depend_kernel(dims, last, *refs):
    n_row, n_col, slots, rows = dims
    tile_index, tile_count, sources, tiles = refs[:4]
    states, refs = refs[4 : 4 + n_col], refs[4 + n_col :]
    low_dist, refs = refs[0], refs[1:]
    n_coef = n_row if last else 1
    given, refs = refs[:n_coef], refs[n_coef:]
    outs, refs = refs[:n_col], refs[n_col:]
    wide_dist, acc, coef = refs
    my_row = lax.axis_index("row")
    my_col = lax.axis_index("col")
    if last:
        for step in range(n_row):
            coef[partner(my_row, step, n_row)] = given[step][...]
    else:
        count = given[0][...]
        coef[...] = jnp.where(count > 0.5, 1.0 / jnp.maximum(count, 1.0), 0.0)
    for step in range(n_col):
        r = partner(my_col, step, n_col)
        for s, block in enumerate(spread(states[step][0])):
            wide_dist[r * rows + s] = block
    acc[...] = jnp.zeros(acc.shape, jnp.float32)

    def gather(g, _):
        r, c = tile_index[0, g], tile_index[1, g]
        weight = edges(tiles[g])
        for s in range(rows):
            reached = wide_dist[r * rows + s] + weight
            hit = reached == low_dist[c, pl.ds(s, 1), :]
            acc[r * rows + s] += jnp.where(hit, coef[c, pl.ds(s, 1), :], 0.0)
        return 0

    lax.fori_loop(0, tile_count[0], gather, 0)
    lane = lax.broadcasted_iota(jnp.int32, (LANES, LANES), 1)
    ids = source_ids(sources, rows)
    for step in range(n_col):
        r = partner(my_col, step, n_col)
        turned = jnp.zeros((LANES, LANES), jnp.float32)
        for s in range(rows):
            total = jnp.sum(acc[r * rows + s], axis=1, keepdims=True)
            turned = jnp.where(lane == s, total, turned)
        sums = turned.T[:rows]
        if last:
            term = jnp.where(is_source(ids, my_row * n_col + r), 0.0, states[step][1] * sums)
            outs[step][...] = jnp.sum(term, axis=0, keepdims=True)
        else:
            outs[step][...] = sums


def depend_level(dims, last, tile_index, tile_count, sources, tiles, states, low_dist, given):
    n_row, n_col, slots, rows = dims
    out_shape = [piece(1 if last else rows, LANES)] * n_col
    return pl.pallas_call(
        functools.partial(depend_kernel, dims, last),
        out_shape=out_shape,
        in_specs=[in_smem()] * 3 + [in_vmem()] * (2 + len(states) + len(given)),
        out_specs=[in_vmem()] * n_col,
        scratch_shapes=[
            pltpu.VMEM((n_col * rows, LANES, LANES), jnp.float32),
            pltpu.VMEM((n_col * rows, LANES, LANES), jnp.float32),
            pltpu.VMEM((n_row, rows, LANES), jnp.float32),
        ],
        compiler_params=params(),
        name="depend_level",
    )(tile_index, tile_count, sources, tiles, *states, low_dist, *given)


def coef_kernel(ways, *refs):
    own, parts, out = refs[0], refs[1 : 1 + ways], refs[1 + ways]
    count = own[1]
    dependency = count * functools.reduce(jnp.add, [part[...] for part in parts])
    out[...] = jnp.where(count > 0.5, (1.0 + dependency) / jnp.maximum(count, 1.0), 0.0)


def coefficient(own, parts):
    return pl.pallas_call(
        functools.partial(coef_kernel, len(parts)),
        out_shape=piece(*parts[0].shape),
        in_specs=[in_vmem()] * (1 + len(parts)),
        out_specs=in_vmem(),
        name="coefficient",
    )(own, *parts)


def swap(value, axis, step):
    if step == 0 and lax.axis_size(axis) & (lax.axis_size(axis) - 1) == 0:
        return value
    size = lax.axis_size(axis)
    return lax.ppermute(value, axis, [(at, partner(at, step, size)) for at in range(size)])


def swap_pieces(parts, axis):
    return [swap(part, axis, step) for step, part in enumerate(parts)]


def spread_piece(part, axis):
    return [swap(part, axis, step) for step in range(lax.axis_size(axis))]


def per_device(tiles, tile_index, tile_count, sources):
    slots = tiles.shape[0]
    rows = sources.shape[0]
    dims = (lax.axis_size("row"), lax.axis_size("col"), slots, rows)
    places = tile_index.T
    given = (places, tile_count, sources, tiles)

    outs = first_level(dims, places, sources, tiles)
    for level_no in range(1, LEVELS):
        own = merge_shares(swap_pieces(outs, "row"), level_no > 1)
        came = spread_piece(own, "col")
        outs = relax_level(dims, level_no > 1, level_no == LEVELS - 1, *given, came)
    wholes = spread_piece(outs[0], "row")
    own, shown, own_paths, low_dist, low_paths = settle_band(dims, sources, wholes)
    states = spread_piece(own, "col")
    sums = depend_level(dims, False, *given, states, low_dist, [low_paths])
    for back_no in range(1, BACK):
        coef = coefficient(own, swap_pieces(sums, "col"))
        last = back_no == BACK - 1
        sums = depend_level(dims, last, *given, states, low_dist, spread_piece(coef, "row"))
    total = functools.reduce(jnp.add, swap_pieces(sums, "col"))
    return shown, own_paths, total.reshape(LANES) / rows


def solution(mesh):
    in_specs = (
        P(("groups", "row", "col"), None, None),
        P(("groups", "row", "col"), None),
        P(("groups", "row", "col")),
        P("groups"),
    )
    out_specs = (
        P("groups", ("row", "col")),
        P("groups", ("row", "col")),
        P(("groups", "row", "col")),
    )
    return jax.shard_map(
        per_device, mesh=mesh, in_specs=in_specs, out_specs=out_specs, check_vma=False
    )
```

```python
import functools

import jax
import jax.numpy as jnp
from jax import lax
from jax.experimental import pallas as pl
from jax.experimental.pallas import tpu as pltpu
from jax.sharding import PartitionSpec as P

LEVELS = 3
BACK = 2
LANES = 128
SUB = 8
PAIR = 2

far_value = 1000000.0
no_edge = 2000000.0
large_limit = 8 * 1024 * 1024
small_limit = 2 * 1024 * 1024


def in_vmem():
    return pl.BlockSpec(memory_space=pltpu.VMEM)


def in_smem():
    return pl.BlockSpec(memory_space=pltpu.SMEM)


def piece(*shape):
    return jax.ShapeDtypeStruct(shape, jnp.float32)


def params(limit):
    return pltpu.CompilerParams(vmem_limit_bytes=limit)


def partner(at, step, size):
    if size & (size - 1) == 0:
        return at ^ step
    return (step + size - at) % size if isinstance(at, int) else lax.rem(step + size - at, size)


def is_dense(dims):
    return dims[2] == dims[0] * dims[1]


def position():
    my_row = lax.axis_index("row")
    return my_row // PAIR, lax.rem(my_row, PAIR), lax.axis_index("col")


def source_ids(sources, first, half):
    row = lax.broadcasted_iota(jnp.int32, (half, LANES), 0)
    ids = jnp.zeros((half, LANES), jnp.int32)
    for s in range(half):
        ids = jnp.where(row == s, sources[first + s], ids)
    return ids


def is_source(ids, block):
    return ids == block * LANES + lax.broadcasted_iota(jnp.int32, ids.shape, 1)


def settle(found_dist, found_count, at_source):
    dist = jnp.where(at_source, 0.0, jnp.minimum(found_dist, far_value))
    count = jnp.where(found_dist == dist, found_count, 0.0)
    return dist, jnp.where(at_source, 1.0, 0.0) + count


def merge(pairs):
    best = functools.reduce(jnp.minimum, [p[0] for p in pairs])
    total = functools.reduce(jnp.add, [jnp.where(p[0] == best, p[1], 0.0) for p in pairs])
    return best, total


def turn_kernel(dims, places, tiles, out):
    n_row, n_col, slots, half = dims

    def turn(g, _):
        at = places[0, g] * n_row + places[1, g] if is_dense(dims) else g
        raw = tiles[g]
        out[at] = jnp.where(raw > 0, raw, no_edge).T
        return 0

    lax.fori_loop(0, slots, turn, 0)


def turn_tiles(dims, places, tiles):
    return pl.pallas_call(
        functools.partial(turn_kernel, dims),
        out_shape=piece(*tiles.shape),
        in_specs=[in_smem(), in_vmem()],
        out_specs=in_vmem(),
        compiler_params=params(large_limit),
        name="turn_tiles",
    )(places, tiles)


def first_kernel(dims, places, sources, tiles, *rest):
    n_row, n_col, slots, half = dims
    chips = n_row // PAIR
    mine, theirs = rest[:chips], rest[chips]
    slot_of, lines, sems = rest[chips + 1 :]
    my_row = lax.axis_index("row")
    my_x, my_core, my_col = position()

    def clear(at, _):
        slot_of[at] = -1
        return 0

    lax.fori_loop(0, n_row * n_col, clear, 0)
    for g in range(slots):
        slot_of[places[0, g] * n_row + places[1, g]] = g
    lines[...] = jnp.zeros(lines.shape, jnp.float32)

    def each(act):
        for s in range(PAIR * half):
            vertex = sources[s]
            block, place = vertex // LANES, lax.rem(vertex, LANES)
            r = lax.rem(block, n_col)
            other = (s // half) ^ my_core

            @pl.when(block // n_col == my_row)
            def _():
                for step in range(chips):
                    for h in range(PAIR):
                        g = slot_of[r * n_row + PAIR * partner(my_x, step, chips) + h]

                        @pl.when(g >= 0)
                        def _():
                            source = tiles.at[g, pl.ds(place, 1), :]
                            line = lines.at[other, step, h, pl.ds(s % half, 1), :]
                            act(pltpu.make_async_copy(source, line, sems.at[step, h, s]))

    each(lambda copy: copy.start())
    each(lambda copy: copy.wait())
    for step in range(chips):
        mine[step][...] = jnp.where(lines[0, step] > 0, lines[0, step], far_value)
    theirs[...] = jnp.where(lines[1] > 0, lines[1], far_value)


def first_level(dims, places, sources, tiles):
    n_row, n_col, slots, half = dims
    chips = n_row // PAIR
    out_shape = [piece(PAIR, half, LANES)] * chips + [piece(chips, PAIR, half, LANES)]
    return pl.pallas_call(
        functools.partial(first_kernel, dims),
        out_shape=out_shape,
        in_specs=[in_smem(), in_smem(), pl.BlockSpec(memory_space=pl.ANY)],
        out_specs=[in_vmem()] * len(out_shape),
        scratch_shapes=[
            pltpu.SMEM((n_row * n_col,), jnp.int32),
            pltpu.VMEM((PAIR, chips, PAIR, half, LANES), jnp.float32),
            pltpu.SemaphoreType.DMA((chips, PAIR, PAIR * half)),
        ],
        compiler_params=params(small_limit),
        name="first_level",
    )(places, sources, tiles)


def merge_kernel(ways, half, *refs):
    parts, out = refs[:ways], refs[ways]
    for h in range(PAIR):
        best, total = merge([(part[h, :half], part[h, half:]) for part in parts])
        out[h, :half] = best
        out[h, half:] = total


def merge_shares(dims, parts):
    return pl.pallas_call(
        functools.partial(merge_kernel, len(parts), dims[3]),
        out_shape=piece(*parts[0].shape),
        in_specs=[in_vmem()] * len(parts),
        out_specs=in_vmem(),
        compiler_params=params(small_limit),
        name="merge_shares",
    )(*parts)


def list_slots(dims, places, table, filled):
    n_row, n_col, slots, half = dims
    if is_dense(dims):
        return

    def clear(at, _):
        filled[at] = 0
        return 0

    lax.fori_loop(0, PAIR * n_row, clear, 0)
    for k in range(PAIR):

        def enter(g, _):
            at = k * n_row + places[k][1, g]
            table[at * n_col + filled[at]] = g
            filled[at] += 1
            return 0

        lax.fori_loop(0, slots, enter, 0)


def over_slots(dims, places, table, filled, c, step, carry):
    n_row, n_col, slots, half = dims
    for k in range(PAIR):
        if is_dense(dims):
            for r in range(n_col):
                carry = step(k, r * n_row + c, k * n_col + r, carry)
        else:
            at = k * n_row + c

            def entry(e, carry):
                g = table[at * n_col + e]
                return step(k, g, k * n_col + places[k][0, g], carry)

            carry = lax.fori_loop(0, filled[at], entry, carry)
    return carry


def slot_scratch(dims):
    n_row, n_col, slots, half = dims
    return [
        pltpu.SMEM((PAIR * n_row * n_col,), jnp.int32),
        pltpu.SMEM((PAIR * n_row,), jnp.int32),
    ]


def relax_kernel(dims, counted, whole, *refs):
    n_row, n_col, slots, half = dims
    chips = n_row // PAIR
    n_places = 0 if is_dense(dims) else PAIR
    places, refs = refs[:n_places], refs[n_places:]
    sources, tiles, refs = refs[0], refs[1 : 1 + PAIR], refs[1 + PAIR :]
    came, refs = refs[:n_col], refs[n_col:]
    n_out = 1 if whole else chips
    outs, refs = refs[:n_out], refs[n_out:]
    near, found, table, filled = refs
    my_x, my_core, my_col = position()
    ids = source_ids(sources, my_core * half, half)
    list_slots(dims, places, table, filled)
    for step in range(n_col):
        r = partner(my_col, step, n_col)
        for k in range(PAIR):
            h = my_core ^ k
            at_source = is_source(ids, (PAIR * my_x + h) * n_col + r)
            block = came[step][h]
            reached = block[:half]
            if counted:
                count = block[half:]
            else:
                count = jnp.where(reached < far_value, 1.0, 0.0)
            dist, count = settle(reached, count, at_source)
            near[k * n_col + r, :half, :] = dist
            near[k * n_col + r, half:, :] = count
    lane = lax.broadcasted_iota(jnp.int32, (LANES, LANES), 1)

    def column(c, _):
        def lowest(s):
            def step(k, g, b, carry):
                return jnp.minimum(carry, tiles[k][g] + near[b, pl.ds(s, 1), :])

            start = jnp.full((LANES, LANES), far_value, jnp.float32)
            reached = over_slots(dims, places, table, filled, c, step, start)
            return jnp.min(reached, axis=1, keepdims=True)

        def tally(s, best):
            def step(k, g, b, carry):
                hit = tiles[k][g] + near[b, pl.ds(s, 1), :] == best
                return carry + jnp.where(hit, near[b, pl.ds(half + s, 1), :], 0.0)

            start = jnp.zeros((LANES, LANES), jnp.float32)
            counts = over_slots(dims, places, table, filled, c, step, start)
            return jnp.sum(counts, axis=1, keepdims=True)

        turned = jnp.zeros((LANES, LANES), jnp.float32)
        best = lowest(0)
        for s in range(half):
            later = lowest(s + 1) if s + 1 < half else None
            total = tally(s, best)
            turned = jnp.where(lane == s, best, jnp.where(lane == half + s, total, turned))
            best = later
        found[c] = turned.T[: 2 * half]
        return 0

    lax.fori_loop(0, n_row, column, 0)
    if whole:
        outs[0][...] = found[...]
    else:
        for step in range(chips):
            for h in range(PAIR):
                outs[step][h] = found[PAIR * partner(my_x, step, chips) + h]


def relax_level(dims, counted, whole, places, sources, tiles, came):
    n_row, n_col, slots, half = dims
    if whole:
        out_shape = [piece(n_row, 2 * half, LANES)]
    else:
        out_shape = [piece(PAIR, 2 * half, LANES)] * (n_row // PAIR)
    return pl.pallas_call(
        functools.partial(relax_kernel, dims, counted, whole),
        out_shape=out_shape,
        in_specs=[in_smem()] * (len(places) + 1) + [in_vmem()] * (PAIR + n_col),
        out_specs=[in_vmem()] * len(out_shape),
        scratch_shapes=[
            pltpu.VMEM((PAIR * n_col, 2 * half, LANES), jnp.float32),
            pltpu.VMEM((n_row, 2 * half, LANES), jnp.float32),
        ]
        + slot_scratch(dims),
        compiler_params=params(large_limit),
        name="relax_level",
    )(*places, sources, *tiles, *came)


def band_kernel(dims, *refs):
    n_row, n_col, slots, half = dims
    chips = n_row // PAIR
    sources, wholes = refs[0], refs[1 : 1 + chips]
    low, own, own_count, keep, give = refs[1 + chips :]
    my_x, my_core, my_col = position()
    ids = source_ids(sources, my_core * half, half)
    for c in range(n_row):
        at_source = is_source(ids, c * n_col + my_col)
        pairs = [(part[c, :half], part[c, half:]) for part in wholes]
        dist, count = settle(*merge(pairs), at_source)
        low[c, :half] = dist
        low[c, half:] = count
    for h in range(PAIR):
        block = low[PAIR * my_x + h]
        own[h] = block
        own_count[pl.ds(h * half, half), :] = block[half:]
    keep[...] = low[PAIR * my_x + my_core]
    give[...] = low[PAIR * my_x + 1 - my_core]


def settle_band(dims, sources, wholes):
    n_row, n_col, slots, half = dims
    out_shape = [
        piece(n_row, 2 * half, LANES),
        piece(PAIR, 2 * half, LANES),
        piece(PAIR * half, LANES),
        piece(2 * half, LANES),
        piece(2 * half, LANES),
    ]
    return pl.pallas_call(
        functools.partial(band_kernel, dims),
        out_shape=out_shape,
        in_specs=[in_smem()] + [in_vmem()] * len(wholes),
        out_specs=[in_vmem()] * len(out_shape),
        compiler_params=params(small_limit),
        name="settle_band",
    )(sources, *wholes)


def show_kernel(half, keep, came, shown, paths):
    my_x, my_core, my_col = position()
    for core in range(PAIR):
        block = jnp.where(my_core == core, keep[...], came[...])
        dist = block[:half]
        shown[pl.ds(core * half, half), :] = jnp.where(dist < 0.5 * far_value, dist, -1.0)
        paths[pl.ds(core * half, half), :] = block[half:]


def show_block(dims, keep, came):
    half = dims[3]
    return pl.pallas_call(
        functools.partial(show_kernel, half),
        out_shape=[piece(PAIR * half, LANES)] * 2,
        in_specs=[in_vmem()] * 2,
        out_specs=[in_vmem()] * 2,
        compiler_params=params(small_limit),
        name="show_block",
    )(keep, came)


def depend_kernel(dims, first, last, *refs):
    n_row, n_col, slots, half = dims
    chips = n_row // PAIR
    n_places = 0 if is_dense(dims) else PAIR
    places, refs = refs[:n_places], refs[n_places:]
    sources, tiles, refs = refs[0], refs[1 : 1 + PAIR], refs[1 + PAIR :]
    states, low, refs = refs[:n_col], refs[n_col], refs[n_col + 1 :]
    n_coef = 0 if first else chips
    coefs, refs = refs[:n_coef], refs[n_coef:]
    outs, refs = refs[:n_col], refs[n_col:]
    near, lower, acc, table, filled = refs
    my_x, my_core, my_col = position()
    list_slots(dims, places, table, filled)
    for step in range(n_col):
        r = partner(my_col, step, n_col)
        for k in range(PAIR):
            near[k * n_col + r] = states[step][my_core ^ k]
    if first:
        for c in range(n_row):
            count = low[c, half:]
            lower[c, :half, :] = low[c, :half]
            lower[c, half:, :] = jnp.where(count > 0.5, 1.0 / jnp.maximum(count, 1.0), 0.0)
    else:
        for step in range(chips):
            for h in range(PAIR):
                c = PAIR * partner(my_x, step, chips) + h
                lower[c, :half, :] = low[c, :half]
                lower[c, half:, :] = coefs[step][pl.ds(h * half, half), :]
    acc[...] = jnp.zeros(acc.shape, jnp.float32)

    def column(c, _):
        turned = lower[c].T
        for s in range(half):
            dist = jnp.broadcast_to(turned[:, s : s + 1], (LANES, LANES))
            coef = jnp.broadcast_to(turned[:, half + s : half + s + 1], (LANES, LANES))

            def step(k, g, b, carry):
                hit = tiles[k][g] + near[b, pl.ds(s, 1), :] == dist
                terms = jnp.where(hit, coef, 0.0).reshape(LANES // SUB, SUB, LANES)
                acc[b, s] += jnp.sum(terms, axis=0)
                return carry

            over_slots(dims, places, table, filled, c, step, 0)
        return 0

    lax.fori_loop(0, n_row, column, 0)
    ids = source_ids(sources, my_core * half, half)
    for step in range(n_col):
        r = partner(my_col, step, n_col)
        for k in range(PAIR):
            h = my_core ^ k
            b = k * n_col + r
            if last:
                sums = jnp.sum(acc[b], axis=1)
                at_source = is_source(ids, (PAIR * my_x + h) * n_col + r)
                term = jnp.where(at_source, 0.0, near[b, half:, :] * sums)
                outs[step][pl.ds(k, 1), :] = jnp.sum(term, axis=0, keepdims=True)
            else:
                b = (my_core ^ k) * n_col + r
                outs[step][pl.ds(k * half, half), :] = jnp.sum(acc[b], axis=1)


def depend_level(dims, first, last, places, sources, tiles, states, low, coefs):
    n_row, n_col, slots, half = dims
    out_shape = [piece(PAIR if last else PAIR * half, LANES)] * n_col
    vectors = PAIR + len(states) + 1 + len(coefs)
    return pl.pallas_call(
        functools.partial(depend_kernel, dims, first, last),
        out_shape=out_shape,
        in_specs=[in_smem()] * (len(places) + 1) + [in_vmem()] * vectors,
        out_specs=[in_vmem()] * n_col,
        scratch_shapes=[
            pltpu.VMEM((PAIR * n_col, 2 * half, LANES), jnp.float32),
            pltpu.VMEM((n_row, 2 * half, LANES), jnp.float32),
            pltpu.VMEM((PAIR * n_col, half, SUB, LANES), jnp.float32),
        ]
        + slot_scratch(dims),
        compiler_params=params(large_limit),
        name="depend_level",
    )(*places, sources, *tiles, *states, low, *coefs)


def swap_col(value, step):
    size = lax.axis_size("col")
    if step == 0 and size & (size - 1) == 0:
        return value
    return lax.ppermute(value, "col", [(at, partner(at, step, size)) for at in range(size)])


def swap_chip(value, step):
    size = lax.axis_size("row")
    chips = size // PAIR
    if step == 0 and chips & (chips - 1) == 0:
        return value
    pairs = [(at, PAIR * partner(at // PAIR, step, chips) + at % PAIR) for at in range(size)]
    return lax.ppermute(value, "row", pairs)


def swap_core(value):
    return lax.ppermute(value, "row", [(at, at ^ 1) for at in range(lax.axis_size("row"))])


def spread_col(value):
    return [swap_col(value, step) for step in range(lax.axis_size("col"))]


def spread_chip(value):
    return [swap_chip(value, step) for step in range(lax.axis_size("row") // PAIR)]


def per_device(tiles, tile_index, tile_count, sources):
    slots = tiles.shape[0]
    rows = sources.shape[0]
    dims = (lax.axis_size("row"), lax.axis_size("col"), slots, rows // PAIR)
    own_places = tile_index.T

    firsts = first_level(dims, own_places, sources, tiles)
    theirs = swap_core(firsts[-1])
    shares = [jnp.minimum(part, theirs[step]) for step, part in enumerate(firsts[:-1])]
    turned = turn_tiles(dims, own_places, tiles)
    both = [turned, swap_core(turned)]
    places = [] if is_dense(dims) else [own_places, swap_core(own_places)]
    own = functools.reduce(jnp.minimum, [swap_chip(part, t) for t, part in enumerate(shares)])
    for level_no in range(1, LEVELS):
        if level_no > 1:
            own = merge_shares(dims, [swap_chip(part, t) for t, part in enumerate(outs)])
        whole = level_no == LEVELS - 1
        outs = relax_level(dims, level_no > 1, whole, places, sources, both, spread_col(own))
    low, own, own_count, keep, give = settle_band(dims, sources, spread_chip(outs[0]))
    states = spread_col(own)
    shown, paths = show_block(dims, keep, swap_core(give))
    coefs = []
    for back_no in range(BACK):
        first, last = back_no == 0, back_no == BACK - 1
        outs = depend_level(dims, first, last, places, sources, both, states, low, coefs)
        total = functools.reduce(jnp.add, [swap_col(part, t) for t, part in enumerate(outs)])
        if not last:
            coef = (1.0 + own_count * total) / jnp.maximum(own_count, 1.0)
            coefs = spread_chip(jnp.where(own_count > 0.5, coef, 0.0))
    centrality = (total[0] + swap_core(total[1:])[0]) / rows
    return shown, paths, centrality


def solution(mesh):
    in_specs = (
        P(("groups", "row", "col"), None, None),
        P(("groups", "row", "col"), None),
        P(("groups", "row", "col")),
        P("groups"),
    )
    out_specs = (
        P("groups", ("row", "col")),
        P("groups", ("row", "col")),
        P(("groups", "row", "col")),
    )
    return jax.shard_map(
        per_device, mesh=mesh, in_specs=in_specs, out_specs=out_specs, check_vma=False
    )
```

```python
import functools

import jax
import jax.numpy as jnp
from jax import lax
from jax.experimental import pallas as pl
from jax.experimental.pallas import tpu as pltpu
from jax.sharding import PartitionSpec as P

LEVELS = 3
BACK = 2
LANES = 128
SUB = 8
PAIR = 2

far_value = 1000000.0
no_edge = 2000000.0
large_limit = 8 * 1024 * 1024
small_limit = 2 * 1024 * 1024


def in_vmem():
    return pl.BlockSpec(memory_space=pltpu.VMEM)


def in_smem():
    return pl.BlockSpec(memory_space=pltpu.SMEM)


def piece(*shape):
    return jax.ShapeDtypeStruct(shape, jnp.float32)


def params(limit):
    return pltpu.CompilerParams(vmem_limit_bytes=limit)


def is_dense(dims):
    return dims[2] == dims[0] * dims[1]


def position():
    return lax.axis_index("chip"), lax.axis_index("core"), lax.axis_index("col")


def source_ids(sources, first, half):
    row = lax.broadcasted_iota(jnp.int32, (half, LANES), 0)
    ids = jnp.zeros((half, LANES), jnp.int32)
    for s in range(half):
        ids = jnp.where(row == s, sources[first + s], ids)
    return ids


def is_source(ids, block):
    return ids == block * LANES + lax.broadcasted_iota(jnp.int32, ids.shape, 1)


def settle(found_dist, found_count, at_source):
    dist = jnp.where(at_source, 0.0, jnp.minimum(found_dist, far_value))
    count = jnp.where(found_dist == dist, found_count, 0.0)
    return dist, jnp.where(at_source, 1.0, 0.0) + count


def merge(pairs):
    best = functools.reduce(jnp.minimum, [p[0] for p in pairs])
    total = functools.reduce(jnp.add, [jnp.where(p[0] == best, p[1], 0.0) for p in pairs])
    return best, total


def turn_kernel(dims, places, tiles, out):
    n_row, n_col, slots, half = dims

    def turn(g, _):
        at = places[0, g] * n_row + places[1, g] if is_dense(dims) else g
        raw = tiles[g]
        out[at] = jnp.where(raw > 0, raw, no_edge).T
        return 0

    lax.fori_loop(0, slots, turn, 0)


def turn_tiles(dims, places, tiles):
    return pl.pallas_call(
        functools.partial(turn_kernel, dims),
        out_shape=piece(*tiles.shape),
        in_specs=[in_smem(), in_vmem()],
        out_specs=in_vmem(),
        compiler_params=params(large_limit),
        name="turn_tiles",
    )(places, tiles)


def first_kernel(dims, places, sources, tiles, out, slot_of, lines, sems):
    n_row, n_col, slots, half = dims
    my_x, my_core, my_col = position()
    my_row = my_x * PAIR + my_core

    def clear(at, _):
        slot_of[at] = -1
        return 0

    lax.fori_loop(0, n_row * n_col, clear, 0)
    for g in range(slots):
        slot_of[places[0, g] * n_row + places[1, g]] = g
    lines[...] = jnp.zeros(lines.shape, jnp.float32)

    def each(act):
        for s in range(PAIR * half):
            vertex = sources[s]
            block, place = vertex // LANES, lax.rem(vertex, LANES)
            r = lax.rem(block, n_col)

            @pl.when(block // n_col == my_row)
            def _():
                for c in range(n_row):
                    g = slot_of[r * n_row + c]

                    @pl.when(g >= 0)
                    def _():
                        source = tiles.at[g, pl.ds(place, 1), :]
                        line = c % PAIR * half + s % half
                        target = lines.at[c // PAIR, s // half, pl.ds(line, 1), :]
                        act(pltpu.make_async_copy(source, target, sems.at[c, s]))

    each(lambda copy: copy.start())
    each(lambda copy: copy.wait())
    for chip in range(n_row // PAIR):
        for core in range(PAIR):
            line = lines[chip, core]
            line = jnp.where(line > 0, line, far_value)
            for col in range(n_col):
                out[(chip * PAIR + core) * n_col + col] = line


def first_level(dims, places, sources, tiles):
    n_row, n_col, slots, half = dims
    return pl.pallas_call(
        functools.partial(first_kernel, dims),
        out_shape=piece(n_row * n_col, PAIR * half, LANES),
        in_specs=[in_smem(), in_smem(), pl.BlockSpec(memory_space=pl.ANY)],
        out_specs=in_vmem(),
        scratch_shapes=[
            pltpu.SMEM((n_row * n_col,), jnp.int32),
            pltpu.VMEM((n_row // PAIR, PAIR, PAIR * half, LANES), jnp.float32),
            pltpu.SemaphoreType.DMA((n_row, PAIR * half)),
        ],
        compiler_params=params(small_limit),
        name="first_level",
    )(places, sources, tiles)


def list_slots(dims, places, table, filled):
    n_row, n_col, slots, half = dims
    if is_dense(dims):
        return

    def clear(at, _):
        filled[at] = 0
        return 0

    lax.fori_loop(0, PAIR * n_row, clear, 0)
    for k in range(PAIR):

        def enter(g, _):
            at = k * n_row + places[k][1, g]
            table[at * n_col + filled[at]] = g
            filled[at] += 1
            return 0

        lax.fori_loop(0, slots, enter, 0)


def over_slots(dims, places, table, filled, c, step, carry):
    n_row, n_col, slots, half = dims
    for k in range(PAIR):
        if is_dense(dims):
            for r in range(n_col):
                carry = step(k, r * n_row + c, k * n_col + r, carry)
        else:
            at = k * n_row + c

            def entry(e, carry):
                g = table[at * n_col + e]
                return step(k, g, k * n_col + places[k][0, g], carry)

            carry = lax.fori_loop(0, filled[at], entry, carry)
    return carry


def slot_scratch(dims):
    n_row, n_col, slots, half = dims
    return [
        pltpu.SMEM((PAIR * n_row * n_col,), jnp.int32),
        pltpu.SMEM((PAIR * n_row,), jnp.int32),
    ]


def relax_kernel(dims, counted, whole, *refs):
    n_row, n_col, slots, half = dims
    chips = n_row // PAIR
    n_places = 0 if is_dense(dims) else PAIR
    places, refs = refs[:n_places], refs[n_places:]
    sources, tiles, refs = refs[0], refs[1 : 1 + PAIR], refs[1 + PAIR :]
    came, out, near, found, table, filled = refs
    my_x, my_core, my_col = position()
    ids = source_ids(sources, my_core * half, half)
    list_slots(dims, places, table, filled)
    for r in range(n_col):
        for k in range(PAIR):
            h = my_core ^ k
            at_source = is_source(ids, (PAIR * my_x + h) * n_col + r)
            if counted:
                blocks = [came[chip * n_col + r, h] for chip in range(chips)]
                reached, count = merge([(block[:half], block[half:]) for block in blocks])
            else:
                parts = [came[at * n_col + r, pl.ds(h * half, half), :] for at in range(n_row)]
                reached = functools.reduce(jnp.minimum, parts)
                count = jnp.where(reached < far_value, 1.0, 0.0)
            dist, count = settle(reached, count, at_source)
            near[k * n_col + r, :half, :] = dist
            near[k * n_col + r, half:, :] = count
    lane = lax.broadcasted_iota(jnp.int32, (LANES, LANES), 1)

    def column(c, _):
        def lowest(s):
            def step(k, g, b, carry):
                return jnp.minimum(carry, tiles[k][g] + near[b, pl.ds(s, 1), :])

            start = jnp.full((LANES, LANES), far_value, jnp.float32)
            reached = over_slots(dims, places, table, filled, c, step, start)
            return jnp.min(reached, axis=1, keepdims=True)

        def tally(s, best):
            def step(k, g, b, carry):
                hit = tiles[k][g] + near[b, pl.ds(s, 1), :] == best
                return carry + jnp.where(hit, near[b, pl.ds(half + s, 1), :], 0.0)

            start = jnp.zeros((LANES, LANES), jnp.float32)
            counts = over_slots(dims, places, table, filled, c, step, start)
            return jnp.sum(counts, axis=1, keepdims=True)

        turned = jnp.zeros((LANES, LANES), jnp.float32)
        best = lowest(0)
        for s in range(half):
            later = lowest(s + 1) if s + 1 < half else None
            total = tally(s, best)
            turned = jnp.where(lane == s, best, jnp.where(lane == half + s, total, turned))
            best = later
        found[c] = turned.T[: 2 * half]
        return 0

    lax.fori_loop(0, n_row, column, 0)
    for chip in range(chips):
        for col in range(n_col):
            if whole:
                out[chip * n_col + col] = found[...]
            else:
                out[chip * n_col + col] = found[pl.ds(PAIR * chip, PAIR)]


def relax_level(dims, counted, whole, places, sources, tiles, came):
    n_row, n_col, slots, half = dims
    blocks = n_row if whole else PAIR
    return pl.pallas_call(
        functools.partial(relax_kernel, dims, counted, whole),
        out_shape=piece(n_row // PAIR * n_col, blocks, 2 * half, LANES),
        in_specs=[in_smem()] * (len(places) + 1) + [in_vmem()] * (PAIR + 1),
        out_specs=in_vmem(),
        scratch_shapes=[
            pltpu.VMEM((PAIR * n_col, 2 * half, LANES), jnp.float32),
            pltpu.VMEM((n_row, 2 * half, LANES), jnp.float32),
        ]
        + slot_scratch(dims),
        compiler_params=params(large_limit),
        name="relax_level",
    )(*places, sources, *tiles, came)


def show_kernel(half, keep, came, shown, paths):
    my_x, my_core, my_col = position()
    for core in range(PAIR):
        block = jnp.where(my_core == core, keep[...], came[...])
        dist = block[:half]
        shown[pl.ds(core * half, half), :] = jnp.where(dist < 0.5 * far_value, dist, -1.0)
        paths[pl.ds(core * half, half), :] = block[half:]


def show_block(dims, keep, came):
    half = dims[3]
    return pl.pallas_call(
        functools.partial(show_kernel, half),
        out_shape=[piece(PAIR * half, LANES)] * 2,
        in_specs=[in_vmem()] * 2,
        out_specs=[in_vmem()] * 2,
        compiler_params=params(small_limit),
        name="show_block",
    )(keep, came)


def depend_kernel(dims, first, last, *refs):
    n_row, n_col, slots, half = dims
    chips = n_row // PAIR
    n_places = 0 if is_dense(dims) else PAIR
    places, refs = refs[:n_places], refs[n_places:]
    sources, tiles, refs = refs[0], refs[1 : 1 + PAIR], refs[1 + PAIR :]
    if first:
        came, out, near, low, keep, give, lower, acc, table, filled = refs
    else:
        near, low, came, out, lower, acc, table, filled = refs
    my_x, my_core, my_col = position()
    ids = source_ids(sources, my_core * half, half)
    list_slots(dims, places, table, filled)
    if first:
        for r in range(n_col):
            for k in range(PAIR):
                h = my_core ^ k
                at_source = is_source(ids, (PAIR * my_x + h) * n_col + r)
                blocks = [came[chip * n_col + r, PAIR * my_x + h] for chip in range(chips)]
                found = merge([(block[:half], block[half:]) for block in blocks])
                dist, count = settle(*found, at_source)
                near[k * n_col + r, :half, :] = dist
                near[k * n_col + r, half:, :] = count
        for c in range(n_row):
            at_source = is_source(ids, c * n_col + my_col)
            blocks = [came[chip * n_col + my_col, c] for chip in range(chips)]
            found = merge([(block[:half], block[half:]) for block in blocks])
            dist, count = settle(*found, at_source)
            low[c, :half, :] = dist
            low[c, half:, :] = count
            lower[c, :half, :] = dist
            lower[c, half:, :] = jnp.where(count > 0.5, 1.0 / jnp.maximum(count, 1.0), 0.0)
        keep[...] = near[my_col]
        give[...] = near[n_col + my_col]
    else:
        for chip in range(chips):
            parts = [came[chip * n_col + col] for col in range(n_col)]
            total = functools.reduce(jnp.add, parts)
            for h in range(PAIR):
                c = PAIR * chip + h
                count = low[c, half:, :]
                coef = (1.0 + count * total[h * half : h * half + half]) / jnp.maximum(count, 1.0)
                lower[c, :half, :] = low[c, :half, :]
                lower[c, half:, :] = jnp.where(count > 0.5, coef, 0.0)
    acc[...] = jnp.zeros(acc.shape, jnp.float32)

    def column(c, _):
        turned = lower[c].T
        for s in range(half):
            dist = jnp.broadcast_to(turned[:, s : s + 1], (LANES, LANES))
            coef = jnp.broadcast_to(turned[:, half + s : half + s + 1], (LANES, LANES))

            def step(k, g, b, carry):
                hit = tiles[k][g] + near[b, pl.ds(s, 1), :] == dist
                terms = jnp.where(hit, coef, 0.0).reshape(LANES // SUB, SUB, LANES)
                acc[b, s] += jnp.sum(terms, axis=0)
                return carry

            over_slots(dims, places, table, filled, c, step, 0)
        return 0

    lax.fori_loop(0, n_row, column, 0)
    for r in range(n_col):
        for k in range(PAIR):
            if last:
                b = k * n_col + r
                at_source = is_source(ids, (PAIR * my_x + (my_core ^ k)) * n_col + r)
                term = jnp.where(at_source, 0.0, near[b, half:, :] * jnp.sum(acc[b], axis=1))
                out[r, pl.ds(k, 1), :] = jnp.sum(term, axis=0, keepdims=True)
            else:
                sums = jnp.sum(acc[(my_core ^ k) * n_col + r], axis=1)
                for chip in range(chips):
                    out[chip * n_col + r, pl.ds(k * half, half), :] = sums


def depend_level(dims, first, last, places, sources, tiles, bands, came):
    n_row, n_col, slots, half = dims
    if last:
        out_shape = [piece(n_col, PAIR, LANES)]
    else:
        out_shape = [piece(n_row // PAIR * n_col, PAIR * half, LANES)]
    if first:
        out_shape += [
            piece(PAIR * n_col, 2 * half, LANES),
            piece(n_row, 2 * half, LANES),
            piece(2 * half, LANES),
            piece(2 * half, LANES),
        ]
    return pl.pallas_call(
        functools.partial(depend_kernel, dims, first, last),
        out_shape=out_shape,
        in_specs=[in_smem()] * (len(places) + 1) + [in_vmem()] * (PAIR + len(bands) + 1),
        out_specs=[in_vmem()] * len(out_shape),
        scratch_shapes=[
            pltpu.VMEM((n_row, 2 * half, LANES), jnp.float32),
            pltpu.VMEM((PAIR * n_col, half, SUB, LANES), jnp.float32),
        ]
        + slot_scratch(dims),
        compiler_params=params(large_limit),
        name="depend_level",
    )(*places, sources, *tiles, *bands, came)


def all_to_all(value, axes):
    return lax.all_to_all(value, axes, split_axis=0, concat_axis=0, tiled=True)


def swap_core(value):
    return lax.ppermute(value, "core", [(0, 1), (1, 0)])


def per_device(tiles, tile_index, tile_count, sources):
    slots = tiles.shape[0]
    rows = sources.shape[0]
    dims = (lax.axis_size("chip") * PAIR, lax.axis_size("col"), slots, rows // PAIR)
    own_places = tile_index.T
    line = ("chip", "col")

    firsts = first_level(dims, own_places, sources, tiles)
    firsts, tiles = lax.optimization_barrier((firsts, tiles))
    turned = turn_tiles(dims, own_places, tiles)
    both = [turned, swap_core(turned)]
    places = [] if is_dense(dims) else [own_places, swap_core(own_places)]
    came = all_to_all(firsts, ("chip", "core", "col"))
    for level_no in range(1, LEVELS):
        whole = level_no == LEVELS - 1
        outs = relax_level(dims, level_no > 1, whole, places, sources, both, came)
        came = all_to_all(outs, line)
    bands = []
    for back_no in range(BACK):
        first, last = back_no == 0, back_no == BACK - 1
        outs = depend_level(dims, first, last, places, sources, both, bands, came)
        if first:
            bands = outs[1:3]
            shown, paths = show_block(dims, outs[3], swap_core(outs[4]))
        came = all_to_all(outs[0], "col" if last else line)
    total = jnp.sum(came, axis=0)
    centrality = (total[0] + swap_core(total[1:])[0]) / rows
    return shown, paths, centrality


def solution(mesh):
    groups, rows, cols = mesh.devices.shape
    pairs = mesh.devices.reshape(groups, rows // PAIR, PAIR, cols)
    paired = jax.sharding.Mesh(pairs, ("groups", "chip", "core", "col"))
    vertices = ("chip", "core", "col")
    everywhere = ("groups",) + vertices
    in_specs = (P(everywhere, None, None), P(everywhere, None), P(everywhere), P("groups"))
    out_specs = (P("groups", vertices), P("groups", vertices), P(everywhere))
    return jax.shard_map(
        per_device, mesh=paired, in_specs=in_specs, out_specs=out_specs, check_vma=False
    )
```

```python
import functools

import jax
import jax.numpy as jnp
from jax import lax
from jax.experimental import pallas as pl
from jax.experimental.pallas import tpu as pltpu
from jax.sharding import PartitionSpec as P

LEVELS = 3
BACK = 2
LANES = 128
SUB = 8
PAIR = 2

far_value = 1000000.0
no_edge = 2000000.0


def in_vmem():
    return pl.BlockSpec(memory_space=pltpu.VMEM)


def in_smem():
    return pl.BlockSpec(memory_space=pltpu.SMEM)


def in_hbm():
    return pl.BlockSpec(memory_space=pltpu.HBM)


def piece(*shape):
    return jax.ShapeDtypeStruct(shape, jnp.float32)


def params(dims):
    tiles = 2 * dims[0] * dims[1] * LANES * LANES * 4
    return pltpu.CompilerParams(vmem_limit_bytes=8 * 1024 * 1024 + tiles)


def partner(at, step, size):
    if size & (size - 1) == 0:
        return at ^ step
    return (step + size - at) % size if isinstance(at, int) else lax.rem(step + size - at, size)


def is_dense(dims):
    return dims[2] == dims[0] * dims[1]


def position():
    return lax.axis_index("chip"), lax.axis_index("core"), lax.axis_index("col")


def source_ids(sources, first, half):
    row = lax.broadcasted_iota(jnp.int32, (half, LANES), 0)
    ids = jnp.zeros((half, LANES), jnp.int32)
    for s in range(half):
        ids = jnp.where(row == s, sources[first + s], ids)
    return ids


def is_source(ids, block):
    return ids == block * LANES + lax.broadcasted_iota(jnp.int32, ids.shape, 1)


def settle(found_dist, found_count, at_source):
    dist = jnp.where(at_source, 0.0, jnp.minimum(found_dist, far_value))
    count = jnp.where(found_dist == dist, found_count, 0.0)
    return dist, jnp.where(at_source, 1.0, 0.0) + count


def merge(pairs):
    best = functools.reduce(jnp.minimum, [p[0] for p in pairs])
    total = functools.reduce(jnp.add, [jnp.where(p[0] == best, p[1], 0.0) for p in pairs])
    return best, total


def first_kernel(dims, *refs):
    n_row, n_col, slots, half = dims
    places_in, sources_in, tiles_in, out, turned = refs[:5]
    owned = refs[5 : 5 + n_col]
    places, sources, slot_of, tiles, lines, sems = refs[5 + n_col :]
    my_x, my_core, my_col = position()
    my_row = my_x * PAIR + my_core
    parts = sems.shape[0] - 2
    size = slots // parts
    fetch = []
    for part in range(parts):
        span = pl.ds(part * size, size)
        fetch.append(pltpu.make_async_copy(tiles_in.at[span], tiles.at[span], sems.at[part]))
    given = [
        pltpu.make_async_copy(places_in, places, sems.at[parts]),
        pltpu.make_async_copy(sources_in, sources, sems.at[parts + 1]),
    ]
    for copy in given + fetch:
        copy.start()
    lines[...] = jnp.zeros(lines.shape, jnp.float32)

    def clear(at, _):
        slot_of[at] = -1
        return 0

    if not is_dense(dims):
        lax.fori_loop(0, n_row * n_col, clear, 0)
    for copy in given:
        copy.wait()
    for g in range(slots):
        slot_of[places[0, g] * n_row + places[1, g]] = g
    for copy in fetch:
        copy.wait()
    for s in range(PAIR * half):
        vertex = sources[s]
        block, place = vertex // LANES, lax.rem(vertex, LANES)
        r = lax.rem(block, n_col)

        @pl.when(block // n_col == my_row)
        def _():
            for c in range(n_row):
                g = slot_of[r * n_row + c]

                @pl.when(g >= 0)
                def _():
                    line = c % PAIR * half + s % half
                    row = tiles[g, pl.ds(place, 1), :]
                    lines[c // PAIR, s // half, pl.ds(line, 1), :] = row

    for chip in range(n_row // PAIR):
        for core in range(PAIR):
            line = lines[chip, core]
            line = jnp.where(line > 0, line, far_value)
            for col in range(n_col):
                out[(chip * PAIR + core) * n_col + col] = line

    def edges(g):
        raw = tiles[g]
        return jnp.where(raw > 0, raw, no_edge)

    if is_dense(dims):
        for step in range(n_col):
            r = partner(my_col, step, n_col)
            for c in range(n_row):
                weight = edges(slot_of[r * n_row + c])
                owned[step][c] = weight
                turned[r * n_row + c] = weight.T
    else:

        def turn(g, _):
            turned[g] = edges(g).T
            return 0

        lax.fori_loop(0, slots, turn, 0)
        for step in range(n_col):
            r = partner(my_col, step, n_col)

            def place_tile(c, _):
                g = slot_of[r * n_row + c]
                weight = edges(jnp.maximum(g, 0))
                owned[step][c] = jnp.where(g >= 0, weight, no_edge)
                return 0

            lax.fori_loop(0, n_row, place_tile, 0)


def first_level(dims, places, sources, tiles):
    n_row, n_col, slots, half = dims
    parts = 4 if slots % 4 == 0 else 1
    out_shape = [piece(n_row * n_col, PAIR * half, LANES), piece(*tiles.shape)]
    out_shape += [piece(n_row, LANES, LANES)] * n_col
    return pl.pallas_call(
        functools.partial(first_kernel, dims),
        out_shape=out_shape,
        in_specs=[in_hbm()] * 3,
        out_specs=[in_vmem()] * len(out_shape),
        scratch_shapes=[
            pltpu.SMEM(places.shape, jnp.int32),
            pltpu.SMEM(sources.shape, jnp.int32),
            pltpu.SMEM((n_row * n_col,), jnp.int32),
            pltpu.VMEM(tiles.shape, jnp.float32),
            pltpu.VMEM((n_row // PAIR, PAIR, PAIR * half, LANES), jnp.float32),
            pltpu.SemaphoreType.DMA((parts + 2,)),
        ],
        compiler_params=params(dims),
        name="first_level",
    )(places, sources, tiles)


def list_slots(dims, places, table, filled):
    n_row, n_col, slots, half = dims
    if is_dense(dims):
        return

    def clear(at, _):
        filled[at] = 0
        return 0

    lax.fori_loop(0, PAIR * n_row, clear, 0)
    for k in range(PAIR):

        def enter(g, _):
            at = k * n_row + places[k][1, g]
            table[at * n_col + filled[at]] = g
            filled[at] += 1
            return 0

        lax.fori_loop(0, slots, enter, 0)


def over_slots(dims, places, table, filled, c, step, carry):
    n_row, n_col, slots, half = dims
    for k in range(PAIR):
        if is_dense(dims):
            for r in range(n_col):
                carry = step(k, r * n_row + c, k * n_col + r, carry)
        else:
            at = k * n_row + c

            def entry(e, carry):
                g = table[at * n_col + e]
                return step(k, g, k * n_col + places[k][0, g], carry)

            carry = lax.fori_loop(0, filled[at], entry, carry)
    return carry


def slot_scratch(dims):
    n_row, n_col, slots, half = dims
    return [
        pltpu.SMEM((PAIR * n_row * n_col,), jnp.int32),
        pltpu.SMEM((PAIR * n_row,), jnp.int32),
    ]


def relax_kernel(dims, counted, whole, *refs):
    n_row, n_col, slots, half = dims
    chips = n_row // PAIR
    n_places = 0 if is_dense(dims) else PAIR
    places, refs = refs[:n_places], refs[n_places:]
    sources, tiles, refs = refs[0], refs[1 : 1 + PAIR], refs[1 + PAIR :]
    came, out, near, found, table, filled = refs
    my_x, my_core, my_col = position()
    ids = source_ids(sources, my_core * half, half)
    list_slots(dims, places, table, filled)
    for r in range(n_col):
        for k in range(PAIR):
            h = my_core ^ k
            at_source = is_source(ids, (PAIR * my_x + h) * n_col + r)
            if counted:
                blocks = [came[chip * n_col + r, h] for chip in range(chips)]
                reached, count = merge([(block[:half], block[half:]) for block in blocks])
            else:
                parts = [came[at * n_col + r, pl.ds(h * half, half), :] for at in range(n_row)]
                reached = functools.reduce(jnp.minimum, parts)
                count = jnp.where(reached < far_value, 1.0, 0.0)
            dist, count = settle(reached, count, at_source)
            near[k * n_col + r, :half, :] = dist
            near[k * n_col + r, half:, :] = count
    lane = lax.broadcasted_iota(jnp.int32, (LANES, LANES), 1)

    def column(c, _):
        def lowest(s):
            def step(k, g, b, carry):
                return jnp.minimum(carry, tiles[k][g] + near[b, pl.ds(s, 1), :])

            start = jnp.full((LANES, LANES), far_value, jnp.float32)
            reached = over_slots(dims, places, table, filled, c, step, start)
            return jnp.min(reached, axis=1, keepdims=True)

        def tally(s, best):
            def step(k, g, b, carry):
                hit = tiles[k][g] + near[b, pl.ds(s, 1), :] == best
                return carry + jnp.where(hit, near[b, pl.ds(half + s, 1), :], 0.0)

            start = jnp.zeros((LANES, LANES), jnp.float32)
            counts = over_slots(dims, places, table, filled, c, step, start)
            return jnp.sum(counts, axis=1, keepdims=True)

        turned = jnp.zeros((LANES, LANES), jnp.float32)
        best = lowest(0)
        for s in range(half):
            later = lowest(s + 1) if s + 1 < half else None
            total = tally(s, best)
            turned = jnp.where(lane == s, best, jnp.where(lane == half + s, total, turned))
            best = later
        found[c] = turned.T[: 2 * half]
        return 0

    lax.fori_loop(0, n_row, column, 0)
    for chip in range(chips):
        for col in range(n_col):
            if whole:
                out[chip * n_col + col] = found[...]
            else:
                out[chip * n_col + col] = found[pl.ds(PAIR * chip, PAIR)]


def relax_level(dims, counted, whole, places, sources, tiles, came):
    n_row, n_col, slots, half = dims
    blocks = n_row if whole else PAIR
    return pl.pallas_call(
        functools.partial(relax_kernel, dims, counted, whole),
        out_shape=piece(n_row // PAIR * n_col, blocks, 2 * half, LANES),
        in_specs=[in_smem()] * (len(places) + 1) + [in_vmem()] * (PAIR + 1),
        out_specs=in_vmem(),
        scratch_shapes=[
            pltpu.VMEM((PAIR * n_col, 2 * half, LANES), jnp.float32),
            pltpu.VMEM((n_row, 2 * half, LANES), jnp.float32),
        ]
        + slot_scratch(dims),
        compiler_params=params(dims),
        name="relax_level",
    )(*places, sources, *tiles, came)


def sum_successors(dims, tiles, dist, coef, wide, turned):
    n_row, n_col, slots, half = dims
    my_x, my_core, my_col = position()
    own = (my_x * PAIR + my_core) * n_col + my_col
    upper = dist[own].T
    for s in range(PAIR * half):
        wide[s] = jnp.broadcast_to(upper[:, s : s + 1], (LANES, LANES))
    turned[...] = jnp.zeros(turned.shape, jnp.float32)
    lane = lax.broadcasted_iota(jnp.int32, (LANES, LANES), 1)

    def one_source(s, _):
        reach = wide[s]

        def add_tile(step, c, total):
            b = c * n_col + partner(my_col, step, n_col)
            hit = tiles[step][c] + reach == dist[b, pl.ds(s, 1), :]
            return total + jnp.where(hit, coef[b, pl.ds(s, 1), :], 0.0)

        total = jnp.zeros((LANES, LANES), jnp.float32)
        for step in range(n_col):
            if is_dense(dims):
                for c in range(n_row):
                    total = add_tile(step, c, total)
            else:
                add = functools.partial(add_tile, step)
                total = lax.fori_loop(0, n_row, add, total)
        sums = jnp.sum(total, axis=1, keepdims=True)
        turned[...] = jnp.where(lane == s, sums, turned[...])
        return 0

    lax.fori_loop(0, PAIR * half, one_source, 0)
    return turned[...].T[: PAIR * half]


def lower_kernel(dims, *refs):
    n_row, n_col, slots, half = dims
    chips = n_row // PAIR
    sources, mine, theirs, tiles, refs = refs[0], refs[1], refs[2], refs[3 : 3 + n_col], refs[3 + n_col :]
    out, shown, paths, own_count, dist, coef, wide, turned = refs
    my_x, my_core, my_col = position()
    own = (my_x * PAIR + my_core) * n_col + my_col
    ids = source_ids(sources, 0, PAIR * half)
    for c in range(n_row):
        for col in range(n_col):
            pairs = []
            for chip in range(chips):
                a = mine[chip * n_col + col, c]
                b = theirs[chip * n_col + col, c]
                low = jnp.where(my_core == 0, a, b)
                high = jnp.where(my_core == 0, b, a)
                found = jnp.concatenate([low[:half], high[:half]], axis=0)
                count = jnp.concatenate([low[half:], high[half:]], axis=0)
                pairs.append((found, count))
            b = c * n_col + col
            lower, count = settle(*merge(pairs), is_source(ids, b))
            dist[b] = lower
            coef[b] = jnp.where(count > 0.5, 1.0 / jnp.maximum(count, 1.0), 0.0)

            @pl.when(b == own)
            def _():
                shown[...] = jnp.where(lower < 0.5 * far_value, lower, -1.0)
                paths[...] = count
                own_count[...] = count

    sums = sum_successors(dims, tiles, dist, coef, wide, turned)
    count = own_count[...]
    found = jnp.where(count > 0.5, (1.0 + count * sums) / jnp.maximum(count, 1.0), 0.0)
    for at in range(n_row * n_col):
        out[at] = found


def upper_kernel(dims, last, *refs):
    n_row, n_col, slots, half = dims
    sources, own_count, dist, coef, tiles = refs[0], refs[1], refs[2], refs[3], refs[4 : 4 + n_col]
    out, wide, turned = refs[4 + n_col :]
    my_x, my_core, my_col = position()
    own = (my_x * PAIR + my_core) * n_col + my_col
    count = own_count[...]
    dependency = count * sum_successors(dims, tiles, dist, coef, wide, turned)
    if last:
        ids = source_ids(sources, 0, PAIR * half)
        term = jnp.where(is_source(ids, own), 0.0, dependency)
        out[...] = jnp.sum(term, axis=0, keepdims=True) / (PAIR * half)
    else:
        found = jnp.where(count > 0.5, (1.0 + dependency) / jnp.maximum(count, 1.0), 0.0)
        for at in range(n_row * n_col):
            out[at] = found


def successor_scratch(dims):
    half = dims[3]
    return [
        pltpu.VMEM((PAIR * half, LANES, LANES), jnp.float32),
        pltpu.VMEM((LANES, LANES), jnp.float32),
    ]


def lower_level(dims, sources, mine, theirs, tiles):
    n_row, n_col, slots, half = dims
    rows = PAIR * half
    blocks = n_row * n_col
    return pl.pallas_call(
        functools.partial(lower_kernel, dims),
        out_shape=[piece(blocks, rows, LANES)]
        + [piece(rows, LANES)] * 3
        + [piece(blocks, rows, LANES)],
        in_specs=[in_smem()] + [in_vmem()] * (2 + n_col),
        out_specs=[in_vmem()] * 5,
        scratch_shapes=[pltpu.VMEM((blocks, rows, LANES), jnp.float32)] + successor_scratch(dims),
        compiler_params=params(dims),
        name="lower_level",
    )(sources, mine, theirs, *tiles)


def upper_level(dims, last, sources, own_count, dist, coef, tiles):
    n_row, n_col, slots, half = dims
    rows = PAIR * half
    out_shape = piece(1, LANES) if last else piece(n_row * n_col, rows, LANES)
    return pl.pallas_call(
        functools.partial(upper_kernel, dims, last),
        out_shape=out_shape,
        in_specs=[in_smem()] + [in_vmem()] * (3 + n_col),
        out_specs=in_vmem(),
        scratch_shapes=successor_scratch(dims),
        compiler_params=params(dims),
        name="upper_level",
    )(sources, own_count, dist, coef, *tiles)


def all_to_all(value, axes):
    return lax.all_to_all(value, axes, split_axis=0, concat_axis=0, tiled=True)


def swap_core(value):
    return lax.ppermute(value, "core", [(0, 1), (1, 0)])


def swap_col(value, step):
    size = lax.axis_size("col")
    if step == 0 and size & (size - 1) == 0:
        return value
    return lax.ppermute(value, "col", [(at, partner(at, step, size)) for at in range(size)])


def per_device(tiles, tile_index, tile_count, sources):
    slots = tiles.shape[0]
    rows = sources.shape[0]
    dims = (lax.axis_size("chip") * PAIR, lax.axis_size("col"), slots, rows // PAIR)
    own_places = tile_index.T
    line = ("chip", "col")
    everyone = ("chip", "core", "col")

    firsts, turned, *owned = first_level(dims, own_places, sources, tiles)
    both = [turned, swap_core(turned)]
    places = [] if is_dense(dims) else [own_places, swap_core(own_places)]
    came = all_to_all(firsts, everyone)
    for level_no in range(1, LEVELS):
        whole = level_no == LEVELS - 1
        outs = relax_level(dims, level_no > 1, whole, places, sources, both, came)
        came = all_to_all(outs, line)
    leaving = [swap_col(part, step) for step, part in enumerate(owned)]
    coef, shown, paths, own_count, dist = lower_level(
        dims, sources, came, swap_core(came), leaving
    )
    for back_no in range(1, BACK):
        coef = all_to_all(coef, everyone)
        coef = upper_level(dims, back_no == BACK - 1, sources, own_count, dist, coef, leaving)
    return shown, paths, coef.reshape(LANES)


def solution(mesh):
    groups, rows, cols = mesh.devices.shape
    pairs = mesh.devices.reshape(groups, rows // PAIR, PAIR, cols)
    paired = jax.sharding.Mesh(pairs, ("groups", "chip", "core", "col"))
    vertices = ("chip", "core", "col")
    everywhere = ("groups",) + vertices
    in_specs = (P(everywhere, None, None), P(everywhere, None), P(everywhere), P("groups"))
    out_specs = (P("groups", vertices), P("groups", vertices), P(everywhere))
    return jax.shard_map(
        per_device, mesh=paired, in_specs=in_specs, out_specs=out_specs, check_vma=False
    )
```

```python
import functools

import jax
import jax.numpy as jnp
from jax import lax
from jax.experimental import pallas as pl
from jax.experimental.pallas import tpu as pltpu
from jax.sharding import PartitionSpec as P

LEVELS = 3
BACK = 2
LANES = 128
SUB = 8
PAIR = 2

far_value = 1000000.0
no_edge = 2000000.0


def in_vmem():
    return pl.BlockSpec(memory_space=pltpu.VMEM)


def in_smem():
    return pl.BlockSpec(memory_space=pltpu.SMEM)


def in_hbm():
    return pl.BlockSpec(memory_space=pltpu.HBM)


def piece(*shape):
    return jax.ShapeDtypeStruct(shape, jnp.float32)


def params(dims):
    tiles = 2 * dims[0] * dims[1] * LANES * LANES * 4
    return pltpu.CompilerParams(vmem_limit_bytes=8 * 1024 * 1024 + tiles)


def partner(at, step, size):
    if size & (size - 1) == 0:
        return at ^ step
    return (step + size - at) % size if isinstance(at, int) else lax.rem(step + size - at, size)


def is_dense(dims):
    return dims[2] == dims[0] * dims[1]


def position():
    return lax.axis_index("chip"), lax.axis_index("core"), lax.axis_index("col")


def source_ids(sources, first, half):
    row = lax.broadcasted_iota(jnp.int32, (half, LANES), 0)
    ids = jnp.zeros((half, LANES), jnp.int32)
    for s in range(half):
        ids = jnp.where(row == s, sources[first + s], ids)
    return ids


def is_source(ids, block):
    return ids == block * LANES + lax.broadcasted_iota(jnp.int32, ids.shape, 1)


def settle(found_dist, found_count, at_source):
    dist = jnp.where(at_source, 0.0, jnp.minimum(found_dist, far_value))
    count = jnp.where(found_dist == dist, found_count, 0.0)
    return dist, jnp.where(at_source, 1.0, 0.0) + count


def merge(pairs):
    best = functools.reduce(jnp.minimum, [p[0] for p in pairs])
    total = functools.reduce(jnp.add, [jnp.where(p[0] == best, p[1], 0.0) for p in pairs])
    return best, total


def first_kernel(dims, *refs):
    n_row, n_col, slots, half = dims
    places_in, sources_in, tiles_in, out, turned = refs[:5]
    owned = refs[5 : 5 + n_col]
    places, sources, slot_of, tiles, lines, sems = refs[5 + n_col :]
    my_x, my_core, my_col = position()
    my_row = my_x * PAIR + my_core
    parts = sems.shape[0] - 2
    size = slots // parts
    fetch = []
    for part in range(parts):
        span = pl.ds(part * size, size)
        fetch.append(pltpu.make_async_copy(tiles_in.at[span], tiles.at[span], sems.at[part]))
    given = [
        pltpu.make_async_copy(places_in, places, sems.at[parts]),
        pltpu.make_async_copy(sources_in, sources, sems.at[parts + 1]),
    ]
    for copy in given + fetch:
        copy.start()
    lines[...] = jnp.zeros(lines.shape, jnp.float32)

    def clear(at, _):
        slot_of[at] = -1
        return 0

    if not is_dense(dims):
        lax.fori_loop(0, n_row * n_col, clear, 0)
    for copy in given:
        copy.wait()
    for g in range(slots):
        slot_of[places[0, g] * n_row + places[1, g]] = g
    for copy in fetch:
        copy.wait()
    for s in range(PAIR * half):
        vertex = sources[s]
        block, place = vertex // LANES, lax.rem(vertex, LANES)
        r = lax.rem(block, n_col)

        @pl.when(block // n_col == my_row)
        def _():
            for c in range(n_row):
                g = slot_of[r * n_row + c]

                @pl.when(g >= 0)
                def _():
                    line = c % PAIR * half + s % half
                    row = tiles[g, pl.ds(place, 1), :]
                    lines[c // PAIR, s // half, pl.ds(line, 1), :] = row

    for chip in range(n_row // PAIR):
        for core in range(PAIR):
            line = lines[chip, core]
            line = jnp.where(line > 0, line, far_value)
            for col in range(n_col):
                out[(chip * PAIR + core) * n_col + col] = line

    def edges(g):
        raw = tiles[g]
        return jnp.where(raw > 0, raw, no_edge)

    if is_dense(dims):
        for step in range(n_col):
            r = partner(my_col, step, n_col)
            for c in range(n_row):
                weight = edges(slot_of[r * n_row + c])
                owned[step][c] = weight
                turned[r * n_row + c] = weight.T
    else:

        def turn(g, _):
            turned[g] = edges(g).T
            return 0

        lax.fori_loop(0, slots, turn, 0)
        for step in range(n_col):
            r = partner(my_col, step, n_col)

            def place_tile(c, _):
                g = slot_of[r * n_row + c]
                weight = edges(jnp.maximum(g, 0))
                owned[step][c] = jnp.where(g >= 0, weight, no_edge)
                return 0

            lax.fori_loop(0, n_row, place_tile, 0)


def first_level(dims, places, sources, tiles):
    n_row, n_col, slots, half = dims
    parts = 4 if slots % 4 == 0 else 1
    out_shape = [piece(n_row * n_col, PAIR * half, LANES), piece(*tiles.shape)]
    out_shape += [piece(n_row, LANES, LANES)] * n_col
    return pl.pallas_call(
        functools.partial(first_kernel, dims),
        out_shape=out_shape,
        in_specs=[in_hbm()] * 3,
        out_specs=[in_vmem()] * len(out_shape),
        scratch_shapes=[
            pltpu.SMEM(places.shape, jnp.int32),
            pltpu.SMEM(sources.shape, jnp.int32),
            pltpu.SMEM((n_row * n_col,), jnp.int32),
            pltpu.VMEM(tiles.shape, jnp.float32),
            pltpu.VMEM((n_row // PAIR, PAIR, PAIR * half, LANES), jnp.float32),
            pltpu.SemaphoreType.DMA((parts + 2,)),
        ],
        compiler_params=params(dims),
        name="first_level",
    )(places, sources, tiles)


def list_slots(dims, places, table, filled):
    n_row, n_col, slots, half = dims
    if is_dense(dims):
        return

    def clear(at, _):
        filled[at] = 0
        return 0

    lax.fori_loop(0, PAIR * n_row, clear, 0)
    for k in range(PAIR):

        def enter(g, _):
            at = k * n_row + places[k][1, g]
            table[at * n_col + filled[at]] = g
            filled[at] += 1
            return 0

        lax.fori_loop(0, slots, enter, 0)


def over_slots(dims, places, table, filled, c, step, carry):
    n_row, n_col, slots, half = dims
    for k in range(PAIR):
        if is_dense(dims):
            for r in range(n_col):
                carry = step(k, r * n_row + c, k * n_col + r, carry)
        else:
            at = k * n_row + c

            def entry(e, carry):
                g = table[at * n_col + e]
                return step(k, g, k * n_col + places[k][0, g], carry)

            carry = lax.fori_loop(0, filled[at], entry, carry)
    return carry


def slot_scratch(dims):
    n_row, n_col, slots, half = dims
    return [
        pltpu.SMEM((PAIR * n_row * n_col,), jnp.int32),
        pltpu.SMEM((PAIR * n_row,), jnp.int32),
    ]


def relax_kernel(dims, counted, whole, *refs):
    n_row, n_col, slots, half = dims
    chips = n_row // PAIR
    n_places = 0 if is_dense(dims) else PAIR
    places, refs = refs[:n_places], refs[n_places:]
    sources, tiles, refs = refs[0], refs[1 : 1 + PAIR], refs[1 + PAIR :]
    came, out, near, found, table, filled = refs
    my_x, my_core, my_col = position()
    ids = source_ids(sources, my_core * half, half)
    list_slots(dims, places, table, filled)
    for r in range(n_col):
        for k in range(PAIR):
            h = my_core ^ k
            at_source = is_source(ids, (PAIR * my_x + h) * n_col + r)
            if counted:
                blocks = [came[chip * n_col + r, h] for chip in range(chips)]
                reached, count = merge([(block[:half], block[half:]) for block in blocks])
            else:
                parts = [came[at * n_col + r, pl.ds(h * half, half), :] for at in range(n_row)]
                reached = functools.reduce(jnp.minimum, parts)
                count = jnp.where(reached < far_value, 1.0, 0.0)
            dist, count = settle(reached, count, at_source)
            near[k * n_col + r, :half, :] = dist
            near[k * n_col + r, half:, :] = count
    lane = lax.broadcasted_iota(jnp.int32, (LANES, LANES), 1)

    def column(c, _):
        def lowest(s):
            def step(k, g, b, carry):
                return jnp.minimum(carry, tiles[k][g] + near[b, pl.ds(s, 1), :])

            start = jnp.full((LANES, LANES), far_value, jnp.float32)
            reached = over_slots(dims, places, table, filled, c, step, start)
            return jnp.min(reached, axis=1, keepdims=True)

        def tally(s, best):
            def step(k, g, b, carry):
                hit = tiles[k][g] + near[b, pl.ds(s, 1), :] == best
                return carry + jnp.where(hit, near[b, pl.ds(half + s, 1), :], 0.0)

            start = jnp.zeros((LANES, LANES), jnp.float32)
            counts = over_slots(dims, places, table, filled, c, step, start)
            return jnp.sum(counts, axis=1, keepdims=True)

        turned = jnp.zeros((LANES, LANES), jnp.float32)
        best = lowest(0)
        for s in range(half):
            later = lowest(s + 1) if s + 1 < half else None
            total = tally(s, best)
            turned = jnp.where(lane == s, best, jnp.where(lane == half + s, total, turned))
            best = later
        found[c] = turned.T[: 2 * half]
        return 0

    lax.fori_loop(0, n_row, column, 0)
    for chip in range(chips):
        for col in range(n_col):
            if whole:
                out[chip * n_col + col] = found[...]
            else:
                out[chip * n_col + col] = found[pl.ds(PAIR * chip, PAIR)]


def relax_level(dims, counted, whole, places, sources, tiles, came):
    n_row, n_col, slots, half = dims
    blocks = n_row if whole else PAIR
    return pl.pallas_call(
        functools.partial(relax_kernel, dims, counted, whole),
        out_shape=piece(n_row // PAIR * n_col, blocks, 2 * half, LANES),
        in_specs=[in_smem()] * (len(places) + 1) + [in_vmem()] * (PAIR + 1),
        out_specs=in_vmem(),
        scratch_shapes=[
            pltpu.VMEM((PAIR * n_col, 2 * half, LANES), jnp.float32),
            pltpu.VMEM((n_row, 2 * half, LANES), jnp.float32),
        ]
        + slot_scratch(dims),
        compiler_params=params(dims),
        name="relax_level",
    )(*places, sources, *tiles, came)


def sum_successors(dims, tiles, dist, coef, wide, turned):
    n_row, n_col, slots, half = dims
    my_x, my_core, my_col = position()
    own = (my_x * PAIR + my_core) * n_col + my_col
    upper = dist[own].T
    for s in range(PAIR * half):
        wide[s] = jnp.broadcast_to(upper[:, s : s + 1], (LANES, LANES))
    turned[...] = jnp.zeros(turned.shape, jnp.float32)
    lane = lax.broadcasted_iota(jnp.int32, (LANES, LANES), 1)

    def one_source(s, _):
        reach = wide[s]

        def add_tile(step, c, total):
            b = c * n_col + partner(my_col, step, n_col)
            hit = tiles[step][c] + reach == dist[b, pl.ds(s, 1), :]
            return total + jnp.where(hit, coef[b, pl.ds(s, 1), :], 0.0)

        total = jnp.zeros((LANES, LANES), jnp.float32)
        for step in range(n_col):
            if is_dense(dims):
                for c in range(n_row):
                    total = add_tile(step, c, total)
            else:
                add = functools.partial(add_tile, step)
                total = lax.fori_loop(0, n_row, add, total)
        sums = jnp.sum(total, axis=1, keepdims=True)
        turned[...] = jnp.where(lane == s, sums, turned[...])
        return 0

    lax.fori_loop(0, PAIR * half, one_source, 0)
    return turned[...].T[: PAIR * half]


def lower_kernel(dims, *refs):
    n_row, n_col, slots, half = dims
    chips = n_row // PAIR
    sources, mine, theirs, tiles, refs = refs[0], refs[1], refs[2], refs[3 : 3 + n_col], refs[3 + n_col :]
    out, shown, paths, own_count, dist, coef, wide, turned = refs
    my_x, my_core, my_col = position()
    own = (my_x * PAIR + my_core) * n_col + my_col
    ids = source_ids(sources, 0, PAIR * half)
    for c in range(n_row):
        for col in range(n_col):
            pairs = []
            for chip in range(chips):
                a = mine[chip * n_col + col, c]
                b = theirs[chip * n_col + col, c]
                low = jnp.where(my_core == 0, a, b)
                high = jnp.where(my_core == 0, b, a)
                found = jnp.concatenate([low[:half], high[:half]], axis=0)
                count = jnp.concatenate([low[half:], high[half:]], axis=0)
                pairs.append((found, count))
            b = c * n_col + col
            lower, count = settle(*merge(pairs), is_source(ids, b))
            dist[b] = lower
            coef[b] = jnp.where(count > 0.5, 1.0 / jnp.maximum(count, 1.0), 0.0)

            @pl.when(b == own)
            def _():
                shown[...] = jnp.where(lower < 0.5 * far_value, lower, -1.0)
                paths[...] = count
                own_count[...] = count

    sums = sum_successors(dims, tiles, dist, coef, wide, turned)
    count = own_count[...]
    found = jnp.where(count > 0.5, (1.0 + count * sums) / jnp.maximum(count, 1.0), 0.0)
    for at in range(n_row * n_col):
        out[at] = found


def upper_kernel(dims, last, *refs):
    n_row, n_col, slots, half = dims
    sources, own_count, dist, coef, tiles = refs[0], refs[1], refs[2], refs[3], refs[4 : 4 + n_col]
    out, wide, turned = refs[4 + n_col :]
    my_x, my_core, my_col = position()
    own = (my_x * PAIR + my_core) * n_col + my_col
    count = own_count[...]
    dependency = count * sum_successors(dims, tiles, dist, coef, wide, turned)
    if last:
        ids = source_ids(sources, 0, PAIR * half)
        term = jnp.where(is_source(ids, own), 0.0, dependency)
        out[...] = jnp.sum(term, axis=0, keepdims=True) / (PAIR * half)
    else:
        found = jnp.where(count > 0.5, (1.0 + dependency) / jnp.maximum(count, 1.0), 0.0)
        for at in range(n_row * n_col):
            out[at] = found


def successor_scratch(dims):
    half = dims[3]
    return [
        pltpu.VMEM((PAIR * half, LANES, LANES), jnp.float32),
        pltpu.VMEM((LANES, LANES), jnp.float32),
    ]


def lower_level(dims, sources, mine, theirs, tiles):
    n_row, n_col, slots, half = dims
    rows = PAIR * half
    blocks = n_row * n_col
    return pl.pallas_call(
        functools.partial(lower_kernel, dims),
        out_shape=[piece(blocks, rows, LANES)]
        + [piece(rows, LANES)] * 3
        + [piece(blocks, rows, LANES)],
        in_specs=[in_smem()] + [in_vmem()] * (2 + n_col),
        out_specs=[in_vmem()] * 5,
        scratch_shapes=[pltpu.VMEM((blocks, rows, LANES), jnp.float32)] + successor_scratch(dims),
        compiler_params=params(dims),
        name="lower_level",
    )(sources, mine, theirs, *tiles)


def upper_level(dims, last, sources, own_count, dist, coef, tiles):
    n_row, n_col, slots, half = dims
    rows = PAIR * half
    out_shape = piece(1, LANES) if last else piece(n_row * n_col, rows, LANES)
    return pl.pallas_call(
        functools.partial(upper_kernel, dims, last),
        out_shape=out_shape,
        in_specs=[in_smem()] + [in_vmem()] * (3 + n_col),
        out_specs=in_vmem(),
        scratch_shapes=successor_scratch(dims),
        compiler_params=params(dims),
        name="upper_level",
    )(sources, own_count, dist, coef, *tiles)


def all_to_all(value, axes):
    return lax.all_to_all(value, axes, split_axis=0, concat_axis=0, tiled=True)


def swap_core(value):
    return lax.ppermute(value, "core", [(0, 1), (1, 0)])


def swap_col(value, step):
    size = lax.axis_size("col")
    if step == 0 and size & (size - 1) == 0:
        return value
    return lax.ppermute(value, "col", [(at, partner(at, step, size)) for at in range(size)])


def round_of(step):
    return {0: 0, 1: 0, 3: 1}.get(step, 2)


def per_device(tiles, tile_index, tile_count, sources):
    slots = tiles.shape[0]
    rows = sources.shape[0]
    dims = (lax.axis_size("chip") * PAIR, lax.axis_size("col"), slots, rows // PAIR)
    own_places = tile_index.T
    n_col = dims[1]
    line = ("chip", "col")
    everyone = ("chip", "core", "col")

    firsts, turned, *owned = first_level(dims, own_places, sources, tiles)
    both = [turned, swap_core(turned)]
    places = [] if is_dense(dims) else [own_places, swap_core(own_places)]
    leaving = [None] * n_col
    came = all_to_all(firsts, everyone)
    for level_no in range(1, LEVELS):
        steps = [at for at in range(n_col) if round_of(at) == level_no - 1]
        moved, came = lax.optimization_barrier(([swap_col(owned[at], at) for at in steps], came))
        for at, part in zip(steps, moved):
            leaving[at] = part
        owned, came = lax.optimization_barrier((owned, came))
        whole = level_no == LEVELS - 1
        outs = relax_level(dims, level_no > 1, whole, places, sources, both, came)
        came = all_to_all(outs, line)
    leaving = [swap_col(owned[at], at) if leaving[at] is None else leaving[at] for at in range(n_col)]
    coef, shown, paths, own_count, dist = lower_level(
        dims, sources, came, swap_core(came), leaving
    )
    for back_no in range(1, BACK):
        coef = all_to_all(coef, everyone)
        coef = upper_level(dims, back_no == BACK - 1, sources, own_count, dist, coef, leaving)
    return shown, paths, coef.reshape(LANES)


def solution(mesh):
    groups, rows, cols = mesh.devices.shape
    pairs = mesh.devices.reshape(groups, rows // PAIR, PAIR, cols)
    paired = jax.sharding.Mesh(pairs, ("groups", "chip", "core", "col"))
    vertices = ("chip", "core", "col")
    everywhere = ("groups",) + vertices
    in_specs = (P(everywhere, None, None), P(everywhere, None), P(everywhere), P("groups"))
    out_specs = (P("groups", vertices), P("groups", vertices), P(everywhere))
    return jax.shard_map(
        per_device, mesh=paired, in_specs=in_specs, out_specs=out_specs, check_vma=False
    )
```

```python
import functools

import jax
import jax.numpy as jnp
from jax import lax
from jax.experimental import pallas as pl
from jax.experimental.pallas import tpu as pltpu
from jax.sharding import PartitionSpec as P

LEVELS = 3
BACK = 2
LANES = 128
SUB = 8
PAIR = 2

far_value = 1000000.0
no_edge = 2000000.0
large_limit = 8 * 1024 * 1024
small_limit = 2 * 1024 * 1024


def in_vmem():
    return pl.BlockSpec(memory_space=pltpu.VMEM)


def in_smem():
    return pl.BlockSpec(memory_space=pltpu.SMEM)


def piece(*shape):
    return jax.ShapeDtypeStruct(shape, jnp.float32)


def params(limit):
    return pltpu.CompilerParams(vmem_limit_bytes=limit)


def is_dense(dims):
    return dims[2] == dims[0] * dims[1]


def position():
    return lax.axis_index("chip"), lax.axis_index("core"), lax.axis_index("col")


def source_ids(sources, first, half):
    row = lax.broadcasted_iota(jnp.int32, (half, LANES), 0)
    ids = jnp.zeros((half, LANES), jnp.int32)
    for s in range(half):
        ids = jnp.where(row == s, sources[first + s], ids)
    return ids


def is_source(ids, block):
    return ids == block * LANES + lax.broadcasted_iota(jnp.int32, ids.shape, 1)


def settle(found_dist, found_count, at_source):
    dist = jnp.where(at_source, 0.0, jnp.minimum(found_dist, far_value))
    count = jnp.where(found_dist == dist, found_count, 0.0)
    return dist, jnp.where(at_source, 1.0, 0.0) + count


def merge(pairs):
    best = functools.reduce(jnp.minimum, [p[0] for p in pairs])
    total = functools.reduce(jnp.add, [jnp.where(p[0] == best, p[1], 0.0) for p in pairs])
    return best, total


def first_kernel(dims, places, sources, tiles, out, turned, slot_of, lines):
    n_row, n_col, slots, half = dims
    my_x, my_core, my_col = position()
    my_row = my_x * PAIR + my_core

    def clear(at, _):
        slot_of[at] = -1
        return 0

    if not is_dense(dims):
        lax.fori_loop(0, n_row * n_col, clear, 0)
    for g in range(slots):
        slot_of[places[0, g] * n_row + places[1, g]] = g
    lines[...] = jnp.zeros(lines.shape, jnp.float32)
    for s in range(PAIR * half):
        vertex = sources[s]
        block, place = vertex // LANES, lax.rem(vertex, LANES)
        r = lax.rem(block, n_col)

        @pl.when(block // n_col == my_row)
        def _():
            for c in range(n_row):
                g = slot_of[r * n_row + c]

                @pl.when(g >= 0)
                def _():
                    line = c % PAIR * half + s % half
                    row = tiles[g, pl.ds(place, 1), :]
                    lines[c // PAIR, s // half, pl.ds(line, 1), :] = row

    for chip in range(n_row // PAIR):
        for core in range(PAIR):
            line = lines[chip, core]
            line = jnp.where(line > 0, line, far_value)
            for col in range(n_col):
                out[(chip * PAIR + core) * n_col + col] = line
    for at in range(slots):
        raw = tiles[slot_of[at] if is_dense(dims) else at]
        turned[at] = jnp.where(raw > 0, raw, no_edge).T


def first_level(dims, places, sources, tiles):
    n_row, n_col, slots, half = dims
    return pl.pallas_call(
        functools.partial(first_kernel, dims),
        out_shape=[piece(n_row * n_col, PAIR * half, LANES), piece(*tiles.shape)],
        in_specs=[in_smem(), in_smem(), in_vmem()],
        out_specs=[in_vmem()] * 2,
        scratch_shapes=[
            pltpu.SMEM((n_row * n_col,), jnp.int32),
            pltpu.VMEM((n_row // PAIR, PAIR, PAIR * half, LANES), jnp.float32),
        ],
        compiler_params=params(large_limit),
        name="first_level",
    )(places, sources, tiles)


def list_slots(dims, places, table, filled):
    n_row, n_col, slots, half = dims
    if is_dense(dims):
        return

    def clear(at, _):
        filled[at] = 0
        return 0

    lax.fori_loop(0, PAIR * n_row, clear, 0)
    for k in range(PAIR):

        def enter(g, _):
            at = k * n_row + places[k][1, g]
            table[at * n_col + filled[at]] = g
            filled[at] += 1
            return 0

        lax.fori_loop(0, slots, enter, 0)


def over_slots(dims, places, table, filled, c, step, carry):
    n_row, n_col, slots, half = dims
    for k in range(PAIR):
        if is_dense(dims):
            for r in range(n_col):
                carry = step(k, r * n_row + c, k * n_col + r, carry)
        else:
            at = k * n_row + c

            def entry(e, carry):
                g = table[at * n_col + e]
                return step(k, g, k * n_col + places[k][0, g], carry)

            carry = lax.fori_loop(0, filled[at], entry, carry)
    return carry


def slot_scratch(dims):
    n_row, n_col, slots, half = dims
    return [
        pltpu.SMEM((PAIR * n_row * n_col,), jnp.int32),
        pltpu.SMEM((PAIR * n_row,), jnp.int32),
    ]


def relax_kernel(dims, counted, whole, *refs):
    n_row, n_col, slots, half = dims
    chips = n_row // PAIR
    n_places = 0 if is_dense(dims) else PAIR
    places, refs = refs[:n_places], refs[n_places:]
    sources, tiles, refs = refs[0], refs[1 : 1 + PAIR], refs[1 + PAIR :]
    came, out, near, found, table, filled = refs
    my_x, my_core, my_col = position()
    ids = source_ids(sources, my_core * half, half)
    list_slots(dims, places, table, filled)
    for r in range(n_col):
        for k in range(PAIR):
            h = my_core ^ k
            at_source = is_source(ids, (PAIR * my_x + h) * n_col + r)
            if counted:
                blocks = [came[chip * n_col + r, h] for chip in range(chips)]
                reached, count = merge([(block[:half], block[half:]) for block in blocks])
            else:
                parts = [came[at * n_col + r, pl.ds(h * half, half), :] for at in range(n_row)]
                reached = functools.reduce(jnp.minimum, parts)
                count = jnp.where(reached < far_value, 1.0, 0.0)
            dist, count = settle(reached, count, at_source)
            near[k * n_col + r, :half, :] = dist
            near[k * n_col + r, half:, :] = count
    lane = lax.broadcasted_iota(jnp.int32, (LANES, LANES), 1)

    def column(c, _):
        def lowest(s):
            def step(k, g, b, carry):
                return jnp.minimum(carry, tiles[k][g] + near[b, pl.ds(s, 1), :])

            start = jnp.full((LANES, LANES), far_value, jnp.float32)
            reached = over_slots(dims, places, table, filled, c, step, start)
            return jnp.min(reached, axis=1, keepdims=True)

        def tally(s, best):
            def step(k, g, b, carry):
                hit = tiles[k][g] + near[b, pl.ds(s, 1), :] == best
                return carry + jnp.where(hit, near[b, pl.ds(half + s, 1), :], 0.0)

            start = jnp.zeros((LANES, LANES), jnp.float32)
            counts = over_slots(dims, places, table, filled, c, step, start)
            return jnp.sum(counts, axis=1, keepdims=True)

        turned = jnp.zeros((LANES, LANES), jnp.float32)
        best = lowest(0)
        for s in range(half):
            later = lowest(s + 1) if s + 1 < half else None
            total = tally(s, best)
            turned = jnp.where(lane == s, best, jnp.where(lane == half + s, total, turned))
            best = later
        found[c] = turned.T[: 2 * half]
        return 0

    lax.fori_loop(0, n_row, column, 0)
    for chip in range(chips):
        for col in range(n_col):
            if whole:
                out[chip * n_col + col] = found[...]
            else:
                out[chip * n_col + col] = found[pl.ds(PAIR * chip, PAIR)]


def relax_level(dims, counted, whole, places, sources, tiles, came):
    n_row, n_col, slots, half = dims
    blocks = n_row if whole else PAIR
    return pl.pallas_call(
        functools.partial(relax_kernel, dims, counted, whole),
        out_shape=piece(n_row // PAIR * n_col, blocks, 2 * half, LANES),
        in_specs=[in_smem()] * (len(places) + 1) + [in_vmem()] * (PAIR + 1),
        out_specs=in_vmem(),
        scratch_shapes=[
            pltpu.VMEM((PAIR * n_col, 2 * half, LANES), jnp.float32),
            pltpu.VMEM((n_row, 2 * half, LANES), jnp.float32),
        ]
        + slot_scratch(dims),
        compiler_params=params(large_limit),
        name="relax_level",
    )(*places, sources, *tiles, came)


def depend_kernel(dims, first, last, *refs):
    n_row, n_col, slots, half = dims
    chips = n_row // PAIR
    n_places = 0 if is_dense(dims) else PAIR
    places, refs = refs[:n_places], refs[n_places:]
    sources, tiles, refs = refs[0], refs[1 : 1 + PAIR], refs[1 + PAIR :]
    if first:
        came, out, near, low, lower, acc, table, filled = refs
    else:
        near, low, came, out, shown, paths, lower, acc, table, filled = refs
    my_x, my_core, my_col = position()
    ids = source_ids(sources, my_core * half, half)
    list_slots(dims, places, table, filled)
    if first:
        for r in range(n_col):
            for k in range(PAIR):
                h = my_core ^ k
                at_source = is_source(ids, (PAIR * my_x + h) * n_col + r)
                blocks = [came[chip * n_col + r, PAIR * my_x + h] for chip in range(chips)]
                found = merge([(block[:half], block[half:]) for block in blocks])
                dist, count = settle(*found, at_source)
                near[k * n_col + r, :half, :] = dist
                near[k * n_col + r, half:, :] = count
        for c in range(n_row):
            at_source = is_source(ids, c * n_col + my_col)
            blocks = [came[chip * n_col + my_col, c] for chip in range(chips)]
            found = merge([(block[:half], block[half:]) for block in blocks])
            dist, count = settle(*found, at_source)
            low[c, :half, :] = dist
            low[c, half:, :] = count
            lower[c, :half, :] = dist
            lower[c, half:, :] = jnp.where(count > 0.5, 1.0 / jnp.maximum(count, 1.0), 0.0)
    else:
        other = came[(PAIR * my_x + 1 - my_core) * n_col + my_col]
        for core in range(PAIR):
            block = jnp.where(my_core == core, near[my_col], other)
            dist = block[:half]
            shown[pl.ds(core * half, half), :] = jnp.where(dist < 0.5 * far_value, dist, -1.0)
            paths[pl.ds(core * half, half), :] = block[half:]
        for chip in range(chips):
            line = (PAIR * chip + my_core) * n_col
            parts = [came[line + col] for col in range(n_col)]
            total = functools.reduce(jnp.add, parts)
            for h in range(PAIR):
                c = PAIR * chip + h
                count = low[c, half:, :]
                coef = (1.0 + count * total[h * half : h * half + half]) / jnp.maximum(count, 1.0)
                lower[c, :half, :] = low[c, :half, :]
                lower[c, half:, :] = jnp.where(count > 0.5, coef, 0.0)
    acc[...] = jnp.zeros(acc.shape, jnp.float32)

    def column(c, _):
        turned = lower[c].T
        for s in range(half):
            dist = jnp.broadcast_to(turned[:, s : s + 1], (LANES, LANES))
            coef = jnp.broadcast_to(turned[:, half + s : half + s + 1], (LANES, LANES))

            def step(k, g, b, carry):
                hit = tiles[k][g] + near[b, pl.ds(s, 1), :] == dist
                terms = jnp.where(hit, coef, 0.0).reshape(LANES // SUB, SUB, LANES)
                acc[b, s] += jnp.sum(terms, axis=0)
                return carry

            over_slots(dims, places, table, filled, c, step, 0)
        return 0

    lax.fori_loop(0, n_row, column, 0)
    for r in range(n_col):
        for k in range(PAIR):
            if last:
                b = k * n_col + r
                at_source = is_source(ids, (PAIR * my_x + (my_core ^ k)) * n_col + r)
                term = jnp.where(at_source, 0.0, near[b, half:, :] * jnp.sum(acc[b], axis=1))
                out[(my_core ^ k) * n_col + r] = jnp.sum(term, axis=0, keepdims=True)
            else:
                sums = jnp.sum(acc[(my_core ^ k) * n_col + r], axis=1)
                for chip in range(chips):
                    line = (PAIR * chip + my_core) * n_col
                    out[line + r, pl.ds(k * half, half), :] = sums
    if not last:
        for chip in range(chips):
            for r in range(n_col):
                out[(PAIR * chip + 1 - my_core) * n_col + r] = near[n_col + my_col]


def depend_level(dims, first, last, places, sources, tiles, bands, came):
    n_row, n_col, slots, half = dims
    if last:
        out_shape = [piece(PAIR * n_col, 1, LANES)]
    else:
        out_shape = [piece(n_row * n_col, PAIR * half, LANES)]
    if first:
        out_shape += [piece(PAIR * n_col, 2 * half, LANES), piece(n_row, 2 * half, LANES)]
    else:
        out_shape += [piece(PAIR * half, LANES)] * 2
    return pl.pallas_call(
        functools.partial(depend_kernel, dims, first, last),
        out_shape=out_shape,
        in_specs=[in_smem()] * (len(places) + 1) + [in_vmem()] * (PAIR + len(bands) + 1),
        out_specs=[in_vmem()] * len(out_shape),
        scratch_shapes=[
            pltpu.VMEM((n_row, 2 * half, LANES), jnp.float32),
            pltpu.VMEM((PAIR * n_col, half, SUB, LANES), jnp.float32),
        ]
        + slot_scratch(dims),
        compiler_params=params(large_limit),
        name="depend_level",
    )(*places, sources, *tiles, *bands, came)


def all_to_all(value, axes):
    return lax.all_to_all(value, axes, split_axis=0, concat_axis=0, tiled=True)


def swap_core(value):
    return lax.ppermute(value, "core", [(0, 1), (1, 0)])


def per_device(tiles, tile_index, tile_count, sources):
    slots = tiles.shape[0]
    rows = sources.shape[0]
    dims = (lax.axis_size("chip") * PAIR, lax.axis_size("col"), slots, rows // PAIR)
    own_places = tile_index.T
    line = ("chip", "col")

    everyone = ("chip", "core", "col")

    firsts, turned = first_level(dims, own_places, sources, tiles)
    both = [turned, swap_core(turned)]
    places = [] if is_dense(dims) else [own_places, swap_core(own_places)]
    came = all_to_all(firsts, everyone)
    for level_no in range(1, LEVELS):
        whole = level_no == LEVELS - 1
        outs = relax_level(dims, level_no > 1, whole, places, sources, both, came)
        came = all_to_all(outs, line)
    sums, *bands = depend_level(dims, True, False, places, sources, both, [], came)
    for back_no in range(1, BACK):
        last = back_no == BACK - 1
        came = all_to_all(sums, everyone)
        sums, shown, paths = depend_level(dims, False, last, places, sources, both, bands, came)
    total = jnp.sum(all_to_all(sums, ("core", "col")), axis=(0, 1))
    return shown, paths, total / rows


def solution(mesh):
    groups, rows, cols = mesh.devices.shape
    pairs = mesh.devices.reshape(groups, rows // PAIR, PAIR, cols)
    paired = jax.sharding.Mesh(pairs, ("groups", "chip", "core", "col"))
    vertices = ("chip", "core", "col")
    everywhere = ("groups",) + vertices
    in_specs = (P(everywhere, None, None), P(everywhere, None), P(everywhere), P("groups"))
    out_specs = (P("groups", vertices), P("groups", vertices), P(everywhere))
    return jax.shard_map(
        per_device, mesh=paired, in_specs=in_specs, out_specs=out_specs, check_vma=False
    )
```

```python
import functools

import jax
import jax.numpy as jnp
from jax import lax
from jax.experimental import pallas as pl
from jax.experimental.pallas import tpu as pltpu
from jax.sharding import PartitionSpec as P

LEVELS = 3
BACK = 2
LANES = 128
SUB = 8
PAIR = 2
UNROLL = 2

far_value = 1000000.0
no_edge = 2000000.0
large_limit = 8 * 1024 * 1024
small_limit = 2 * 1024 * 1024


def in_vmem():
    return pl.BlockSpec(memory_space=pltpu.VMEM)


def in_smem():
    return pl.BlockSpec(memory_space=pltpu.SMEM)


def piece(*shape):
    return jax.ShapeDtypeStruct(shape, jnp.float32)


def params(limit):
    return pltpu.CompilerParams(vmem_limit_bytes=limit)


def is_dense(dims):
    return dims[2] == dims[0] * dims[1]


def position():
    return lax.axis_index("chip"), lax.axis_index("core"), lax.axis_index("col")


def source_ids(sources, first, half):
    row = lax.broadcasted_iota(jnp.int32, (half, LANES), 0)
    ids = jnp.zeros((half, LANES), jnp.int32)
    for s in range(half):
        ids = jnp.where(row == s, sources[first + s], ids)
    return ids


def is_source(ids, block):
    return ids == block * LANES + lax.broadcasted_iota(jnp.int32, ids.shape, 1)


def settle(found_dist, found_count, at_source):
    dist = jnp.where(at_source, 0.0, jnp.minimum(found_dist, far_value))
    count = jnp.where(found_dist == dist, found_count, 0.0)
    return dist, jnp.where(at_source, 1.0, 0.0) + count


def merge(pairs):
    best = functools.reduce(jnp.minimum, [p[0] for p in pairs])
    total = functools.reduce(jnp.add, [jnp.where(p[0] == best, p[1], 0.0) for p in pairs])
    return best, total


def first_kernel(dims, places, sources, tiles, out, turned, ids, slot_of, lines):
    n_row, n_col, slots, half = dims
    my_x, my_core, my_col = position()
    my_row = my_x * PAIR + my_core

    def clear(at, _):
        slot_of[at] = -1
        return 0

    if not is_dense(dims):
        lax.fori_loop(0, n_row * n_col, clear, 0)
    for g in range(slots):
        slot_of[places[0, g] * n_row + places[1, g]] = g
    ids[...] = source_ids(sources, my_core * half, half)
    lines[...] = jnp.zeros(lines.shape, jnp.float32)
    for s in range(PAIR * half):
        vertex = sources[s]
        block, place = vertex // LANES, lax.rem(vertex, LANES)
        r = lax.rem(block, n_col)

        @pl.when(block // n_col == my_row)
        def _():
            for c in range(n_row):
                g = slot_of[r * n_row + c]

                @pl.when(g >= 0)
                def _():
                    line = c % PAIR * half + s % half
                    row = tiles[g, pl.ds(place, 1), :]
                    lines[c // PAIR, s // half, pl.ds(line, 1), :] = row

    for chip in range(n_row // PAIR):
        for core in range(PAIR):
            line = lines[chip, core]
            line = jnp.where(line > 0, line, far_value)
            for col in range(n_col):
                out[(chip * PAIR + core) * n_col + col] = line
    for at in range(slots):
        raw = tiles[slot_of[at] if is_dense(dims) else at]
        turned[at] = jnp.where(raw > 0, raw, no_edge).T


def first_level(dims, places, sources, tiles):
    n_row, n_col, slots, half = dims
    return pl.pallas_call(
        functools.partial(first_kernel, dims),
        out_shape=[
            piece(n_row * n_col, PAIR * half, LANES),
            piece(*tiles.shape),
            jax.ShapeDtypeStruct((half, LANES), jnp.int32),
        ],
        in_specs=[in_smem(), in_smem(), in_vmem()],
        out_specs=[in_vmem()] * 3,
        scratch_shapes=[
            pltpu.SMEM((n_row * n_col,), jnp.int32),
            pltpu.VMEM((n_row // PAIR, PAIR, PAIR * half, LANES), jnp.float32),
        ],
        compiler_params=params(large_limit),
        name="first_level",
    )(places, sources, tiles)


def list_slots(dims, places, table, filled):
    n_row, n_col, slots, half = dims
    if is_dense(dims):
        return

    def clear(at, _):
        filled[at] = 0
        return 0

    lax.fori_loop(0, PAIR * n_row, clear, 0)
    for k in range(PAIR):

        def enter(g, _):
            at = k * n_row + places[k][1, g]
            table[at * n_col + filled[at]] = g
            filled[at] += 1
            return 0

        lax.fori_loop(0, slots, enter, 0)


def over_slots(dims, places, table, filled, c, step, carry):
    n_row, n_col, slots, half = dims
    for k in range(PAIR):
        if is_dense(dims):
            for r in range(n_col):
                carry = step(k, r * n_row + c, k * n_col + r, carry)
        else:
            at = k * n_row + c

            def entry(e, carry):
                g = table[at * n_col + e]
                return step(k, g, k * n_col + places[k][0, g], carry)

            carry = lax.fori_loop(0, filled[at], entry, carry)
    return carry


def slot_scratch(dims):
    n_row, n_col, slots, half = dims
    return [
        pltpu.SMEM((PAIR * n_row * n_col,), jnp.int32),
        pltpu.SMEM((PAIR * n_row,), jnp.int32),
    ]


def relax_kernel(dims, counted, whole, *refs):
    n_row, n_col, slots, half = dims
    chips = n_row // PAIR
    n_places = 0 if is_dense(dims) else PAIR
    places, refs = refs[:n_places], refs[n_places:]
    source_rows, tiles, refs = refs[0], refs[1 : 1 + PAIR], refs[1 + PAIR :]
    came, out, near, found, table, filled = refs
    my_x, my_core, my_col = position()
    ids = source_rows[...]
    list_slots(dims, places, table, filled)
    for r in range(n_col):
        for k in range(PAIR):
            h = my_core ^ k
            at_source = is_source(ids, (PAIR * my_x + h) * n_col + r)
            if counted:
                blocks = [came[chip * n_col + r, h] for chip in range(chips)]
                reached, count = merge([(block[:half], block[half:]) for block in blocks])
            else:
                parts = [came[at * n_col + r, pl.ds(h * half, half), :] for at in range(n_row)]
                reached = functools.reduce(jnp.minimum, parts)
                count = jnp.where(reached < far_value, 1.0, 0.0)
            dist, count = settle(reached, count, at_source)
            near[k * n_col + r, :half, :] = dist
            near[k * n_col + r, half:, :] = count
    lane = lax.broadcasted_iota(jnp.int32, (LANES, LANES), 1)

    def column(c, _):
        def lowest(s):
            def step(k, g, b, carry):
                return jnp.minimum(carry, tiles[k][g] + near[b, pl.ds(s, 1), :])

            start = jnp.full((LANES, LANES), far_value, jnp.float32)
            reached = over_slots(dims, places, table, filled, c, step, start)
            return jnp.min(reached, axis=1, keepdims=True)

        def tally(s, best):
            def step(k, g, b, carry):
                hit = tiles[k][g] + near[b, pl.ds(s, 1), :] == best
                return carry + jnp.where(hit, near[b, pl.ds(half + s, 1), :], 0.0)

            start = jnp.zeros((LANES, LANES), jnp.float32)
            counts = over_slots(dims, places, table, filled, c, step, start)
            return jnp.sum(counts, axis=1, keepdims=True)

        turned = jnp.zeros((LANES, LANES), jnp.float32)
        best = lowest(0)
        for s in range(half):
            later = lowest(s + 1) if s + 1 < half else None
            total = tally(s, best)
            turned = jnp.where(lane == s, best, jnp.where(lane == half + s, total, turned))
            best = later
        found[c] = turned.T[: 2 * half]
        return 0

    lax.fori_loop(0, n_row, column, 0, unroll=UNROLL)
    for chip in range(chips):
        for col in range(n_col):
            if whole:
                out[chip * n_col + col] = found[...]
            else:
                out[chip * n_col + col] = found[pl.ds(PAIR * chip, PAIR)]


def relax_level(dims, counted, whole, places, ids, tiles, came):
    n_row, n_col, slots, half = dims
    blocks = n_row if whole else PAIR
    return pl.pallas_call(
        functools.partial(relax_kernel, dims, counted, whole),
        out_shape=piece(n_row // PAIR * n_col, blocks, 2 * half, LANES),
        in_specs=[in_smem()] * len(places) + [in_vmem()] * (PAIR + 2),
        out_specs=in_vmem(),
        scratch_shapes=[
            pltpu.VMEM((PAIR * n_col, 2 * half, LANES), jnp.float32),
            pltpu.VMEM((n_row, 2 * half, LANES), jnp.float32),
        ]
        + slot_scratch(dims),
        compiler_params=params(large_limit),
        name="relax_level",
    )(*places, ids, *tiles, came)


def depend_kernel(dims, first, last, *refs):
    n_row, n_col, slots, half = dims
    chips = n_row // PAIR
    n_places = 0 if is_dense(dims) else PAIR
    places, refs = refs[:n_places], refs[n_places:]
    source_rows, tiles, refs = refs[0], refs[1 : 1 + PAIR], refs[1 + PAIR :]
    if first:
        came, out, near, low, lower, acc, table, filled = refs
    else:
        near, low, came, out, shown, paths, lower, acc, table, filled = refs
    my_x, my_core, my_col = position()
    ids = source_rows[...]
    list_slots(dims, places, table, filled)
    if first:
        for r in range(n_col):
            for k in range(PAIR):
                h = my_core ^ k
                at_source = is_source(ids, (PAIR * my_x + h) * n_col + r)
                blocks = [came[chip * n_col + r, PAIR * my_x + h] for chip in range(chips)]
                found = merge([(block[:half], block[half:]) for block in blocks])
                dist, count = settle(*found, at_source)
                near[k * n_col + r, :half, :] = dist
                near[k * n_col + r, half:, :] = count
        for c in range(n_row):
            at_source = is_source(ids, c * n_col + my_col)
            blocks = [came[chip * n_col + my_col, c] for chip in range(chips)]
            found = merge([(block[:half], block[half:]) for block in blocks])
            dist, count = settle(*found, at_source)
            low[c, :half, :] = dist
            low[c, half:, :] = count
            lower[c, :half, :] = dist
            lower[c, half:, :] = jnp.where(count > 0.5, 1.0 / jnp.maximum(count, 1.0), 0.0)
    else:
        other = came[(PAIR * my_x + 1 - my_core) * n_col + my_col]
        for core in range(PAIR):
            block = jnp.where(my_core == core, near[my_col], other)
            dist = block[:half]
            shown[pl.ds(core * half, half), :] = jnp.where(dist < 0.5 * far_value, dist, -1.0)
            paths[pl.ds(core * half, half), :] = block[half:]
        for chip in range(chips):
            line = (PAIR * chip + my_core) * n_col
            parts = [came[line + col] for col in range(n_col)]
            total = functools.reduce(jnp.add, parts)
            for h in range(PAIR):
                c = PAIR * chip + h
                count = low[c, half:, :]
                coef = (1.0 + count * total[h * half : h * half + half]) / jnp.maximum(count, 1.0)
                lower[c, :half, :] = low[c, :half, :]
                lower[c, half:, :] = jnp.where(count > 0.5, coef, 0.0)
    acc[...] = jnp.zeros(acc.shape, jnp.float32)

    def column(c, _):
        turned = lower[c].T
        for s in range(half):
            dist = jnp.broadcast_to(turned[:, s : s + 1], (LANES, LANES))
            coef = jnp.broadcast_to(turned[:, half + s : half + s + 1], (LANES, LANES))

            def step(k, g, b, carry):
                hit = tiles[k][g] + near[b, pl.ds(s, 1), :] == dist
                terms = jnp.where(hit, coef, 0.0).reshape(LANES // SUB, SUB, LANES)
                acc[b, s] += jnp.sum(terms, axis=0)
                return carry

            over_slots(dims, places, table, filled, c, step, 0)
        return 0

    lax.fori_loop(0, n_row, column, 0, unroll=UNROLL)
    for r in range(n_col):
        for k in range(PAIR):
            if last:
                b = k * n_col + r
                at_source = is_source(ids, (PAIR * my_x + (my_core ^ k)) * n_col + r)
                term = jnp.where(at_source, 0.0, near[b, half:, :] * jnp.sum(acc[b], axis=1))
                out[(my_core ^ k) * n_col + r] = jnp.sum(term, axis=0, keepdims=True)
            else:
                sums = jnp.sum(acc[(my_core ^ k) * n_col + r], axis=1)
                for chip in range(chips):
                    line = (PAIR * chip + my_core) * n_col
                    out[line + r, pl.ds(k * half, half), :] = sums
    if not last:
        for chip in range(chips):
            for r in range(n_col):
                out[(PAIR * chip + 1 - my_core) * n_col + r] = near[n_col + my_col]


def depend_level(dims, first, last, places, ids, tiles, bands, came):
    n_row, n_col, slots, half = dims
    if last:
        out_shape = [piece(PAIR * n_col, 1, LANES)]
    else:
        out_shape = [piece(n_row * n_col, PAIR * half, LANES)]
    if first:
        out_shape += [piece(PAIR * n_col, 2 * half, LANES), piece(n_row, 2 * half, LANES)]
    else:
        out_shape += [piece(PAIR * half, LANES)] * 2
    return pl.pallas_call(
        functools.partial(depend_kernel, dims, first, last),
        out_shape=out_shape,
        in_specs=[in_smem()] * len(places) + [in_vmem()] * (PAIR + len(bands) + 2),
        out_specs=[in_vmem()] * len(out_shape),
        scratch_shapes=[
            pltpu.VMEM((n_row, 2 * half, LANES), jnp.float32),
            pltpu.VMEM((PAIR * n_col, half, SUB, LANES), jnp.float32),
        ]
        + slot_scratch(dims),
        compiler_params=params(large_limit),
        name="depend_level",
    )(*places, ids, *tiles, *bands, came)


def all_to_all(value, axes):
    return lax.all_to_all(value, axes, split_axis=0, concat_axis=0, tiled=True)


def swap_core(value):
    return lax.ppermute(value, "core", [(0, 1), (1, 0)])


def per_device(tiles, tile_index, tile_count, sources):
    slots = tiles.shape[0]
    rows = sources.shape[0]
    dims = (lax.axis_size("chip") * PAIR, lax.axis_size("col"), slots, rows // PAIR)
    own_places = tile_index.T
    line = ("chip", "col")

    everyone = ("chip", "core", "col")

    firsts, turned, ids = first_level(dims, own_places, sources, tiles)
    both = [turned, swap_core(turned)]
    places = [] if is_dense(dims) else [own_places, swap_core(own_places)]
    came = all_to_all(firsts, everyone)
    for level_no in range(1, LEVELS):
        whole = level_no == LEVELS - 1
        outs = relax_level(dims, level_no > 1, whole, places, ids, both, came)
        came = all_to_all(outs, line)
    sums, *bands = depend_level(dims, True, False, places, ids, both, [], came)
    for back_no in range(1, BACK):
        last = back_no == BACK - 1
        came = all_to_all(sums, everyone)
        sums, shown, paths = depend_level(dims, False, last, places, ids, both, bands, came)
    total = jnp.sum(all_to_all(sums, ("core", "col")), axis=(0, 1))
    return shown, paths, total / rows


def solution(mesh):
    groups, rows, cols = mesh.devices.shape
    pairs = mesh.devices.reshape(groups, rows // PAIR, PAIR, cols)
    paired = jax.sharding.Mesh(pairs, ("groups", "chip", "core", "col"))
    vertices = ("chip", "core", "col")
    everywhere = ("groups",) + vertices
    in_specs = (P(everywhere, None, None), P(everywhere, None), P(everywhere), P("groups"))
    out_specs = (P("groups", vertices), P("groups", vertices), P(everywhere))
    return jax.shard_map(
        per_device, mesh=paired, in_specs=in_specs, out_specs=out_specs, check_vma=False
    )
```

```python
import functools

import jax
import jax.numpy as jnp
from jax import lax
from jax.experimental import pallas as pl
from jax.experimental.pallas import tpu as pltpu
from jax.sharding import PartitionSpec as P

LEVELS = 3
BACK = 2
LANES = 128
SUB = 8
PAIR = 2
UNROLL = 4

far_value = 1000000.0
no_edge = 2000000.0
large_limit = 8 * 1024 * 1024
small_limit = 2 * 1024 * 1024


def in_vmem():
    return pl.BlockSpec(memory_space=pltpu.VMEM)


def in_smem():
    return pl.BlockSpec(memory_space=pltpu.SMEM)


def piece(*shape):
    return jax.ShapeDtypeStruct(shape, jnp.float32)


def params(limit):
    return pltpu.CompilerParams(vmem_limit_bytes=limit)


def is_dense(dims):
    return dims[2] == dims[0] * dims[1]


def position():
    return lax.axis_index("chip"), lax.axis_index("core"), lax.axis_index("col")


def source_ids(scalars, first, half):
    row = lax.broadcasted_iota(jnp.int32, (half, LANES), 0)
    ids = jnp.zeros((half, LANES), jnp.int32)
    for s in range(half):
        ids = jnp.where(row == s, scalars[first + s], ids)
    return ids


def is_source(ids, block):
    return ids == block * LANES + lax.broadcasted_iota(jnp.int32, ids.shape, 1)


def settle(found_dist, found_count, at_source):
    dist = jnp.where(at_source, 0.0, jnp.minimum(found_dist, far_value))
    count = jnp.where(found_dist == dist, found_count, 0.0)
    return dist, jnp.where(at_source, 1.0, 0.0) + count


def merge(pairs):
    best = functools.reduce(jnp.minimum, [p[0] for p in pairs])
    total = functools.reduce(jnp.add, [jnp.where(p[0] == best, p[1], 0.0) for p in pairs])
    return best, total


def first_kernel(dims, scalars, tiles, out, turned, ids, slot_of, lines):
    n_row, n_col, slots, half = dims
    first_source = 2 * slots
    my_x, my_core, my_col = position()
    my_row = my_x * PAIR + my_core

    def clear(at, _):
        slot_of[at] = -1
        return 0

    if not is_dense(dims):
        lax.fori_loop(0, n_row * n_col, clear, 0)
    for g in range(slots):
        slot_of[scalars[g] * n_row + scalars[slots + g]] = g
    ids[...] = source_ids(scalars, first_source + my_core * half, half)
    lines[...] = jnp.zeros(lines.shape, jnp.float32)
    for s in range(PAIR * half):
        vertex = scalars[first_source + s]
        block, place = vertex // LANES, lax.rem(vertex, LANES)
        r = lax.rem(block, n_col)

        @pl.when(block // n_col == my_row)
        def _():
            for c in range(n_row):
                g = slot_of[r * n_row + c]

                @pl.when(g >= 0)
                def _():
                    line = c % PAIR * half + s % half
                    row = tiles[g, pl.ds(place, 1), :]
                    lines[c // PAIR, s // half, pl.ds(line, 1), :] = row

    for chip in range(n_row // PAIR):
        for core in range(PAIR):
            line = lines[chip, core]
            line = jnp.where(line > 0, line, far_value)
            for col in range(n_col):
                out[(chip * PAIR + core) * n_col + col] = line
    for at in range(slots):
        raw = tiles[slot_of[at] if is_dense(dims) else at]
        turned[at] = jnp.where(raw > 0, raw, no_edge).T


def first_level(dims, scalars, tiles):
    n_row, n_col, slots, half = dims
    return pl.pallas_call(
        functools.partial(first_kernel, dims),
        out_shape=[
            piece(n_row * n_col, PAIR * half, LANES),
            piece(*tiles.shape),
            jax.ShapeDtypeStruct((half, LANES), jnp.int32),
        ],
        in_specs=[in_smem(), in_vmem()],
        out_specs=[in_vmem()] * 3,
        scratch_shapes=[
            pltpu.SMEM((n_row * n_col,), jnp.int32),
            pltpu.VMEM((n_row // PAIR, PAIR, PAIR * half, LANES), jnp.float32),
        ],
        compiler_params=params(large_limit),
        name="first_level",
    )(scalars, tiles)


def list_slots(dims, places, table, filled):
    n_row, n_col, slots, half = dims
    if is_dense(dims):
        return

    def clear(at, _):
        filled[at] = 0
        return 0

    lax.fori_loop(0, PAIR * n_row, clear, 0)
    for k in range(PAIR):

        def enter(g, _):
            at = k * n_row + places[k][1, g]
            table[at * n_col + filled[at]] = g
            filled[at] += 1
            return 0

        lax.fori_loop(0, slots, enter, 0)


def over_slots(dims, places, table, filled, c, step, carry):
    n_row, n_col, slots, half = dims
    for k in range(PAIR):
        if is_dense(dims):
            for r in range(n_col):
                carry = step(k, r * n_row + c, k * n_col + r, carry)
        else:
            at = k * n_row + c

            def entry(e, carry):
                g = table[at * n_col + e]
                return step(k, g, k * n_col + places[k][0, g], carry)

            carry = lax.fori_loop(0, filled[at], entry, carry)
    return carry


def slot_scratch(dims):
    n_row, n_col, slots, half = dims
    return [
        pltpu.SMEM((PAIR * n_row * n_col,), jnp.int32),
        pltpu.SMEM((PAIR * n_row,), jnp.int32),
    ]


def relax_kernel(dims, counted, whole, *refs):
    n_row, n_col, slots, half = dims
    chips = n_row // PAIR
    n_places = 0 if is_dense(dims) else PAIR
    places, refs = refs[:n_places], refs[n_places:]
    source_rows, tiles, refs = refs[0], refs[1 : 1 + PAIR], refs[1 + PAIR :]
    came, out, near, found, table, filled = refs
    my_x, my_core, my_col = position()
    ids = source_rows[...]
    list_slots(dims, places, table, filled)
    for r in range(n_col):
        for k in range(PAIR):
            h = my_core ^ k
            at_source = is_source(ids, (PAIR * my_x + h) * n_col + r)
            if counted:
                blocks = [came[r * chips + chip, h] for chip in range(chips)]
                reached, count = merge([(block[:half], block[half:]) for block in blocks])
            else:
                parts = [came[at * n_col + r, pl.ds(h * half, half), :] for at in range(n_row)]
                reached = functools.reduce(jnp.minimum, parts)
                count = jnp.where(reached < far_value, 1.0, 0.0)
            dist, count = settle(reached, count, at_source)
            near[k * n_col + r, :half, :] = dist
            near[k * n_col + r, half:, :] = count
    lane = lax.broadcasted_iota(jnp.int32, (LANES, LANES), 1)

    def column(c, _):
        def lowest(s):
            def step(k, g, b, carry):
                return jnp.minimum(carry, tiles[k][g] + near[b, pl.ds(s, 1), :])

            start = jnp.full((LANES, LANES), far_value, jnp.float32)
            reached = over_slots(dims, places, table, filled, c, step, start)
            return jnp.min(reached, axis=1, keepdims=True)

        def tally(s, best):
            def step(k, g, b, carry):
                hit = tiles[k][g] + near[b, pl.ds(s, 1), :] == best
                return carry + jnp.where(hit, near[b, pl.ds(half + s, 1), :], 0.0)

            start = jnp.zeros((LANES, LANES), jnp.float32)
            counts = over_slots(dims, places, table, filled, c, step, start)
            return jnp.sum(counts, axis=1, keepdims=True)

        turned = jnp.zeros((LANES, LANES), jnp.float32)
        best = lowest(0)
        for s in range(half):
            later = lowest(s + 1) if s + 1 < half else None
            total = tally(s, best)
            turned = jnp.where(lane == s, best, jnp.where(lane == half + s, total, turned))
            best = later
        found[c] = turned.T[: 2 * half]
        return 0

    lax.fori_loop(0, n_row, column, 0, unroll=UNROLL)
    for chip in range(chips):
        for col in range(n_col):
            if whole:
                out[col * chips + chip] = found[...]
            else:
                out[col * chips + chip] = found[pl.ds(PAIR * chip, PAIR)]


def relax_level(dims, counted, whole, places, ids, tiles, came):
    n_row, n_col, slots, half = dims
    blocks = n_row if whole else PAIR
    return pl.pallas_call(
        functools.partial(relax_kernel, dims, counted, whole),
        out_shape=piece(n_row // PAIR * n_col, blocks, 2 * half, LANES),
        in_specs=[in_smem()] * len(places) + [in_vmem()] * (PAIR + 2),
        out_specs=in_vmem(),
        scratch_shapes=[
            pltpu.VMEM((PAIR * n_col, 2 * half, LANES), jnp.float32),
            pltpu.VMEM((n_row, 2 * half, LANES), jnp.float32),
        ]
        + slot_scratch(dims),
        compiler_params=params(large_limit),
        name="relax_level",
    )(*places, ids, *tiles, came)


def depend_kernel(dims, first, last, *refs):
    n_row, n_col, slots, half = dims
    chips = n_row // PAIR
    n_places = 0 if is_dense(dims) else PAIR
    places, refs = refs[:n_places], refs[n_places:]
    source_rows, tiles, refs = refs[0], refs[1 : 1 + PAIR], refs[1 + PAIR :]
    if first:
        came, out, near, low, lower, acc, table, filled = refs
    else:
        near, low, came, out, shown, paths, lower, acc, table, filled, held, sems = refs
    my_x, my_core, my_col = position()
    ids = source_rows[...]
    list_slots(dims, places, table, filled)
    if first:
        for r in range(n_col):
            for k in range(PAIR):
                h = my_core ^ k
                at_source = is_source(ids, (PAIR * my_x + h) * n_col + r)
                blocks = [came[r * chips + chip, PAIR * my_x + h] for chip in range(chips)]
                found = merge([(block[:half], block[half:]) for block in blocks])
                dist, count = settle(*found, at_source)
                near[k * n_col + r, :half, :] = dist
                near[k * n_col + r, half:, :] = count
        for c in range(n_row):
            at_source = is_source(ids, c * n_col + my_col)
            blocks = [came[my_col * chips + chip, c] for chip in range(chips)]
            found = merge([(block[:half], block[half:]) for block in blocks])
            dist, count = settle(*found, at_source)
            low[c, :half, :] = dist
            low[c, half:, :] = count
            lower[c, :half, :] = dist
            lower[c, half:, :] = jnp.where(count > 0.5, 1.0 / jnp.maximum(count, 1.0), 0.0)
    else:
        other = came[(PAIR * my_x + 1 - my_core) * n_col + my_col]
        for core in range(PAIR):
            block = jnp.where(my_core == core, near[my_col], other)
            dist = block[:half]
            rows = pl.ds(core * half, half)
            held[0, rows, :] = jnp.where(dist < 0.5 * far_value, dist, -1.0)
            held[1, rows, :] = block[half:]
        results = [
            pltpu.make_async_copy(held.at[0], shown, sems.at[0]),
            pltpu.make_async_copy(held.at[1], paths, sems.at[1]),
        ]
        for copy in results:
            copy.start()
        for chip in range(chips):
            line = (PAIR * chip + my_core) * n_col
            parts = [came[line + col] for col in range(n_col)]
            total = functools.reduce(jnp.add, parts)
            for h in range(PAIR):
                c = PAIR * chip + h
                count = low[c, half:, :]
                coef = (1.0 + count * total[h * half : h * half + half]) / jnp.maximum(count, 1.0)
                lower[c, :half, :] = low[c, :half, :]
                lower[c, half:, :] = jnp.where(count > 0.5, coef, 0.0)
    acc[...] = jnp.zeros(acc.shape, jnp.float32)

    def column(c, _):
        turned = lower[c].T
        for s in range(half):
            dist = jnp.broadcast_to(turned[:, s : s + 1], (LANES, LANES))
            coef = jnp.broadcast_to(turned[:, half + s : half + s + 1], (LANES, LANES))

            def step(k, g, b, carry):
                hit = tiles[k][g] + near[b, pl.ds(s, 1), :] == dist
                terms = jnp.where(hit, coef, 0.0).reshape(LANES // SUB, SUB, LANES)
                acc[b, s] += jnp.sum(terms, axis=0)
                return carry

            over_slots(dims, places, table, filled, c, step, 0)
        return 0

    lax.fori_loop(0, n_row, column, 0, unroll=UNROLL)
    for r in range(n_col):
        for k in range(PAIR):
            if last:
                b = k * n_col + r
                at_source = is_source(ids, (PAIR * my_x + (my_core ^ k)) * n_col + r)
                term = jnp.where(at_source, 0.0, near[b, half:, :] * jnp.sum(acc[b], axis=1))
                out[(my_core ^ k) * n_col + r] = jnp.sum(term, axis=0, keepdims=True)
            else:
                sums = jnp.sum(acc[(my_core ^ k) * n_col + r], axis=1)
                for chip in range(chips):
                    line = (PAIR * chip + my_core) * n_col
                    out[line + r, pl.ds(k * half, half), :] = sums
    if not first:
        for copy in results:
            copy.wait()
    if not last:
        for chip in range(chips):
            for r in range(n_col):
                out[(PAIR * chip + 1 - my_core) * n_col + r] = near[n_col + my_col]


def depend_level(dims, first, last, places, ids, tiles, bands, came):
    n_row, n_col, slots, half = dims
    if last:
        out_shape = [piece(PAIR * n_col, 1, LANES)]
    else:
        out_shape = [piece(n_row * n_col, PAIR * half, LANES)]
    scratch = [
        pltpu.VMEM((n_row, 2 * half, LANES), jnp.float32),
        pltpu.VMEM((PAIR * n_col, half, SUB, LANES), jnp.float32),
    ] + slot_scratch(dims)
    if first:
        out_shape += [piece(PAIR * n_col, 2 * half, LANES), piece(n_row, 2 * half, LANES)]
        out_specs = [in_vmem()] * 3
    else:
        out_shape += [piece(PAIR * half, LANES)] * 2
        out_specs = [in_vmem()] + [pl.BlockSpec(memory_space=pl.ANY)] * 2
        scratch += [
            pltpu.VMEM((2, PAIR * half, LANES), jnp.float32),
            pltpu.SemaphoreType.DMA((2,)),
        ]
    return pl.pallas_call(
        functools.partial(depend_kernel, dims, first, last),
        out_shape=out_shape,
        in_specs=[in_smem()] * len(places) + [in_vmem()] * (PAIR + len(bands) + 2),
        out_specs=out_specs,
        scratch_shapes=scratch,
        compiler_params=params(large_limit),
        name="depend_level",
    )(*places, ids, *tiles, *bands, came)


def all_to_all(value, axes):
    return lax.all_to_all(value, axes, split_axis=0, concat_axis=0, tiled=True)


def swap_core(value):
    return lax.ppermute(value, "core", [(0, 1), (1, 0)])


def per_device(tiles, tile_index, tile_count, sources):
    slots = tiles.shape[0]
    rows = sources.shape[0]
    dims = (lax.axis_size("chip") * PAIR, lax.axis_size("col"), slots, rows // PAIR)
    own_places = tile_index.T
    line = ("col", "chip")

    everyone = ("chip", "core", "col")

    scalars = jnp.concatenate([own_places.reshape(2 * slots), sources])
    firsts, turned, ids = first_level(dims, scalars, tiles)
    both = [turned, swap_core(turned)]
    places = [] if is_dense(dims) else [own_places, swap_core(own_places)]
    came = all_to_all(firsts, everyone)
    for level_no in range(1, LEVELS):
        whole = level_no == LEVELS - 1
        outs = relax_level(dims, level_no > 1, whole, places, ids, both, came)
        came = all_to_all(outs, line)
    sums, *bands = depend_level(dims, True, False, places, ids, both, [], came)
    for back_no in range(1, BACK):
        last = back_no == BACK - 1
        came = all_to_all(sums, everyone)
        sums, shown, paths = depend_level(dims, False, last, places, ids, both, bands, came)
    total = jnp.sum(all_to_all(sums, ("core", "col")), axis=(0, 1))
    return shown, paths, total / rows


def solution(mesh):
    groups, rows, cols = mesh.devices.shape
    pairs = mesh.devices.reshape(groups, rows // PAIR, PAIR, cols)
    paired = jax.sharding.Mesh(pairs, ("groups", "chip", "core", "col"))
    vertices = ("chip", "core", "col")
    everywhere = ("groups",) + vertices
    in_specs = (P(everywhere, None, None), P(everywhere, None), P(everywhere), P("groups"))
    out_specs = (P("groups", vertices), P("groups", vertices), P(everywhere))
    return jax.shard_map(
        per_device, mesh=paired, in_specs=in_specs, out_specs=out_specs, check_vma=False
    )
```

```python
import functools

import jax
import jax.numpy as jnp
from jax import lax
from jax.experimental import pallas as pl
from jax.experimental.pallas import tpu as pltpu
from jax.sharding import PartitionSpec as P

LEVELS = 3
BACK = 2
LANES = 128
SUB = 8
PAIR = 2
UNROLL = 2

far_value = 1000000.0
no_edge = 2000000.0
large_limit = 8 * 1024 * 1024
small_limit = 2 * 1024 * 1024


def in_vmem():
    return pl.BlockSpec(memory_space=pltpu.VMEM)


def in_smem():
    return pl.BlockSpec(memory_space=pltpu.SMEM)


def piece(*shape):
    return jax.ShapeDtypeStruct(shape, jnp.float32)


def params(limit):
    return pltpu.CompilerParams(vmem_limit_bytes=limit)


def is_dense(dims):
    return dims[2] == dims[0] * dims[1]


def position():
    return lax.axis_index("chip"), lax.axis_index("core"), lax.axis_index("col")


def source_ids(sources, first, half):
    row = lax.broadcasted_iota(jnp.int32, (half, LANES), 0)
    ids = jnp.zeros((half, LANES), jnp.int32)
    for s in range(half):
        ids = jnp.where(row == s, sources[first + s], ids)
    return ids


def is_source(ids, block):
    return ids == block * LANES + lax.broadcasted_iota(jnp.int32, ids.shape, 1)


def settle(found_dist, found_count, at_source):
    dist = jnp.where(at_source, 0.0, jnp.minimum(found_dist, far_value))
    count = jnp.where(found_dist == dist, found_count, 0.0)
    return dist, jnp.where(at_source, 1.0, 0.0) + count


def merge(pairs):
    best = functools.reduce(jnp.minimum, [p[0] for p in pairs])
    total = functools.reduce(jnp.add, [jnp.where(p[0] == best, p[1], 0.0) for p in pairs])
    return best, total


def first_kernel(dims, places, sources, tiles, out, turned, ids, slot_of, lines):
    n_row, n_col, slots, half = dims
    my_x, my_core, my_col = position()
    my_row = my_x * PAIR + my_core

    def clear(at, _):
        slot_of[at] = -1
        return 0

    if not is_dense(dims):
        lax.fori_loop(0, n_row * n_col, clear, 0)
    for g in range(slots):
        slot_of[places[0, g] * n_row + places[1, g]] = g
    ids[...] = source_ids(sources, my_core * half, half)
    lines[...] = jnp.zeros(lines.shape, jnp.float32)
    for s in range(PAIR * half):
        vertex = sources[s]
        block, place = vertex // LANES, lax.rem(vertex, LANES)
        r = lax.rem(block, n_col)

        @pl.when(block // n_col == my_row)
        def _():
            for c in range(n_row):
                g = slot_of[r * n_row + c]

                @pl.when(g >= 0)
                def _():
                    line = c % PAIR * half + s % half
                    row = tiles[g, pl.ds(place, 1), :]
                    lines[c // PAIR, s // half, pl.ds(line, 1), :] = row

    for chip in range(n_row // PAIR):
        for core in range(PAIR):
            line = lines[chip, core]
            line = jnp.where(line > 0, line, far_value)
            for col in range(n_col):
                out[(chip * PAIR + core) * n_col + col] = line
    for at in range(slots):
        raw = tiles[slot_of[at] if is_dense(dims) else at]
        turned[at] = jnp.where(raw > 0, raw, no_edge).T


def first_level(dims, places, sources, tiles):
    n_row, n_col, slots, half = dims
    return pl.pallas_call(
        functools.partial(first_kernel, dims),
        out_shape=[
            piece(n_row * n_col, PAIR * half, LANES),
            piece(*tiles.shape),
            jax.ShapeDtypeStruct((half, LANES), jnp.int32),
        ],
        in_specs=[in_smem(), in_smem(), in_vmem()],
        out_specs=[in_vmem()] * 3,
        scratch_shapes=[
            pltpu.SMEM((n_row * n_col,), jnp.int32),
            pltpu.VMEM((n_row // PAIR, PAIR, PAIR * half, LANES), jnp.float32),
        ],
        compiler_params=params(large_limit),
        name="first_level",
    )(places, sources, tiles)


def list_slots(dims, places, table, filled):
    n_row, n_col, slots, half = dims
    if is_dense(dims):
        return

    def clear(at, _):
        filled[at] = 0
        return 0

    lax.fori_loop(0, PAIR * n_row, clear, 0)
    for k in range(PAIR):

        def enter(g, _):
            at = k * n_row + places[k][1, g]
            table[at * n_col + filled[at]] = g
            filled[at] += 1
            return 0

        lax.fori_loop(0, slots, enter, 0)


def over_slots(dims, places, table, filled, c, step, carry):
    n_row, n_col, slots, half = dims
    for k in range(PAIR):
        if is_dense(dims):
            for r in range(n_col):
                carry = step(k, r * n_row + c, k * n_col + r, carry)
        else:
            at = k * n_row + c

            def entry(e, carry):
                g = table[at * n_col + e]
                return step(k, g, k * n_col + places[k][0, g], carry)

            carry = lax.fori_loop(0, filled[at], entry, carry)
    return carry


def slot_scratch(dims):
    n_row, n_col, slots, half = dims
    return [
        pltpu.SMEM((PAIR * n_row * n_col,), jnp.int32),
        pltpu.SMEM((PAIR * n_row,), jnp.int32),
    ]


def relax_kernel(dims, counted, whole, *refs):
    n_row, n_col, slots, half = dims
    chips = n_row // PAIR
    n_places = 0 if is_dense(dims) else PAIR
    places, refs = refs[:n_places], refs[n_places:]
    source_rows, tiles, refs = refs[0], refs[1 : 1 + PAIR], refs[1 + PAIR :]
    came, out, near, found, table, filled = refs
    my_x, my_core, my_col = position()
    ids = source_rows[...]
    list_slots(dims, places, table, filled)
    for r in range(n_col):
        for k in range(PAIR):
            h = my_core ^ k
            at_source = is_source(ids, (PAIR * my_x + h) * n_col + r)
            if counted:
                blocks = [came[r * chips + chip, h] for chip in range(chips)]
                reached, count = merge([(block[:half], block[half:]) for block in blocks])
            else:
                parts = [came[at * n_col + r, pl.ds(h * half, half), :] for at in range(n_row)]
                reached = functools.reduce(jnp.minimum, parts)
                count = jnp.where(reached < far_value, 1.0, 0.0)
            dist, count = settle(reached, count, at_source)
            near[k * n_col + r, :half, :] = dist
            near[k * n_col + r, half:, :] = count
    lane = lax.broadcasted_iota(jnp.int32, (LANES, LANES), 1)

    def column(c, _):
        def lowest(s):
            def step(k, g, b, carry):
                return jnp.minimum(carry, tiles[k][g] + near[b, pl.ds(s, 1), :])

            start = jnp.full((LANES, LANES), far_value, jnp.float32)
            reached = over_slots(dims, places, table, filled, c, step, start)
            return jnp.min(reached, axis=1, keepdims=True)

        def tally(s, best):
            def step(k, g, b, carry):
                hit = tiles[k][g] + near[b, pl.ds(s, 1), :] == best
                return carry + jnp.where(hit, near[b, pl.ds(half + s, 1), :], 0.0)

            start = jnp.zeros((LANES, LANES), jnp.float32)
            counts = over_slots(dims, places, table, filled, c, step, start)
            return jnp.sum(counts, axis=1, keepdims=True)

        turned = jnp.zeros((LANES, LANES), jnp.float32)
        best = lowest(0)
        for s in range(half):
            later = lowest(s + 1) if s + 1 < half else None
            total = tally(s, best)
            turned = jnp.where(lane == s, best, jnp.where(lane == half + s, total, turned))
            best = later
        found[c] = turned.T[: 2 * half]
        return 0

    lax.fori_loop(0, n_row, column, 0, unroll=UNROLL)
    for chip in range(chips):
        for col in range(n_col):
            if whole:
                out[col * chips + chip] = found[...]
            else:
                out[col * chips + chip] = found[pl.ds(PAIR * chip, PAIR)]


def relax_level(dims, counted, whole, places, ids, tiles, came):
    n_row, n_col, slots, half = dims
    blocks = n_row if whole else PAIR
    return pl.pallas_call(
        functools.partial(relax_kernel, dims, counted, whole),
        out_shape=piece(n_row // PAIR * n_col, blocks, 2 * half, LANES),
        in_specs=[in_smem()] * len(places) + [in_vmem()] * (PAIR + 2),
        out_specs=in_vmem(),
        scratch_shapes=[
            pltpu.VMEM((PAIR * n_col, 2 * half, LANES), jnp.float32),
            pltpu.VMEM((n_row, 2 * half, LANES), jnp.float32),
        ]
        + slot_scratch(dims),
        compiler_params=params(large_limit),
        name="relax_level",
    )(*places, ids, *tiles, came)


def depend_kernel(dims, first, last, *refs):
    n_row, n_col, slots, half = dims
    chips = n_row // PAIR
    n_places = 0 if is_dense(dims) else PAIR
    places, refs = refs[:n_places], refs[n_places:]
    source_rows, tiles, refs = refs[0], refs[1 : 1 + PAIR], refs[1 + PAIR :]
    if first:
        came, out, near, low, lower, acc, table, filled = refs
    else:
        near, low, came, out, state, lower, acc, table, filled = refs
    my_x, my_core, my_col = position()
    ids = source_rows[...]
    list_slots(dims, places, table, filled)
    if first:
        for r in range(n_col):
            for k in range(PAIR):
                h = my_core ^ k
                at_source = is_source(ids, (PAIR * my_x + h) * n_col + r)
                blocks = [came[r * chips + chip, PAIR * my_x + h] for chip in range(chips)]
                found = merge([(block[:half], block[half:]) for block in blocks])
                dist, count = settle(*found, at_source)
                near[k * n_col + r, :half, :] = dist
                near[k * n_col + r, half:, :] = count
        for c in range(n_row):
            at_source = is_source(ids, c * n_col + my_col)
            blocks = [came[my_col * chips + chip, c] for chip in range(chips)]
            found = merge([(block[:half], block[half:]) for block in blocks])
            dist, count = settle(*found, at_source)
            low[c, :half, :] = dist
            low[c, half:, :] = count
            lower[c, :half, :] = dist
            lower[c, half:, :] = jnp.where(count > 0.5, 1.0 / jnp.maximum(count, 1.0), 0.0)
    else:
        other = came[(PAIR * my_x + 1 - my_core) * n_col + my_col]
        for core in range(PAIR):
            block = jnp.where(my_core == core, near[my_col], other)
            dist = block[:half]
            rows = pl.ds(core * half, half)
            state[0, rows, :] = jnp.where(dist < 0.5 * far_value, dist, -1.0)
            state[1, rows, :] = block[half:]
        for chip in range(chips):
            line = (PAIR * chip + my_core) * n_col
            parts = [came[line + col] for col in range(n_col)]
            total = functools.reduce(jnp.add, parts)
            for h in range(PAIR):
                c = PAIR * chip + h
                count = low[c, half:, :]
                coef = (1.0 + count * total[h * half : h * half + half]) / jnp.maximum(count, 1.0)
                lower[c, :half, :] = low[c, :half, :]
                lower[c, half:, :] = jnp.where(count > 0.5, coef, 0.0)
    acc[...] = jnp.zeros(acc.shape, jnp.float32)

    def column(c, _):
        turned = lower[c].T
        for s in range(half):
            dist = jnp.broadcast_to(turned[:, s : s + 1], (LANES, LANES))
            coef = jnp.broadcast_to(turned[:, half + s : half + s + 1], (LANES, LANES))

            def step(k, g, b, carry):
                hit = tiles[k][g] + near[b, pl.ds(s, 1), :] == dist
                terms = jnp.where(hit, coef, 0.0).reshape(LANES // SUB, SUB, LANES)
                acc[b, s] += jnp.sum(terms, axis=0)
                return carry

            over_slots(dims, places, table, filled, c, step, 0)
        return 0

    lax.fori_loop(0, n_row, column, 0, unroll=UNROLL)
    for r in range(n_col):
        for k in range(PAIR):
            if last:
                b = k * n_col + r
                at_source = is_source(ids, (PAIR * my_x + (my_core ^ k)) * n_col + r)
                term = jnp.where(at_source, 0.0, near[b, half:, :] * jnp.sum(acc[b], axis=1))
                out[(my_core ^ k) * n_col + r] = jnp.sum(term, axis=0, keepdims=True)
            else:
                sums = jnp.sum(acc[(my_core ^ k) * n_col + r], axis=1)
                for chip in range(chips):
                    line = (PAIR * chip + my_core) * n_col
                    out[line + r, pl.ds(k * half, half), :] = sums
    if not last:
        for chip in range(chips):
            for r in range(n_col):
                out[(PAIR * chip + 1 - my_core) * n_col + r] = near[n_col + my_col]


def depend_level(dims, first, last, places, ids, tiles, bands, came):
    n_row, n_col, slots, half = dims
    if last:
        out_shape = [piece(PAIR * n_col, 1, LANES)]
    else:
        out_shape = [piece(n_row * n_col, PAIR * half, LANES)]
    if first:
        out_shape += [piece(PAIR * n_col, 2 * half, LANES), piece(n_row, 2 * half, LANES)]
    else:
        out_shape += [piece(2, PAIR * half, LANES)]
    return pl.pallas_call(
        functools.partial(depend_kernel, dims, first, last),
        out_shape=out_shape,
        in_specs=[in_smem()] * len(places) + [in_vmem()] * (PAIR + len(bands) + 2),
        out_specs=[in_vmem()] * len(out_shape),
        scratch_shapes=[
            pltpu.VMEM((n_row, 2 * half, LANES), jnp.float32),
            pltpu.VMEM((PAIR * n_col, half, SUB, LANES), jnp.float32),
        ]
        + slot_scratch(dims),
        compiler_params=params(large_limit),
        name="depend_level",
    )(*places, ids, *tiles, *bands, came)


def result_kernel(rows, came, state, shown, paths, centrality):
    shown[...] = state[0]
    paths[...] = state[1]
    shares = [came[at] for at in range(came.shape[0])]
    centrality[...] = functools.reduce(jnp.add, shares) / rows


def results(dims, came, state):
    rows = PAIR * dims[3]
    return pl.pallas_call(
        functools.partial(result_kernel, rows),
        out_shape=[piece(rows, LANES)] * 2 + [piece(1, LANES)],
        in_specs=[in_vmem()] * 2,
        out_specs=[in_vmem()] * 3,
        compiler_params=params(small_limit),
        name="results",
    )(came, state)


def all_to_all(value, axes):
    return lax.all_to_all(value, axes, split_axis=0, concat_axis=0, tiled=True)


def swap_core(value):
    return lax.ppermute(value, "core", [(0, 1), (1, 0)])


def per_device(tiles, tile_index, tile_count, sources):
    slots = tiles.shape[0]
    rows = sources.shape[0]
    dims = (lax.axis_size("chip") * PAIR, lax.axis_size("col"), slots, rows // PAIR)
    own_places = tile_index.T
    line = ("col", "chip")

    everyone = ("chip", "core", "col")

    firsts, turned, ids = first_level(dims, own_places, sources, tiles)
    both = [turned, swap_core(turned)]
    places = [] if is_dense(dims) else [own_places, swap_core(own_places)]
    came = all_to_all(firsts, everyone)
    for level_no in range(1, LEVELS):
        whole = level_no == LEVELS - 1
        outs = relax_level(dims, level_no > 1, whole, places, ids, both, came)
        came = all_to_all(outs, line)
    sums, *bands = depend_level(dims, True, False, places, ids, both, [], came)
    for back_no in range(1, BACK):
        last = back_no == BACK - 1
        came = all_to_all(sums, everyone)
        sums, state = depend_level(dims, False, last, places, ids, both, bands, came)
    shown, paths, centrality = results(dims, all_to_all(sums, ("core", "col")), state)
    return shown, paths, centrality.reshape(LANES)


def solution(mesh):
    groups, rows, cols = mesh.devices.shape
    pairs = mesh.devices.reshape(groups, rows // PAIR, PAIR, cols)
    paired = jax.sharding.Mesh(pairs, ("groups", "chip", "core", "col"))
    vertices = ("chip", "core", "col")
    everywhere = ("groups",) + vertices
    in_specs = (P(everywhere, None, None), P(everywhere, None), P(everywhere), P("groups"))
    out_specs = (P("groups", vertices), P("groups", vertices), P(everywhere))
    return jax.shard_map(
        per_device, mesh=paired, in_specs=in_specs, out_specs=out_specs, check_vma=False
    )
```

```python
import functools

import jax
import jax.numpy as jnp
from jax import lax
from jax.experimental import pallas as pl
from jax.experimental.pallas import tpu as pltpu
from jax.sharding import PartitionSpec as P

LEVELS = 3
BACK = 2
LANES = 128
SUB = 8
PAIR = 2
UNROLL = 2

far_value = 1000000.0
no_edge = 2000000.0
large_limit = 8 * 1024 * 1024
small_limit = 2 * 1024 * 1024


def in_vmem():
    return pl.BlockSpec(memory_space=pltpu.VMEM)


def in_smem():
    return pl.BlockSpec(memory_space=pltpu.SMEM)


def piece(*shape):
    return jax.ShapeDtypeStruct(shape, jnp.float32)


def params(limit):
    return pltpu.CompilerParams(vmem_limit_bytes=limit)


def is_dense(dims):
    return dims[2] == dims[0] * dims[1]


def position(dims):
    n_row, n_col, slots, half = dims
    at = lax.axis_index("device")
    chip, core = at // (PAIR * n_col), lax.rem(at // n_col, PAIR)
    return chip, core, lax.rem(at, n_col), half_of(chip, core)


def half_of(chip, core):
    return core ^ (chip & 1)


def source_ids(sources, first, half):
    row = lax.broadcasted_iota(jnp.int32, (half, LANES), 0)
    ids = jnp.zeros((half, LANES), jnp.int32)
    for s in range(half):
        ids = jnp.where(row == s, sources[first + s], ids)
    return ids


def is_source(ids, block):
    return ids == block * LANES + lax.broadcasted_iota(jnp.int32, ids.shape, 1)


def settle(found_dist, found_count, at_source):
    dist = jnp.where(at_source, 0.0, jnp.minimum(found_dist, far_value))
    count = jnp.where(found_dist == dist, found_count, 0.0)
    return dist, jnp.where(at_source, 1.0, 0.0) + count


def merge(pairs):
    best = functools.reduce(jnp.minimum, [p[0] for p in pairs])
    total = functools.reduce(jnp.add, [jnp.where(p[0] == best, p[1], 0.0) for p in pairs])
    return best, total


def first_kernel(dims, places, sources, tiles, out, turned, ids, slot_of, lines):
    n_row, n_col, slots, half = dims
    my_x, my_core, my_col, my_half = position(dims)
    my_row = my_x * PAIR + my_core

    def clear(at, _):
        slot_of[at] = -1
        return 0

    if not is_dense(dims):
        lax.fori_loop(0, n_row * n_col, clear, 0)
    for g in range(slots):
        slot_of[places[0, g] * n_row + places[1, g]] = g
    ids[...] = source_ids(sources, my_half * half, half)
    lines[...] = jnp.zeros(lines.shape, jnp.float32)
    for s in range(PAIR * half):
        vertex = sources[s]
        block, place = vertex // LANES, lax.rem(vertex, LANES)
        r = lax.rem(block, n_col)

        @pl.when(block // n_col == my_row)
        def _():
            for c in range(n_row):
                g = slot_of[r * n_row + c]

                @pl.when(g >= 0)
                def _():
                    line = c % PAIR * half + s % half
                    row = tiles[g, pl.ds(place, 1), :]
                    lines[c // PAIR, s // half, pl.ds(line, 1), :] = row

    for chip in range(n_row // PAIR):
        for core in range(PAIR):
            line = lines[chip, half_of(chip, core)]
            line = jnp.where(line > 0, line, far_value)
            for col in range(n_col):
                out[(chip * PAIR + core) * n_col + col] = line
    for at in range(slots):
        raw = tiles[slot_of[at] if is_dense(dims) else at]
        turned[at] = jnp.where(raw > 0, raw, no_edge).T


def first_level(dims, places, sources, tiles):
    n_row, n_col, slots, half = dims
    return pl.pallas_call(
        functools.partial(first_kernel, dims),
        out_shape=[
            piece(n_row * n_col, PAIR * half, LANES),
            piece(*tiles.shape),
            jax.ShapeDtypeStruct((half, LANES), jnp.int32),
        ],
        in_specs=[in_smem(), in_smem(), in_vmem()],
        out_specs=[in_vmem()] * 3,
        scratch_shapes=[
            pltpu.SMEM((n_row * n_col,), jnp.int32),
            pltpu.VMEM((n_row // PAIR, PAIR, PAIR * half, LANES), jnp.float32),
        ],
        compiler_params=params(large_limit),
        name="first_level",
    )(places, sources, tiles)


def list_slots(dims, places, table, filled):
    n_row, n_col, slots, half = dims
    if is_dense(dims):
        return

    def clear(at, _):
        filled[at] = 0
        return 0

    lax.fori_loop(0, PAIR * n_row, clear, 0)
    for k in range(PAIR):

        def enter(g, _):
            at = k * n_row + places[k][1, g]
            table[at * n_col + filled[at]] = g
            filled[at] += 1
            return 0

        lax.fori_loop(0, slots, enter, 0)


def over_slots(dims, places, table, filled, c, step, carry):
    n_row, n_col, slots, half = dims
    for k in range(PAIR):
        if is_dense(dims):
            for r in range(n_col):
                carry = step(k, r * n_row + c, k * n_col + r, carry)
        else:
            at = k * n_row + c

            def entry(e, carry):
                g = table[at * n_col + e]
                return step(k, g, k * n_col + places[k][0, g], carry)

            carry = lax.fori_loop(0, filled[at], entry, carry)
    return carry


def slot_scratch(dims):
    n_row, n_col, slots, half = dims
    return [
        pltpu.SMEM((PAIR * n_row * n_col,), jnp.int32),
        pltpu.SMEM((PAIR * n_row,), jnp.int32),
    ]


def relax_kernel(dims, counted, whole, *refs):
    n_row, n_col, slots, half = dims
    chips = n_row // PAIR
    n_places = 0 if is_dense(dims) else PAIR
    places, refs = refs[:n_places], refs[n_places:]
    source_rows, tiles, refs = refs[0], refs[1 : 1 + PAIR], refs[1 + PAIR :]
    came, out, near, found, table, filled = refs
    my_x, my_core, my_col, my_half = position(dims)
    ids = source_rows[...]
    list_slots(dims, places, table, filled)
    for r in range(n_col):
        for k in range(PAIR):
            h = my_core ^ k
            at_source = is_source(ids, (PAIR * my_x + h) * n_col + r)
            if counted:
                blocks = [came[r * chips + chip, h] for chip in range(chips)]
                reached, count = merge([(block[:half], block[half:]) for block in blocks])
            else:
                parts = [came[at * n_col + r, pl.ds(h * half, half), :] for at in range(n_row)]
                reached = functools.reduce(jnp.minimum, parts)
                count = jnp.where(reached < far_value, 1.0, 0.0)
            dist, count = settle(reached, count, at_source)
            near[k * n_col + r, :half, :] = dist
            near[k * n_col + r, half:, :] = count
    lane = lax.broadcasted_iota(jnp.int32, (LANES, LANES), 1)

    def column(c, _):
        def lowest(s):
            def step(k, g, b, carry):
                return jnp.minimum(carry, tiles[k][g] + near[b, pl.ds(s, 1), :])

            start = jnp.full((LANES, LANES), far_value, jnp.float32)
            reached = over_slots(dims, places, table, filled, c, step, start)
            return jnp.min(reached, axis=1, keepdims=True)

        def tally(s, best):
            def step(k, g, b, carry):
                hit = tiles[k][g] + near[b, pl.ds(s, 1), :] == best
                return carry + jnp.where(hit, near[b, pl.ds(half + s, 1), :], 0.0)

            start = jnp.zeros((LANES, LANES), jnp.float32)
            counts = over_slots(dims, places, table, filled, c, step, start)
            return jnp.sum(counts, axis=1, keepdims=True)

        turned = jnp.zeros((LANES, LANES), jnp.float32)
        best = lowest(0)
        for s in range(half):
            later = lowest(s + 1) if s + 1 < half else None
            total = tally(s, best)
            turned = jnp.where(lane == s, best, jnp.where(lane == half + s, total, turned))
            best = later
        found[c] = turned.T[: 2 * half]
        return 0

    lax.fori_loop(0, n_row, column, 0, unroll=UNROLL)
    for chip in range(chips):
        for col in range(n_col):
            if whole:
                out[col * chips + chip] = found[...]
            else:
                out[col * chips + chip] = found[pl.ds(PAIR * chip, PAIR)]


def relax_level(dims, counted, whole, places, ids, tiles, came):
    n_row, n_col, slots, half = dims
    blocks = n_row if whole else PAIR
    return pl.pallas_call(
        functools.partial(relax_kernel, dims, counted, whole),
        out_shape=piece(n_row // PAIR * n_col, blocks, 2 * half, LANES),
        in_specs=[in_smem()] * len(places) + [in_vmem()] * (PAIR + 2),
        out_specs=in_vmem(),
        scratch_shapes=[
            pltpu.VMEM((PAIR * n_col, 2 * half, LANES), jnp.float32),
            pltpu.VMEM((n_row, 2 * half, LANES), jnp.float32),
        ]
        + slot_scratch(dims),
        compiler_params=params(large_limit),
        name="relax_level",
    )(*places, ids, *tiles, came)


def depend_kernel(dims, first, last, *refs):
    n_row, n_col, slots, half = dims
    chips = n_row // PAIR
    n_places = 0 if is_dense(dims) else PAIR
    places, refs = refs[:n_places], refs[n_places:]
    source_rows, tiles, refs = refs[0], refs[1 : 1 + PAIR], refs[1 + PAIR :]
    if first:
        came, out, near, low, lower, acc, table, filled = refs
    else:
        near, low, came, out, state, lower, acc, table, filled = refs
    my_x, my_core, my_col, my_half = position(dims)
    ids = source_rows[...]
    list_slots(dims, places, table, filled)
    if first:
        for r in range(n_col):
            for k in range(PAIR):
                h = my_core ^ k
                at_source = is_source(ids, (PAIR * my_x + h) * n_col + r)
                blocks = [came[r * chips + chip, PAIR * my_x + h] for chip in range(chips)]
                found = merge([(block[:half], block[half:]) for block in blocks])
                dist, count = settle(*found, at_source)
                near[k * n_col + r, :half, :] = dist
                near[k * n_col + r, half:, :] = count
        for c in range(n_row):
            at_source = is_source(ids, c * n_col + my_col)
            blocks = [came[my_col * chips + chip, c] for chip in range(chips)]
            found = merge([(block[:half], block[half:]) for block in blocks])
            dist, count = settle(*found, at_source)
            low[c, :half, :] = dist
            low[c, half:, :] = count
            lower[c, :half, :] = dist
            lower[c, half:, :] = jnp.where(count > 0.5, 1.0 / jnp.maximum(count, 1.0), 0.0)
    else:
        other = came[(PAIR * my_x + 1 - my_core) * n_col + my_col]
        for core in range(PAIR):
            block = jnp.where(my_half == core, near[my_col], other)
            dist = block[:half]
            rows = pl.ds(core * half, half)
            state[0, rows, :] = jnp.where(dist < 0.5 * far_value, dist, -1.0)
            state[1, rows, :] = block[half:]
        for chip in range(chips):
            line = (PAIR * chip + half_of(chip, my_half)) * n_col
            parts = [came[line + col] for col in range(n_col)]
            total = functools.reduce(jnp.add, parts)
            for h in range(PAIR):
                c = PAIR * chip + h
                count = low[c, half:, :]
                coef = (1.0 + count * total[h * half : h * half + half]) / jnp.maximum(count, 1.0)
                lower[c, :half, :] = low[c, :half, :]
                lower[c, half:, :] = jnp.where(count > 0.5, coef, 0.0)
    acc[...] = jnp.zeros(acc.shape, jnp.float32)

    def column(c, _):
        turned = lower[c].T
        for s in range(half):
            dist = jnp.broadcast_to(turned[:, s : s + 1], (LANES, LANES))
            coef = jnp.broadcast_to(turned[:, half + s : half + s + 1], (LANES, LANES))

            def step(k, g, b, carry):
                hit = tiles[k][g] + near[b, pl.ds(s, 1), :] == dist
                terms = jnp.where(hit, coef, 0.0).reshape(LANES // SUB, SUB, LANES)
                acc[b, s] += jnp.sum(terms, axis=0)
                return carry

            over_slots(dims, places, table, filled, c, step, 0)
        return 0

    lax.fori_loop(0, n_row, column, 0, unroll=UNROLL)
    for r in range(n_col):
        for k in range(PAIR):
            if last:
                b = k * n_col + r
                at_source = is_source(ids, (PAIR * my_x + (my_core ^ k)) * n_col + r)
                term = jnp.where(at_source, 0.0, near[b, half:, :] * jnp.sum(acc[b], axis=1))
                out[(my_core ^ k) * n_col + r] = jnp.sum(term, axis=0, keepdims=True)
            else:
                sums = jnp.sum(acc[(my_core ^ k) * n_col + r], axis=1)
                for chip in range(chips):
                    line = (PAIR * chip + half_of(chip, my_half)) * n_col
                    out[line + r, pl.ds(k * half, half), :] = sums
    if not last:
        for chip in range(chips):
            for r in range(n_col):
                out[(PAIR * chip + 1 - half_of(chip, my_half)) * n_col + r] = near[n_col + my_col]


def depend_level(dims, first, last, places, ids, tiles, bands, came):
    n_row, n_col, slots, half = dims
    if last:
        out_shape = [piece(PAIR * n_col, 1, LANES)]
    else:
        out_shape = [piece(n_row * n_col, PAIR * half, LANES)]
    if first:
        out_shape += [piece(PAIR * n_col, 2 * half, LANES), piece(n_row, 2 * half, LANES)]
    else:
        out_shape += [piece(2, PAIR * half, LANES)]
    return pl.pallas_call(
        functools.partial(depend_kernel, dims, first, last),
        out_shape=out_shape,
        in_specs=[in_smem()] * len(places) + [in_vmem()] * (PAIR + len(bands) + 2),
        out_specs=[in_vmem()] * len(out_shape),
        scratch_shapes=[
            pltpu.VMEM((n_row, 2 * half, LANES), jnp.float32),
            pltpu.VMEM((PAIR * n_col, half, SUB, LANES), jnp.float32),
        ]
        + slot_scratch(dims),
        compiler_params=params(large_limit),
        name="depend_level",
    )(*places, ids, *tiles, *bands, came)


def result_kernel(rows, came, state, shown, paths, centrality):
    shown[...] = state[0]
    paths[...] = state[1]
    shares = [came[at] for at in range(came.shape[0])]
    centrality[...] = functools.reduce(jnp.add, shares) / rows


def results(dims, came, state):
    rows = PAIR * dims[3]
    return pl.pallas_call(
        functools.partial(result_kernel, rows),
        out_shape=[piece(rows, LANES)] * 2 + [piece(1, LANES)],
        in_specs=[in_vmem()] * 2,
        out_specs=[in_vmem()] * 3,
        compiler_params=params(small_limit),
        name="results",
    )(came, state)


def all_to_all(value, groups=None):
    return lax.all_to_all(
        value, "device", split_axis=0, concat_axis=0, axis_index_groups=groups, tiled=True
    )


def per_device(n_row, n_col, tiles, tile_index, tile_count, sources):
    slots = tiles.shape[0]
    rows = sources.shape[0]
    dims = (n_row, n_col, slots, rows // PAIR)
    own_places = tile_index.T
    chips, cols = range(n_row // PAIR), range(n_col)
    device = lambda chip, core, col: (PAIR * chip + core) * n_col + col
    lines = [
        [device(chip, half_of(chip, part), col) for col in cols for chip in chips]
        for part in range(PAIR)
    ]
    columns = [[device(chip, core, col) for core in range(PAIR) for col in cols] for chip in chips]
    swaps = [
        (device(chip, core, col), device(chip, 1 - core, col))
        for chip in chips
        for core in range(PAIR)
        for col in cols
    ]

    def swap_core(value):
        return lax.ppermute(value, "device", swaps)

    firsts, turned, ids = first_level(dims, own_places, sources, tiles)
    both = [turned, swap_core(turned)]
    places = [] if is_dense(dims) else [own_places, swap_core(own_places)]
    came = all_to_all(firsts)
    for level_no in range(1, LEVELS):
        whole = level_no == LEVELS - 1
        outs = relax_level(dims, level_no > 1, whole, places, ids, both, came)
        came = all_to_all(outs, lines)
    sums, *bands = depend_level(dims, True, False, places, ids, both, [], came)
    for back_no in range(1, BACK):
        last = back_no == BACK - 1
        came = all_to_all(sums)
        sums, state = depend_level(dims, False, last, places, ids, both, bands, came)
    shown, paths, centrality = results(dims, all_to_all(sums, columns), state)
    return shown, paths, centrality.reshape(LANES)


def solution(mesh):
    groups, n_row, n_col = mesh.devices.shape
    flat = jax.sharding.Mesh(mesh.devices.reshape(groups, n_row * n_col), ("groups", "device"))
    everywhere = ("groups", "device")
    in_specs = (P(everywhere, None, None), P(everywhere, None), P(everywhere), P("groups"))
    out_specs = (P("groups", "device"), P("groups", "device"), P(everywhere))
    return jax.shard_map(
        functools.partial(per_device, n_row, n_col),
        mesh=flat,
        in_specs=in_specs,
        out_specs=out_specs,
        check_vma=False,
    )
```

```python
import functools

import jax
import jax.numpy as jnp
from jax import lax
from jax.experimental import pallas as pl
from jax.experimental.pallas import tpu as pltpu
from jax.sharding import PartitionSpec as P

LEVELS = 3
BACK = 2
LANES = 128
SUB = 8
PAIR = 2
UNROLL = 2

far_value = 1000000.0
no_edge = 2000000.0
large_limit = 8 * 1024 * 1024
small_limit = 2 * 1024 * 1024


def in_vmem():
    return pl.BlockSpec(memory_space=pltpu.VMEM)


def in_smem():
    return pl.BlockSpec(memory_space=pltpu.SMEM)


def in_hbm():
    return pl.BlockSpec(memory_space=pltpu.HBM)


def piece(*shape):
    return jax.ShapeDtypeStruct(shape, jnp.float32)


def params(limit):
    return pltpu.CompilerParams(vmem_limit_bytes=limit)


def is_dense(dims):
    return dims[2] == dims[0] * dims[1]


def position():
    return lax.axis_index("chip"), lax.axis_index("core"), lax.axis_index("col")


def source_ids(sources, first, half):
    row = lax.broadcasted_iota(jnp.int32, (half, LANES), 0)
    ids = jnp.zeros((half, LANES), jnp.int32)
    for s in range(half):
        ids = jnp.where(row == s, sources[first + s], ids)
    return ids


def is_source(ids, block):
    return ids == block * LANES + lax.broadcasted_iota(jnp.int32, ids.shape, 1)


def settle(found_dist, found_count, at_source):
    dist = jnp.where(at_source, 0.0, jnp.minimum(found_dist, far_value))
    count = jnp.where(found_dist == dist, found_count, 0.0)
    return dist, jnp.where(at_source, 1.0, 0.0) + count


def merge(pairs):
    best = functools.reduce(jnp.minimum, [p[0] for p in pairs])
    total = functools.reduce(jnp.add, [jnp.where(p[0] == best, p[1], 0.0) for p in pairs])
    return best, total


def first_kernel(dims, *refs):
    n_row, n_col, slots, half = dims
    places_in, sources_in, tiles_in, out, turned, ids = refs[:6]
    places, sources, slot_of, tiles, lines, sems = refs[6:]
    my_x, my_core, my_col = position()
    my_row = my_x * PAIR + my_core
    parts = sems.shape[0] - 2
    size = slots // parts
    given = [
        pltpu.make_async_copy(places_in, places, sems.at[parts]),
        pltpu.make_async_copy(sources_in, sources, sems.at[parts + 1]),
    ]
    fetch = []
    for part in range(parts):
        span = pl.ds(part * size, size)
        fetch.append(pltpu.make_async_copy(tiles_in.at[span], tiles.at[span], sems.at[part]))
    for copy in given + fetch:
        copy.start()
    lines[...] = jnp.zeros(lines.shape, jnp.float32)

    def clear(at, _):
        slot_of[at] = -1
        return 0

    if not is_dense(dims):
        lax.fori_loop(0, n_row * n_col, clear, 0)
    for copy in given:
        copy.wait()
    for g in range(slots):
        slot_of[places[0, g] * n_row + places[1, g]] = g
    ids[...] = source_ids(sources, my_core * half, half)
    for part in range(parts):
        fetch[part].wait()
        for g in range(part * size, part * size + size):
            at = places[0, g] * n_row + places[1, g] if is_dense(dims) else g
            raw = tiles[g]
            turned[at] = jnp.where(raw > 0, raw, no_edge).T
    for s in range(PAIR * half):
        vertex = sources[s]
        block, place = vertex // LANES, lax.rem(vertex, LANES)
        r = lax.rem(block, n_col)

        @pl.when(block // n_col == my_row)
        def _():
            for c in range(n_row):
                g = slot_of[r * n_row + c]

                @pl.when(g >= 0)
                def _():
                    line = c % PAIR * half + s % half
                    row = tiles[g, pl.ds(place, 1), :]
                    lines[c // PAIR, s // half, pl.ds(line, 1), :] = row

    for chip in range(n_row // PAIR):
        for core in range(PAIR):
            line = lines[chip, core]
            line = jnp.where(line > 0, line, far_value)
            for col in range(n_col):
                out[(chip * PAIR + core) * n_col + col] = line


def first_level(dims, places, sources, tiles):
    n_row, n_col, slots, half = dims
    parts = 4 if slots % 4 == 0 else 1
    inputs = [pltpu.with_memory_space_constraint(x, pltpu.HBM) for x in (places, sources, tiles)]
    return pl.pallas_call(
        functools.partial(first_kernel, dims),
        out_shape=[
            piece(n_row * n_col, PAIR * half, LANES),
            piece(*tiles.shape),
            jax.ShapeDtypeStruct((half, LANES), jnp.int32),
        ],
        in_specs=[in_hbm()] * 3,
        out_specs=[in_vmem()] * 3,
        scratch_shapes=[
            pltpu.SMEM(places.shape, jnp.int32),
            pltpu.SMEM(sources.shape, jnp.int32),
            pltpu.SMEM((n_row * n_col,), jnp.int32),
            pltpu.VMEM(tiles.shape, jnp.float32),
            pltpu.VMEM((n_row // PAIR, PAIR, PAIR * half, LANES), jnp.float32),
            pltpu.SemaphoreType.DMA((parts + 2,)),
        ],
        compiler_params=params(large_limit),
        name="first_level",
    )(*inputs)


def list_slots(dims, places, table, filled):
    n_row, n_col, slots, half = dims
    if is_dense(dims):
        return

    def clear(at, _):
        filled[at] = 0
        return 0

    lax.fori_loop(0, PAIR * n_row, clear, 0)
    for k in range(PAIR):

        def enter(g, _):
            at = k * n_row + places[k][1, g]
            table[at * n_col + filled[at]] = g
            filled[at] += 1
            return 0

        lax.fori_loop(0, slots, enter, 0)


def over_slots(dims, places, table, filled, c, step, carry):
    n_row, n_col, slots, half = dims
    for k in range(PAIR):
        if is_dense(dims):
            for r in range(n_col):
                carry = step(k, r * n_row + c, k * n_col + r, carry)
        else:
            at = k * n_row + c

            def entry(e, carry):
                g = table[at * n_col + e]
                return step(k, g, k * n_col + places[k][0, g], carry)

            carry = lax.fori_loop(0, filled[at], entry, carry)
    return carry


def slot_scratch(dims):
    n_row, n_col, slots, half = dims
    return [
        pltpu.SMEM((PAIR * n_row * n_col,), jnp.int32),
        pltpu.SMEM((PAIR * n_row,), jnp.int32),
    ]


def relax_kernel(dims, counted, whole, *refs):
    n_row, n_col, slots, half = dims
    chips = n_row // PAIR
    n_places = 0 if is_dense(dims) else PAIR
    places, refs = refs[:n_places], refs[n_places:]
    source_rows, tiles, refs = refs[0], refs[1 : 1 + PAIR], refs[1 + PAIR :]
    came, out, near, found, table, filled = refs
    my_x, my_core, my_col = position()
    ids = source_rows[...]
    list_slots(dims, places, table, filled)
    for r in range(n_col):
        for k in range(PAIR):
            h = my_core ^ k
            at_source = is_source(ids, (PAIR * my_x + h) * n_col + r)
            if counted:
                blocks = [came[r * chips + chip, h] for chip in range(chips)]
                reached, count = merge([(block[:half], block[half:]) for block in blocks])
            else:
                parts = [came[at * n_col + r, pl.ds(h * half, half), :] for at in range(n_row)]
                reached = functools.reduce(jnp.minimum, parts)
                count = jnp.where(reached < far_value, 1.0, 0.0)
            dist, count = settle(reached, count, at_source)
            near[k * n_col + r, :half, :] = dist
            near[k * n_col + r, half:, :] = count
    lane = lax.broadcasted_iota(jnp.int32, (LANES, LANES), 1)

    def column(c, _):
        def lowest(s):
            def step(k, g, b, carry):
                return jnp.minimum(carry, tiles[k][g] + near[b, pl.ds(s, 1), :])

            start = jnp.full((LANES, LANES), far_value, jnp.float32)
            reached = over_slots(dims, places, table, filled, c, step, start)
            return jnp.min(reached, axis=1, keepdims=True)

        def tally(s, best):
            def step(k, g, b, carry):
                hit = tiles[k][g] + near[b, pl.ds(s, 1), :] == best
                return carry + jnp.where(hit, near[b, pl.ds(half + s, 1), :], 0.0)

            start = jnp.zeros((LANES, LANES), jnp.float32)
            counts = over_slots(dims, places, table, filled, c, step, start)
            return jnp.sum(counts, axis=1, keepdims=True)

        turned = jnp.zeros((LANES, LANES), jnp.float32)
        best = lowest(0)
        for s in range(half):
            later = lowest(s + 1) if s + 1 < half else None
            total = tally(s, best)
            turned = jnp.where(lane == s, best, jnp.where(lane == half + s, total, turned))
            best = later
        found[c] = turned.T[: 2 * half]
        return 0

    lax.fori_loop(0, n_row, column, 0, unroll=UNROLL)
    for chip in range(chips):
        for col in range(n_col):
            if whole:
                out[col * chips + chip] = found[...]
            else:
                out[col * chips + chip] = found[pl.ds(PAIR * chip, PAIR)]


def relax_level(dims, counted, whole, places, ids, tiles, came):
    n_row, n_col, slots, half = dims
    blocks = n_row if whole else PAIR
    return pl.pallas_call(
        functools.partial(relax_kernel, dims, counted, whole),
        out_shape=piece(n_row // PAIR * n_col, blocks, 2 * half, LANES),
        in_specs=[in_smem()] * len(places) + [in_vmem()] * (PAIR + 2),
        out_specs=in_vmem(),
        scratch_shapes=[
            pltpu.VMEM((PAIR * n_col, 2 * half, LANES), jnp.float32),
            pltpu.VMEM((n_row, 2 * half, LANES), jnp.float32),
        ]
        + slot_scratch(dims),
        compiler_params=params(large_limit),
        name="relax_level",
    )(*places, ids, *tiles, came)


def depend_kernel(dims, first, last, *refs):
    n_row, n_col, slots, half = dims
    chips = n_row // PAIR
    n_places = 0 if is_dense(dims) else PAIR
    places, refs = refs[:n_places], refs[n_places:]
    source_rows, tiles, refs = refs[0], refs[1 : 1 + PAIR], refs[1 + PAIR :]
    if first:
        came, out, near, low, lower, acc, table, filled = refs
    else:
        near, low, came, out, state, lower, acc, table, filled = refs
    my_x, my_core, my_col = position()
    ids = source_rows[...]
    list_slots(dims, places, table, filled)
    if first:
        for r in range(n_col):
            for k in range(PAIR):
                h = my_core ^ k
                at_source = is_source(ids, (PAIR * my_x + h) * n_col + r)
                blocks = [came[r * chips + chip, PAIR * my_x + h] for chip in range(chips)]
                found = merge([(block[:half], block[half:]) for block in blocks])
                dist, count = settle(*found, at_source)
                near[k * n_col + r, :half, :] = dist
                near[k * n_col + r, half:, :] = count
        for c in range(n_row):
            at_source = is_source(ids, c * n_col + my_col)
            blocks = [came[my_col * chips + chip, c] for chip in range(chips)]
            found = merge([(block[:half], block[half:]) for block in blocks])
            dist, count = settle(*found, at_source)
            low[c, :half, :] = dist
            low[c, half:, :] = count
            lower[c, :half, :] = dist
            lower[c, half:, :] = jnp.where(count > 0.5, 1.0 / jnp.maximum(count, 1.0), 0.0)
    else:
        other = came[(PAIR * my_x + 1 - my_core) * n_col + my_col]
        for core in range(PAIR):
            block = jnp.where(my_core == core, near[my_col], other)
            dist = block[:half]
            rows = pl.ds(core * half, half)
            state[0, rows, :] = jnp.where(dist < 0.5 * far_value, dist, -1.0)
            state[1, rows, :] = block[half:]
        for chip in range(chips):
            line = (PAIR * chip + my_core) * n_col
            parts = [came[line + col] for col in range(n_col)]
            total = functools.reduce(jnp.add, parts)
            for h in range(PAIR):
                c = PAIR * chip + h
                count = low[c, half:, :]
                coef = (1.0 + count * total[h * half : h * half + half]) / jnp.maximum(count, 1.0)
                lower[c, :half, :] = low[c, :half, :]
                lower[c, half:, :] = jnp.where(count > 0.5, coef, 0.0)
    acc[...] = jnp.zeros(acc.shape, jnp.float32)

    def column(c, _):
        turned = lower[c].T
        for s in range(half):
            dist = jnp.broadcast_to(turned[:, s : s + 1], (LANES, LANES))
            coef = jnp.broadcast_to(turned[:, half + s : half + s + 1], (LANES, LANES))

            def step(k, g, b, carry):
                hit = tiles[k][g] + near[b, pl.ds(s, 1), :] == dist
                terms = jnp.where(hit, coef, 0.0).reshape(LANES // SUB, SUB, LANES)
                acc[b, s] += jnp.sum(terms, axis=0)
                return carry

            over_slots(dims, places, table, filled, c, step, 0)
        return 0

    lax.fori_loop(0, n_row, column, 0, unroll=UNROLL)
    for r in range(n_col):
        for k in range(PAIR):
            if last:
                b = k * n_col + r
                at_source = is_source(ids, (PAIR * my_x + (my_core ^ k)) * n_col + r)
                term = jnp.where(at_source, 0.0, near[b, half:, :] * jnp.sum(acc[b], axis=1))
                out[(my_core ^ k) * n_col + r] = jnp.sum(term, axis=0, keepdims=True)
            else:
                sums = jnp.sum(acc[(my_core ^ k) * n_col + r], axis=1)
                for chip in range(chips):
                    line = (PAIR * chip + my_core) * n_col
                    out[line + r, pl.ds(k * half, half), :] = sums
    if not last:
        for chip in range(chips):
            for r in range(n_col):
                out[(PAIR * chip + 1 - my_core) * n_col + r] = near[n_col + my_col]


def depend_level(dims, first, last, places, ids, tiles, bands, came):
    n_row, n_col, slots, half = dims
    if last:
        out_shape = [piece(PAIR * n_col, 1, LANES)]
    else:
        out_shape = [piece(n_row * n_col, PAIR * half, LANES)]
    if first:
        out_shape += [piece(PAIR * n_col, 2 * half, LANES), piece(n_row, 2 * half, LANES)]
    else:
        out_shape += [piece(2, PAIR * half, LANES)]
    return pl.pallas_call(
        functools.partial(depend_kernel, dims, first, last),
        out_shape=out_shape,
        in_specs=[in_smem()] * len(places) + [in_vmem()] * (PAIR + len(bands) + 2),
        out_specs=[in_vmem()] * len(out_shape),
        scratch_shapes=[
            pltpu.VMEM((n_row, 2 * half, LANES), jnp.float32),
            pltpu.VMEM((PAIR * n_col, half, SUB, LANES), jnp.float32),
        ]
        + slot_scratch(dims),
        compiler_params=params(large_limit),
        name="depend_level",
    )(*places, ids, *tiles, *bands, came)


def result_kernel(rows, came, state, shown, paths, centrality):
    shown[...] = state[0]
    paths[...] = state[1]
    shares = [came[at] for at in range(came.shape[0])]
    centrality[...] = functools.reduce(jnp.add, shares) / rows


def results(dims, came, state):
    rows = PAIR * dims[3]
    return pl.pallas_call(
        functools.partial(result_kernel, rows),
        out_shape=[piece(rows, LANES)] * 2 + [piece(1, LANES)],
        in_specs=[in_vmem()] * 2,
        out_specs=[in_vmem()] * 3,
        compiler_params=params(small_limit),
        name="results",
    )(came, state)


def all_to_all(value, axes):
    return lax.all_to_all(value, axes, split_axis=0, concat_axis=0, tiled=True)


def swap_core(value):
    return lax.ppermute(value, "core", [(0, 1), (1, 0)])


def per_device(tiles, tile_index, tile_count, sources):
    slots = tiles.shape[0]
    rows = sources.shape[0]
    dims = (lax.axis_size("chip") * PAIR, lax.axis_size("col"), slots, rows // PAIR)
    own_places = tile_index.T
    line = ("col", "chip")

    everyone = ("chip", "core", "col")

    firsts, turned, ids = first_level(dims, own_places, sources, tiles)
    both = [turned, swap_core(turned)]
    places = [] if is_dense(dims) else [own_places, swap_core(own_places)]
    came = all_to_all(firsts, everyone)
    for level_no in range(1, LEVELS):
        whole = level_no == LEVELS - 1
        outs = relax_level(dims, level_no > 1, whole, places, ids, both, came)
        came = all_to_all(outs, line)
    sums, *bands = depend_level(dims, True, False, places, ids, both, [], came)
    for back_no in range(1, BACK):
        last = back_no == BACK - 1
        came = all_to_all(sums, everyone)
        sums, state = depend_level(dims, False, last, places, ids, both, bands, came)
    shown, paths, centrality = results(dims, all_to_all(sums, ("core", "col")), state)
    return shown, paths, centrality.reshape(LANES)


def solution(mesh):
    groups, rows, cols = mesh.devices.shape
    pairs = mesh.devices.reshape(groups, rows // PAIR, PAIR, cols)
    paired = jax.sharding.Mesh(pairs, ("groups", "chip", "core", "col"))
    vertices = ("chip", "core", "col")
    everywhere = ("groups",) + vertices
    in_specs = (P(everywhere, None, None), P(everywhere, None), P(everywhere), P("groups"))
    out_specs = (P("groups", vertices), P("groups", vertices), P(everywhere))
    return jax.shard_map(
        per_device, mesh=paired, in_specs=in_specs, out_specs=out_specs, check_vma=False
    )
```

```python
import functools

import jax
import jax.numpy as jnp
from jax import lax
from jax.experimental import pallas as pl
from jax.experimental.pallas import tpu as pltpu
from jax.sharding import PartitionSpec as P

LEVELS = 3
BACK = 2
LANES = 128
SUB = 8
PAIR = 2
UNROLL = 2

far_value = 1000000.0
no_edge = 2000000.0
large_limit = 8 * 1024 * 1024
small_limit = 2 * 1024 * 1024
terms_limit = 20 * 1024 * 1024


def in_vmem():
    return pl.BlockSpec(memory_space=pltpu.VMEM)


def in_smem():
    return pl.BlockSpec(memory_space=pltpu.SMEM)


def in_hbm():
    return pl.BlockSpec(memory_space=pltpu.HBM)


def piece(*shape):
    return jax.ShapeDtypeStruct(shape, jnp.float32)


def params(limit):
    return pltpu.CompilerParams(vmem_limit_bytes=limit)


def is_dense(dims):
    return dims[2] == dims[0] * dims[1]


def position():
    return lax.axis_index("chip"), lax.axis_index("core"), lax.axis_index("col")


def source_ids(sources, first, half):
    row = lax.broadcasted_iota(jnp.int32, (half, LANES), 0)
    ids = jnp.zeros((half, LANES), jnp.int32)
    for s in range(half):
        ids = jnp.where(row == s, sources[first + s], ids)
    return ids


def is_source(ids, block):
    return ids == block * LANES + lax.broadcasted_iota(jnp.int32, ids.shape, 1)


def settle(found_dist, found_count, at_source):
    dist = jnp.where(at_source, 0.0, jnp.minimum(found_dist, far_value))
    count = jnp.where(found_dist == dist, found_count, 0.0)
    return dist, jnp.where(at_source, 1.0, 0.0) + count


def merge(pairs):
    best = functools.reduce(jnp.minimum, [p[0] for p in pairs])
    total = functools.reduce(jnp.add, [jnp.where(p[0] == best, p[1], 0.0) for p in pairs])
    return best, total


def first_kernel(dims, *refs):
    n_row, n_col, slots, half = dims
    places_in, sources_in, tiles_in, out, turned, ids = refs[:6]
    places, sources, slot_of, tiles, lines, sems = refs[6:]
    my_x, my_core, my_col = position()
    my_row = my_x * PAIR + my_core
    parts = sems.shape[0] - 2
    size = slots // parts
    given = [
        pltpu.make_async_copy(places_in, places, sems.at[parts]),
        pltpu.make_async_copy(sources_in, sources, sems.at[parts + 1]),
    ]
    fetch = []
    for part in range(parts):
        span = pl.ds(part * size, size)
        fetch.append(pltpu.make_async_copy(tiles_in.at[span], tiles.at[span], sems.at[part]))
    for copy in given + fetch:
        copy.start()
    lines[...] = jnp.zeros(lines.shape, jnp.float32)

    def clear(at, _):
        slot_of[at] = -1
        return 0

    if not is_dense(dims):
        lax.fori_loop(0, n_row * n_col, clear, 0)
    for copy in given:
        copy.wait()
    for g in range(slots):
        slot_of[places[0, g] * n_row + places[1, g]] = g
    ids[...] = source_ids(sources, my_core * half, half)
    for part in range(parts):
        fetch[part].wait()
        for g in range(part * size, part * size + size):
            at = places[0, g] * n_row + places[1, g] if is_dense(dims) else g
            raw = tiles[g]
            turned[at] = jnp.where(raw > 0, raw, no_edge).T
    for s in range(PAIR * half):
        vertex = sources[s]
        block, place = vertex // LANES, lax.rem(vertex, LANES)
        r = lax.rem(block, n_col)

        @pl.when(block // n_col == my_row)
        def _():
            for c in range(n_row):
                g = slot_of[r * n_row + c]

                @pl.when(g >= 0)
                def _():
                    line = c % PAIR * half + s % half
                    row = tiles[g, pl.ds(place, 1), :]
                    lines[c // PAIR, s // half, pl.ds(line, 1), :] = row

    for chip in range(n_row // PAIR):
        for core in range(PAIR):
            line = lines[chip, core]
            line = jnp.where(line > 0, line, far_value)
            for col in range(n_col):
                out[(chip * PAIR + core) * n_col + col] = line


def first_level(dims, places, sources, tiles):
    n_row, n_col, slots, half = dims
    parts = 4 if slots % 4 == 0 else 1
    inputs = [pltpu.with_memory_space_constraint(x, pltpu.HBM) for x in (places, sources, tiles)]
    return pl.pallas_call(
        functools.partial(first_kernel, dims),
        out_shape=[
            piece(n_row * n_col, PAIR * half, LANES),
            piece(*tiles.shape),
            jax.ShapeDtypeStruct((half, LANES), jnp.int32),
        ],
        in_specs=[in_hbm()] * 3,
        out_specs=[in_vmem()] * 3,
        scratch_shapes=[
            pltpu.SMEM(places.shape, jnp.int32),
            pltpu.SMEM(sources.shape, jnp.int32),
            pltpu.SMEM((n_row * n_col,), jnp.int32),
            pltpu.VMEM(tiles.shape, jnp.float32),
            pltpu.VMEM((n_row // PAIR, PAIR, PAIR * half, LANES), jnp.float32),
            pltpu.SemaphoreType.DMA((parts + 2,)),
        ],
        compiler_params=params(large_limit),
        name="first_level",
    )(*inputs)


def list_slots(dims, places, table, filled):
    n_row, n_col, slots, half = dims
    if is_dense(dims):
        return

    def clear(at, _):
        filled[at] = 0
        return 0

    lax.fori_loop(0, PAIR * n_row, clear, 0)
    for k in range(PAIR):

        def enter(g, _):
            at = k * n_row + places[k][1, g]
            table[at * n_col + filled[at]] = g
            filled[at] += 1
            return 0

        lax.fori_loop(0, slots, enter, 0)


def over_slots(dims, places, table, filled, c, step, carry):
    n_row, n_col, slots, half = dims
    for k in range(PAIR):
        if is_dense(dims):
            for r in range(n_col):
                carry = step(k, r * n_row + c, k * n_col + r, carry)
        else:
            at = k * n_row + c

            def entry(e, carry):
                g = table[at * n_col + e]
                return step(k, g, k * n_col + places[k][0, g], carry)

            carry = lax.fori_loop(0, filled[at], entry, carry)
    return carry


def slot_scratch(dims):
    n_row, n_col, slots, half = dims
    return [
        pltpu.SMEM((PAIR * n_row * n_col,), jnp.int32),
        pltpu.SMEM((PAIR * n_row,), jnp.int32),
    ]


def relax_kernel(dims, counted, whole, *refs):
    n_row, n_col, slots, half = dims
    chips = n_row // PAIR
    n_places = 0 if is_dense(dims) else PAIR
    places, refs = refs[:n_places], refs[n_places:]
    source_rows, tiles, refs = refs[0], refs[1 : 1 + PAIR], refs[1 + PAIR :]
    came, out, near, found, table, filled = refs
    my_x, my_core, my_col = position()
    ids = source_rows[...]
    list_slots(dims, places, table, filled)
    for r in range(n_col):
        for k in range(PAIR):
            h = my_core ^ k
            at_source = is_source(ids, (PAIR * my_x + h) * n_col + r)
            if counted:
                blocks = [came[r * chips + chip, h] for chip in range(chips)]
                reached, count = merge([(block[:half], block[half:]) for block in blocks])
            else:
                parts = [came[at * n_col + r, pl.ds(h * half, half), :] for at in range(n_row)]
                reached = functools.reduce(jnp.minimum, parts)
                count = jnp.where(reached < far_value, 1.0, 0.0)
            dist, count = settle(reached, count, at_source)
            near[k * n_col + r, :half, :] = dist
            near[k * n_col + r, half:, :] = count
    lane = lax.broadcasted_iota(jnp.int32, (LANES, LANES), 1)

    def column(c, _):
        def lowest(s):
            def step(k, g, b, carry):
                return jnp.minimum(carry, tiles[k][g] + near[b, pl.ds(s, 1), :])

            start = jnp.full((LANES, LANES), far_value, jnp.float32)
            reached = over_slots(dims, places, table, filled, c, step, start)
            return jnp.min(reached, axis=1, keepdims=True)

        def tally(s, best):
            def step(k, g, b, carry):
                hit = tiles[k][g] + near[b, pl.ds(s, 1), :] == best
                return carry + jnp.where(hit, near[b, pl.ds(half + s, 1), :], 0.0)

            start = jnp.zeros((LANES, LANES), jnp.float32)
            counts = over_slots(dims, places, table, filled, c, step, start)
            return jnp.sum(counts, axis=1, keepdims=True)

        turned = jnp.zeros((LANES, LANES), jnp.float32)
        best = lowest(0)
        for s in range(half):
            later = lowest(s + 1) if s + 1 < half else None
            total = tally(s, best)
            turned = jnp.where(lane == s, best, jnp.where(lane == half + s, total, turned))
            best = later
        found[c] = turned.T[: 2 * half]
        return 0

    lax.fori_loop(0, n_row, column, 0, unroll=UNROLL)
    for chip in range(chips):
        for col in range(n_col):
            if whole:
                out[col * chips + chip] = found[...]
            else:
                out[col * chips + chip] = found[pl.ds(PAIR * chip, PAIR)]


def relax_level(dims, counted, whole, places, ids, tiles, came):
    n_row, n_col, slots, half = dims
    blocks = n_row if whole else PAIR
    return pl.pallas_call(
        functools.partial(relax_kernel, dims, counted, whole),
        out_shape=piece(n_row // PAIR * n_col, blocks, 2 * half, LANES),
        in_specs=[in_smem()] * len(places) + [in_vmem()] * (PAIR + 2),
        out_specs=in_vmem(),
        scratch_shapes=[
            pltpu.VMEM((PAIR * n_col, 2 * half, LANES), jnp.float32),
            pltpu.VMEM((n_row, 2 * half, LANES), jnp.float32),
        ]
        + slot_scratch(dims),
        compiler_params=params(large_limit),
        name="relax_level",
    )(*places, ids, *tiles, came)


def depend_kernel(dims, first, last, *refs):
    n_row, n_col, slots, half = dims
    chips = n_row // PAIR
    n_places = 0 if is_dense(dims) else PAIR
    places, refs = refs[:n_places], refs[n_places:]
    source_rows, refs = refs[0], refs[1:]
    if first:
        tiles, refs = refs[:PAIR], refs[PAIR:]
        came, out, near, low, terms, acc, table, filled = refs
    else:
        near, low, terms, came, out, state, acc, table, filled = refs
    my_x, my_core, my_col = position()
    ids = source_rows[...]
    list_slots(dims, places, table, filled)
    if first:
        for r in range(n_col):
            for k in range(PAIR):
                h = my_core ^ k
                at_source = is_source(ids, (PAIR * my_x + h) * n_col + r)
                blocks = [came[r * chips + chip, PAIR * my_x + h] for chip in range(chips)]
                found = merge([(block[:half], block[half:]) for block in blocks])
                dist, count = settle(*found, at_source)
                near[k * n_col + r, :half, :] = dist
                near[k * n_col + r, half:, :] = count
        for c in range(n_row):
            at_source = is_source(ids, c * n_col + my_col)
            blocks = [came[my_col * chips + chip, c] for chip in range(chips)]
            found = merge([(block[:half], block[half:]) for block in blocks])
            dist, count = settle(*found, at_source)
            low[c, :half, :] = dist
            low[c, half:, :] = count
    else:
        other = came[(PAIR * my_x + 1 - my_core) * n_col + my_col]
        for core in range(PAIR):
            block = jnp.where(my_core == core, near[my_col], other)
            dist = block[:half]
            rows = pl.ds(core * half, half)
            state[0, rows, :] = jnp.where(dist < 0.5 * far_value, dist, -1.0)
            state[1, rows, :] = block[half:]
    acc[...] = jnp.zeros(acc.shape, jnp.float32)

    def add_terms(b, s, part):
        acc[b, s] += jnp.sum(part.reshape(LANES // SUB, SUB, LANES), axis=0)

    def select(c, _):
        count = low[c, half:, :]
        share = jnp.where(count > 0.5, 1.0 / jnp.maximum(count, 1.0), 0.0)
        turned = jnp.concatenate([low[c, :half, :], share], axis=0).T
        for s in range(half):
            dist = jnp.broadcast_to(turned[:, s : s + 1], (LANES, LANES))
            coef = jnp.broadcast_to(turned[:, half + s : half + s + 1], (LANES, LANES))

            def step(k, g, b, carry):
                hit = tiles[k][g] + near[b, pl.ds(s, 1), :] == dist
                part = jnp.where(hit, coef, 0.0)
                terms[(k * slots + g) * half + s] = part
                add_terms(b, s, part)
                return carry

            over_slots(dims, places, table, filled, c, step, 0)
        return 0

    def scale(c, _):
        line = (c // PAIR * PAIR + my_core) * n_col
        rows = pl.ds(c % PAIR * half, half)
        total = functools.reduce(jnp.add, [came[line + col, rows, :] for col in range(n_col)])
        turned = (1.0 + low[c, half:, :] * total).T
        for s in range(half):
            factor = jnp.broadcast_to(turned[:, s : s + 1], (LANES, LANES))

            def step(k, g, b, carry):
                add_terms(b, s, terms[(k * slots + g) * half + s] * factor)
                return carry

            over_slots(dims, places, table, filled, c, step, 0)

    if first:
        lax.fori_loop(0, n_row, select, 0, unroll=UNROLL)
    else:
        for c in range(n_row):
            scale(c, 0)
    for r in range(n_col):
        for k in range(PAIR):
            if last:
                b = k * n_col + r
                at_source = is_source(ids, (PAIR * my_x + (my_core ^ k)) * n_col + r)
                term = jnp.where(at_source, 0.0, near[b, half:, :] * jnp.sum(acc[b], axis=1))
                out[(my_core ^ k) * n_col + r] = jnp.sum(term, axis=0, keepdims=True)
            else:
                sums = jnp.sum(acc[(my_core ^ k) * n_col + r], axis=1)
                for chip in range(chips):
                    line = (PAIR * chip + my_core) * n_col
                    out[line + r, pl.ds(k * half, half), :] = sums
    if not last:
        for chip in range(chips):
            for r in range(n_col):
                out[(PAIR * chip + 1 - my_core) * n_col + r] = near[n_col + my_col]


def depend_level(dims, first, last, places, ids, tiles, bands, came):
    n_row, n_col, slots, half = dims
    if last:
        out_shape = [piece(PAIR * n_col, 1, LANES)]
    else:
        out_shape = [piece(n_row * n_col, PAIR * half, LANES)]
    if first:
        out_shape += [
            piece(PAIR * n_col, 2 * half, LANES),
            piece(n_row, 2 * half, LANES),
            piece(PAIR * slots * half, LANES, LANES),
        ]
    else:
        out_shape += [piece(2, PAIR * half, LANES)]
    vectors = [ids, *(tiles if first else []), *bands, came]
    return pl.pallas_call(
        functools.partial(depend_kernel, dims, first, last),
        out_shape=out_shape,
        in_specs=[in_smem()] * len(places) + [in_vmem()] * len(vectors),
        out_specs=[in_vmem()] * len(out_shape),
        scratch_shapes=[pltpu.VMEM((PAIR * n_col, half, SUB, LANES), jnp.float32)]
        + slot_scratch(dims),
        compiler_params=params(terms_limit),
        name="depend_level",
    )(*places, *vectors)


def result_kernel(rows, came, state, shown, paths, centrality):
    shown[...] = state[0]
    paths[...] = state[1]
    shares = [came[at] for at in range(came.shape[0])]
    centrality[...] = functools.reduce(jnp.add, shares) / rows


def results(dims, came, state):
    rows = PAIR * dims[3]
    return pl.pallas_call(
        functools.partial(result_kernel, rows),
        out_shape=[piece(rows, LANES)] * 2 + [piece(1, LANES)],
        in_specs=[in_vmem()] * 2,
        out_specs=[in_vmem()] * 3,
        compiler_params=params(small_limit),
        name="results",
    )(came, state)


def all_to_all(value, axes):
    return lax.all_to_all(value, axes, split_axis=0, concat_axis=0, tiled=True)


def swap_core(value):
    return lax.ppermute(value, "core", [(0, 1), (1, 0)])


def per_device(tiles, tile_index, tile_count, sources):
    slots = tiles.shape[0]
    rows = sources.shape[0]
    dims = (lax.axis_size("chip") * PAIR, lax.axis_size("col"), slots, rows // PAIR)
    own_places = tile_index.T
    line = ("col", "chip")

    everyone = ("chip", "core", "col")

    firsts, turned, ids = first_level(dims, own_places, sources, tiles)
    both = [turned, swap_core(turned)]
    places = [] if is_dense(dims) else [own_places, swap_core(own_places)]
    came = all_to_all(firsts, everyone)
    for level_no in range(1, LEVELS):
        whole = level_no == LEVELS - 1
        outs = relax_level(dims, level_no > 1, whole, places, ids, both, came)
        came = all_to_all(outs, line)
    sums, *bands = depend_level(dims, True, False, places, ids, both, [], came)
    for back_no in range(1, BACK):
        last = back_no == BACK - 1
        came = all_to_all(sums, everyone)
        sums, state = depend_level(dims, False, last, places, ids, both, bands, came)
    shown, paths, centrality = results(dims, all_to_all(sums, ("core", "col")), state)
    return shown, paths, centrality.reshape(LANES)


def solution(mesh):
    groups, rows, cols = mesh.devices.shape
    pairs = mesh.devices.reshape(groups, rows // PAIR, PAIR, cols)
    paired = jax.sharding.Mesh(pairs, ("groups", "chip", "core", "col"))
    vertices = ("chip", "core", "col")
    everywhere = ("groups",) + vertices
    in_specs = (P(everywhere, None, None), P(everywhere, None), P(everywhere), P("groups"))
    out_specs = (P("groups", vertices), P("groups", vertices), P(everywhere))
    return jax.shard_map(
        per_device, mesh=paired, in_specs=in_specs, out_specs=out_specs, check_vma=False
    )
```

```python
import functools

import jax
import jax.numpy as jnp
from jax import lax
from jax.experimental import pallas as pl
from jax.experimental.pallas import tpu as pltpu
from jax.sharding import PartitionSpec as P

LEVELS = 3
BACK = 2
LANES = 128
SUB = 8
PAIR = 2
UNROLL = 2

far_value = 1000000.0
no_edge = 2000000.0
large_limit = 8 * 1024 * 1024
small_limit = 2 * 1024 * 1024
terms_limit = 20 * 1024 * 1024


def in_vmem():
    return pl.BlockSpec(memory_space=pltpu.VMEM)


def in_smem():
    return pl.BlockSpec(memory_space=pltpu.SMEM)


def in_hbm():
    return pl.BlockSpec(memory_space=pltpu.HBM)


def piece(*shape):
    return jax.ShapeDtypeStruct(shape, jnp.float32)


def params(limit):
    return pltpu.CompilerParams(vmem_limit_bytes=limit)


def is_dense(dims):
    return dims[2] == dims[0] * dims[1]


def position():
    return lax.axis_index("chip"), lax.axis_index("core"), lax.axis_index("col")


def source_ids(sources, first, half):
    row = lax.broadcasted_iota(jnp.int32, (half, LANES), 0)
    ids = jnp.zeros((half, LANES), jnp.int32)
    for s in range(half):
        ids = jnp.where(row == s, sources[first + s], ids)
    return ids


def is_source(ids, block):
    return ids == block * LANES + lax.broadcasted_iota(jnp.int32, ids.shape, 1)


def settle(found_dist, found_count, at_source):
    dist = jnp.where(at_source, 0.0, jnp.minimum(found_dist, far_value))
    count = jnp.where(found_dist == dist, found_count, 0.0)
    return dist, jnp.where(at_source, 1.0, 0.0) + count


def merge(pairs):
    best = functools.reduce(jnp.minimum, [p[0] for p in pairs])
    total = functools.reduce(jnp.add, [jnp.where(p[0] == best, p[1], 0.0) for p in pairs])
    return best, total


def first_kernel(dims, *refs):
    n_row, n_col, slots, half = dims
    places_in, sources_in, tiles_in, out, turned, ids = refs[:6]
    places, sources, slot_of, tiles, lines, sems = refs[6:]
    my_x, my_core, my_col = position()
    my_row = my_x * PAIR + my_core
    parts = sems.shape[0] - 2
    size = slots // parts
    given = [
        pltpu.make_async_copy(places_in, places, sems.at[parts]),
        pltpu.make_async_copy(sources_in, sources, sems.at[parts + 1]),
    ]
    fetch = []
    for part in range(parts):
        span = pl.ds(part * size, size)
        fetch.append(pltpu.make_async_copy(tiles_in.at[span], tiles.at[span], sems.at[part]))
    for copy in given + fetch:
        copy.start()
    lines[...] = jnp.zeros(lines.shape, jnp.float32)

    def clear(at, _):
        slot_of[at] = -1
        return 0

    if not is_dense(dims):
        lax.fori_loop(0, n_row * n_col, clear, 0)
    for copy in given:
        copy.wait()
    for g in range(slots):
        slot_of[places[0, g] * n_row + places[1, g]] = g
    ids[...] = source_ids(sources, my_core * half, half)
    for part in range(parts):
        fetch[part].wait()
        for g in range(part * size, part * size + size):
            at = places[0, g] * n_row + places[1, g] if is_dense(dims) else g
            raw = tiles[g]
            turned[at] = jnp.where(raw > 0, raw, no_edge).T
    for s in range(PAIR * half):
        vertex = sources[s]
        block, place = vertex // LANES, lax.rem(vertex, LANES)
        r = lax.rem(block, n_col)

        @pl.when(block // n_col == my_row)
        def _():
            for c in range(n_row):
                g = slot_of[r * n_row + c]

                @pl.when(g >= 0)
                def _():
                    line = c % PAIR * half + s % half
                    row = tiles[g, pl.ds(place, 1), :]
                    lines[c // PAIR, s // half, pl.ds(line, 1), :] = row

    for chip in range(n_row // PAIR):
        for core in range(PAIR):
            line = lines[chip, core]
            line = jnp.where(line > 0, line, far_value)
            for col in range(n_col):
                out[(chip * PAIR + core) * n_col + col] = line


def first_level(dims, places, sources, tiles):
    n_row, n_col, slots, half = dims
    parts = 4 if slots % 4 == 0 else 1
    inputs = [pltpu.with_memory_space_constraint(x, pltpu.HBM) for x in (places, sources, tiles)]
    return pl.pallas_call(
        functools.partial(first_kernel, dims),
        out_shape=[
            piece(n_row * n_col, PAIR * half, LANES),
            piece(*tiles.shape),
            jax.ShapeDtypeStruct((half, LANES), jnp.int32),
        ],
        in_specs=[in_hbm()] * 3,
        out_specs=[in_vmem()] * 3,
        scratch_shapes=[
            pltpu.SMEM(places.shape, jnp.int32),
            pltpu.SMEM(sources.shape, jnp.int32),
            pltpu.SMEM((n_row * n_col,), jnp.int32),
            pltpu.VMEM(tiles.shape, jnp.float32),
            pltpu.VMEM((n_row // PAIR, PAIR, PAIR * half, LANES), jnp.float32),
            pltpu.SemaphoreType.DMA((parts + 2,)),
        ],
        compiler_params=params(large_limit),
        name="first_level",
    )(*inputs)


def list_slots(dims, places, table, filled):
    n_row, n_col, slots, half = dims
    if is_dense(dims):
        return

    def clear(at, _):
        filled[at] = 0
        return 0

    lax.fori_loop(0, PAIR * n_row, clear, 0)
    for k in range(PAIR):

        def enter(g, _):
            at = k * n_row + places[k][1, g]
            table[at * n_col + filled[at]] = g
            filled[at] += 1
            return 0

        lax.fori_loop(0, slots, enter, 0)


def over_slots(dims, places, table, filled, c, step, carry):
    n_row, n_col, slots, half = dims
    for k in range(PAIR):
        if is_dense(dims):
            for r in range(n_col):
                carry = step(k, r * n_row + c, k * n_col + r, carry)
        else:
            at = k * n_row + c

            def entry(e, carry):
                g = table[at * n_col + e]
                return step(k, g, k * n_col + places[k][0, g], carry)

            carry = lax.fori_loop(0, filled[at], entry, carry)
    return carry


def slot_scratch(dims):
    n_row, n_col, slots, half = dims
    return [
        pltpu.SMEM((PAIR * n_row * n_col,), jnp.int32),
        pltpu.SMEM((PAIR * n_row,), jnp.int32),
    ]


def relax_kernel(dims, counted, whole, *refs):
    n_row, n_col, slots, half = dims
    chips = n_row // PAIR
    n_places = 0 if is_dense(dims) else PAIR
    places, refs = refs[:n_places], refs[n_places:]
    source_rows, tiles, refs = refs[0], refs[1 : 1 + PAIR], refs[1 + PAIR :]
    came, out, near, found, table, filled = refs
    my_x, my_core, my_col = position()
    ids = source_rows[...]
    list_slots(dims, places, table, filled)
    for r in range(n_col):
        for k in range(PAIR):
            h = my_core ^ k
            at_source = is_source(ids, (PAIR * my_x + h) * n_col + r)
            if counted:
                blocks = [came[r * chips + chip, h] for chip in range(chips)]
                reached, count = merge([(block[:half], block[half:]) for block in blocks])
            else:
                parts = [came[at * n_col + r, pl.ds(h * half, half), :] for at in range(n_row)]
                reached = functools.reduce(jnp.minimum, parts)
                count = jnp.where(reached < far_value, 1.0, 0.0)
            dist, count = settle(reached, count, at_source)
            near[k * n_col + r, :half, :] = dist
            near[k * n_col + r, half:, :] = count
    lane = lax.broadcasted_iota(jnp.int32, (LANES, LANES), 1)

    def lowest(c, s):
        def step(k, g, b, carry):
            return jnp.minimum(carry, tiles[k][g] + near[b, pl.ds(s, 1), :])

        start = jnp.full((LANES, LANES), far_value, jnp.float32)
        reached = over_slots(dims, places, table, filled, c, step, start)
        best = jnp.min(reached, axis=1, keepdims=True)
        return jnp.broadcast_to(best, (LANES, LANES))

    def tally(c, s, best):
        def step(k, g, b, carry):
            hit = tiles[k][g] + near[b, pl.ds(s, 1), :] == best
            return carry + jnp.where(hit, near[b, pl.ds(half + s, 1), :], 0.0)

        start = jnp.zeros((LANES, LANES), jnp.float32)
        counts = over_slots(dims, places, table, filled, c, step, start)
        return jnp.sum(counts, axis=1, keepdims=True)

    def column(c, best):
        turned = jnp.zeros((LANES, LANES), jnp.float32)
        for s in range(half):
            if s + 1 < half:
                later = lowest(c, s + 1)
            else:
                later = lowest(jnp.minimum(c + 1, n_row - 1), 0)
            total = tally(c, s, best)
            turned = jnp.where(lane == s, best, jnp.where(lane == half + s, total, turned))
            best = later
        found[c] = turned.T[: 2 * half]
        return best

    lax.fori_loop(0, n_row, column, lowest(0, 0), unroll=UNROLL)
    for chip in range(chips):
        for col in range(n_col):
            if whole:
                out[col * chips + chip] = found[...]
            else:
                out[col * chips + chip] = found[pl.ds(PAIR * chip, PAIR)]


def relax_level(dims, counted, whole, places, ids, tiles, came):
    n_row, n_col, slots, half = dims
    blocks = n_row if whole else PAIR
    return pl.pallas_call(
        functools.partial(relax_kernel, dims, counted, whole),
        out_shape=piece(n_row // PAIR * n_col, blocks, 2 * half, LANES),
        in_specs=[in_smem()] * len(places) + [in_vmem()] * (PAIR + 2),
        out_specs=in_vmem(),
        scratch_shapes=[
            pltpu.VMEM((PAIR * n_col, 2 * half, LANES), jnp.float32),
            pltpu.VMEM((n_row, 2 * half, LANES), jnp.float32),
        ]
        + slot_scratch(dims),
        compiler_params=params(large_limit),
        name="relax_level",
    )(*places, ids, *tiles, came)


def depend_kernel(dims, first, last, *refs):
    n_row, n_col, slots, half = dims
    chips = n_row // PAIR
    n_places = 0 if is_dense(dims) else PAIR
    places, refs = refs[:n_places], refs[n_places:]
    source_rows, refs = refs[0], refs[1:]
    if first:
        tiles, refs = refs[:PAIR], refs[PAIR:]
        came, out, near, low, terms, acc, table, filled = refs
    else:
        near, low, terms, came, out, state, acc, table, filled = refs
    my_x, my_core, my_col = position()
    ids = source_rows[...]
    list_slots(dims, places, table, filled)
    if first:
        for r in range(n_col):
            for k in range(PAIR):
                h = my_core ^ k
                at_source = is_source(ids, (PAIR * my_x + h) * n_col + r)
                blocks = [came[r * chips + chip, PAIR * my_x + h] for chip in range(chips)]
                found = merge([(block[:half], block[half:]) for block in blocks])
                dist, count = settle(*found, at_source)
                near[k * n_col + r, :half, :] = dist
                near[k * n_col + r, half:, :] = count
        for c in range(n_row):
            at_source = is_source(ids, c * n_col + my_col)
            blocks = [came[my_col * chips + chip, c] for chip in range(chips)]
            found = merge([(block[:half], block[half:]) for block in blocks])
            dist, count = settle(*found, at_source)
            low[c, :half, :] = dist
            low[c, half:, :] = count
    else:
        other = came[(PAIR * my_x + 1 - my_core) * n_col + my_col]
        for core in range(PAIR):
            block = jnp.where(my_core == core, near[my_col], other)
            dist = block[:half]
            rows = pl.ds(core * half, half)
            state[0, rows, :] = jnp.where(dist < 0.5 * far_value, dist, -1.0)
            state[1, rows, :] = block[half:]
    acc[...] = jnp.zeros(acc.shape, jnp.float32)

    def add_terms(b, s, part):
        acc[b, s] += jnp.sum(part.reshape(LANES // SUB, SUB, LANES), axis=0)

    def select(c, _):
        count = low[c, half:, :]
        share = jnp.where(count > 0.5, 1.0 / jnp.maximum(count, 1.0), 0.0)
        turned = jnp.concatenate([low[c, :half, :], share], axis=0).T
        for s in range(half):
            dist = jnp.broadcast_to(turned[:, s : s + 1], (LANES, LANES))
            coef = jnp.broadcast_to(turned[:, half + s : half + s + 1], (LANES, LANES))

            def step(k, g, b, carry):
                hit = tiles[k][g] + near[b, pl.ds(s, 1), :] == dist
                part = jnp.where(hit, coef, 0.0)
                terms[(k * slots + g) * half + s] = part
                add_terms(b, s, part)
                return carry

            over_slots(dims, places, table, filled, c, step, 0)
        return 0

    def scale(c, _):
        line = (c // PAIR * PAIR + my_core) * n_col
        rows = pl.ds(c % PAIR * half, half)
        total = functools.reduce(jnp.add, [came[line + col, rows, :] for col in range(n_col)])
        turned = (1.0 + low[c, half:, :] * total).T
        for s in range(half):
            factor = jnp.broadcast_to(turned[:, s : s + 1], (LANES, LANES))

            def step(k, g, b, carry):
                add_terms(b, s, terms[(k * slots + g) * half + s] * factor)
                return carry

            over_slots(dims, places, table, filled, c, step, 0)

    if first:
        lax.fori_loop(0, n_row, select, 0, unroll=UNROLL)
    else:
        for c in range(n_row):
            scale(c, 0)
    for r in range(n_col):
        for k in range(PAIR):
            if last:
                b = k * n_col + r
                at_source = is_source(ids, (PAIR * my_x + (my_core ^ k)) * n_col + r)
                term = jnp.where(at_source, 0.0, near[b, half:, :] * jnp.sum(acc[b], axis=1))
                out[(my_core ^ k) * n_col + r] = jnp.sum(term, axis=0, keepdims=True)
            else:
                sums = jnp.sum(acc[(my_core ^ k) * n_col + r], axis=1)
                for chip in range(chips):
                    line = (PAIR * chip + my_core) * n_col
                    out[line + r, pl.ds(k * half, half), :] = sums
    if not last:
        for chip in range(chips):
            for r in range(n_col):
                out[(PAIR * chip + 1 - my_core) * n_col + r] = near[n_col + my_col]


def depend_level(dims, first, last, places, ids, tiles, bands, came):
    n_row, n_col, slots, half = dims
    if last:
        out_shape = [piece(PAIR * n_col, 1, LANES)]
    else:
        out_shape = [piece(n_row * n_col, PAIR * half, LANES)]
    if first:
        out_shape += [
            piece(PAIR * n_col, 2 * half, LANES),
            piece(n_row, 2 * half, LANES),
            piece(PAIR * slots * half, LANES, LANES),
        ]
    else:
        out_shape += [piece(2, PAIR * half, LANES)]
    vectors = [ids, *(tiles if first else []), *bands, came]
    return pl.pallas_call(
        functools.partial(depend_kernel, dims, first, last),
        out_shape=out_shape,
        in_specs=[in_smem()] * len(places) + [in_vmem()] * len(vectors),
        out_specs=[in_vmem()] * len(out_shape),
        scratch_shapes=[pltpu.VMEM((PAIR * n_col, half, SUB, LANES), jnp.float32)]
        + slot_scratch(dims),
        compiler_params=params(terms_limit),
        name="depend_level",
    )(*places, *vectors)


def result_kernel(rows, came, state, shown, paths, centrality):
    shown[...] = state[0]
    paths[...] = state[1]
    shares = [came[at] for at in range(came.shape[0])]
    centrality[...] = functools.reduce(jnp.add, shares) / rows


def results(dims, came, state):
    rows = PAIR * dims[3]
    return pl.pallas_call(
        functools.partial(result_kernel, rows),
        out_shape=[piece(rows, LANES)] * 2 + [piece(1, LANES)],
        in_specs=[in_vmem()] * 2,
        out_specs=[in_vmem()] * 3,
        compiler_params=params(small_limit),
        name="results",
    )(came, state)


def all_to_all(value, axes):
    return lax.all_to_all(value, axes, split_axis=0, concat_axis=0, tiled=True)


def swap_core(value):
    return lax.ppermute(value, "core", [(0, 1), (1, 0)])


def per_device(tiles, tile_index, tile_count, sources):
    slots = tiles.shape[0]
    rows = sources.shape[0]
    dims = (lax.axis_size("chip") * PAIR, lax.axis_size("col"), slots, rows // PAIR)
    own_places = tile_index.T
    line = ("col", "chip")

    everyone = ("chip", "core", "col")

    firsts, turned, ids = first_level(dims, own_places, sources, tiles)
    both = [turned, swap_core(turned)]
    places = [] if is_dense(dims) else [own_places, swap_core(own_places)]
    came = all_to_all(firsts, everyone)
    for level_no in range(1, LEVELS):
        whole = level_no == LEVELS - 1
        outs = relax_level(dims, level_no > 1, whole, places, ids, both, came)
        came = all_to_all(outs, line)
    sums, *bands = depend_level(dims, True, False, places, ids, both, [], came)
    for back_no in range(1, BACK):
        last = back_no == BACK - 1
        came = all_to_all(sums, everyone)
        sums, state = depend_level(dims, False, last, places, ids, both, bands, came)
    shown, paths, centrality = results(dims, all_to_all(sums, ("core", "col")), state)
    return shown, paths, centrality.reshape(LANES)


def solution(mesh):
    groups, rows, cols = mesh.devices.shape
    pairs = mesh.devices.reshape(groups, rows // PAIR, PAIR, cols)
    paired = jax.sharding.Mesh(pairs, ("groups", "chip", "core", "col"))
    vertices = ("chip", "core", "col")
    everywhere = ("groups",) + vertices
    in_specs = (P(everywhere, None, None), P(everywhere, None), P(everywhere), P("groups"))
    out_specs = (P("groups", vertices), P("groups", vertices), P(everywhere))
    return jax.shard_map(
        per_device, mesh=paired, in_specs=in_specs, out_specs=out_specs, check_vma=False
    )
```

```python
import functools

import jax
import jax.numpy as jnp
from jax import lax
from jax.experimental import pallas as pl
from jax.experimental.pallas import tpu as pltpu
from jax.sharding import PartitionSpec as P

LEVELS = 3
BACK = 2
LANES = 128
SUB = 8
PAIR = 2

far_value = 1000000.0
no_edge = 2000000.0
large_limit = 8 * 1024 * 1024
small_limit = 2 * 1024 * 1024
terms_limit = 20 * 1024 * 1024


def in_vmem():
    return pl.BlockSpec(memory_space=pltpu.VMEM)


def in_smem():
    return pl.BlockSpec(memory_space=pltpu.SMEM)


def in_hbm():
    return pl.BlockSpec(memory_space=pltpu.HBM)


def piece(*shape):
    return jax.ShapeDtypeStruct(shape, jnp.float32)


def params(limit):
    return pltpu.CompilerParams(vmem_limit_bytes=limit)


def is_dense(dims):
    return dims[2] == dims[0] * dims[1]


def position():
    return lax.axis_index("chip"), lax.axis_index("core"), lax.axis_index("col")


def source_ids(sources, first, half):
    row = lax.broadcasted_iota(jnp.int32, (PAIR * half, LANES), 0)
    ids = jnp.zeros((PAIR * half, LANES), jnp.int32)
    for s in range(half):
        ids = jnp.where(lax.rem(row, half) == s, sources[first + s], ids)
    return ids


def is_source(dims, ids, chip, col):
    n_row, n_col, slots, half = dims
    block = lax.broadcasted_iota(jnp.int32, ids.shape, 0) // half
    lane = lax.broadcasted_iota(jnp.int32, ids.shape, 1)
    return ids == ((PAIR * chip + block) * n_col + col) * LANES + lane


def own_first(rows, my_core):
    half = rows.shape[0] // PAIR
    return jnp.where(my_core == 0, rows, jnp.concatenate([rows[half:], rows[:half]], axis=0))


def settle(found_dist, found_count, at_source):
    dist = jnp.where(at_source, 0.0, jnp.minimum(found_dist, far_value))
    count = jnp.where(found_dist == dist, found_count, 0.0)
    return dist, jnp.where(at_source, 1.0, 0.0) + count


def merge(pairs):
    best = functools.reduce(jnp.minimum, [p[0] for p in pairs])
    total = functools.reduce(jnp.add, [jnp.where(p[0] == best, p[1], 0.0) for p in pairs])
    return best, total


def first_kernel(dims, *refs):
    n_row, n_col, slots, half = dims
    places_in, sources_in, tiles_in, out, turned, ids = refs[:6]
    places, sources, slot_of, tiles, lines, sems = refs[6:]
    my_x, my_core, my_col = position()
    my_row = my_x * PAIR + my_core
    parts = sems.shape[0] - 2
    size = slots // parts
    given = [
        pltpu.make_async_copy(places_in, places, sems.at[parts]),
        pltpu.make_async_copy(sources_in, sources, sems.at[parts + 1]),
    ]
    fetch = []
    for part in range(parts):
        span = pl.ds(part * size, size)
        fetch.append(pltpu.make_async_copy(tiles_in.at[span], tiles.at[span], sems.at[part]))
    for copy in given + fetch:
        copy.start()
    lines[...] = jnp.zeros(lines.shape, jnp.float32)

    def clear(at, _):
        slot_of[at] = -1
        return 0

    if not is_dense(dims):
        lax.fori_loop(0, n_row * n_col, clear, 0)
    for copy in given:
        copy.wait()
    for g in range(slots):
        slot_of[places[0, g] * n_row + places[1, g]] = g
    ids[...] = source_ids(sources, my_core * half, half)
    for part in range(parts):
        fetch[part].wait()
        for g in range(part * size, part * size + size):
            at = places[0, g] * n_row + places[1, g] if is_dense(dims) else g
            raw = tiles[g]
            turned[at] = jnp.where(raw > 0, raw, no_edge).T
    for s in range(PAIR * half):
        vertex = sources[s]
        block, place = vertex // LANES, lax.rem(vertex, LANES)
        r = lax.rem(block, n_col)

        @pl.when(block // n_col == my_row)
        def _():
            for c in range(n_row):
                g = slot_of[r * n_row + c]

                @pl.when(g >= 0)
                def _():
                    line = c % PAIR * half + s % half
                    row = tiles[g, pl.ds(place, 1), :]
                    lines[c // PAIR, s // half, pl.ds(line, 1), :] = row

    for chip in range(n_row // PAIR):
        for core in range(PAIR):
            line = lines[chip, core]
            line = jnp.where(line > 0, line, far_value)
            for col in range(n_col):
                out[(chip * PAIR + core) * n_col + col] = line


def first_level(dims, places, sources, tiles):
    n_row, n_col, slots, half = dims
    parts = 4 if slots % 4 == 0 else 1
    inputs = [pltpu.with_memory_space_constraint(x, pltpu.HBM) for x in (places, sources, tiles)]
    return pl.pallas_call(
        functools.partial(first_kernel, dims),
        out_shape=[
            piece(n_row * n_col, PAIR * half, LANES),
            piece(*tiles.shape),
            jax.ShapeDtypeStruct((PAIR * half, LANES), jnp.int32),
        ],
        in_specs=[in_hbm()] * 3,
        out_specs=[in_vmem()] * 3,
        scratch_shapes=[
            pltpu.SMEM(places.shape, jnp.int32),
            pltpu.SMEM(sources.shape, jnp.int32),
            pltpu.SMEM((n_row * n_col,), jnp.int32),
            pltpu.VMEM(tiles.shape, jnp.float32),
            pltpu.VMEM((n_row // PAIR, PAIR, PAIR * half, LANES), jnp.float32),
            pltpu.SemaphoreType.DMA((parts + 2,)),
        ],
        compiler_params=params(large_limit),
        name="first_level",
    )(*inputs)


def list_slots(dims, places, table, filled):
    n_row, n_col, slots, half = dims
    if is_dense(dims):
        return

    def clear(at, _):
        filled[at] = 0
        return 0

    lax.fori_loop(0, PAIR * n_row, clear, 0)
    for k in range(PAIR):

        def enter(g, _):
            at = k * n_row + places[k][1, g]
            table[at * n_col + filled[at]] = g
            filled[at] += 1
            return 0

        lax.fori_loop(0, slots, enter, 0)


def over_slots(dims, places, table, filled, c, step, carry):
    n_row, n_col, slots, half = dims
    for k in range(PAIR):
        if is_dense(dims):
            for r in range(n_col):
                carry = step(k, r * n_row + c, r, carry)
        else:
            at = k * n_row + c

            def entry(e, carry):
                g = table[at * n_col + e]
                return step(k, g, places[k][0, g], carry)

            carry = lax.fori_loop(0, filled[at], entry, carry)
    return carry


def slot_scratch(dims):
    n_row, n_col, slots, half = dims
    return [
        pltpu.SMEM((PAIR * n_row * n_col,), jnp.int32),
        pltpu.SMEM((PAIR * n_row,), jnp.int32),
    ]


def relax_kernel(dims, counted, whole, *refs):
    n_row, n_col, slots, half = dims
    chips = n_row // PAIR
    n_places = 0 if is_dense(dims) else PAIR
    places, refs = refs[:n_places], refs[n_places:]
    source_rows, tiles, refs = refs[0], refs[1 : 1 + PAIR], refs[1 + PAIR :]
    came, out, near, found, table, filled = refs
    my_x, my_core, my_col = position()
    ids = source_rows[...]
    list_slots(dims, places, table, filled)
    for r in range(n_col):
        if counted:
            blocks = [came[r * chips + chip, 0] for chip in range(chips)]
            reached, count = merge([(block[0], block[1]) for block in blocks])
        else:
            parts = [came[at * n_col + r] for at in range(n_row)]
            reached = functools.reduce(jnp.minimum, parts)
            count = jnp.where(reached < far_value, 1.0, 0.0)
        dist, count = settle(reached, count, is_source(dims, ids, my_x, r))
        near[r, 0] = own_first(dist, my_core)
        near[r, 1] = own_first(count, my_core)
    lane = lax.broadcasted_iota(jnp.int32, (LANES, LANES), 1)

    def lowest(c, s):
        def step(k, g, r, carry):
            return jnp.minimum(carry, tiles[k][g] + near[r, 0, pl.ds(k * half + s, 1), :])

        start = jnp.full((LANES, LANES), far_value, jnp.float32)
        reached = over_slots(dims, places, table, filled, c, step, start)
        return jnp.min(reached, axis=1, keepdims=True)

    def tally(c, s, best):
        def step(k, g, r, carry):
            row = pl.ds(k * half + s, 1)
            hit = tiles[k][g] + near[r, 0, row, :] == best
            return carry + jnp.where(hit, near[r, 1, row, :], 0.0)

        start = jnp.zeros((LANES, LANES), jnp.float32)
        counts = over_slots(dims, places, table, filled, c, step, start)
        return jnp.sum(counts, axis=1, keepdims=True)

    def columns(chip, _):
        turned = jnp.zeros((LANES, LANES), jnp.float32)
        rows = PAIR * half
        best = lowest(PAIR * chip, 0)
        for at in range(rows):
            later = None
            if at + 1 < rows:
                later = lowest(PAIR * chip + (at + 1) // half, (at + 1) % half)
            total = tally(PAIR * chip + at // half, at % half, best)
            turned = jnp.where(lane == at, best, jnp.where(lane == rows + at, total, turned))
            best = later
        both = turned.T
        found[chip, 0] = both[:rows]
        found[chip, 1] = both[rows : 2 * rows]
        return 0

    lax.fori_loop(0, chips, columns, 0)
    for chip in range(chips):
        for col in range(n_col):
            if whole:
                out[col * chips + chip] = found[...]
            else:
                out[col * chips + chip, 0] = found[chip]


def relax_level(dims, counted, whole, places, ids, tiles, came):
    n_row, n_col, slots, half = dims
    chips = n_row // PAIR
    return pl.pallas_call(
        functools.partial(relax_kernel, dims, counted, whole),
        out_shape=piece(chips * n_col, chips if whole else 1, 2, PAIR * half, LANES),
        in_specs=[in_smem()] * len(places) + [in_vmem()] * (PAIR + 2),
        out_specs=in_vmem(),
        scratch_shapes=[
            pltpu.VMEM((n_col, 2, PAIR * half, LANES), jnp.float32),
            pltpu.VMEM((chips, 2, PAIR * half, LANES), jnp.float32),
        ]
        + slot_scratch(dims),
        compiler_params=params(large_limit),
        name="relax_level",
    )(*places, ids, *tiles, came)


def depend_kernel(dims, first, last, *refs):
    n_row, n_col, slots, half = dims
    chips = n_row // PAIR
    n_places = 0 if is_dense(dims) else PAIR
    places, refs = refs[:n_places], refs[n_places:]
    source_rows, refs = refs[0], refs[1:]
    if first:
        tiles, refs = refs[:PAIR], refs[PAIR:]
        came, out, near, low, terms, acc, table, filled = refs
    else:
        near, low, terms, came, out, state, acc, table, filled = refs
    my_x, my_core, my_col = position()
    ids = source_rows[...]
    list_slots(dims, places, table, filled)
    if first:
        for r in range(n_col):
            blocks = [came[r * chips + chip, my_x] for chip in range(chips)]
            found = merge([(block[0], block[1]) for block in blocks])
            dist, count = settle(*found, is_source(dims, ids, my_x, r))
            near[r, 0] = own_first(dist, my_core)
            near[r, 1] = own_first(count, my_core)
        for at in range(chips):
            blocks = [came[my_col * chips + chip, at] for chip in range(chips)]
            found = merge([(block[0], block[1]) for block in blocks])
            dist, count = settle(*found, is_source(dims, ids, at, my_col))
            low[at, 0] = dist
            low[at, 1] = count
    else:
        other = came[(PAIR * my_x + 1 - my_core) * n_col + my_col]
        mine = jnp.concatenate([near[my_col, 0, :half, :], near[my_col, 1, :half, :]], axis=0)
        for core in range(PAIR):
            block = jnp.where(my_core == core, mine, other)
            dist = block[:half]
            rows = pl.ds(core * half, half)
            state[0, rows, :] = jnp.where(dist < 0.5 * far_value, dist, -1.0)
            state[1, rows, :] = block[half:]
    acc[...] = jnp.zeros(acc.shape, jnp.float32)

    def add_terms(k, r, s, part):
        acc[k * n_col + r, s] += jnp.sum(part.reshape(LANES // SUB, SUB, LANES), axis=0)

    def select(chip, _):
        rows = PAIR * half
        count = low[chip, 1]
        share = jnp.where(count > 0.5, 1.0 / jnp.maximum(count, 1.0), 0.0)
        turned = jnp.concatenate([low[chip, 0], share], axis=0).T
        for at in range(rows):
            c, s = PAIR * chip + at // half, at % half
            dist = jnp.broadcast_to(turned[:, at : at + 1], (LANES, LANES))
            coef = jnp.broadcast_to(turned[:, rows + at : rows + at + 1], (LANES, LANES))

            def step(k, g, r, carry):
                hit = tiles[k][g] + near[r, 0, pl.ds(k * half + s, 1), :] == dist
                part = jnp.where(hit, coef, 0.0)
                terms[(k * slots + g) * half + s] = part
                add_terms(k, r, s, part)
                return carry

            over_slots(dims, places, table, filled, c, step, 0)
        return 0

    def scale(chip):
        line = (PAIR * chip + my_core) * n_col
        total = functools.reduce(jnp.add, [came[line + col] for col in range(n_col)])
        turned = (1.0 + low[chip, 1] * total).T
        for at in range(PAIR * half):
            c, s = PAIR * chip + at // half, at % half
            factor = jnp.broadcast_to(turned[:, at : at + 1], (LANES, LANES))

            def step(k, g, r, carry):
                add_terms(k, r, s, terms[(k * slots + g) * half + s] * factor)
                return carry

            over_slots(dims, places, table, filled, c, step, 0)

    if first:
        lax.fori_loop(0, chips, select, 0)
    else:
        for chip in range(chips):
            scale(chip)
    for r in range(n_col):
        if last:
            counted = jnp.where(is_source(dims, ids, my_x, r), 0.0, 1.0)
            weight = own_first(counted, my_core) * near[r, 1]
        for k in range(PAIR):
            if last:
                sums = jnp.sum(acc[k * n_col + r], axis=1)
                term = weight[k * half : k * half + half] * sums
                out[(my_core ^ k) * n_col + r] = jnp.sum(term, axis=0, keepdims=True)
            else:
                sums = jnp.sum(acc[(my_core ^ k) * n_col + r], axis=1)
                for chip in range(chips):
                    line = (PAIR * chip + my_core) * n_col
                    out[line + r, pl.ds(k * half, half), :] = sums
    if not last:
        give = jnp.concatenate([near[my_col, 0, half:, :], near[my_col, 1, half:, :]], axis=0)
        for chip in range(chips):
            for r in range(n_col):
                out[(PAIR * chip + 1 - my_core) * n_col + r] = give


def depend_level(dims, first, last, places, ids, tiles, bands, came):
    n_row, n_col, slots, half = dims
    if last:
        out_shape = [piece(PAIR * n_col, 1, LANES)]
    else:
        out_shape = [piece(n_row * n_col, PAIR * half, LANES)]
    if first:
        out_shape += [
            piece(n_col, 2, PAIR * half, LANES),
            piece(n_row // PAIR, 2, PAIR * half, LANES),
            piece(PAIR * slots * half, LANES, LANES),
        ]
    else:
        out_shape += [piece(2, PAIR * half, LANES)]
    vectors = [ids, *(tiles if first else []), *bands, came]
    return pl.pallas_call(
        functools.partial(depend_kernel, dims, first, last),
        out_shape=out_shape,
        in_specs=[in_smem()] * len(places) + [in_vmem()] * len(vectors),
        out_specs=[in_vmem()] * len(out_shape),
        scratch_shapes=[pltpu.VMEM((PAIR * n_col, half, SUB, LANES), jnp.float32)]
        + slot_scratch(dims),
        compiler_params=params(terms_limit),
        name="depend_level",
    )(*places, *vectors)


def result_kernel(rows, came, state, shown, paths, centrality):
    shown[...] = state[0]
    paths[...] = state[1]
    shares = [came[at] for at in range(came.shape[0])]
    centrality[...] = functools.reduce(jnp.add, shares) / rows


def results(dims, came, state):
    rows = PAIR * dims[3]
    return pl.pallas_call(
        functools.partial(result_kernel, rows),
        out_shape=[piece(rows, LANES)] * 2 + [piece(1, LANES)],
        in_specs=[in_vmem()] * 2,
        out_specs=[in_vmem()] * 3,
        compiler_params=params(small_limit),
        name="results",
    )(came, state)


def all_to_all(value, axes):
    return lax.all_to_all(value, axes, split_axis=0, concat_axis=0, tiled=True)


def swap_core(value):
    return lax.ppermute(value, "core", [(0, 1), (1, 0)])


def per_device(tiles, tile_index, tile_count, sources):
    slots = tiles.shape[0]
    rows = sources.shape[0]
    dims = (lax.axis_size("chip") * PAIR, lax.axis_size("col"), slots, rows // PAIR)
    own_places = tile_index.T
    line = ("col", "chip")

    everyone = ("chip", "core", "col")

    firsts, turned, ids = first_level(dims, own_places, sources, tiles)
    both = [turned, swap_core(turned)]
    places = [] if is_dense(dims) else [own_places, swap_core(own_places)]
    came = all_to_all(firsts, everyone)
    for level_no in range(1, LEVELS):
        whole = level_no == LEVELS - 1
        outs = relax_level(dims, level_no > 1, whole, places, ids, both, came)
        came = all_to_all(outs, line)
    sums, *bands = depend_level(dims, True, False, places, ids, both, [], came)
    for back_no in range(1, BACK):
        last = back_no == BACK - 1
        came = all_to_all(sums, everyone)
        sums, state = depend_level(dims, False, last, places, ids, both, bands, came)
    shown, paths, centrality = results(dims, all_to_all(sums, ("core", "col")), state)
    return shown, paths, centrality.reshape(LANES)


def solution(mesh):
    groups, rows, cols = mesh.devices.shape
    pairs = mesh.devices.reshape(groups, rows // PAIR, PAIR, cols)
    paired = jax.sharding.Mesh(pairs, ("groups", "chip", "core", "col"))
    vertices = ("chip", "core", "col")
    everywhere = ("groups",) + vertices
    in_specs = (P(everywhere, None, None), P(everywhere, None), P(everywhere), P("groups"))
    out_specs = (P("groups", vertices), P("groups", vertices), P(everywhere))
    return jax.shard_map(
        per_device, mesh=paired, in_specs=in_specs, out_specs=out_specs, check_vma=False
    )
```

```python
import functools

import jax
import jax.numpy as jnp
from jax import lax
from jax.experimental import pallas as pl
from jax.experimental.pallas import tpu as pltpu
from jax.sharding import PartitionSpec as P

LEVELS = 3
BACK = 2
LANES = 128
SUB = 8
PAIR = 2
SPAN = 64

far_value = 1000000.0
no_edge = 2000000.0
large_limit = 8 * 1024 * 1024
small_limit = 2 * 1024 * 1024
terms_limit = 20 * 1024 * 1024


def in_vmem():
    return pl.BlockSpec(memory_space=pltpu.VMEM)


def in_smem():
    return pl.BlockSpec(memory_space=pltpu.SMEM)


def in_hbm():
    return pl.BlockSpec(memory_space=pltpu.HBM)


def piece(*shape):
    return jax.ShapeDtypeStruct(shape, jnp.float32)


def params(limit):
    return pltpu.CompilerParams(vmem_limit_bytes=limit)


def is_dense(dims):
    return dims[2] == dims[0] * dims[1]


def position():
    return lax.axis_index("chip"), lax.axis_index("core"), lax.axis_index("col")


def source_ids(sources, first, half):
    row = lax.broadcasted_iota(jnp.int32, (PAIR * half, LANES), 0)
    ids = jnp.zeros((PAIR * half, LANES), jnp.int32)
    for s in range(half):
        ids = jnp.where(lax.rem(row, half) == s, sources[first + s], ids)
    return ids


def is_source(dims, ids, chip, col):
    n_row, n_col, slots, half = dims
    block = lax.broadcasted_iota(jnp.int32, ids.shape, 0) // half
    lane = lax.broadcasted_iota(jnp.int32, ids.shape, 1)
    return ids == ((PAIR * chip + block) * n_col + col) * LANES + lane


def own_first(rows, my_core):
    half = rows.shape[0] // PAIR
    return jnp.where(my_core == 0, rows, jnp.concatenate([rows[half:], rows[:half]], axis=0))


def settle(found_dist, found_count, at_source):
    dist = jnp.where(at_source, 0.0, jnp.minimum(found_dist, far_value))
    count = jnp.where(found_dist == dist, found_count, 0.0)
    return dist, jnp.where(at_source, 1.0, 0.0) + count


def merge(pairs):
    best = functools.reduce(jnp.minimum, [p[0] for p in pairs])
    total = functools.reduce(jnp.add, [jnp.where(p[0] == best, p[1], 0.0) for p in pairs])
    return best, total


def first_kernel(dims, *refs):
    n_row, n_col, slots, half = dims
    places_in, sources_in, tiles_in, out, turned, ids = refs[:6]
    places, sources, slot_of, tiles, lines, sems = refs[6:]
    my_x, my_core, my_col = position()
    my_row = my_x * PAIR + my_core
    parts = sems.shape[0] - 2
    size = slots // parts
    given = [
        pltpu.make_async_copy(places_in, places, sems.at[parts]),
        pltpu.make_async_copy(sources_in, sources, sems.at[parts + 1]),
    ]
    fetch = []
    for part in range(parts):
        span = pl.ds(part * size, size)
        fetch.append(pltpu.make_async_copy(tiles_in.at[span], tiles.at[span], sems.at[part]))
    for copy in given + fetch:
        copy.start()
    lines[...] = jnp.zeros(lines.shape, jnp.float32)

    def clear(at, _):
        slot_of[at] = -1
        return 0

    if not is_dense(dims):
        lax.fori_loop(0, n_row * n_col, clear, 0)
    for copy in given:
        copy.wait()
    for g in range(slots):
        slot_of[places[0, g] * n_row + places[1, g]] = g
    ids[...] = source_ids(sources, my_core * half, half)
    for part in range(parts):
        fetch[part].wait()
        for g in range(part * size, part * size + size):
            at = places[0, g] * n_row + places[1, g] if is_dense(dims) else g
            raw = tiles[g]
            turned[at] = jnp.where(raw > 0, raw, no_edge).T
    for s in range(PAIR * half):
        vertex = sources[s]
        block, place = vertex // LANES, lax.rem(vertex, LANES)
        r = lax.rem(block, n_col)

        @pl.when(block // n_col == my_row)
        def _():
            for c in range(n_row):
                g = slot_of[r * n_row + c]

                @pl.when(g >= 0)
                def _():
                    line = c % PAIR * half + s % half
                    row = tiles[g, pl.ds(place, 1), :]
                    lines[c // PAIR, s // half, pl.ds(line, 1), :] = row

    for chip in range(n_row // PAIR):
        for core in range(PAIR):
            line = lines[chip, core]
            line = jnp.where(line > 0, line, far_value)
            for col in range(n_col):
                out[(chip * PAIR + core) * n_col + col] = line


def first_level(dims, places, sources, tiles):
    n_row, n_col, slots, half = dims
    parts = 4 if slots % 4 == 0 else 1
    inputs = [pltpu.with_memory_space_constraint(x, pltpu.HBM) for x in (places, sources, tiles)]
    return pl.pallas_call(
        functools.partial(first_kernel, dims),
        out_shape=[
            piece(n_row * n_col, PAIR * half, LANES),
            piece(*tiles.shape),
            jax.ShapeDtypeStruct((PAIR * half, LANES), jnp.int32),
        ],
        in_specs=[in_hbm()] * 3,
        out_specs=[in_vmem()] * 3,
        scratch_shapes=[
            pltpu.SMEM(places.shape, jnp.int32),
            pltpu.SMEM(sources.shape, jnp.int32),
            pltpu.SMEM((n_row * n_col,), jnp.int32),
            pltpu.VMEM(tiles.shape, jnp.float32),
            pltpu.VMEM((n_row // PAIR, PAIR, PAIR * half, LANES), jnp.float32),
            pltpu.SemaphoreType.DMA((parts + 2,)),
        ],
        compiler_params=params(large_limit),
        name="first_level",
    )(*inputs)


def list_slots(dims, places, table, filled):
    n_row, n_col, slots, half = dims
    if is_dense(dims):
        return

    def clear(at, _):
        filled[at] = 0
        return 0

    lax.fori_loop(0, PAIR * n_row, clear, 0)
    for k in range(PAIR):

        def enter(g, _):
            at = k * n_row + places[k][1, g]
            table[at * n_col + filled[at]] = g
            filled[at] += 1
            return 0

        lax.fori_loop(0, slots, enter, 0)


def over_slots(dims, places, table, filled, c, step, carry):
    n_row, n_col, slots, half = dims
    for k in range(PAIR):
        if is_dense(dims):
            for r in range(n_col):
                carry = step(k, r * n_row + c, r, carry)
        else:
            at = k * n_row + c

            def entry(e, carry):
                g = table[at * n_col + e]
                return step(k, g, places[k][0, g], carry)

            carry = lax.fori_loop(0, filled[at], entry, carry)
    return carry


def slot_scratch(dims):
    n_row, n_col, slots, half = dims
    return [
        pltpu.SMEM((PAIR * n_row * n_col,), jnp.int32),
        pltpu.SMEM((PAIR * n_row,), jnp.int32),
    ]


def relax_kernel(dims, counted, whole, *refs):
    n_row, n_col, slots, half = dims
    chips = n_row // PAIR
    n_places = 0 if is_dense(dims) else PAIR
    places, refs = refs[:n_places], refs[n_places:]
    source_rows, tiles, refs = refs[0], refs[1 : 1 + PAIR], refs[1 + PAIR :]
    came, out, near, found, table, filled = refs
    my_x, my_core, my_col = position()
    ids = source_rows[...]
    list_slots(dims, places, table, filled)
    for r in range(n_col):
        if counted:
            blocks = [came[r * chips + chip, 0] for chip in range(chips)]
            reached, count = merge([(block[0], block[1]) for block in blocks])
        else:
            parts = [came[at * n_col + r] for at in range(n_row)]
            reached = functools.reduce(jnp.minimum, parts)
            count = jnp.where(reached < far_value, 1.0, 0.0)
        dist, count = settle(reached, count, is_source(dims, ids, my_x, r))
        near[r, 0] = own_first(dist, my_core)
        near[r, 1] = own_first(count, my_core)
    lane = lax.broadcasted_iota(jnp.int32, (SPAN, LANES), 1)

    def lowest(chip, item):
        h, s, q = item

        def step(k, g, r, carry):
            weight = tiles[k][g, pl.ds(q, SPAN), :]
            return jnp.minimum(carry, weight + near[r, 0, pl.ds(k * half + s, 1), :])

        start = jnp.full((SPAN, LANES), far_value, jnp.float32)
        reached = over_slots(dims, places, table, filled, PAIR * chip + h, step, start)
        return jnp.min(reached, axis=1, keepdims=True)

    def tally(chip, item, best):
        h, s, q = item

        def step(k, g, r, carry):
            row = pl.ds(k * half + s, 1)
            hit = tiles[k][g, pl.ds(q, SPAN), :] + near[r, 0, row, :] == best
            return carry + jnp.where(hit, near[r, 1, row, :], 0.0)

        start = jnp.zeros((SPAN, LANES), jnp.float32)
        counts = over_slots(dims, places, table, filled, PAIR * chip + h, step, start)
        return jnp.sum(counts, axis=1, keepdims=True)

    spans = range(0, LANES, SPAN)
    items = [(h, s, q) for h in range(PAIR) for q in spans for s in range(half)]

    def columns(chip, _):
        rows = PAIR * half
        turned = {q: jnp.zeros((SPAN, LANES), jnp.float32) for q in spans}
        best = lowest(chip, items[0])
        for at, item in enumerate(items):
            later = lowest(chip, items[at + 1]) if at + 1 < len(items) else None
            total = tally(chip, item, best)
            h, s, q = item
            to = h * half + s
            with_total = jnp.where(lane == rows + to, total, turned[q])
            turned[q] = jnp.where(lane == to, best, with_total)
            best = later
        both = jnp.concatenate([turned[q] for q in spans], axis=0).T
        found[chip, 0] = both[:rows]
        found[chip, 1] = both[rows : 2 * rows]
        return 0

    lax.fori_loop(0, chips, columns, 0)
    for chip in range(chips):
        for col in range(n_col):
            if whole:
                out[col * chips + chip] = found[...]
            else:
                out[col * chips + chip, 0] = found[chip]


def relax_level(dims, counted, whole, places, ids, tiles, came):
    n_row, n_col, slots, half = dims
    chips = n_row // PAIR
    return pl.pallas_call(
        functools.partial(relax_kernel, dims, counted, whole),
        out_shape=piece(chips * n_col, chips if whole else 1, 2, PAIR * half, LANES),
        in_specs=[in_smem()] * len(places) + [in_vmem()] * (PAIR + 2),
        out_specs=in_vmem(),
        scratch_shapes=[
            pltpu.VMEM((n_col, 2, PAIR * half, LANES), jnp.float32),
            pltpu.VMEM((chips, 2, PAIR * half, LANES), jnp.float32),
        ]
        + slot_scratch(dims),
        compiler_params=params(large_limit),
        name="relax_level",
    )(*places, ids, *tiles, came)


def depend_kernel(dims, first, last, *refs):
    n_row, n_col, slots, half = dims
    chips = n_row // PAIR
    n_places = 0 if is_dense(dims) else PAIR
    places, refs = refs[:n_places], refs[n_places:]
    source_rows, refs = refs[0], refs[1:]
    if first:
        tiles, refs = refs[:PAIR], refs[PAIR:]
        came, out, near, low, terms, acc, table, filled = refs
    else:
        near, low, terms, came, out, state, acc, table, filled = refs
    my_x, my_core, my_col = position()
    ids = source_rows[...]
    list_slots(dims, places, table, filled)
    if first:
        for r in range(n_col):
            blocks = [came[r * chips + chip, my_x] for chip in range(chips)]
            found = merge([(block[0], block[1]) for block in blocks])
            dist, count = settle(*found, is_source(dims, ids, my_x, r))
            near[r, 0] = own_first(dist, my_core)
            near[r, 1] = own_first(count, my_core)
        for at in range(chips):
            blocks = [came[my_col * chips + chip, at] for chip in range(chips)]
            found = merge([(block[0], block[1]) for block in blocks])
            dist, count = settle(*found, is_source(dims, ids, at, my_col))
            low[at, 0] = dist
            low[at, 1] = count
    else:
        other = came[(PAIR * my_x + 1 - my_core) * n_col + my_col]
        mine = jnp.concatenate([near[my_col, 0, :half, :], near[my_col, 1, :half, :]], axis=0)
        for core in range(PAIR):
            block = jnp.where(my_core == core, mine, other)
            dist = block[:half]
            rows = pl.ds(core * half, half)
            state[0, rows, :] = jnp.where(dist < 0.5 * far_value, dist, -1.0)
            state[1, rows, :] = block[half:]
    acc[...] = jnp.zeros(acc.shape, jnp.float32)

    def add_terms(k, r, s, part):
        acc[k * n_col + r, s] += jnp.sum(part.reshape(-1, SUB, LANES), axis=0)

    def select(chip, _):
        rows = PAIR * half
        count = low[chip, 1]
        share = jnp.where(count > 0.5, 1.0 / jnp.maximum(count, 1.0), 0.0)
        turned = jnp.concatenate([low[chip, 0], share], axis=0).T
        for at, q in [(at, q) for at in range(rows) for q in range(0, LANES, SPAN)]:
            c, s = PAIR * chip + at // half, at % half
            span = slice(q, q + SPAN)
            dist = jnp.broadcast_to(turned[span, at : at + 1], (SPAN, LANES))
            coef = jnp.broadcast_to(turned[span, rows + at : rows + at + 1], (SPAN, LANES))

            def step(k, g, r, carry):
                row = near[r, 0, pl.ds(k * half + s, 1), :]
                hit = tiles[k][g, pl.ds(q, SPAN), :] + row == dist
                part = jnp.where(hit, coef, 0.0)
                terms[(k * slots + g) * half + s, pl.ds(q, SPAN), :] = part
                add_terms(k, r, s, part)
                return carry

            over_slots(dims, places, table, filled, c, step, 0)
        return 0

    def scale(chip):
        line = (PAIR * chip + my_core) * n_col
        total = functools.reduce(jnp.add, [came[line + col] for col in range(n_col)])
        turned = (1.0 + low[chip, 1] * total).T
        for at in range(PAIR * half):
            c, s = PAIR * chip + at // half, at % half
            factor = jnp.broadcast_to(turned[:, at : at + 1], (LANES, LANES))

            def step(k, g, r, carry):
                add_terms(k, r, s, terms[(k * slots + g) * half + s] * factor)
                return carry

            over_slots(dims, places, table, filled, c, step, 0)

    if first:
        lax.fori_loop(0, chips, select, 0)
    else:
        for chip in range(chips):
            scale(chip)
    for r in range(n_col):
        if last:
            counted = jnp.where(is_source(dims, ids, my_x, r), 0.0, 1.0)
            weight = own_first(counted, my_core) * near[r, 1]
        for k in range(PAIR):
            if last:
                sums = jnp.sum(acc[k * n_col + r], axis=1)
                term = weight[k * half : k * half + half] * sums
                out[(my_core ^ k) * n_col + r] = jnp.sum(term, axis=0, keepdims=True)
            else:
                sums = jnp.sum(acc[(my_core ^ k) * n_col + r], axis=1)
                for chip in range(chips):
                    line = (PAIR * chip + my_core) * n_col
                    out[line + r, pl.ds(k * half, half), :] = sums
    if not last:
        give = jnp.concatenate([near[my_col, 0, half:, :], near[my_col, 1, half:, :]], axis=0)
        for chip in range(chips):
            for r in range(n_col):
                out[(PAIR * chip + 1 - my_core) * n_col + r] = give


def depend_level(dims, first, last, places, ids, tiles, bands, came):
    n_row, n_col, slots, half = dims
    if last:
        out_shape = [piece(PAIR * n_col, 1, LANES)]
    else:
        out_shape = [piece(n_row * n_col, PAIR * half, LANES)]
    if first:
        out_shape += [
            piece(n_col, 2, PAIR * half, LANES),
            piece(n_row // PAIR, 2, PAIR * half, LANES),
            piece(PAIR * slots * half, LANES, LANES),
        ]
    else:
        out_shape += [piece(2, PAIR * half, LANES)]
    vectors = [ids, *(tiles if first else []), *bands, came]
    return pl.pallas_call(
        functools.partial(depend_kernel, dims, first, last),
        out_shape=out_shape,
        in_specs=[in_smem()] * len(places) + [in_vmem()] * len(vectors),
        out_specs=[in_vmem()] * len(out_shape),
        scratch_shapes=[pltpu.VMEM((PAIR * n_col, half, SUB, LANES), jnp.float32)]
        + slot_scratch(dims),
        compiler_params=params(terms_limit),
        name="depend_level",
    )(*places, *vectors)


def result_kernel(rows, came, state, shown, paths, centrality):
    shown[...] = state[0]
    paths[...] = state[1]
    shares = [came[at] for at in range(came.shape[0])]
    centrality[...] = functools.reduce(jnp.add, shares) / rows


def results(dims, came, state):
    rows = PAIR * dims[3]
    return pl.pallas_call(
        functools.partial(result_kernel, rows),
        out_shape=[piece(rows, LANES)] * 2 + [piece(1, LANES)],
        in_specs=[in_vmem()] * 2,
        out_specs=[in_vmem()] * 3,
        compiler_params=params(small_limit),
        name="results",
    )(came, state)


def all_to_all(value, axes):
    return lax.all_to_all(value, axes, split_axis=0, concat_axis=0, tiled=True)


def swap_core(value):
    return lax.ppermute(value, "core", [(0, 1), (1, 0)])


def per_device(tiles, tile_index, tile_count, sources):
    slots = tiles.shape[0]
    rows = sources.shape[0]
    dims = (lax.axis_size("chip") * PAIR, lax.axis_size("col"), slots, rows // PAIR)
    own_places = tile_index.T
    line = ("col", "chip")

    everyone = ("chip", "core", "col")

    firsts, turned, ids = first_level(dims, own_places, sources, tiles)
    both = [turned, swap_core(turned)]
    places = [] if is_dense(dims) else [own_places, swap_core(own_places)]
    came = all_to_all(firsts, everyone)
    for level_no in range(1, LEVELS):
        whole = level_no == LEVELS - 1
        outs = relax_level(dims, level_no > 1, whole, places, ids, both, came)
        came = all_to_all(outs, line)
    sums, *bands = depend_level(dims, True, False, places, ids, both, [], came)
    for back_no in range(1, BACK):
        last = back_no == BACK - 1
        came = all_to_all(sums, everyone)
        sums, state = depend_level(dims, False, last, places, ids, both, bands, came)
    shown, paths, centrality = results(dims, all_to_all(sums, ("core", "col")), state)
    return shown, paths, centrality.reshape(LANES)


def solution(mesh):
    groups, rows, cols = mesh.devices.shape
    pairs = mesh.devices.reshape(groups, rows // PAIR, PAIR, cols)
    paired = jax.sharding.Mesh(pairs, ("groups", "chip", "core", "col"))
    vertices = ("chip", "core", "col")
    everywhere = ("groups",) + vertices
    in_specs = (P(everywhere, None, None), P(everywhere, None), P(everywhere), P("groups"))
    out_specs = (P("groups", vertices), P("groups", vertices), P(everywhere))
    return jax.shard_map(
        per_device, mesh=paired, in_specs=in_specs, out_specs=out_specs, check_vma=False
    )
```

```python
import functools

import jax
import jax.numpy as jnp
from jax import lax
from jax.experimental import pallas as pl
from jax.experimental.pallas import tpu as pltpu
from jax.sharding import PartitionSpec as P

LEVELS = 3
BACK = 2
LANES = 128
SUB = 8
PAIR = 2
SPAN = 64

far_value = 1000000.0
no_edge = 2000000.0
large_limit = 8 * 1024 * 1024
small_limit = 2 * 1024 * 1024
terms_limit = 20 * 1024 * 1024


def in_vmem():
    return pl.BlockSpec(memory_space=pltpu.VMEM)


def in_smem():
    return pl.BlockSpec(memory_space=pltpu.SMEM)


def in_hbm():
    return pl.BlockSpec(memory_space=pltpu.HBM)


def piece(*shape):
    return jax.ShapeDtypeStruct(shape, jnp.float32)


def params(limit):
    return pltpu.CompilerParams(vmem_limit_bytes=limit)


def is_dense(dims):
    return dims[2] == dims[0] * dims[1]


def position():
    return lax.axis_index("chip"), lax.axis_index("core"), lax.axis_index("col")


def source_ids(sources, first, half):
    row = lax.broadcasted_iota(jnp.int32, (PAIR * half, LANES), 0)
    ids = jnp.zeros((PAIR * half, LANES), jnp.int32)
    for s in range(half):
        ids = jnp.where(lax.rem(row, half) == s, sources[first + s], ids)
    return ids


def is_source(dims, ids, chip, col):
    n_row, n_col, slots, half = dims
    block = lax.broadcasted_iota(jnp.int32, ids.shape, 0) // half
    lane = lax.broadcasted_iota(jnp.int32, ids.shape, 1)
    return ids == ((PAIR * chip + block) * n_col + col) * LANES + lane


def own_first(rows, my_core):
    half = rows.shape[0] // PAIR
    return jnp.where(my_core == 0, rows, jnp.concatenate([rows[half:], rows[:half]], axis=0))


def settle(found_dist, found_count, at_source):
    dist = jnp.where(at_source, 0.0, jnp.minimum(found_dist, far_value))
    count = jnp.where(found_dist == dist, found_count, 0.0)
    return dist, jnp.where(at_source, 1.0, 0.0) + count


def merge(pairs):
    best = functools.reduce(jnp.minimum, [p[0] for p in pairs])
    total = functools.reduce(jnp.add, [jnp.where(p[0] == best, p[1], 0.0) for p in pairs])
    return best, total


def first_kernel(dims, *refs):
    n_row, n_col, slots, half = dims
    places_in, sources_in, tiles_in, out, turned, ids = refs[:6]
    places, sources, slot_of, tiles, lines, sems = refs[6:]
    my_x, my_core, my_col = position()
    my_row = my_x * PAIR + my_core
    parts = sems.shape[0] - 2
    size = slots // parts
    given = [
        pltpu.make_async_copy(places_in, places, sems.at[parts]),
        pltpu.make_async_copy(sources_in, sources, sems.at[parts + 1]),
    ]
    fetch = []
    for part in range(parts):
        span = pl.ds(part * size, size)
        fetch.append(pltpu.make_async_copy(tiles_in.at[span], tiles.at[span], sems.at[part]))
    for copy in given + fetch:
        copy.start()
    lines[...] = jnp.zeros(lines.shape, jnp.float32)

    def clear(at, _):
        slot_of[at] = -1
        return 0

    if not is_dense(dims):
        lax.fori_loop(0, n_row * n_col, clear, 0)
    for copy in given:
        copy.wait()
    for g in range(slots):
        slot_of[places[0, g] * n_row + places[1, g]] = g
    ids[...] = source_ids(sources, my_core * half, half)
    for part in range(parts):
        fetch[part].wait()
        for g in range(part * size, part * size + size):
            at = places[0, g] * n_row + places[1, g] if is_dense(dims) else g
            raw = tiles[g]
            turned[at] = jnp.where(raw > 0, raw, no_edge).T
    for s in range(PAIR * half):
        vertex = sources[s]
        block, place = vertex // LANES, lax.rem(vertex, LANES)
        r = lax.rem(block, n_col)

        @pl.when(block // n_col == my_row)
        def _():
            for c in range(n_row):
                g = slot_of[r * n_row + c]

                @pl.when(g >= 0)
                def _():
                    line = c % PAIR * half + s % half
                    row = tiles[g, pl.ds(place, 1), :]
                    lines[c // PAIR, s // half, pl.ds(line, 1), :] = row

    for chip in range(n_row // PAIR):
        for core in range(PAIR):
            line = lines[chip, core]
            line = jnp.where(line > 0, line, far_value)
            for col in range(n_col):
                out[(chip * PAIR + core) * n_col + col] = line


def first_level(dims, places, sources, tiles):
    n_row, n_col, slots, half = dims
    parts = 4 if slots % 4 == 0 else 1
    inputs = [pltpu.with_memory_space_constraint(x, pltpu.HBM) for x in (places, sources, tiles)]
    return pl.pallas_call(
        functools.partial(first_kernel, dims),
        out_shape=[
            piece(n_row * n_col, PAIR * half, LANES),
            piece(*tiles.shape),
            jax.ShapeDtypeStruct((PAIR * half, LANES), jnp.int32),
        ],
        in_specs=[in_hbm()] * 3,
        out_specs=[in_vmem()] * 3,
        scratch_shapes=[
            pltpu.SMEM(places.shape, jnp.int32),
            pltpu.SMEM(sources.shape, jnp.int32),
            pltpu.SMEM((n_row * n_col,), jnp.int32),
            pltpu.VMEM(tiles.shape, jnp.float32),
            pltpu.VMEM((n_row // PAIR, PAIR, PAIR * half, LANES), jnp.float32),
            pltpu.SemaphoreType.DMA((parts + 2,)),
        ],
        compiler_params=params(large_limit),
        name="first_level",
    )(*inputs)


def list_slots(dims, places, table, filled):
    n_row, n_col, slots, half = dims
    if is_dense(dims):
        return

    def clear(at, _):
        filled[at] = 0
        return 0

    lax.fori_loop(0, PAIR * n_row, clear, 0)
    for k in range(PAIR):

        def enter(g, _):
            at = k * n_row + places[k][1, g]
            table[at * n_col + filled[at]] = g
            filled[at] += 1
            return 0

        lax.fori_loop(0, slots, enter, 0)


def over_slots(dims, places, table, filled, c, step, carry):
    n_row, n_col, slots, half = dims
    for k in range(PAIR):
        if is_dense(dims):
            for r in range(n_col):
                carry = step(k, r * n_row + c, r, carry)
        else:
            at = k * n_row + c

            def entry(e, carry):
                g = table[at * n_col + e]
                return step(k, g, places[k][0, g], carry)

            carry = lax.fori_loop(0, filled[at], entry, carry)
    return carry


def slot_scratch(dims):
    n_row, n_col, slots, half = dims
    return [
        pltpu.SMEM((PAIR * n_row * n_col,), jnp.int32),
        pltpu.SMEM((PAIR * n_row,), jnp.int32),
    ]


def relax_kernel(dims, counted, whole, *refs):
    n_row, n_col, slots, half = dims
    chips = n_row // PAIR
    n_places = 0 if is_dense(dims) else PAIR
    places, refs = refs[:n_places], refs[n_places:]
    source_rows, tiles, refs = refs[0], refs[1 : 1 + PAIR], refs[1 + PAIR :]
    came, out, near, found, table, filled = refs
    my_x, my_core, my_col = position()
    ids = source_rows[...]
    list_slots(dims, places, table, filled)
    for r in range(n_col):
        if counted:
            blocks = [came[r * chips + chip, 0] for chip in range(chips)]
            reached, count = merge([(block[0], block[1]) for block in blocks])
        else:
            parts = [came[at * n_col + r] for at in range(n_row)]
            reached = functools.reduce(jnp.minimum, parts)
            count = jnp.where(reached < far_value, 1.0, 0.0)
        dist, count = settle(reached, count, is_source(dims, ids, my_x, r))
        near[r, 0] = own_first(dist, my_core)
        near[r, 1] = own_first(count, my_core)
    lane = lax.broadcasted_iota(jnp.int32, (SPAN, LANES), 1)

    def lowest(chip, item):
        h, s, q = item

        def step(k, g, r, carry):
            weight = tiles[k][g, pl.ds(q, SPAN), :]
            return jnp.minimum(carry, weight + near[r, 0, pl.ds(k * half + s, 1), :])

        start = jnp.full((SPAN, LANES), far_value, jnp.float32)
        reached = over_slots(dims, places, table, filled, PAIR * chip + h, step, start)
        return jnp.min(reached, axis=1, keepdims=True)

    def tally(chip, item, best):
        h, s, q = item

        def step(k, g, r, carry):
            row = pl.ds(k * half + s, 1)
            hit = tiles[k][g, pl.ds(q, SPAN), :] + near[r, 0, row, :] == best
            return carry + jnp.where(hit, near[r, 1, row, :], 0.0)

        start = jnp.zeros((SPAN, LANES), jnp.float32)
        counts = over_slots(dims, places, table, filled, PAIR * chip + h, step, start)
        return jnp.sum(counts, axis=1, keepdims=True)

    spans = range(0, LANES, SPAN)
    items = [(h, s, q) for h in range(PAIR) for q in spans for s in range(half)]

    def columns(chip, _):
        rows = PAIR * half
        turned = {q: jnp.zeros((SPAN, LANES), jnp.float32) for q in spans}
        best = lowest(chip, items[0])
        for at, item in enumerate(items):
            later = lowest(chip, items[at + 1]) if at + 1 < len(items) else None
            total = tally(chip, item, best)
            h, s, q = item
            to = h * half + s
            with_total = jnp.where(lane == rows + to, total, turned[q])
            turned[q] = jnp.where(lane == to, best, with_total)
            best = later
        both = jnp.concatenate([turned[q] for q in spans], axis=0).T
        found[chip, 0] = both[:rows]
        found[chip, 1] = both[rows : 2 * rows]
        return 0

    lax.fori_loop(0, chips, columns, 0)
    for chip in range(chips):
        for col in range(n_col):
            if whole:
                out[col * chips + chip] = found[...]
            else:
                out[col * chips + chip, 0] = found[chip]


def relax_level(dims, counted, whole, places, ids, tiles, came):
    n_row, n_col, slots, half = dims
    chips = n_row // PAIR
    return pl.pallas_call(
        functools.partial(relax_kernel, dims, counted, whole),
        out_shape=piece(chips * n_col, chips if whole else 1, 2, PAIR * half, LANES),
        in_specs=[in_smem()] * len(places) + [in_vmem()] * (PAIR + 2),
        out_specs=in_vmem(),
        scratch_shapes=[
            pltpu.VMEM((n_col, 2, PAIR * half, LANES), jnp.float32),
            pltpu.VMEM((chips, 2, PAIR * half, LANES), jnp.float32),
        ]
        + slot_scratch(dims),
        compiler_params=params(large_limit),
        name="relax_level",
    )(*places, ids, *tiles, came)


def depend_kernel(dims, first, last, *refs):
    n_row, n_col, slots, half = dims
    chips = n_row // PAIR
    n_places = 0 if is_dense(dims) else PAIR
    places, refs = refs[:n_places], refs[n_places:]
    source_rows, refs = refs[0], refs[1:]
    if first:
        tiles, refs = refs[:PAIR], refs[PAIR:]
        came, out, near, low, terms, keep, give, acc, table, filled = refs
    else:
        near, low, terms, came, out, acc, table, filled = refs
    my_x, my_core, my_col = position()
    ids = source_rows[...]
    list_slots(dims, places, table, filled)
    if first:
        for r in range(n_col):
            blocks = [came[r * chips + chip, my_x] for chip in range(chips)]
            found = merge([(block[0], block[1]) for block in blocks])
            dist, count = settle(*found, is_source(dims, ids, my_x, r))
            near[r, 0] = own_first(dist, my_core)
            near[r, 1] = own_first(count, my_core)
        for at in range(chips):
            blocks = [came[my_col * chips + chip, at] for chip in range(chips)]
            found = merge([(block[0], block[1]) for block in blocks])
            dist, count = settle(*found, is_source(dims, ids, at, my_col))
            low[at, 0] = dist
            low[at, 1] = count
        for part in range(2):
            keep[pl.ds(part * half, half), :] = near[my_col, part, :half, :]
            give[pl.ds(part * half, half), :] = near[my_col, part, half:, :]
    acc[...] = jnp.zeros(acc.shape, jnp.float32)

    def add_terms(k, r, s, part):
        acc[k * n_col + r, s] += jnp.sum(part.reshape(-1, SUB, LANES), axis=0)

    def select(chip, _):
        rows = PAIR * half
        count = low[chip, 1]
        share = jnp.where(count > 0.5, 1.0 / jnp.maximum(count, 1.0), 0.0)
        turned = jnp.concatenate([low[chip, 0], share], axis=0).T
        for at, q in [(at, q) for at in range(rows) for q in range(0, LANES, SPAN)]:
            c, s = PAIR * chip + at // half, at % half
            span = slice(q, q + SPAN)
            dist = jnp.broadcast_to(turned[span, at : at + 1], (SPAN, LANES))
            coef = jnp.broadcast_to(turned[span, rows + at : rows + at + 1], (SPAN, LANES))

            def step(k, g, r, carry):
                row = near[r, 0, pl.ds(k * half + s, 1), :]
                hit = tiles[k][g, pl.ds(q, SPAN), :] + row == dist
                part = jnp.where(hit, coef, 0.0)
                terms[(k * slots + g) * half + s, pl.ds(q, SPAN), :] = part
                add_terms(k, r, s, part)
                return carry

            over_slots(dims, places, table, filled, c, step, 0)
        return 0

    def scale(chip):
        parts = [came[col * chips + chip] for col in range(n_col)]
        total = functools.reduce(jnp.add, parts)
        turned = (1.0 + low[chip, 1] * total).T
        for at in range(PAIR * half):
            c, s = PAIR * chip + at // half, at % half
            factor = jnp.broadcast_to(turned[:, at : at + 1], (LANES, LANES))

            def step(k, g, r, carry):
                add_terms(k, r, s, terms[(k * slots + g) * half + s] * factor)
                return carry

            over_slots(dims, places, table, filled, c, step, 0)

    if first:
        lax.fori_loop(0, chips, select, 0)
    else:
        for chip in range(chips):
            scale(chip)
    for r in range(n_col):
        if last:
            counted = jnp.where(is_source(dims, ids, my_x, r), 0.0, 1.0)
            weight = own_first(counted, my_core) * near[r, 1]
        for k in range(PAIR):
            if last:
                sums = jnp.sum(acc[k * n_col + r], axis=1)
                term = weight[k * half : k * half + half] * sums
                out[(my_core ^ k) * n_col + r] = jnp.sum(term, axis=0, keepdims=True)
            else:
                sums = jnp.sum(acc[(my_core ^ k) * n_col + r], axis=1)
                for chip in range(chips):
                    out[r * chips + chip, pl.ds(k * half, half), :] = sums


def depend_level(dims, first, last, places, ids, tiles, bands, came):
    n_row, n_col, slots, half = dims
    if last:
        out_shape = [piece(PAIR * n_col, 1, LANES)]
    else:
        out_shape = [piece(n_row // PAIR * n_col, PAIR * half, LANES)]
    if first:
        out_shape += [
            piece(n_col, 2, PAIR * half, LANES),
            piece(n_row // PAIR, 2, PAIR * half, LANES),
            piece(PAIR * slots * half, LANES, LANES),
            piece(2 * half, LANES),
            piece(2 * half, LANES),
        ]
    vectors = [ids, *(tiles if first else []), *bands, came]
    return pl.pallas_call(
        functools.partial(depend_kernel, dims, first, last),
        out_shape=out_shape,
        in_specs=[in_smem()] * len(places) + [in_vmem()] * len(vectors),
        out_specs=[in_vmem()] * len(out_shape),
        scratch_shapes=[pltpu.VMEM((PAIR * n_col, half, SUB, LANES), jnp.float32)]
        + slot_scratch(dims),
        compiler_params=params(terms_limit),
        name="depend_level",
    )(*places, *vectors)


def result_kernel(half, came, keep, other, shown, paths, centrality):
    my_x, my_core, my_col = position()
    for core in range(PAIR):
        block = jnp.where(my_core == core, keep[...], other[...])
        dist = block[:half]
        rows = pl.ds(core * half, half)
        shown[rows, :] = jnp.where(dist < 0.5 * far_value, dist, -1.0)
        paths[rows, :] = block[half:]
    shares = [came[at] for at in range(came.shape[0])]
    centrality[...] = functools.reduce(jnp.add, shares) / (PAIR * half)


def results(dims, came, keep, other):
    half = dims[3]
    return pl.pallas_call(
        functools.partial(result_kernel, half),
        out_shape=[piece(PAIR * half, LANES)] * 2 + [piece(1, LANES)],
        in_specs=[in_vmem()] * 3,
        out_specs=[in_vmem()] * 3,
        compiler_params=params(small_limit),
        name="results",
    )(came, keep, other)


def all_to_all(value, axes):
    return lax.all_to_all(value, axes, split_axis=0, concat_axis=0, tiled=True)


def swap_core(value):
    return lax.ppermute(value, "core", [(0, 1), (1, 0)])


def per_device(tiles, tile_index, tile_count, sources):
    slots = tiles.shape[0]
    rows = sources.shape[0]
    dims = (lax.axis_size("chip") * PAIR, lax.axis_size("col"), slots, rows // PAIR)
    own_places = tile_index.T
    line = ("col", "chip")

    everyone = ("chip", "core", "col")

    firsts, turned, ids = first_level(dims, own_places, sources, tiles)
    both = [turned, swap_core(turned)]
    places = [] if is_dense(dims) else [own_places, swap_core(own_places)]
    came = all_to_all(firsts, everyone)
    for level_no in range(1, LEVELS):
        whole = level_no == LEVELS - 1
        outs = relax_level(dims, level_no > 1, whole, places, ids, both, came)
        came = all_to_all(outs, line)
    sums, *bands, keep, give = depend_level(dims, True, False, places, ids, both, [], came)
    other = swap_core(give)
    for back_no in range(1, BACK):
        last = back_no == BACK - 1
        came = all_to_all(sums, line)
        (sums,) = depend_level(dims, False, last, places, ids, both, bands, came)
    shown, paths, centrality = results(dims, all_to_all(sums, ("core", "col")), keep, other)
    return shown, paths, centrality.reshape(LANES)


def solution(mesh):
    groups, rows, cols = mesh.devices.shape
    pairs = mesh.devices.reshape(groups, rows // PAIR, PAIR, cols)
    paired = jax.sharding.Mesh(pairs, ("groups", "chip", "core", "col"))
    vertices = ("chip", "core", "col")
    everywhere = ("groups",) + vertices
    in_specs = (P(everywhere, None, None), P(everywhere, None), P(everywhere), P("groups"))
    out_specs = (P("groups", vertices), P("groups", vertices), P(everywhere))
    return jax.shard_map(
        per_device, mesh=paired, in_specs=in_specs, out_specs=out_specs, check_vma=False
    )
```

```python
import functools

import jax
import jax.numpy as jnp
from jax import lax
from jax.experimental import pallas as pl
from jax.experimental.pallas import tpu as pltpu
from jax.sharding import PartitionSpec as P

LEVELS = 3
BACK = 2
LANES = 128
SUB = 8
PAIR = 2
SPAN = 64

far_value = 1000000.0
no_edge = 2000000.0
large_limit = 8 * 1024 * 1024
small_limit = 2 * 1024 * 1024
terms_limit = 20 * 1024 * 1024


def in_vmem():
    return pl.BlockSpec(memory_space=pltpu.VMEM)


def in_smem():
    return pl.BlockSpec(memory_space=pltpu.SMEM)


def in_hbm():
    return pl.BlockSpec(memory_space=pltpu.HBM)


def piece(*shape):
    return jax.ShapeDtypeStruct(shape, jnp.float32)


def params(limit):
    return pltpu.CompilerParams(vmem_limit_bytes=limit)


def is_dense(dims):
    return dims[2] == dims[0] * dims[1]


def position():
    return lax.axis_index("chip"), lax.axis_index("core"), lax.axis_index("col")


def source_ids(sources, first, half):
    row = lax.broadcasted_iota(jnp.int32, (PAIR * half, LANES), 0)
    ids = jnp.zeros((PAIR * half, LANES), jnp.int32)
    for s in range(half):
        ids = jnp.where(lax.rem(row, half) == s, sources[first + s], ids)
    return ids


def is_source(dims, ids, chip, col):
    n_row, n_col, slots, half = dims
    block = lax.broadcasted_iota(jnp.int32, ids.shape, 0) // half
    lane = lax.broadcasted_iota(jnp.int32, ids.shape, 1)
    return ids == ((PAIR * chip + block) * n_col + col) * LANES + lane


def own_first(rows, my_core):
    half = rows.shape[0] // PAIR
    return jnp.where(my_core == 0, rows, jnp.concatenate([rows[half:], rows[:half]], axis=0))


def settle(found_dist, found_count, at_source):
    dist = jnp.where(at_source, 0.0, jnp.minimum(found_dist, far_value))
    count = jnp.where(found_dist == dist, found_count, 0.0)
    return dist, jnp.where(at_source, 1.0, 0.0) + count


def merge(pairs):
    best = functools.reduce(jnp.minimum, [p[0] for p in pairs])
    total = functools.reduce(jnp.add, [jnp.where(p[0] == best, p[1], 0.0) for p in pairs])
    return best, total


def first_kernel(dims, *refs):
    n_row, n_col, slots, half = dims
    places_in, sources_in, tiles_in, out, turned, ids = refs[:6]
    places, sources, slot_of, tiles, sems = refs[6:]
    my_x, my_core, my_col = position()
    my_row = my_x * PAIR + my_core
    parts = sems.shape[0] - 2
    size = slots // parts
    given = [
        pltpu.make_async_copy(places_in, places, sems.at[parts]),
        pltpu.make_async_copy(sources_in, sources, sems.at[parts + 1]),
    ]
    fetch = []
    for part in range(parts):
        span = pl.ds(part * size, size)
        fetch.append(pltpu.make_async_copy(tiles_in.at[span], tiles.at[span], sems.at[part]))
    for copy in given + fetch:
        copy.start()

    def clear(at, _):
        slot_of[at] = -1
        return 0

    if not is_dense(dims):
        lax.fori_loop(0, n_row * n_col, clear, 0)
    for copy in given:
        copy.wait()
    for g in range(slots):
        slot_of[places[0, g] * n_row + places[1, g]] = g
    ids[...] = source_ids(sources, my_core * half, half)

    def turn(part):
        for g in range(part * size, part * size + size):
            at = places[0, g] * n_row + places[1, g] if is_dense(dims) else g
            raw = tiles[g]
            turned[at] = jnp.where(raw > 0, raw, no_edge).T

    for part in range(parts):
        fetch[part].wait()
        if part + 1 < parts:
            turn(part)
    row_at = lax.broadcasted_iota(jnp.int32, (PAIR * half, LANES), 0)
    lines = {}
    for c in range(n_row):
        for s in range(PAIR * half):
            vertex = sources[s]
            block, place = vertex // LANES, lax.rem(vertex, LANES)
            g = slot_of[lax.rem(block, n_col) * n_row + c]
            here = jnp.logical_and(block // n_col == my_row, g >= 0)
            row = tiles[jnp.maximum(g, 0), pl.ds(place, 1), :]
            to = jnp.where(here, c % PAIR * half + s % half, -1)
            line = lines.get((c // PAIR, s // half), jnp.zeros(row_at.shape, jnp.float32))
            lines[c // PAIR, s // half] = jnp.where(row_at == to, row, line)
    for (chip, core), line in lines.items():
        line = jnp.where(line > 0, line, far_value)
        for col in range(n_col):
            out[(chip * PAIR + core) * n_col + col] = line
    turn(parts - 1)


def first_level(dims, places, sources, tiles):
    n_row, n_col, slots, half = dims
    parts = 4 if slots % 4 == 0 else 1
    inputs = [pltpu.with_memory_space_constraint(x, pltpu.HBM) for x in (places, sources, tiles)]
    return pl.pallas_call(
        functools.partial(first_kernel, dims),
        out_shape=[
            piece(n_row * n_col, PAIR * half, LANES),
            piece(*tiles.shape),
            jax.ShapeDtypeStruct((PAIR * half, LANES), jnp.int32),
        ],
        in_specs=[in_hbm()] * 3,
        out_specs=[in_vmem()] * 3,
        scratch_shapes=[
            pltpu.SMEM(places.shape, jnp.int32),
            pltpu.SMEM(sources.shape, jnp.int32),
            pltpu.SMEM((n_row * n_col,), jnp.int32),
            pltpu.VMEM(tiles.shape, jnp.float32),
            pltpu.SemaphoreType.DMA((parts + 2,)),
        ],
        compiler_params=params(large_limit),
        name="first_level",
    )(*inputs)


def list_slots(dims, places, table, filled):
    n_row, n_col, slots, half = dims
    if is_dense(dims):
        return

    def clear(at, _):
        filled[at] = 0
        return 0

    lax.fori_loop(0, PAIR * n_row, clear, 0)
    for k in range(PAIR):

        def enter(g, _):
            at = k * n_row + places[k][1, g]
            table[at * n_col + filled[at]] = g
            filled[at] += 1
            return 0

        lax.fori_loop(0, slots, enter, 0)


def over_slots(dims, places, table, filled, c, step, carry):
    n_row, n_col, slots, half = dims
    for k in range(PAIR):
        if is_dense(dims):
            for r in range(n_col):
                carry = step(k, r * n_row + c, r, carry)
        else:
            at = k * n_row + c

            def entry(e, carry):
                g = table[at * n_col + e]
                return step(k, g, places[k][0, g], carry)

            carry = lax.fori_loop(0, filled[at], entry, carry)
    return carry


def slot_scratch(dims):
    n_row, n_col, slots, half = dims
    return [
        pltpu.SMEM((PAIR * n_row * n_col,), jnp.int32),
        pltpu.SMEM((PAIR * n_row,), jnp.int32),
    ]


def relax_kernel(dims, counted, whole, *refs):
    n_row, n_col, slots, half = dims
    chips = n_row // PAIR
    n_places = 0 if is_dense(dims) else PAIR
    places, refs = refs[:n_places], refs[n_places:]
    source_rows, tiles, refs = refs[0], refs[1 : 1 + PAIR], refs[1 + PAIR :]
    came, out, near, found, held, table, filled = refs
    my_x, my_core, my_col = position()
    ids = source_rows[...]
    list_slots(dims, places, table, filled)
    for r in range(n_col):
        if counted:
            blocks = [came[r * chips + chip, 0] for chip in range(chips)]
            reached, count = merge([(block[0], block[1]) for block in blocks])
        else:
            parts = [came[at * n_col + r] for at in range(n_row)]
            reached = functools.reduce(jnp.minimum, parts)
            count = jnp.where(reached < far_value, 1.0, 0.0)
        dist, count = settle(reached, count, is_source(dims, ids, my_x, r))
        near[r, 0] = own_first(dist, my_core)
        near[r, 1] = own_first(count, my_core)
    lane = lax.broadcasted_iota(jnp.int32, (SPAN, LANES), 1)

    def lowest(chip, at):
        h, s, q = items[at]

        def step(k, g, r, carry):
            weight = tiles[k][g, pl.ds(q, SPAN), :]
            reached = weight + near[r, 0, pl.ds(k * half + s, 1), :]
            held[at % 2, k * n_col + r] = reached
            return jnp.minimum(carry, reached)

        start = jnp.full((SPAN, LANES), far_value, jnp.float32)
        reached = over_slots(dims, places, table, filled, PAIR * chip + h, step, start)
        return jnp.min(reached, axis=1, keepdims=True)

    def tally(chip, at, best):
        h, s, q = items[at]

        def step(k, g, r, carry):
            hit = held[at % 2, k * n_col + r] == best
            return carry + jnp.where(hit, near[r, 1, pl.ds(k * half + s, 1), :], 0.0)

        start = jnp.zeros((SPAN, LANES), jnp.float32)
        counts = over_slots(dims, places, table, filled, PAIR * chip + h, step, start)
        return jnp.sum(counts, axis=1, keepdims=True)

    spans = range(0, LANES, SPAN)
    items = [(h, s, q) for h in range(PAIR) for q in spans for s in range(half)]

    def columns(chip, _):
        rows = PAIR * half
        turned = {q: jnp.zeros((SPAN, LANES), jnp.float32) for q in spans}
        best = lowest(chip, 0)
        for at, item in enumerate(items):
            later = lowest(chip, at + 1) if at + 1 < len(items) else None
            total = tally(chip, at, best)
            h, s, q = item
            to = h * half + s
            with_total = jnp.where(lane == rows + to, total, turned[q])
            turned[q] = jnp.where(lane == to, best, with_total)
            best = later
        both = jnp.concatenate([turned[q] for q in spans], axis=0).T
        found[chip, 0] = both[:rows]
        found[chip, 1] = both[rows : 2 * rows]
        return 0

    lax.fori_loop(0, chips, columns, 0)
    for chip in range(chips):
        for col in range(n_col):
            if whole:
                out[col * chips + chip] = found[...]
            else:
                out[col * chips + chip, 0] = found[chip]


def relax_level(dims, counted, whole, places, ids, tiles, came):
    n_row, n_col, slots, half = dims
    chips = n_row // PAIR
    return pl.pallas_call(
        functools.partial(relax_kernel, dims, counted, whole),
        out_shape=piece(chips * n_col, chips if whole else 1, 2, PAIR * half, LANES),
        in_specs=[in_smem()] * len(places) + [in_vmem()] * (PAIR + 2),
        out_specs=in_vmem(),
        scratch_shapes=[
            pltpu.VMEM((n_col, 2, PAIR * half, LANES), jnp.float32),
            pltpu.VMEM((chips, 2, PAIR * half, LANES), jnp.float32),
            pltpu.VMEM((2, PAIR * n_col, SPAN, LANES), jnp.float32),
        ]
        + slot_scratch(dims),
        compiler_params=params(large_limit),
        name="relax_level",
    )(*places, ids, *tiles, came)


def depend_kernel(dims, first, last, *refs):
    n_row, n_col, slots, half = dims
    chips = n_row // PAIR
    n_places = 0 if is_dense(dims) else PAIR
    places, refs = refs[:n_places], refs[n_places:]
    source_rows, refs = refs[0], refs[1:]
    if first:
        tiles, refs = refs[:PAIR], refs[PAIR:]
        came, out, near, low, terms, acc, table, filled = refs
    else:
        near, low, terms, came, out, state, acc, table, filled = refs
    my_x, my_core, my_col = position()
    ids = source_rows[...]
    list_slots(dims, places, table, filled)
    if first:
        for r in range(n_col):
            blocks = [came[r * chips + chip, my_x] for chip in range(chips)]
            found = merge([(block[0], block[1]) for block in blocks])
            dist, count = settle(*found, is_source(dims, ids, my_x, r))
            near[r, 0] = own_first(dist, my_core)
            near[r, 1] = own_first(count, my_core)
        for at in range(chips):
            blocks = [came[my_col * chips + chip, at] for chip in range(chips)]
            found = merge([(block[0], block[1]) for block in blocks])
            dist, count = settle(*found, is_source(dims, ids, at, my_col))
            low[at, 0] = dist
            low[at, 1] = count
    else:
        other = came[(PAIR * my_x + 1 - my_core) * n_col + my_col]
        mine = jnp.concatenate([near[my_col, 0, :half, :], near[my_col, 1, :half, :]], axis=0)
        for core in range(PAIR):
            block = jnp.where(my_core == core, mine, other)
            dist = block[:half]
            rows = pl.ds(core * half, half)
            state[0, rows, :] = jnp.where(dist < 0.5 * far_value, dist, -1.0)
            state[1, rows, :] = block[half:]
    acc[...] = jnp.zeros(acc.shape, jnp.float32)

    def add_terms(k, r, s, part):
        acc[k * n_col + r, s] += jnp.sum(part.reshape(-1, SUB, LANES), axis=0)

    def select(chip, _):
        rows = PAIR * half
        count = low[chip, 1]
        share = jnp.where(count > 0.5, 1.0 / jnp.maximum(count, 1.0), 0.0)
        turned = jnp.concatenate([low[chip, 0], share], axis=0).T
        for at, q in [(at, q) for at in range(rows) for q in range(0, LANES, SPAN)]:
            c, s = PAIR * chip + at // half, at % half
            span = slice(q, q + SPAN)
            dist = jnp.broadcast_to(turned[span, at : at + 1], (SPAN, LANES))
            coef = jnp.broadcast_to(turned[span, rows + at : rows + at + 1], (SPAN, LANES))

            def step(k, g, r, carry):
                row = near[r, 0, pl.ds(k * half + s, 1), :]
                hit = tiles[k][g, pl.ds(q, SPAN), :] + row == dist
                part = jnp.where(hit, coef, 0.0)
                terms[(k * slots + g) * half + s, pl.ds(q, SPAN), :] = part
                add_terms(k, r, s, part)
                return carry

            over_slots(dims, places, table, filled, c, step, 0)
        return 0

    def scale(chip):
        line = (PAIR * chip + my_core) * n_col
        total = functools.reduce(jnp.add, [came[line + col] for col in range(n_col)])
        turned = (1.0 + low[chip, 1] * total).T
        for at in range(PAIR * half):
            c, s = PAIR * chip + at // half, at % half
            factor = jnp.broadcast_to(turned[:, at : at + 1], (LANES, LANES))

            def step(k, g, r, carry):
                add_terms(k, r, s, terms[(k * slots + g) * half + s] * factor)
                return carry

            over_slots(dims, places, table, filled, c, step, 0)

    if first:
        lax.fori_loop(0, chips, select, 0)
    else:
        for chip in range(chips):
            scale(chip)
    for r in range(n_col):
        if last:
            counted = jnp.where(is_source(dims, ids, my_x, r), 0.0, 1.0)
            weight = own_first(counted, my_core) * near[r, 1]
        for k in range(PAIR):
            if last:
                sums = jnp.sum(acc[k * n_col + r], axis=1)
                term = weight[k * half : k * half + half] * sums
                out[(my_core ^ k) * n_col + r] = jnp.sum(term, axis=0, keepdims=True)
            else:
                sums = jnp.sum(acc[(my_core ^ k) * n_col + r], axis=1)
                for chip in range(chips):
                    line = (PAIR * chip + my_core) * n_col
                    out[line + r, pl.ds(k * half, half), :] = sums
    if not last:
        give = jnp.concatenate([near[my_col, 0, half:, :], near[my_col, 1, half:, :]], axis=0)
        for chip in range(chips):
            for r in range(n_col):
                out[(PAIR * chip + 1 - my_core) * n_col + r] = give


def depend_level(dims, first, last, places, ids, tiles, bands, came):
    n_row, n_col, slots, half = dims
    if last:
        out_shape = [piece(PAIR * n_col, 1, LANES)]
    else:
        out_shape = [piece(n_row * n_col, PAIR * half, LANES)]
    if first:
        out_shape += [
            piece(n_col, 2, PAIR * half, LANES),
            piece(n_row // PAIR, 2, PAIR * half, LANES),
            piece(PAIR * slots * half, LANES, LANES),
        ]
    else:
        out_shape += [piece(2, PAIR * half, LANES)]
    vectors = [ids, *(tiles if first else []), *bands, came]
    return pl.pallas_call(
        functools.partial(depend_kernel, dims, first, last),
        out_shape=out_shape,
        in_specs=[in_smem()] * len(places) + [in_vmem()] * len(vectors),
        out_specs=[in_vmem()] * len(out_shape),
        scratch_shapes=[pltpu.VMEM((PAIR * n_col, half, SUB, LANES), jnp.float32)]
        + slot_scratch(dims),
        compiler_params=params(terms_limit),
        name="depend_level",
    )(*places, *vectors)


def result_kernel(rows, came, state, shown, paths, centrality):
    shown[...] = state[0]
    paths[...] = state[1]
    shares = [came[at] for at in range(came.shape[0])]
    centrality[...] = functools.reduce(jnp.add, shares) / rows


def results(dims, came, state):
    rows = PAIR * dims[3]
    return pl.pallas_call(
        functools.partial(result_kernel, rows),
        out_shape=[piece(rows, LANES)] * 2 + [piece(1, LANES)],
        in_specs=[in_vmem()] * 2,
        out_specs=[in_vmem()] * 3,
        compiler_params=params(small_limit),
        name="results",
    )(came, state)


def all_to_all(value, axes):
    return lax.all_to_all(value, axes, split_axis=0, concat_axis=0, tiled=True)


def swap_core(value):
    return lax.ppermute(value, "core", [(0, 1), (1, 0)])


def per_device(tiles, tile_index, tile_count, sources):
    slots = tiles.shape[0]
    rows = sources.shape[0]
    dims = (lax.axis_size("chip") * PAIR, lax.axis_size("col"), slots, rows // PAIR)
    own_places = tile_index.T
    line = ("col", "chip")

    everyone = ("chip", "core", "col")

    firsts, turned, ids = first_level(dims, own_places, sources, tiles)
    both = [turned, swap_core(turned)]
    places = [] if is_dense(dims) else [own_places, swap_core(own_places)]
    came = all_to_all(firsts, everyone)
    for level_no in range(1, LEVELS):
        whole = level_no == LEVELS - 1
        outs = relax_level(dims, level_no > 1, whole, places, ids, both, came)
        came = all_to_all(outs, line)
    sums, *bands = depend_level(dims, True, False, places, ids, both, [], came)
    for back_no in range(1, BACK):
        last = back_no == BACK - 1
        came = all_to_all(sums, everyone)
        sums, state = depend_level(dims, False, last, places, ids, both, bands, came)
    shown, paths, centrality = results(dims, all_to_all(sums, ("core", "col")), state)
    return shown, paths, centrality.reshape(LANES)


def solution(mesh):
    groups, rows, cols = mesh.devices.shape
    pairs = mesh.devices.reshape(groups, rows // PAIR, PAIR, cols)
    paired = jax.sharding.Mesh(pairs, ("groups", "chip", "core", "col"))
    vertices = ("chip", "core", "col")
    everywhere = ("groups",) + vertices
    in_specs = (P(everywhere, None, None), P(everywhere, None), P(everywhere), P("groups"))
    out_specs = (P("groups", vertices), P("groups", vertices), P(everywhere))
    return jax.shard_map(
        per_device, mesh=paired, in_specs=in_specs, out_specs=out_specs, check_vma=False
    )
```

```python
import functools

import jax
import jax.numpy as jnp
from jax import lax
from jax.experimental import pallas as pl
from jax.experimental.pallas import tpu as pltpu
from jax.sharding import PartitionSpec as P

LEVELS = 3
BACK = 2
LANES = 128
SUB = 8
PAIR = 2
SPAN = 32

far_value = 1000000.0
no_edge = 2000000.0
large_limit = 8 * 1024 * 1024
small_limit = 2 * 1024 * 1024
terms_limit = 20 * 1024 * 1024


def in_vmem():
    return pl.BlockSpec(memory_space=pltpu.VMEM)


def in_smem():
    return pl.BlockSpec(memory_space=pltpu.SMEM)


def in_hbm():
    return pl.BlockSpec(memory_space=pltpu.HBM)


def piece(*shape):
    return jax.ShapeDtypeStruct(shape, jnp.float32)


def params(limit):
    return pltpu.CompilerParams(vmem_limit_bytes=limit)


def is_dense(dims):
    return dims[2] == dims[0] * dims[1]


def position():
    return lax.axis_index("chip"), lax.axis_index("core"), lax.axis_index("col")


def source_ids(sources, first, half):
    row = lax.broadcasted_iota(jnp.int32, (PAIR * half, LANES), 0)
    ids = jnp.zeros((PAIR * half, LANES), jnp.int32)
    for s in range(half):
        ids = jnp.where(lax.rem(row, half) == s, sources[first + s], ids)
    return ids


def is_source(dims, ids, chip, col):
    n_row, n_col, slots, half = dims
    block = lax.broadcasted_iota(jnp.int32, ids.shape, 0) // half
    lane = lax.broadcasted_iota(jnp.int32, ids.shape, 1)
    return ids == ((PAIR * chip + block) * n_col + col) * LANES + lane


def own_first(rows, my_core):
    half = rows.shape[0] // PAIR
    return jnp.where(my_core == 0, rows, jnp.concatenate([rows[half:], rows[:half]], axis=0))


def settle(found_dist, found_count, at_source):
    dist = jnp.where(at_source, 0.0, jnp.minimum(found_dist, far_value))
    count = jnp.where(found_dist == dist, found_count, 0.0)
    return dist, jnp.where(at_source, 1.0, 0.0) + count


def merge(pairs):
    best = functools.reduce(jnp.minimum, [p[0] for p in pairs])
    total = functools.reduce(jnp.add, [jnp.where(p[0] == best, p[1], 0.0) for p in pairs])
    return best, total


def first_kernel(dims, *refs):
    n_row, n_col, slots, half = dims
    places_in, sources_in, tiles_in, out, turned, ids = refs[:6]
    places, sources, slot_of, tiles, sems = refs[6:]
    my_x, my_core, my_col = position()
    my_row = my_x * PAIR + my_core
    parts = sems.shape[0] - 2
    size = slots // parts
    given = [
        pltpu.make_async_copy(places_in, places, sems.at[parts]),
        pltpu.make_async_copy(sources_in, sources, sems.at[parts + 1]),
    ]
    fetch = []
    for part in range(parts):
        span = pl.ds(part * size, size)
        fetch.append(pltpu.make_async_copy(tiles_in.at[span], tiles.at[span], sems.at[part]))
    for copy in given + fetch:
        copy.start()

    def clear(at, _):
        slot_of[at] = -1
        return 0

    if not is_dense(dims):
        lax.fori_loop(0, n_row * n_col, clear, 0)
    for copy in given:
        copy.wait()
    for g in range(slots):
        slot_of[places[0, g] * n_row + places[1, g]] = g
    ids[...] = source_ids(sources, my_core * half, half)

    def turn(part):
        for g in range(part * size, part * size + size):
            at = places[0, g] * n_row + places[1, g] if is_dense(dims) else g
            raw = tiles[g]
            turned[at] = jnp.where(raw > 0, raw, no_edge).T

    for part in range(parts):
        fetch[part].wait()
        if part + 1 < parts:
            turn(part)
    row_at = lax.broadcasted_iota(jnp.int32, (PAIR * half, LANES), 0)
    lines = {}
    for c in range(n_row):
        for s in range(PAIR * half):
            vertex = sources[s]
            block, place = vertex // LANES, lax.rem(vertex, LANES)
            g = slot_of[lax.rem(block, n_col) * n_row + c]
            here = jnp.logical_and(block // n_col == my_row, g >= 0)
            row = tiles[jnp.maximum(g, 0), pl.ds(place, 1), :]
            to = jnp.where(here, c % PAIR * half + s % half, -1)
            line = lines.get((c // PAIR, s // half), jnp.zeros(row_at.shape, jnp.float32))
            lines[c // PAIR, s // half] = jnp.where(row_at == to, row, line)
    for (chip, core), line in lines.items():
        line = jnp.where(line > 0, line, far_value)
        for col in range(n_col):
            out[(chip * PAIR + core) * n_col + col] = line
    turn(parts - 1)


def first_level(dims, places, sources, tiles):
    n_row, n_col, slots, half = dims
    parts = 4 if slots % 4 == 0 else 1
    inputs = [pltpu.with_memory_space_constraint(x, pltpu.HBM) for x in (places, sources, tiles)]
    return pl.pallas_call(
        functools.partial(first_kernel, dims),
        out_shape=[
            piece(n_row * n_col, PAIR * half, LANES),
            piece(*tiles.shape),
            jax.ShapeDtypeStruct((PAIR * half, LANES), jnp.int32),
        ],
        in_specs=[in_hbm()] * 3,
        out_specs=[in_vmem()] * 3,
        scratch_shapes=[
            pltpu.SMEM(places.shape, jnp.int32),
            pltpu.SMEM(sources.shape, jnp.int32),
            pltpu.SMEM((n_row * n_col,), jnp.int32),
            pltpu.VMEM(tiles.shape, jnp.float32),
            pltpu.SemaphoreType.DMA((parts + 2,)),
        ],
        compiler_params=params(large_limit),
        name="first_level",
    )(*inputs)


def list_slots(dims, places, table, filled):
    n_row, n_col, slots, half = dims
    if is_dense(dims):
        return

    def clear(at, _):
        filled[at] = 0
        return 0

    lax.fori_loop(0, PAIR * n_row, clear, 0)
    for k in range(PAIR):

        def enter(g, _):
            at = k * n_row + places[k][1, g]
            table[at * n_col + filled[at]] = g
            filled[at] += 1
            return 0

        lax.fori_loop(0, slots, enter, 0)


def over_slots(dims, places, table, filled, c, step, carry):
    n_row, n_col, slots, half = dims
    for k in range(PAIR):
        if is_dense(dims):
            for r in range(n_col):
                carry = step(k, r * n_row + c, r, carry)
        else:
            at = k * n_row + c

            def entry(e, carry):
                g = table[at * n_col + e]
                return step(k, g, places[k][0, g], carry)

            carry = lax.fori_loop(0, filled[at], entry, carry)
    return carry


def slot_scratch(dims):
    n_row, n_col, slots, half = dims
    return [
        pltpu.SMEM((PAIR * n_row * n_col,), jnp.int32),
        pltpu.SMEM((PAIR * n_row,), jnp.int32),
    ]


def relax_kernel(dims, counted, whole, *refs):
    n_row, n_col, slots, half = dims
    chips = n_row // PAIR
    n_places = 0 if is_dense(dims) else PAIR
    places, refs = refs[:n_places], refs[n_places:]
    source_rows, tiles, refs = refs[0], refs[1 : 1 + PAIR], refs[1 + PAIR :]
    came, out, near, found, table, filled = refs
    my_x, my_core, my_col = position()
    ids = source_rows[...]
    list_slots(dims, places, table, filled)
    for r in range(n_col):
        if counted:
            blocks = [came[r * chips + chip, 0] for chip in range(chips)]
            reached, count = merge([(block[0], block[1]) for block in blocks])
        else:
            parts = [came[at * n_col + r] for at in range(n_row)]
            reached = functools.reduce(jnp.minimum, parts)
            count = jnp.where(reached < far_value, 1.0, 0.0)
        dist, count = settle(reached, count, is_source(dims, ids, my_x, r))
        near[r, 0] = own_first(dist, my_core)
        near[r, 1] = own_first(count, my_core)
    lane = lax.broadcasted_iota(jnp.int32, (SPAN, LANES), 1)

    spans = range(0, LANES, SPAN)
    items = [(h, q) for h in range(PAIR) for q in spans]

    def lowest(chip, at):
        h, q = items[at]

        def step(k, g, r, carry):
            weight = tiles[k][g, pl.ds(q, SPAN), :]
            rows = [near[r, 0, pl.ds(k * half + s, 1), :] for s in range(half)]
            return tuple(jnp.minimum(low, weight + row) for low, row in zip(carry, rows))

        start = (jnp.full((SPAN, LANES), far_value, jnp.float32),) * half
        reached = over_slots(dims, places, table, filled, PAIR * chip + h, step, start)
        return [jnp.min(low, axis=1, keepdims=True) for low in reached]

    def tally(chip, at, best):
        h, q = items[at]

        def step(k, g, r, carry):
            weight = tiles[k][g, pl.ds(q, SPAN), :]
            counts = []
            for s in range(half):
                row = pl.ds(k * half + s, 1)
                hit = weight + near[r, 0, row, :] == best[s]
                counts.append(carry[s] + jnp.where(hit, near[r, 1, row, :], 0.0))
            return tuple(counts)

        start = (jnp.zeros((SPAN, LANES), jnp.float32),) * half
        counts = over_slots(dims, places, table, filled, PAIR * chip + h, step, start)
        return [jnp.sum(count, axis=1, keepdims=True) for count in counts]

    def columns(chip, _):
        rows = PAIR * half
        turned = {q: jnp.zeros((SPAN, LANES), jnp.float32) for q in spans}
        best = lowest(chip, 0)
        for at, (h, q) in enumerate(items):
            later = lowest(chip, at + 1) if at + 1 < len(items) else None
            totals = tally(chip, at, best)
            for s in range(half):
                to = h * half + s
                with_total = jnp.where(lane == rows + to, totals[s], turned[q])
                turned[q] = jnp.where(lane == to, best[s], with_total)
            best = later
        both = jnp.concatenate([turned[q] for q in spans], axis=0).T
        found[chip, 0] = both[:rows]
        found[chip, 1] = both[rows : 2 * rows]
        return 0

    lax.fori_loop(0, chips, columns, 0)
    for chip in range(chips):
        for col in range(n_col):
            if whole:
                out[col * chips + chip] = found[...]
            else:
                out[col * chips + chip, 0] = found[chip]


def relax_level(dims, counted, whole, places, ids, tiles, came):
    n_row, n_col, slots, half = dims
    chips = n_row // PAIR
    return pl.pallas_call(
        functools.partial(relax_kernel, dims, counted, whole),
        out_shape=piece(chips * n_col, chips if whole else 1, 2, PAIR * half, LANES),
        in_specs=[in_smem()] * len(places) + [in_vmem()] * (PAIR + 2),
        out_specs=in_vmem(),
        scratch_shapes=[
            pltpu.VMEM((n_col, 2, PAIR * half, LANES), jnp.float32),
            pltpu.VMEM((chips, 2, PAIR * half, LANES), jnp.float32),
        ]
        + slot_scratch(dims),
        compiler_params=params(large_limit),
        name="relax_level",
    )(*places, ids, *tiles, came)


def depend_kernel(dims, first, last, *refs):
    n_row, n_col, slots, half = dims
    chips = n_row // PAIR
    n_places = 0 if is_dense(dims) else PAIR
    places, refs = refs[:n_places], refs[n_places:]
    source_rows, refs = refs[0], refs[1:]
    if first:
        tiles, refs = refs[:PAIR], refs[PAIR:]
        came, out, near, low, terms, acc, table, filled = refs
    else:
        near, low, terms, came, out, state, acc, table, filled = refs
    my_x, my_core, my_col = position()
    ids = source_rows[...]
    list_slots(dims, places, table, filled)
    if first:
        for r in range(n_col):
            blocks = [came[r * chips + chip, my_x] for chip in range(chips)]
            found = merge([(block[0], block[1]) for block in blocks])
            dist, count = settle(*found, is_source(dims, ids, my_x, r))
            near[r, 0] = own_first(dist, my_core)
            near[r, 1] = own_first(count, my_core)
        for at in range(chips):
            blocks = [came[my_col * chips + chip, at] for chip in range(chips)]
            found = merge([(block[0], block[1]) for block in blocks])
            dist, count = settle(*found, is_source(dims, ids, at, my_col))
            low[at, 0] = dist
            low[at, 1] = count
    else:
        other = came[(PAIR * my_x + 1 - my_core) * n_col + my_col]
        mine = jnp.concatenate([near[my_col, 0, :half, :], near[my_col, 1, :half, :]], axis=0)
        for core in range(PAIR):
            block = jnp.where(my_core == core, mine, other)
            dist = block[:half]
            rows = pl.ds(core * half, half)
            state[0, rows, :] = jnp.where(dist < 0.5 * far_value, dist, -1.0)
            state[1, rows, :] = block[half:]
    acc[...] = jnp.zeros(acc.shape, jnp.float32)

    def add_terms(k, r, s, part):
        acc[k * n_col + r, s] += jnp.sum(part.reshape(-1, SUB, LANES), axis=0)

    def select(chip, _):
        rows = PAIR * half
        count = low[chip, 1]
        share = jnp.where(count > 0.5, 1.0 / jnp.maximum(count, 1.0), 0.0)
        turned = jnp.concatenate([low[chip, 0], share], axis=0).T
        for h, q in [(h, q) for h in range(PAIR) for q in range(0, LANES, SPAN)]:
            span = slice(q, q + SPAN)
            wide = [
                jnp.broadcast_to(turned[span, at : at + 1], (SPAN, LANES))
                for first_row in (h * half, rows + h * half)
                for at in range(first_row, first_row + half)
            ]

            def step(k, g, r, carry):
                weight = tiles[k][g, pl.ds(q, SPAN), :]
                for s in range(half):
                    hit = weight + near[r, 0, pl.ds(k * half + s, 1), :] == wide[s]
                    part = jnp.where(hit, wide[half + s], 0.0)
                    terms[(k * slots + g) * half + s, pl.ds(q, SPAN), :] = part
                    add_terms(k, r, s, part)
                return carry

            over_slots(dims, places, table, filled, PAIR * chip + h, step, 0)
        return 0

    def scale(chip):
        line = (PAIR * chip + my_core) * n_col
        total = functools.reduce(jnp.add, [came[line + col] for col in range(n_col)])
        turned = (1.0 + low[chip, 1] * total).T
        for at in range(PAIR * half):
            c, s = PAIR * chip + at // half, at % half
            factor = jnp.broadcast_to(turned[:, at : at + 1], (LANES, LANES))

            def step(k, g, r, carry):
                add_terms(k, r, s, terms[(k * slots + g) * half + s] * factor)
                return carry

            over_slots(dims, places, table, filled, c, step, 0)

    if first:
        lax.fori_loop(0, chips, select, 0)
    else:
        for chip in range(chips):
            scale(chip)
    for r in range(n_col):
        if last:
            counted = jnp.where(is_source(dims, ids, my_x, r), 0.0, 1.0)
            weight = own_first(counted, my_core) * near[r, 1]
        for k in range(PAIR):
            if last:
                sums = jnp.sum(acc[k * n_col + r], axis=1)
                term = weight[k * half : k * half + half] * sums
                out[(my_core ^ k) * n_col + r] = jnp.sum(term, axis=0, keepdims=True)
            else:
                sums = jnp.sum(acc[(my_core ^ k) * n_col + r], axis=1)
                for chip in range(chips):
                    line = (PAIR * chip + my_core) * n_col
                    out[line + r, pl.ds(k * half, half), :] = sums
    if not last:
        give = jnp.concatenate([near[my_col, 0, half:, :], near[my_col, 1, half:, :]], axis=0)
        for chip in range(chips):
            for r in range(n_col):
                out[(PAIR * chip + 1 - my_core) * n_col + r] = give


def depend_level(dims, first, last, places, ids, tiles, bands, came):
    n_row, n_col, slots, half = dims
    if last:
        out_shape = [piece(PAIR * n_col, 1, LANES)]
    else:
        out_shape = [piece(n_row * n_col, PAIR * half, LANES)]
    if first:
        out_shape += [
            piece(n_col, 2, PAIR * half, LANES),
            piece(n_row // PAIR, 2, PAIR * half, LANES),
            piece(PAIR * slots * half, LANES, LANES),
        ]
    else:
        out_shape += [piece(2, PAIR * half, LANES)]
    vectors = [ids, *(tiles if first else []), *bands, came]
    return pl.pallas_call(
        functools.partial(depend_kernel, dims, first, last),
        out_shape=out_shape,
        in_specs=[in_smem()] * len(places) + [in_vmem()] * len(vectors),
        out_specs=[in_vmem()] * len(out_shape),
        scratch_shapes=[pltpu.VMEM((PAIR * n_col, half, SUB, LANES), jnp.float32)]
        + slot_scratch(dims),
        compiler_params=params(terms_limit),
        name="depend_level",
    )(*places, *vectors)


def result_kernel(rows, came, state, shown, paths, centrality):
    shown[...] = state[0]
    paths[...] = state[1]
    shares = [came[at] for at in range(came.shape[0])]
    centrality[...] = functools.reduce(jnp.add, shares) / rows


def results(dims, came, state):
    rows = PAIR * dims[3]
    return pl.pallas_call(
        functools.partial(result_kernel, rows),
        out_shape=[piece(rows, LANES)] * 2 + [piece(1, LANES)],
        in_specs=[in_vmem()] * 2,
        out_specs=[in_vmem()] * 3,
        compiler_params=params(small_limit),
        name="results",
    )(came, state)


def all_to_all(value, axes):
    return lax.all_to_all(value, axes, split_axis=0, concat_axis=0, tiled=True)


def swap_core(value):
    return lax.ppermute(value, "core", [(0, 1), (1, 0)])


def per_device(tiles, tile_index, tile_count, sources):
    slots = tiles.shape[0]
    rows = sources.shape[0]
    dims = (lax.axis_size("chip") * PAIR, lax.axis_size("col"), slots, rows // PAIR)
    own_places = tile_index.T
    line = ("col", "chip")

    everyone = ("chip", "core", "col")

    firsts, turned, ids = first_level(dims, own_places, sources, tiles)
    both = [turned, swap_core(turned)]
    places = [] if is_dense(dims) else [own_places, swap_core(own_places)]
    came = all_to_all(firsts, everyone)
    for level_no in range(1, LEVELS):
        whole = level_no == LEVELS - 1
        outs = relax_level(dims, level_no > 1, whole, places, ids, both, came)
        came = all_to_all(outs, line)
    sums, *bands = depend_level(dims, True, False, places, ids, both, [], came)
    for back_no in range(1, BACK):
        last = back_no == BACK - 1
        came = all_to_all(sums, everyone)
        sums, state = depend_level(dims, False, last, places, ids, both, bands, came)
    shown, paths, centrality = results(dims, all_to_all(sums, ("core", "col")), state)
    return shown, paths, centrality.reshape(LANES)


def solution(mesh):
    groups, rows, cols = mesh.devices.shape
    pairs = mesh.devices.reshape(groups, rows // PAIR, PAIR, cols)
    paired = jax.sharding.Mesh(pairs, ("groups", "chip", "core", "col"))
    vertices = ("chip", "core", "col")
    everywhere = ("groups",) + vertices
    in_specs = (P(everywhere, None, None), P(everywhere, None), P(everywhere), P("groups"))
    out_specs = (P("groups", vertices), P("groups", vertices), P(everywhere))
    return jax.shard_map(
        per_device, mesh=paired, in_specs=in_specs, out_specs=out_specs, check_vma=False
    )
```

```python
import functools

import jax
import jax.numpy as jnp
from jax import lax
from jax.experimental import pallas as pl
from jax.experimental.pallas import tpu as pltpu
from jax.sharding import PartitionSpec as P

LEVELS = 3
BACK = 2
LANES = 128
SUB = 8
PAIR = 2
SPAN = 16

far_value = 1000000.0
no_edge = 2000000.0
large_limit = 8 * 1024 * 1024
small_limit = 2 * 1024 * 1024
terms_limit = 20 * 1024 * 1024


def in_vmem():
    return pl.BlockSpec(memory_space=pltpu.VMEM)


def in_smem():
    return pl.BlockSpec(memory_space=pltpu.SMEM)


def in_hbm():
    return pl.BlockSpec(memory_space=pltpu.HBM)


def piece(*shape):
    return jax.ShapeDtypeStruct(shape, jnp.float32)


def params(limit):
    return pltpu.CompilerParams(vmem_limit_bytes=limit)


def is_dense(dims):
    return dims[2] == dims[0] * dims[1]


def position():
    return lax.axis_index("chip"), lax.axis_index("core"), lax.axis_index("col")


def source_ids(sources, first, half):
    row = lax.broadcasted_iota(jnp.int32, (PAIR * half, LANES), 0)
    ids = jnp.zeros((PAIR * half, LANES), jnp.int32)
    for s in range(half):
        ids = jnp.where(lax.rem(row, half) == s, sources[first + s], ids)
    return ids


def is_source(dims, ids, chip, col):
    n_row, n_col, slots, half = dims
    block = lax.broadcasted_iota(jnp.int32, ids.shape, 0) // half
    lane = lax.broadcasted_iota(jnp.int32, ids.shape, 1)
    return ids == ((PAIR * chip + block) * n_col + col) * LANES + lane


def own_first(rows, my_core):
    half = rows.shape[0] // PAIR
    return jnp.where(my_core == 0, rows, jnp.concatenate([rows[half:], rows[:half]], axis=0))


def settle(found_dist, found_count, at_source):
    dist = jnp.where(at_source, 0.0, jnp.minimum(found_dist, far_value))
    count = jnp.where(found_dist == dist, found_count, 0.0)
    return dist, jnp.where(at_source, 1.0, 0.0) + count


def merge(pairs):
    best = functools.reduce(jnp.minimum, [p[0] for p in pairs])
    total = functools.reduce(jnp.add, [jnp.where(p[0] == best, p[1], 0.0) for p in pairs])
    return best, total


def first_kernel(dims, *refs):
    n_row, n_col, slots, half = dims
    places_in, sources_in, tiles_in, out, turned, ids = refs[:6]
    places, sources, slot_of, tiles, sems = refs[6:]
    my_x, my_core, my_col = position()
    my_row = my_x * PAIR + my_core
    parts = sems.shape[0] - 2
    size = slots // parts
    given = [
        pltpu.make_async_copy(places_in, places, sems.at[parts]),
        pltpu.make_async_copy(sources_in, sources, sems.at[parts + 1]),
    ]
    fetch = []
    for part in range(parts):
        span = pl.ds(part * size, size)
        fetch.append(pltpu.make_async_copy(tiles_in.at[span], tiles.at[span], sems.at[part]))
    for copy in given + fetch:
        copy.start()

    def clear(at, _):
        slot_of[at] = -1
        return 0

    if not is_dense(dims):
        lax.fori_loop(0, n_row * n_col, clear, 0)
    for copy in given:
        copy.wait()
    for g in range(slots):
        slot_of[places[0, g] * n_row + places[1, g]] = g
    ids[...] = source_ids(sources, my_core * half, half)

    def turn(part):
        for g in range(part * size, part * size + size):
            at = places[0, g] * n_row + places[1, g] if is_dense(dims) else g
            raw = tiles[g]
            turned[at] = jnp.where(raw > 0, raw, no_edge).T

    for part in range(parts):
        fetch[part].wait()
        if part + 1 < parts:
            turn(part)
    row_at = lax.broadcasted_iota(jnp.int32, (PAIR * half, LANES), 0)
    lines = {}
    for c in range(n_row):
        for s in range(PAIR * half):
            vertex = sources[s]
            block, place = vertex // LANES, lax.rem(vertex, LANES)
            g = slot_of[lax.rem(block, n_col) * n_row + c]
            here = jnp.logical_and(block // n_col == my_row, g >= 0)
            row = tiles[jnp.maximum(g, 0), pl.ds(place, 1), :]
            to = jnp.where(here, c % PAIR * half + s % half, -1)
            line = lines.get((c // PAIR, s // half), jnp.zeros(row_at.shape, jnp.float32))
            lines[c // PAIR, s // half] = jnp.where(row_at == to, row, line)
    for (chip, core), line in lines.items():
        line = jnp.where(line > 0, line, far_value)
        for col in range(n_col):
            out[(chip * PAIR + core) * n_col + col] = line
    turn(parts - 1)


def first_level(dims, places, sources, tiles):
    n_row, n_col, slots, half = dims
    parts = 4 if slots % 4 == 0 else 1
    inputs = [pltpu.with_memory_space_constraint(x, pltpu.HBM) for x in (places, sources, tiles)]
    return pl.pallas_call(
        functools.partial(first_kernel, dims),
        out_shape=[
            piece(n_row * n_col, PAIR * half, LANES),
            piece(*tiles.shape),
            jax.ShapeDtypeStruct((PAIR * half, LANES), jnp.int32),
        ],
        in_specs=[in_hbm()] * 3,
        out_specs=[in_vmem()] * 3,
        scratch_shapes=[
            pltpu.SMEM(places.shape, jnp.int32),
            pltpu.SMEM(sources.shape, jnp.int32),
            pltpu.SMEM((n_row * n_col,), jnp.int32),
            pltpu.VMEM(tiles.shape, jnp.float32),
            pltpu.SemaphoreType.DMA((parts + 2,)),
        ],
        compiler_params=params(large_limit),
        name="first_level",
    )(*inputs)


def list_slots(dims, places, table, filled):
    n_row, n_col, slots, half = dims
    if is_dense(dims):
        return

    def clear(at, _):
        filled[at] = 0
        return 0

    lax.fori_loop(0, PAIR * n_row, clear, 0)
    for k in range(PAIR):

        def enter(g, _):
            at = k * n_row + places[k][1, g]
            table[at * n_col + filled[at]] = g
            filled[at] += 1
            return 0

        lax.fori_loop(0, slots, enter, 0)


def over_slots(dims, places, table, filled, c, step, carry):
    n_row, n_col, slots, half = dims
    for k in range(PAIR):
        if is_dense(dims):
            for r in range(n_col):
                carry = step(k, r * n_row + c, r, carry)
        else:
            at = k * n_row + c

            def entry(e, carry):
                g = table[at * n_col + e]
                return step(k, g, places[k][0, g], carry)

            carry = lax.fori_loop(0, filled[at], entry, carry)
    return carry


def slot_scratch(dims):
    n_row, n_col, slots, half = dims
    return [
        pltpu.SMEM((PAIR * n_row * n_col,), jnp.int32),
        pltpu.SMEM((PAIR * n_row,), jnp.int32),
    ]


def relax_kernel(dims, counted, whole, *refs):
    n_row, n_col, slots, half = dims
    chips = n_row // PAIR
    n_places = 0 if is_dense(dims) else PAIR
    places, refs = refs[:n_places], refs[n_places:]
    source_rows, tiles, refs = refs[0], refs[1 : 1 + PAIR], refs[1 + PAIR :]
    came, out, near, found, table, filled = refs
    my_x, my_core, my_col = position()
    ids = source_rows[...]
    list_slots(dims, places, table, filled)
    for r in range(n_col):
        if counted:
            blocks = [came[r * chips + chip, 0] for chip in range(chips)]
            reached, count = merge([(block[0], block[1]) for block in blocks])
        else:
            parts = [came[at * n_col + r] for at in range(n_row)]
            reached = functools.reduce(jnp.minimum, parts)
            count = jnp.where(reached < far_value, 1.0, 0.0)
        dist, count = settle(reached, count, is_source(dims, ids, my_x, r))
        near[r, 0] = own_first(dist, my_core)
        near[r, 1] = own_first(count, my_core)
    lane = lax.broadcasted_iota(jnp.int32, (SPAN, LANES), 1)

    spans = range(0, LANES, SPAN)
    items = [(h, q) for h in range(PAIR) for q in spans]

    def lowest(chip, at):
        h, q = items[at]

        def step(k, g, r, carry):
            weight = tiles[k][g, pl.ds(q, SPAN), :]
            rows = [near[r, 0, pl.ds(k * half + s, 1), :] for s in range(half)]
            return tuple(jnp.minimum(low, weight + row) for low, row in zip(carry, rows))

        start = (jnp.full((SPAN, LANES), far_value, jnp.float32),) * half
        reached = over_slots(dims, places, table, filled, PAIR * chip + h, step, start)
        return [jnp.min(low, axis=1, keepdims=True) for low in reached]

    def tally(chip, at, best):
        h, q = items[at]

        def step(k, g, r, carry):
            weight = tiles[k][g, pl.ds(q, SPAN), :]
            counts = []
            for s in range(half):
                row = pl.ds(k * half + s, 1)
                hit = weight + near[r, 0, row, :] == best[s]
                counts.append(carry[s] + jnp.where(hit, near[r, 1, row, :], 0.0))
            return tuple(counts)

        start = (jnp.zeros((SPAN, LANES), jnp.float32),) * half
        counts = over_slots(dims, places, table, filled, PAIR * chip + h, step, start)
        return [jnp.sum(count, axis=1, keepdims=True) for count in counts]

    def columns(chip, _):
        rows = PAIR * half
        turned = {q: jnp.zeros((SPAN, LANES), jnp.float32) for q in spans}
        best = lowest(chip, 0)
        for at, (h, q) in enumerate(items):
            later = lowest(chip, at + 1) if at + 1 < len(items) else None
            totals = tally(chip, at, best)
            for s in range(half):
                to = h * half + s
                with_total = jnp.where(lane == rows + to, totals[s], turned[q])
                turned[q] = jnp.where(lane == to, best[s], with_total)
            best = later
        both = jnp.concatenate([turned[q] for q in spans], axis=0).T
        found[chip, 0] = both[:rows]
        found[chip, 1] = both[rows : 2 * rows]
        return 0

    lax.fori_loop(0, chips, columns, 0)
    for chip in range(chips):
        for col in range(n_col):
            if whole:
                out[col * chips + chip] = found[...]
            else:
                out[col * chips + chip, 0] = found[chip]


def relax_level(dims, counted, whole, places, ids, tiles, came):
    n_row, n_col, slots, half = dims
    chips = n_row // PAIR
    return pl.pallas_call(
        functools.partial(relax_kernel, dims, counted, whole),
        out_shape=piece(chips * n_col, chips if whole else 1, 2, PAIR * half, LANES),
        in_specs=[in_smem()] * len(places) + [in_vmem()] * (PAIR + 2),
        out_specs=in_vmem(),
        scratch_shapes=[
            pltpu.VMEM((n_col, 2, PAIR * half, LANES), jnp.float32),
            pltpu.VMEM((chips, 2, PAIR * half, LANES), jnp.float32),
        ]
        + slot_scratch(dims),
        compiler_params=params(large_limit),
        name="relax_level",
    )(*places, ids, *tiles, came)


def depend_kernel(dims, first, last, *refs):
    n_row, n_col, slots, half = dims
    chips = n_row // PAIR
    n_places = 0 if is_dense(dims) else PAIR
    places, refs = refs[:n_places], refs[n_places:]
    source_rows, refs = refs[0], refs[1:]
    if first:
        tiles, refs = refs[:PAIR], refs[PAIR:]
        came, out, near, low, terms, acc, table, filled = refs
    else:
        near, low, terms, came, out, state, acc, table, filled = refs
    my_x, my_core, my_col = position()
    ids = source_rows[...]
    list_slots(dims, places, table, filled)
    if first:
        for r in range(n_col):
            blocks = [came[r * chips + chip, my_x] for chip in range(chips)]
            found = merge([(block[0], block[1]) for block in blocks])
            dist, count = settle(*found, is_source(dims, ids, my_x, r))
            near[r, 0] = own_first(dist, my_core)
            near[r, 1] = own_first(count, my_core)
        for at in range(chips):
            blocks = [came[my_col * chips + chip, at] for chip in range(chips)]
            found = merge([(block[0], block[1]) for block in blocks])
            dist, count = settle(*found, is_source(dims, ids, at, my_col))
            low[at, 0] = dist
            low[at, 1] = count
    else:
        other = came[(PAIR * my_x + 1 - my_core) * n_col + my_col]
        mine = jnp.concatenate([near[my_col, 0, :half, :], near[my_col, 1, :half, :]], axis=0)
        for core in range(PAIR):
            block = jnp.where(my_core == core, mine, other)
            dist = block[:half]
            rows = pl.ds(core * half, half)
            state[0, rows, :] = jnp.where(dist < 0.5 * far_value, dist, -1.0)
            state[1, rows, :] = block[half:]
    acc[...] = jnp.zeros(acc.shape, jnp.float32)

    def add_terms(k, r, s, part):
        acc[k * n_col + r, s] += jnp.sum(part.reshape(-1, SUB, LANES), axis=0)

    def select(chip, _):
        rows = PAIR * half
        count = low[chip, 1]
        share = jnp.where(count > 0.5, 1.0 / jnp.maximum(count, 1.0), 0.0)
        turned = jnp.concatenate([low[chip, 0], share], axis=0).T
        for at in range(rows):
            h, s = at // half, at % half
            dist = jnp.broadcast_to(turned[:, at : at + 1], (LANES, LANES))
            coef = jnp.broadcast_to(turned[:, rows + at : rows + at + 1], (LANES, LANES))

            def step(k, g, r, carry):
                hit = tiles[k][g] + near[r, 0, pl.ds(k * half + s, 1), :] == dist
                part = jnp.where(hit, coef, 0.0)
                terms[(k * slots + g) * half + s] = part
                add_terms(k, r, s, part)
                return carry

            over_slots(dims, places, table, filled, PAIR * chip + h, step, 0)
        return 0

    def scale(chip):
        line = (PAIR * chip + my_core) * n_col
        total = functools.reduce(jnp.add, [came[line + col] for col in range(n_col)])
        turned = (1.0 + low[chip, 1] * total).T
        for at in range(PAIR * half):
            c, s = PAIR * chip + at // half, at % half
            factor = jnp.broadcast_to(turned[:, at : at + 1], (LANES, LANES))

            def step(k, g, r, carry):
                add_terms(k, r, s, terms[(k * slots + g) * half + s] * factor)
                return carry

            over_slots(dims, places, table, filled, c, step, 0)

    if first:
        lax.fori_loop(0, chips, select, 0)
    else:
        for chip in range(chips):
            scale(chip)
    for r in range(n_col):
        if last:
            counted = jnp.where(is_source(dims, ids, my_x, r), 0.0, 1.0)
            weight = own_first(counted, my_core) * near[r, 1]
        for k in range(PAIR):
            if last:
                sums = jnp.sum(acc[k * n_col + r], axis=1)
                term = weight[k * half : k * half + half] * sums
                out[(my_core ^ k) * n_col + r] = jnp.sum(term, axis=0, keepdims=True)
            else:
                sums = jnp.sum(acc[(my_core ^ k) * n_col + r], axis=1)
                for chip in range(chips):
                    line = (PAIR * chip + my_core) * n_col
                    out[line + r, pl.ds(k * half, half), :] = sums
    if not last:
        give = jnp.concatenate([near[my_col, 0, half:, :], near[my_col, 1, half:, :]], axis=0)
        for chip in range(chips):
            for r in range(n_col):
                out[(PAIR * chip + 1 - my_core) * n_col + r] = give


def depend_level(dims, first, last, places, ids, tiles, bands, came):
    n_row, n_col, slots, half = dims
    if last:
        out_shape = [piece(PAIR * n_col, 1, LANES)]
    else:
        out_shape = [piece(n_row * n_col, PAIR * half, LANES)]
    if first:
        out_shape += [
            piece(n_col, 2, PAIR * half, LANES),
            piece(n_row // PAIR, 2, PAIR * half, LANES),
            piece(PAIR * slots * half, LANES, LANES),
        ]
    else:
        out_shape += [piece(2, PAIR * half, LANES)]
    vectors = [ids, *(tiles if first else []), *bands, came]
    return pl.pallas_call(
        functools.partial(depend_kernel, dims, first, last),
        out_shape=out_shape,
        in_specs=[in_smem()] * len(places) + [in_vmem()] * len(vectors),
        out_specs=[in_vmem()] * len(out_shape),
        scratch_shapes=[pltpu.VMEM((PAIR * n_col, half, SUB, LANES), jnp.float32)]
        + slot_scratch(dims),
        compiler_params=params(terms_limit),
        name="depend_level",
    )(*places, *vectors)


def result_kernel(rows, came, state, shown, paths, centrality):
    shown[...] = state[0]
    paths[...] = state[1]
    shares = [came[at] for at in range(came.shape[0])]
    centrality[...] = functools.reduce(jnp.add, shares) / rows


def results(dims, came, state):
    rows = PAIR * dims[3]
    return pl.pallas_call(
        functools.partial(result_kernel, rows),
        out_shape=[piece(rows, LANES)] * 2 + [piece(1, LANES)],
        in_specs=[in_vmem()] * 2,
        out_specs=[in_vmem()] * 3,
        compiler_params=params(small_limit),
        name="results",
    )(came, state)


def all_to_all(value, axes):
    return lax.all_to_all(value, axes, split_axis=0, concat_axis=0, tiled=True)


def swap_core(value):
    return lax.ppermute(value, "core", [(0, 1), (1, 0)])


def per_device(tiles, tile_index, tile_count, sources):
    slots = tiles.shape[0]
    rows = sources.shape[0]
    dims = (lax.axis_size("chip") * PAIR, lax.axis_size("col"), slots, rows // PAIR)
    own_places = tile_index.T
    line = ("col", "chip")

    everyone = ("chip", "core", "col")

    firsts, turned, ids = first_level(dims, own_places, sources, tiles)
    both = [turned, swap_core(turned)]
    places = [] if is_dense(dims) else [own_places, swap_core(own_places)]
    came = all_to_all(firsts, everyone)
    for level_no in range(1, LEVELS):
        whole = level_no == LEVELS - 1
        outs = relax_level(dims, level_no > 1, whole, places, ids, both, came)
        came = all_to_all(outs, line)
    sums, *bands = depend_level(dims, True, False, places, ids, both, [], came)
    for back_no in range(1, BACK):
        last = back_no == BACK - 1
        came = all_to_all(sums, everyone)
        sums, state = depend_level(dims, False, last, places, ids, both, bands, came)
    shown, paths, centrality = results(dims, all_to_all(sums, ("core", "col")), state)
    return shown, paths, centrality.reshape(LANES)


def solution(mesh):
    groups, rows, cols = mesh.devices.shape
    pairs = mesh.devices.reshape(groups, rows // PAIR, PAIR, cols)
    paired = jax.sharding.Mesh(pairs, ("groups", "chip", "core", "col"))
    vertices = ("chip", "core", "col")
    everywhere = ("groups",) + vertices
    in_specs = (P(everywhere, None, None), P(everywhere, None), P(everywhere), P("groups"))
    out_specs = (P("groups", vertices), P("groups", vertices), P(everywhere))
    return jax.shard_map(
        per_device, mesh=paired, in_specs=in_specs, out_specs=out_specs, check_vma=False
    )
```

```python
import functools

import jax
import jax.numpy as jnp
from jax import lax
from jax.experimental import pallas as pl
from jax.experimental.pallas import tpu as pltpu
from jax.sharding import PartitionSpec as P

LEVELS = 3
BACK = 2
LANES = 128
SUB = 8
PAIR = 2
SPAN = 32

far_value = 1000000.0
no_edge = 2000000.0
large_limit = 8 * 1024 * 1024
small_limit = 2 * 1024 * 1024
terms_limit = 20 * 1024 * 1024


def in_vmem():
    return pl.BlockSpec(memory_space=pltpu.VMEM)


def in_smem():
    return pl.BlockSpec(memory_space=pltpu.SMEM)


def in_hbm():
    return pl.BlockSpec(memory_space=pltpu.HBM)


def piece(*shape):
    return jax.ShapeDtypeStruct(shape, jnp.float32)


def params(limit):
    return pltpu.CompilerParams(vmem_limit_bytes=limit)


def is_dense(dims):
    return dims[2] == dims[0] * dims[1]


def position():
    return lax.axis_index("chip"), lax.axis_index("core"), lax.axis_index("col")


def source_ids(sources, first, half):
    row = lax.broadcasted_iota(jnp.int32, (PAIR * half, LANES), 0)
    ids = jnp.zeros((PAIR * half, LANES), jnp.int32)
    for s in range(half):
        ids = jnp.where(lax.rem(row, half) == s, sources[first + s], ids)
    return ids


def is_source(dims, ids, chip, col):
    n_row, n_col, slots, half = dims
    block = lax.broadcasted_iota(jnp.int32, ids.shape, 0) // half
    lane = lax.broadcasted_iota(jnp.int32, ids.shape, 1)
    return ids == ((PAIR * chip + block) * n_col + col) * LANES + lane


def own_first(rows, my_core):
    half = rows.shape[0] // PAIR
    return jnp.where(my_core == 0, rows, jnp.concatenate([rows[half:], rows[:half]], axis=0))


def settle(found_dist, found_count, at_source):
    dist = jnp.where(at_source, 0.0, jnp.minimum(found_dist, far_value))
    count = jnp.where(found_dist == dist, found_count, 0.0)
    return dist, jnp.where(at_source, 1.0, 0.0) + count


def merge(pairs):
    best = functools.reduce(jnp.minimum, [p[0] for p in pairs])
    total = functools.reduce(jnp.add, [jnp.where(p[0] == best, p[1], 0.0) for p in pairs])
    return best, total


def first_kernel(dims, *refs):
    n_row, n_col, slots, half = dims
    places_in, sources_in, tiles_in, out, turned, ids = refs[:6]
    places, sources, slot_of, tiles, sems = refs[6:]
    my_x, my_core, my_col = position()
    my_row = my_x * PAIR + my_core
    parts = sems.shape[0] - 2
    size = slots // parts
    given = [
        pltpu.make_async_copy(places_in, places, sems.at[parts]),
        pltpu.make_async_copy(sources_in, sources, sems.at[parts + 1]),
    ]
    fetch = []
    for part in range(parts):
        span = pl.ds(part * size, size)
        fetch.append(pltpu.make_async_copy(tiles_in.at[span], tiles.at[span], sems.at[part]))
    for copy in given + fetch:
        copy.start()

    def clear(at, _):
        slot_of[at] = -1
        return 0

    if not is_dense(dims):
        lax.fori_loop(0, n_row * n_col, clear, 0)
    for copy in given:
        copy.wait()
    for g in range(slots):
        slot_of[places[0, g] * n_row + places[1, g]] = g
    ids[...] = source_ids(sources, my_core * half, half)

    def turn(part):
        for g in range(part * size, part * size + size):
            at = places[0, g] * n_row + places[1, g] if is_dense(dims) else g
            raw = tiles[g]
            turned[at] = jnp.where(raw > 0, raw, no_edge).T

    for part in range(parts):
        fetch[part].wait()
        if part + 1 < parts:
            turn(part)
    row_at = lax.broadcasted_iota(jnp.int32, (PAIR * half, LANES), 0)
    lines = {}
    for c in range(n_row):
        for s in range(PAIR * half):
            vertex = sources[s]
            block, place = vertex // LANES, lax.rem(vertex, LANES)
            g = slot_of[lax.rem(block, n_col) * n_row + c]
            here = jnp.logical_and(block // n_col == my_row, g >= 0)
            row = tiles[jnp.maximum(g, 0), pl.ds(place, 1), :]
            to = jnp.where(here, c % PAIR * half + s % half, -1)
            line = lines.get((c // PAIR, s // half), jnp.zeros(row_at.shape, jnp.float32))
            lines[c // PAIR, s // half] = jnp.where(row_at == to, row, line)
    for (chip, core), line in lines.items():
        line = jnp.where(line > 0, line, far_value)
        for col in range(n_col):
            out[(chip * PAIR + core) * n_col + col] = line
    turn(parts - 1)


def first_level(dims, places, sources, tiles):
    n_row, n_col, slots, half = dims
    parts = 8 if slots % 8 == 0 else 1
    inputs = [pltpu.with_memory_space_constraint(x, pltpu.HBM) for x in (places, sources, tiles)]
    return pl.pallas_call(
        functools.partial(first_kernel, dims),
        out_shape=[
            piece(n_row * n_col, PAIR * half, LANES),
            piece(*tiles.shape),
            jax.ShapeDtypeStruct((PAIR * half, LANES), jnp.int32),
        ],
        in_specs=[in_hbm()] * 3,
        out_specs=[in_vmem()] * 3,
        scratch_shapes=[
            pltpu.SMEM(places.shape, jnp.int32),
            pltpu.SMEM(sources.shape, jnp.int32),
            pltpu.SMEM((n_row * n_col,), jnp.int32),
            pltpu.VMEM(tiles.shape, jnp.float32),
            pltpu.SemaphoreType.DMA((parts + 2,)),
        ],
        compiler_params=params(large_limit),
        name="first_level",
    )(*inputs)


def list_slots(dims, places, table, filled):
    n_row, n_col, slots, half = dims
    if is_dense(dims):
        return

    def clear(at, _):
        filled[at] = 0
        return 0

    lax.fori_loop(0, PAIR * n_row, clear, 0)
    for k in range(PAIR):

        def enter(g, _):
            at = k * n_row + places[k][1, g]
            table[at * n_col + filled[at]] = g
            filled[at] += 1
            return 0

        lax.fori_loop(0, slots, enter, 0)


def over_slots(dims, places, table, filled, c, step, carry):
    n_row, n_col, slots, half = dims
    for k in range(PAIR):
        if is_dense(dims):
            for r in range(n_col):
                carry = step(k, r * n_row + c, r, carry)
        else:
            at = k * n_row + c

            def entry(e, carry):
                g = table[at * n_col + e]
                return step(k, g, places[k][0, g], carry)

            carry = lax.fori_loop(0, filled[at], entry, carry)
    return carry


def slot_scratch(dims):
    n_row, n_col, slots, half = dims
    return [
        pltpu.SMEM((PAIR * n_row * n_col,), jnp.int32),
        pltpu.SMEM((PAIR * n_row,), jnp.int32),
    ]


def relax_kernel(dims, counted, whole, *refs):
    n_row, n_col, slots, half = dims
    chips = n_row // PAIR
    n_places = 0 if is_dense(dims) else PAIR
    places, refs = refs[:n_places], refs[n_places:]
    source_rows, tiles, refs = refs[0], refs[1 : 1 + PAIR], refs[1 + PAIR :]
    came, out, near, found, table, filled = refs
    my_x, my_core, my_col = position()
    ids = source_rows[...]
    list_slots(dims, places, table, filled)
    for r in range(n_col):
        if counted:
            blocks = [came[r * chips + chip, 0] for chip in range(chips)]
            reached, count = merge([(block[0], block[1]) for block in blocks])
        else:
            parts = [came[at * n_col + r] for at in range(n_row)]
            reached = functools.reduce(jnp.minimum, parts)
            count = jnp.where(reached < far_value, 1.0, 0.0)
        dist, count = settle(reached, count, is_source(dims, ids, my_x, r))
        near[r, 0] = own_first(dist, my_core)
        near[r, 1] = own_first(count, my_core)
    lane = lax.broadcasted_iota(jnp.int32, (SPAN, LANES), 1)

    spans = range(0, LANES, SPAN)
    items = [(h, q) for h in range(PAIR) for q in spans]

    def lowest(chip, at):
        h, q = items[at]

        def step(k, g, r, carry):
            weight = tiles[k][g, pl.ds(q, SPAN), :]
            rows = [near[r, 0, pl.ds(k * half + s, 1), :] for s in range(half)]
            return tuple(jnp.minimum(low, weight + row) for low, row in zip(carry, rows))

        start = (jnp.full((SPAN, LANES), far_value, jnp.float32),) * half
        reached = over_slots(dims, places, table, filled, PAIR * chip + h, step, start)
        return [jnp.min(low, axis=1, keepdims=True) for low in reached]

    def tally(chip, at, best):
        h, q = items[at]

        def step(k, g, r, carry):
            weight = tiles[k][g, pl.ds(q, SPAN), :]
            counts = []
            for s in range(half):
                row = pl.ds(k * half + s, 1)
                hit = weight + near[r, 0, row, :] == best[s]
                counts.append(carry[s] + jnp.where(hit, near[r, 1, row, :], 0.0))
            return tuple(counts)

        start = (jnp.zeros((SPAN, LANES), jnp.float32),) * half
        counts = over_slots(dims, places, table, filled, PAIR * chip + h, step, start)
        return [jnp.sum(count, axis=1, keepdims=True) for count in counts]

    def columns(chip, _):
        rows = PAIR * half
        turned = {q: jnp.zeros((SPAN, LANES), jnp.float32) for q in spans}
        best = lowest(chip, 0)
        for at, (h, q) in enumerate(items):
            later = lowest(chip, at + 1) if at + 1 < len(items) else None
            totals = tally(chip, at, best)
            for s in range(half):
                to = h * half + s
                with_total = jnp.where(lane == rows + to, totals[s], turned[q])
                turned[q] = jnp.where(lane == to, best[s], with_total)
            best = later
        both = jnp.concatenate([turned[q] for q in spans], axis=0).T
        found[chip, 0] = both[:rows]
        found[chip, 1] = both[rows : 2 * rows]
        return 0

    lax.fori_loop(0, chips, columns, 0)
    for chip in range(chips):
        for col in range(n_col):
            if whole:
                out[col * chips + chip] = found[...]
            else:
                out[col * chips + chip, 0] = found[chip]


def relax_level(dims, counted, whole, places, ids, tiles, came):
    n_row, n_col, slots, half = dims
    chips = n_row // PAIR
    return pl.pallas_call(
        functools.partial(relax_kernel, dims, counted, whole),
        out_shape=piece(chips * n_col, chips if whole else 1, 2, PAIR * half, LANES),
        in_specs=[in_smem()] * len(places) + [in_vmem()] * (PAIR + 2),
        out_specs=in_vmem(),
        scratch_shapes=[
            pltpu.VMEM((n_col, 2, PAIR * half, LANES), jnp.float32),
            pltpu.VMEM((chips, 2, PAIR * half, LANES), jnp.float32),
        ]
        + slot_scratch(dims),
        compiler_params=params(large_limit),
        name="relax_level",
    )(*places, ids, *tiles, came)


def depend_kernel(dims, first, last, *refs):
    n_row, n_col, slots, half = dims
    chips = n_row // PAIR
    n_places = 0 if is_dense(dims) else PAIR
    places, refs = refs[:n_places], refs[n_places:]
    source_rows, refs = refs[0], refs[1:]
    if first:
        tiles, refs = refs[:PAIR], refs[PAIR:]
        came, out, near, low, terms, acc, table, filled = refs
    else:
        near, low, terms, came, out, state, acc, table, filled = refs
    my_x, my_core, my_col = position()
    ids = source_rows[...]
    list_slots(dims, places, table, filled)
    if first:
        for r in range(n_col):
            blocks = [came[r * chips + chip, my_x] for chip in range(chips)]
            found = merge([(block[0], block[1]) for block in blocks])
            dist, count = settle(*found, is_source(dims, ids, my_x, r))
            near[r, 0] = own_first(dist, my_core)
            near[r, 1] = own_first(count, my_core)
        for at in range(chips):
            blocks = [came[my_col * chips + chip, at] for chip in range(chips)]
            found = merge([(block[0], block[1]) for block in blocks])
            dist, count = settle(*found, is_source(dims, ids, at, my_col))
            low[at, 0] = dist
            low[at, 1] = count
    else:
        other = came[(PAIR * my_x + 1 - my_core) * n_col + my_col]
        mine = jnp.concatenate([near[my_col, 0, :half, :], near[my_col, 1, :half, :]], axis=0)
        for core in range(PAIR):
            block = jnp.where(my_core == core, mine, other)
            dist = block[:half]
            rows = pl.ds(core * half, half)
            state[0, rows, :] = jnp.where(dist < 0.5 * far_value, dist, -1.0)
            state[1, rows, :] = block[half:]
    acc[...] = jnp.zeros(acc.shape, jnp.float32)

    def add_terms(k, r, s, part):
        acc[k * n_col + r, s] += jnp.sum(part.reshape(-1, SUB, LANES), axis=0)

    def select(chip, _):
        rows = PAIR * half
        count = low[chip, 1]
        share = jnp.where(count > 0.5, 1.0 / jnp.maximum(count, 1.0), 0.0)
        turned = jnp.concatenate([low[chip, 0], share], axis=0).T
        for at in range(rows):
            h, s = at // half, at % half
            dist = jnp.broadcast_to(turned[:, at : at + 1], (LANES, LANES))
            coef = jnp.broadcast_to(turned[:, rows + at : rows + at + 1], (LANES, LANES))

            def step(k, g, r, carry):
                hit = tiles[k][g] + near[r, 0, pl.ds(k * half + s, 1), :] == dist
                part = jnp.where(hit, coef, 0.0)
                terms[(k * slots + g) * half + s] = part
                add_terms(k, r, s, part)
                return carry

            over_slots(dims, places, table, filled, PAIR * chip + h, step, 0)
        return 0

    def scale(chip):
        line = (PAIR * chip + my_core) * n_col
        total = functools.reduce(jnp.add, [came[line + col] for col in range(n_col)])
        turned = (1.0 + low[chip, 1] * total).T
        for at in range(PAIR * half):
            c, s = PAIR * chip + at // half, at % half
            factor = jnp.broadcast_to(turned[:, at : at + 1], (LANES, LANES))

            def step(k, g, r, carry):
                add_terms(k, r, s, terms[(k * slots + g) * half + s] * factor)
                return carry

            over_slots(dims, places, table, filled, c, step, 0)

    if first:
        lax.fori_loop(0, chips, select, 0)
    else:
        for chip in range(chips):
            scale(chip)
    for r in range(n_col):
        if last:
            counted = jnp.where(is_source(dims, ids, my_x, r), 0.0, 1.0)
            weight = own_first(counted, my_core) * near[r, 1]
        for k in range(PAIR):
            if last:
                sums = jnp.sum(acc[k * n_col + r], axis=1)
                term = weight[k * half : k * half + half] * sums
                out[(my_core ^ k) * n_col + r] = jnp.sum(term, axis=0, keepdims=True)
            else:
                sums = jnp.sum(acc[(my_core ^ k) * n_col + r], axis=1)
                for chip in range(chips):
                    line = (PAIR * chip + my_core) * n_col
                    out[line + r, pl.ds(k * half, half), :] = sums
    if not last:
        give = jnp.concatenate([near[my_col, 0, half:, :], near[my_col, 1, half:, :]], axis=0)
        for chip in range(chips):
            for r in range(n_col):
                out[(PAIR * chip + 1 - my_core) * n_col + r] = give


def depend_level(dims, first, last, places, ids, tiles, bands, came):
    n_row, n_col, slots, half = dims
    if last:
        out_shape = [piece(PAIR * n_col, 1, LANES)]
    else:
        out_shape = [piece(n_row * n_col, PAIR * half, LANES)]
    if first:
        out_shape += [
            piece(n_col, 2, PAIR * half, LANES),
            piece(n_row // PAIR, 2, PAIR * half, LANES),
            piece(PAIR * slots * half, LANES, LANES),
        ]
    else:
        out_shape += [piece(2, PAIR * half, LANES)]
    vectors = [ids, *(tiles if first else []), *bands, came]
    return pl.pallas_call(
        functools.partial(depend_kernel, dims, first, last),
        out_shape=out_shape,
        in_specs=[in_smem()] * len(places) + [in_vmem()] * len(vectors),
        out_specs=[in_vmem()] * len(out_shape),
        scratch_shapes=[pltpu.VMEM((PAIR * n_col, half, SUB, LANES), jnp.float32)]
        + slot_scratch(dims),
        compiler_params=params(terms_limit),
        name="depend_level",
    )(*places, *vectors)


def result_kernel(rows, came, state, shown, paths, centrality):
    shown[...] = state[0]
    paths[...] = state[1]
    shares = [came[at] for at in range(came.shape[0])]
    centrality[...] = functools.reduce(jnp.add, shares) / rows


def results(dims, came, state):
    rows = PAIR * dims[3]
    return pl.pallas_call(
        functools.partial(result_kernel, rows),
        out_shape=[piece(rows, LANES)] * 2 + [piece(1, LANES)],
        in_specs=[in_vmem()] * 2,
        out_specs=[in_vmem()] * 3,
        compiler_params=params(small_limit),
        name="results",
    )(came, state)


def all_to_all(value, axes):
    return lax.all_to_all(value, axes, split_axis=0, concat_axis=0, tiled=True)


def swap_core(value):
    return lax.ppermute(value, "core", [(0, 1), (1, 0)])


def per_device(tiles, tile_index, tile_count, sources):
    slots = tiles.shape[0]
    rows = sources.shape[0]
    dims = (lax.axis_size("chip") * PAIR, lax.axis_size("col"), slots, rows // PAIR)
    own_places = tile_index.T
    line = ("col", "chip")

    everyone = ("chip", "core", "col")

    firsts, turned, ids = first_level(dims, own_places, sources, tiles)
    both = [turned, swap_core(turned)]
    places = [] if is_dense(dims) else [own_places, swap_core(own_places)]
    came = all_to_all(firsts, everyone)
    for level_no in range(1, LEVELS):
        whole = level_no == LEVELS - 1
        outs = relax_level(dims, level_no > 1, whole, places, ids, both, came)
        came = all_to_all(outs, line)
    sums, *bands = depend_level(dims, True, False, places, ids, both, [], came)
    for back_no in range(1, BACK):
        last = back_no == BACK - 1
        came = all_to_all(sums, everyone)
        sums, state = depend_level(dims, False, last, places, ids, both, bands, came)
    shown, paths, centrality = results(dims, all_to_all(sums, ("core", "col")), state)
    return shown, paths, centrality.reshape(LANES)


def solution(mesh):
    groups, rows, cols = mesh.devices.shape
    pairs = mesh.devices.reshape(groups, rows // PAIR, PAIR, cols)
    paired = jax.sharding.Mesh(pairs, ("groups", "chip", "core", "col"))
    vertices = ("chip", "core", "col")
    everywhere = ("groups",) + vertices
    in_specs = (P(everywhere, None, None), P(everywhere, None), P(everywhere), P("groups"))
    out_specs = (P("groups", vertices), P("groups", vertices), P(everywhere))
    return jax.shard_map(
        per_device, mesh=paired, in_specs=in_specs, out_specs=out_specs, check_vma=False
    )
```

```python
import functools

import jax
import jax.numpy as jnp
from jax import lax
from jax.experimental import pallas as pl
from jax.experimental.pallas import tpu as pltpu
from jax.sharding import PartitionSpec as P

LEVELS = 3
BACK = 2
LANES = 128
SUB = 8
PAIR = 2
SPAN = 32

far_value = 1000000.0
no_edge = 2000000.0
large_limit = 8 * 1024 * 1024
small_limit = 2 * 1024 * 1024
terms_limit = 20 * 1024 * 1024


def in_vmem():
    return pl.BlockSpec(memory_space=pltpu.VMEM)


def in_smem():
    return pl.BlockSpec(memory_space=pltpu.SMEM)


def in_hbm():
    return pl.BlockSpec(memory_space=pltpu.HBM)


def piece(*shape):
    return jax.ShapeDtypeStruct(shape, jnp.float32)


def params(limit):
    return pltpu.CompilerParams(vmem_limit_bytes=limit)


def is_dense(dims):
    return dims[2] == dims[0] * dims[1]


def position():
    return lax.axis_index("chip"), lax.axis_index("core"), lax.axis_index("col")


def source_ids(sources, first, half):
    row = lax.broadcasted_iota(jnp.int32, (PAIR * half, LANES), 0)
    ids = jnp.zeros((PAIR * half, LANES), jnp.int32)
    for s in range(half):
        ids = jnp.where(lax.rem(row, half) == s, sources[first + s], ids)
    return ids


def is_source(dims, ids, chip, col):
    n_row, n_col, slots, half = dims
    block = lax.broadcasted_iota(jnp.int32, ids.shape, 0) // half
    lane = lax.broadcasted_iota(jnp.int32, ids.shape, 1)
    return ids == ((PAIR * chip + block) * n_col + col) * LANES + lane


def own_first(rows, my_core):
    half = rows.shape[0] // PAIR
    return jnp.where(my_core == 0, rows, jnp.concatenate([rows[half:], rows[:half]], axis=0))


def settle(found_dist, found_count, at_source):
    dist = jnp.where(at_source, 0.0, jnp.minimum(found_dist, far_value))
    count = jnp.where(found_dist == dist, found_count, 0.0)
    return dist, jnp.where(at_source, 1.0, 0.0) + count


def merge(pairs):
    best = functools.reduce(jnp.minimum, [p[0] for p in pairs])
    total = functools.reduce(jnp.add, [jnp.where(p[0] == best, p[1], 0.0) for p in pairs])
    return best, total


def first_kernel(dims, *refs):
    n_row, n_col, slots, half = dims
    places_in, sources_in, tiles_in, out, turned, ids = refs[:6]
    places, sources, slot_of, tiles, sems = refs[6:]
    my_x, my_core, my_col = position()
    my_row = my_x * PAIR + my_core
    parts = sems.shape[0] - 2
    size = slots // parts
    given = [
        pltpu.make_async_copy(places_in, places, sems.at[parts]),
        pltpu.make_async_copy(sources_in, sources, sems.at[parts + 1]),
    ]
    fetch = []
    for part in range(parts):
        span = pl.ds(part * size, size)
        fetch.append(pltpu.make_async_copy(tiles_in.at[span], tiles.at[span], sems.at[part]))
    for copy in given + fetch:
        copy.start()

    def clear(at, _):
        slot_of[at] = -1
        return 0

    if not is_dense(dims):
        lax.fori_loop(0, n_row * n_col, clear, 0)
    for copy in given:
        copy.wait()
    for g in range(slots):
        slot_of[places[0, g] * n_row + places[1, g]] = g
    ids[...] = source_ids(sources, my_core * half, half)

    def turn(part):
        for g in range(part * size, part * size + size):
            at = places[0, g] * n_row + places[1, g] if is_dense(dims) else g
            raw = tiles[g]
            turned[at] = jnp.where(raw > 0, raw, no_edge).T

    for part in range(parts):
        fetch[part].wait()
        if part + 1 < parts:
            turn(part)
    row_at = lax.broadcasted_iota(jnp.int32, (PAIR * half, LANES), 0)
    lines = {}
    for c in range(n_row):
        for s in range(PAIR * half):
            vertex = sources[s]
            block, place = vertex // LANES, lax.rem(vertex, LANES)
            g = slot_of[lax.rem(block, n_col) * n_row + c]
            here = jnp.logical_and(block // n_col == my_row, g >= 0)
            row = tiles[jnp.maximum(g, 0), pl.ds(place, 1), :]
            to = jnp.where(here, c % PAIR * half + s % half, -1)
            line = lines.get((c // PAIR, s // half), jnp.zeros(row_at.shape, jnp.float32))
            lines[c // PAIR, s // half] = jnp.where(row_at == to, row, line)
    for (chip, core), line in lines.items():
        line = jnp.where(line > 0, line, far_value)
        for col in range(n_col):
            out[(chip * PAIR + core) * n_col + col] = line
    turn(parts - 1)


def first_level(dims, places, sources, tiles):
    n_row, n_col, slots, half = dims
    parts = 2 if slots % 2 == 0 else 1
    inputs = [pltpu.with_memory_space_constraint(x, pltpu.HBM) for x in (places, sources, tiles)]
    return pl.pallas_call(
        functools.partial(first_kernel, dims),
        out_shape=[
            piece(n_row * n_col, PAIR * half, LANES),
            piece(*tiles.shape),
            jax.ShapeDtypeStruct((PAIR * half, LANES), jnp.int32),
        ],
        in_specs=[in_hbm()] * 3,
        out_specs=[in_vmem()] * 3,
        scratch_shapes=[
            pltpu.SMEM(places.shape, jnp.int32),
            pltpu.SMEM(sources.shape, jnp.int32),
            pltpu.SMEM((n_row * n_col,), jnp.int32),
            pltpu.VMEM(tiles.shape, jnp.float32),
            pltpu.SemaphoreType.DMA((parts + 2,)),
        ],
        compiler_params=params(large_limit),
        name="first_level",
    )(*inputs)


def list_slots(dims, places, table, filled):
    n_row, n_col, slots, half = dims
    if is_dense(dims):
        return

    def clear(at, _):
        filled[at] = 0
        return 0

    lax.fori_loop(0, PAIR * n_row, clear, 0)
    for k in range(PAIR):

        def enter(g, _):
            at = k * n_row + places[k][1, g]
            table[at * n_col + filled[at]] = g
            filled[at] += 1
            return 0

        lax.fori_loop(0, slots, enter, 0)


def over_slots(dims, places, table, filled, c, step, carry):
    n_row, n_col, slots, half = dims
    for k in range(PAIR):
        if is_dense(dims):
            for r in range(n_col):
                carry = step(k, r * n_row + c, r, carry)
        else:
            at = k * n_row + c

            def entry(e, carry):
                g = table[at * n_col + e]
                return step(k, g, places[k][0, g], carry)

            carry = lax.fori_loop(0, filled[at], entry, carry)
    return carry


def slot_scratch(dims):
    n_row, n_col, slots, half = dims
    return [
        pltpu.SMEM((PAIR * n_row * n_col,), jnp.int32),
        pltpu.SMEM((PAIR * n_row,), jnp.int32),
    ]


def relax_kernel(dims, counted, whole, *refs):
    n_row, n_col, slots, half = dims
    chips = n_row // PAIR
    n_places = 0 if is_dense(dims) else PAIR
    places, refs = refs[:n_places], refs[n_places:]
    source_rows, tiles, refs = refs[0], refs[1 : 1 + PAIR], refs[1 + PAIR :]
    came, out, near, found, table, filled = refs
    my_x, my_core, my_col = position()
    ids = source_rows[...]
    list_slots(dims, places, table, filled)
    for r in range(n_col):
        if counted:
            blocks = [came[r * chips + chip, 0] for chip in range(chips)]
            reached, count = merge([(block[0], block[1]) for block in blocks])
        else:
            parts = [came[at * n_col + r] for at in range(n_row)]
            reached = functools.reduce(jnp.minimum, parts)
            count = jnp.where(reached < far_value, 1.0, 0.0)
        dist, count = settle(reached, count, is_source(dims, ids, my_x, r))
        near[r, 0] = own_first(dist, my_core)
        near[r, 1] = own_first(count, my_core)
    lane = lax.broadcasted_iota(jnp.int32, (SPAN, LANES), 1)

    spans = range(0, LANES, SPAN)
    items = [(h, q) for h in range(PAIR) for q in spans]

    def lowest(chip, at):
        h, q = items[at]

        def step(k, g, r, carry):
            weight = tiles[k][g, pl.ds(q, SPAN), :]
            rows = [near[r, 0, pl.ds(k * half + s, 1), :] for s in range(half)]
            return tuple(jnp.minimum(low, weight + row) for low, row in zip(carry, rows))

        start = (jnp.full((SPAN, LANES), far_value, jnp.float32),) * half
        reached = over_slots(dims, places, table, filled, PAIR * chip + h, step, start)
        return [jnp.min(low, axis=1, keepdims=True) for low in reached]

    def tally(chip, at, best):
        h, q = items[at]

        def step(k, g, r, carry):
            weight = tiles[k][g, pl.ds(q, SPAN), :]
            counts = []
            for s in range(half):
                row = pl.ds(k * half + s, 1)
                hit = weight + near[r, 0, row, :] == best[s]
                counts.append(carry[s] + jnp.where(hit, near[r, 1, row, :], 0.0))
            return tuple(counts)

        start = (jnp.zeros((SPAN, LANES), jnp.float32),) * half
        counts = over_slots(dims, places, table, filled, PAIR * chip + h, step, start)
        return [jnp.sum(count, axis=1, keepdims=True) for count in counts]

    def columns(chip, _):
        rows = PAIR * half
        turned = {q: jnp.zeros((SPAN, LANES), jnp.float32) for q in spans}
        best = lowest(chip, 0)
        for at, (h, q) in enumerate(items):
            later = lowest(chip, at + 1) if at + 1 < len(items) else None
            totals = tally(chip, at, best)
            for s in range(half):
                to = h * half + s
                with_total = jnp.where(lane == rows + to, totals[s], turned[q])
                turned[q] = jnp.where(lane == to, best[s], with_total)
            best = later
        both = jnp.concatenate([turned[q] for q in spans], axis=0).T
        found[chip, 0] = both[:rows]
        found[chip, 1] = both[rows : 2 * rows]
        return 0

    lax.fori_loop(0, chips, columns, 0)
    for chip in range(chips):
        for col in range(n_col):
            if whole:
                out[col * chips + chip] = found[...]
            else:
                out[col * chips + chip, 0] = found[chip]


def relax_level(dims, counted, whole, places, ids, tiles, came):
    n_row, n_col, slots, half = dims
    chips = n_row // PAIR
    return pl.pallas_call(
        functools.partial(relax_kernel, dims, counted, whole),
        out_shape=piece(chips * n_col, chips if whole else 1, 2, PAIR * half, LANES),
        in_specs=[in_smem()] * len(places) + [in_vmem()] * (PAIR + 2),
        out_specs=in_vmem(),
        scratch_shapes=[
            pltpu.VMEM((n_col, 2, PAIR * half, LANES), jnp.float32),
            pltpu.VMEM((chips, 2, PAIR * half, LANES), jnp.float32),
        ]
        + slot_scratch(dims),
        compiler_params=params(large_limit),
        name="relax_level",
    )(*places, ids, *tiles, came)


def depend_kernel(dims, first, last, *refs):
    n_row, n_col, slots, half = dims
    chips = n_row // PAIR
    n_places = 0 if is_dense(dims) else PAIR
    places, refs = refs[:n_places], refs[n_places:]
    source_rows, refs = refs[0], refs[1:]
    if first:
        tiles, refs = refs[:PAIR], refs[PAIR:]
        came, out, near, low, terms, acc, table, filled = refs
    else:
        near, low, terms, came, out, state, acc, table, filled = refs
    my_x, my_core, my_col = position()
    ids = source_rows[...]
    list_slots(dims, places, table, filled)
    if first:
        for r in range(n_col):
            blocks = [came[r * chips + chip, my_x] for chip in range(chips)]
            found = merge([(block[0], block[1]) for block in blocks])
            dist, count = settle(*found, is_source(dims, ids, my_x, r))
            near[r, 0] = own_first(dist, my_core)
            near[r, 1] = own_first(count, my_core)
        for at in range(chips):
            blocks = [came[my_col * chips + chip, at] for chip in range(chips)]
            found = merge([(block[0], block[1]) for block in blocks])
            dist, count = settle(*found, is_source(dims, ids, at, my_col))
            low[at, 0] = dist
            low[at, 1] = count
    else:
        other = came[(PAIR * my_x + 1 - my_core) * n_col + my_col]
        mine = jnp.concatenate([near[my_col, 0, :half, :], near[my_col, 1, :half, :]], axis=0)
        for core in range(PAIR):
            block = jnp.where(my_core == core, mine, other)
            dist = block[:half]
            rows = pl.ds(core * half, half)
            state[0, rows, :] = jnp.where(dist < 0.5 * far_value, dist, -1.0)
            state[1, rows, :] = block[half:]
    acc[...] = jnp.zeros(acc.shape, jnp.float32)

    def add_terms(k, r, s, part):
        acc[k * n_col + r, s] += jnp.sum(part.reshape(-1, SUB, LANES), axis=0)

    def select(chip, _):
        rows = PAIR * half
        count = low[chip, 1]
        share = jnp.where(count > 0.5, 1.0 / jnp.maximum(count, 1.0), 0.0)
        turned = jnp.concatenate([low[chip, 0], share], axis=0).T
        for at in range(rows):
            h, s = at // half, at % half
            dist = jnp.broadcast_to(turned[:, at : at + 1], (LANES, LANES))
            coef = jnp.broadcast_to(turned[:, rows + at : rows + at + 1], (LANES, LANES))

            def step(k, g, r, carry):
                hit = tiles[k][g] + near[r, 0, pl.ds(k * half + s, 1), :] == dist
                part = jnp.where(hit, coef, 0.0)
                terms[(k * slots + g) * half + s] = part
                add_terms(k, r, s, part)
                return carry

            over_slots(dims, places, table, filled, PAIR * chip + h, step, 0)
        return 0

    def scale(chip):
        line = (PAIR * chip + my_core) * n_col
        total = functools.reduce(jnp.add, [came[line + col] for col in range(n_col)])
        turned = (1.0 + low[chip, 1] * total).T
        for at in range(PAIR * half):
            c, s = PAIR * chip + at // half, at % half
            factor = jnp.broadcast_to(turned[:, at : at + 1], (LANES, LANES))

            def step(k, g, r, carry):
                add_terms(k, r, s, terms[(k * slots + g) * half + s] * factor)
                return carry

            over_slots(dims, places, table, filled, c, step, 0)

    if first:
        lax.fori_loop(0, chips, select, 0)
    else:
        for chip in range(chips):
            scale(chip)
    for r in range(n_col):
        if last:
            counted = jnp.where(is_source(dims, ids, my_x, r), 0.0, 1.0)
            weight = own_first(counted, my_core) * near[r, 1]
        for k in range(PAIR):
            if last:
                sums = jnp.sum(acc[k * n_col + r], axis=1)
                term = weight[k * half : k * half + half] * sums
                out[(my_core ^ k) * n_col + r] = jnp.sum(term, axis=0, keepdims=True)
            else:
                sums = jnp.sum(acc[(my_core ^ k) * n_col + r], axis=1)
                for chip in range(chips):
                    line = (PAIR * chip + my_core) * n_col
                    out[line + r, pl.ds(k * half, half), :] = sums
    if not last:
        give = jnp.concatenate([near[my_col, 0, half:, :], near[my_col, 1, half:, :]], axis=0)
        for chip in range(chips):
            for r in range(n_col):
                out[(PAIR * chip + 1 - my_core) * n_col + r] = give


def depend_level(dims, first, last, places, ids, tiles, bands, came):
    n_row, n_col, slots, half = dims
    if last:
        out_shape = [piece(PAIR * n_col, 1, LANES)]
    else:
        out_shape = [piece(n_row * n_col, PAIR * half, LANES)]
    if first:
        out_shape += [
            piece(n_col, 2, PAIR * half, LANES),
            piece(n_row // PAIR, 2, PAIR * half, LANES),
            piece(PAIR * slots * half, LANES, LANES),
        ]
    else:
        out_shape += [piece(2, PAIR * half, LANES)]
    vectors = [ids, *(tiles if first else []), *bands, came]
    return pl.pallas_call(
        functools.partial(depend_kernel, dims, first, last),
        out_shape=out_shape,
        in_specs=[in_smem()] * len(places) + [in_vmem()] * len(vectors),
        out_specs=[in_vmem()] * len(out_shape),
        scratch_shapes=[pltpu.VMEM((PAIR * n_col, half, SUB, LANES), jnp.float32)]
        + slot_scratch(dims),
        compiler_params=params(terms_limit),
        name="depend_level",
    )(*places, *vectors)


def result_kernel(rows, came, state, shown, paths, centrality):
    shown[...] = state[0]
    paths[...] = state[1]
    shares = [came[at] for at in range(came.shape[0])]
    centrality[...] = functools.reduce(jnp.add, shares) / rows


def results(dims, came, state):
    rows = PAIR * dims[3]
    return pl.pallas_call(
        functools.partial(result_kernel, rows),
        out_shape=[piece(rows, LANES)] * 2 + [piece(1, LANES)],
        in_specs=[in_vmem()] * 2,
        out_specs=[in_vmem()] * 3,
        compiler_params=params(small_limit),
        name="results",
    )(came, state)


def all_to_all(value, axes):
    return lax.all_to_all(value, axes, split_axis=0, concat_axis=0, tiled=True)


def swap_core(value):
    return lax.ppermute(value, "core", [(0, 1), (1, 0)])


def per_device(tiles, tile_index, tile_count, sources):
    slots = tiles.shape[0]
    rows = sources.shape[0]
    dims = (lax.axis_size("chip") * PAIR, lax.axis_size("col"), slots, rows // PAIR)
    own_places = tile_index.T
    line = ("col", "chip")

    everyone = ("chip", "core", "col")

    firsts, turned, ids = first_level(dims, own_places, sources, tiles)
    both = [turned, swap_core(turned)]
    places = [] if is_dense(dims) else [own_places, swap_core(own_places)]
    came = all_to_all(firsts, everyone)
    for level_no in range(1, LEVELS):
        whole = level_no == LEVELS - 1
        outs = relax_level(dims, level_no > 1, whole, places, ids, both, came)
        came = all_to_all(outs, line)
    sums, *bands = depend_level(dims, True, False, places, ids, both, [], came)
    for back_no in range(1, BACK):
        last = back_no == BACK - 1
        came = all_to_all(sums, everyone)
        sums, state = depend_level(dims, False, last, places, ids, both, bands, came)
    shown, paths, centrality = results(dims, all_to_all(sums, ("core", "col")), state)
    return shown, paths, centrality.reshape(LANES)


def solution(mesh):
    groups, rows, cols = mesh.devices.shape
    pairs = mesh.devices.reshape(groups, rows // PAIR, PAIR, cols)
    paired = jax.sharding.Mesh(pairs, ("groups", "chip", "core", "col"))
    vertices = ("chip", "core", "col")
    everywhere = ("groups",) + vertices
    in_specs = (P(everywhere, None, None), P(everywhere, None), P(everywhere), P("groups"))
    out_specs = (P("groups", vertices), P("groups", vertices), P(everywhere))
    return jax.shard_map(
        per_device, mesh=paired, in_specs=in_specs, out_specs=out_specs, check_vma=False
    )
```

```python
import functools

import jax
import jax.numpy as jnp
from jax import lax
from jax.experimental import pallas as pl
from jax.experimental.pallas import tpu as pltpu
from jax.sharding import PartitionSpec as P

LEVELS = 3
BACK = 2
LANES = 128
SUB = 8
PAIR = 2
SPAN = 32

far_value = 1000000.0
no_edge = 2000000.0
large_limit = 8 * 1024 * 1024
small_limit = 2 * 1024 * 1024
terms_limit = 20 * 1024 * 1024


def in_vmem():
    return pl.BlockSpec(memory_space=pltpu.VMEM)


def in_smem():
    return pl.BlockSpec(memory_space=pltpu.SMEM)


def in_hbm():
    return pl.BlockSpec(memory_space=pltpu.HBM)


def piece(*shape):
    return jax.ShapeDtypeStruct(shape, jnp.float32)


def params(limit):
    return pltpu.CompilerParams(vmem_limit_bytes=limit)


def is_dense(dims):
    return dims[2] == dims[0] * dims[1]


def position():
    return lax.axis_index("chip"), lax.axis_index("core"), lax.axis_index("col")


def source_ids(sources, first, half):
    row = lax.broadcasted_iota(jnp.int32, (PAIR * half, LANES), 0)
    ids = jnp.zeros((PAIR * half, LANES), jnp.int32)
    for s in range(half):
        ids = jnp.where(lax.rem(row, half) == s, sources[first + s], ids)
    return ids


def is_source(dims, ids, chip, col):
    n_row, n_col, slots, half = dims
    block = lax.broadcasted_iota(jnp.int32, ids.shape, 0) // half
    lane = lax.broadcasted_iota(jnp.int32, ids.shape, 1)
    return ids == ((PAIR * chip + block) * n_col + col) * LANES + lane


def own_first(rows, my_core):
    half = rows.shape[0] // PAIR
    return jnp.where(my_core == 0, rows, jnp.concatenate([rows[half:], rows[:half]], axis=0))


def settle(found_dist, found_count, at_source):
    dist = jnp.where(at_source, 0.0, jnp.minimum(found_dist, far_value))
    count = jnp.where(found_dist == dist, found_count, 0.0)
    return dist, jnp.where(at_source, 1.0, 0.0) + count


def merge(pairs):
    best = functools.reduce(jnp.minimum, [p[0] for p in pairs])
    total = functools.reduce(jnp.add, [jnp.where(p[0] == best, p[1], 0.0) for p in pairs])
    return best, total


def first_kernel(dims, *refs):
    n_row, n_col, slots, half = dims
    places_in, sources_in, tiles_in, out, turned, ids = refs[:6]
    places, sources, slot_of, tiles, sems = refs[6:]
    my_x, my_core, my_col = position()
    my_row = my_x * PAIR + my_core
    parts = sems.shape[0] - 2
    size = slots // parts
    given = [
        pltpu.make_async_copy(places_in, places, sems.at[parts]),
        pltpu.make_async_copy(sources_in, sources, sems.at[parts + 1]),
    ]
    fetch = []
    for part in range(parts):
        span = pl.ds(part * size, size)
        fetch.append(pltpu.make_async_copy(tiles_in.at[span], tiles.at[span], sems.at[part]))
    for copy in given + fetch:
        copy.start()

    def clear(at, _):
        slot_of[at] = -1
        return 0

    if not is_dense(dims):
        lax.fori_loop(0, n_row * n_col, clear, 0)
    for copy in given:
        copy.wait()
    for g in range(slots):
        slot_of[places[0, g] * n_row + places[1, g]] = g
    ids[...] = source_ids(sources, my_core * half, half)

    def turn(part):
        for g in range(part * size, part * size + size):
            at = places[0, g] * n_row + places[1, g] if is_dense(dims) else g
            raw = tiles[g]
            turned[at] = jnp.where(raw > 0, raw, no_edge).T

    for part in range(parts):
        fetch[part].wait()
        if part + 1 < parts:
            turn(part)
    row_at = lax.broadcasted_iota(jnp.int32, (PAIR * half, LANES), 0)
    lines = {}
    for c in range(n_row):
        for s in range(PAIR * half):
            vertex = sources[s]
            block, place = vertex // LANES, lax.rem(vertex, LANES)
            g = slot_of[lax.rem(block, n_col) * n_row + c]
            here = jnp.logical_and(block // n_col == my_row, g >= 0)
            row = tiles[jnp.maximum(g, 0), pl.ds(place, 1), :]
            to = jnp.where(here, c % PAIR * half + s % half, -1)
            line = lines.get((c // PAIR, s // half), jnp.zeros(row_at.shape, jnp.float32))
            lines[c // PAIR, s // half] = jnp.where(row_at == to, row, line)
    for (chip, core), line in lines.items():
        line = jnp.where(line > 0, line, far_value)
        for col in range(n_col):
            out[(chip * PAIR + core) * n_col + col] = line
    turn(parts - 1)


def first_level(dims, places, sources, tiles):
    n_row, n_col, slots, half = dims
    parts = 1
    inputs = [pltpu.with_memory_space_constraint(x, pltpu.HBM) for x in (places, sources, tiles)]
    return pl.pallas_call(
        functools.partial(first_kernel, dims),
        out_shape=[
            piece(n_row * n_col, PAIR * half, LANES),
            piece(*tiles.shape),
            jax.ShapeDtypeStruct((PAIR * half, LANES), jnp.int32),
        ],
        in_specs=[in_hbm()] * 3,
        out_specs=[in_vmem()] * 3,
        scratch_shapes=[
            pltpu.SMEM(places.shape, jnp.int32),
            pltpu.SMEM(sources.shape, jnp.int32),
            pltpu.SMEM((n_row * n_col,), jnp.int32),
            pltpu.VMEM(tiles.shape, jnp.float32),
            pltpu.SemaphoreType.DMA((parts + 2,)),
        ],
        compiler_params=params(large_limit),
        name="first_level",
    )(*inputs)


def list_slots(dims, places, table, filled):
    n_row, n_col, slots, half = dims
    if is_dense(dims):
        return

    def clear(at, _):
        filled[at] = 0
        return 0

    lax.fori_loop(0, PAIR * n_row, clear, 0)
    for k in range(PAIR):

        def enter(g, _):
            at = k * n_row + places[k][1, g]
            table[at * n_col + filled[at]] = g
            filled[at] += 1
            return 0

        lax.fori_loop(0, slots, enter, 0)


def over_slots(dims, places, table, filled, c, step, carry):
    n_row, n_col, slots, half = dims
    for k in range(PAIR):
        if is_dense(dims):
            for r in range(n_col):
                carry = step(k, r * n_row + c, r, carry)
        else:
            at = k * n_row + c

            def entry(e, carry):
                g = table[at * n_col + e]
                return step(k, g, places[k][0, g], carry)

            carry = lax.fori_loop(0, filled[at], entry, carry)
    return carry


def slot_scratch(dims):
    n_row, n_col, slots, half = dims
    return [
        pltpu.SMEM((PAIR * n_row * n_col,), jnp.int32),
        pltpu.SMEM((PAIR * n_row,), jnp.int32),
    ]


def relax_kernel(dims, counted, whole, *refs):
    n_row, n_col, slots, half = dims
    chips = n_row // PAIR
    n_places = 0 if is_dense(dims) else PAIR
    places, refs = refs[:n_places], refs[n_places:]
    source_rows, tiles, refs = refs[0], refs[1 : 1 + PAIR], refs[1 + PAIR :]
    came, out, near, found, table, filled = refs
    my_x, my_core, my_col = position()
    ids = source_rows[...]
    list_slots(dims, places, table, filled)
    for r in range(n_col):
        if counted:
            blocks = [came[r * chips + chip, 0] for chip in range(chips)]
            reached, count = merge([(block[0], block[1]) for block in blocks])
        else:
            parts = [came[at * n_col + r] for at in range(n_row)]
            reached = functools.reduce(jnp.minimum, parts)
            count = jnp.where(reached < far_value, 1.0, 0.0)
        dist, count = settle(reached, count, is_source(dims, ids, my_x, r))
        near[r, 0] = own_first(dist, my_core)
        near[r, 1] = own_first(count, my_core)
    lane = lax.broadcasted_iota(jnp.int32, (SPAN, LANES), 1)

    spans = range(0, LANES, SPAN)
    items = [(h, q) for h in range(PAIR) for q in spans]

    def lowest(chip, at):
        h, q = items[at]

        def step(k, g, r, carry):
            weight = tiles[k][g, pl.ds(q, SPAN), :]
            rows = [near[r, 0, pl.ds(k * half + s, 1), :] for s in range(half)]
            return tuple(jnp.minimum(low, weight + row) for low, row in zip(carry, rows))

        start = (jnp.full((SPAN, LANES), far_value, jnp.float32),) * half
        reached = over_slots(dims, places, table, filled, PAIR * chip + h, step, start)
        return [jnp.min(low, axis=1, keepdims=True) for low in reached]

    def tally(chip, at, best):
        h, q = items[at]

        def step(k, g, r, carry):
            weight = tiles[k][g, pl.ds(q, SPAN), :]
            counts = []
            for s in range(half):
                row = pl.ds(k * half + s, 1)
                hit = weight + near[r, 0, row, :] == best[s]
                counts.append(carry[s] + jnp.where(hit, near[r, 1, row, :], 0.0))
            return tuple(counts)

        start = (jnp.zeros((SPAN, LANES), jnp.float32),) * half
        counts = over_slots(dims, places, table, filled, PAIR * chip + h, step, start)
        return [jnp.sum(count, axis=1, keepdims=True) for count in counts]

    def columns(chip, _):
        rows = PAIR * half
        turned = {q: jnp.zeros((SPAN, LANES), jnp.float32) for q in spans}
        best = lowest(chip, 0)
        for at, (h, q) in enumerate(items):
            later = lowest(chip, at + 1) if at + 1 < len(items) else None
            totals = tally(chip, at, best)
            for s in range(half):
                to = h * half + s
                with_total = jnp.where(lane == rows + to, totals[s], turned[q])
                turned[q] = jnp.where(lane == to, best[s], with_total)
            best = later
        both = jnp.concatenate([turned[q] for q in spans], axis=0).T
        found[chip, 0] = both[:rows]
        found[chip, 1] = both[rows : 2 * rows]
        return 0

    lax.fori_loop(0, chips, columns, 0)
    for chip in range(chips):
        for col in range(n_col):
            if whole:
                out[col * chips + chip] = found[...]
            else:
                out[col * chips + chip, 0] = found[chip]


def relax_level(dims, counted, whole, places, ids, tiles, came):
    n_row, n_col, slots, half = dims
    chips = n_row // PAIR
    return pl.pallas_call(
        functools.partial(relax_kernel, dims, counted, whole),
        out_shape=piece(chips * n_col, chips if whole else 1, 2, PAIR * half, LANES),
        in_specs=[in_smem()] * len(places) + [in_vmem()] * (PAIR + 2),
        out_specs=in_vmem(),
        scratch_shapes=[
            pltpu.VMEM((n_col, 2, PAIR * half, LANES), jnp.float32),
            pltpu.VMEM((chips, 2, PAIR * half, LANES), jnp.float32),
        ]
        + slot_scratch(dims),
        compiler_params=params(large_limit),
        name="relax_level",
    )(*places, ids, *tiles, came)


def depend_kernel(dims, first, last, *refs):
    n_row, n_col, slots, half = dims
    chips = n_row // PAIR
    n_places = 0 if is_dense(dims) else PAIR
    places, refs = refs[:n_places], refs[n_places:]
    source_rows, refs = refs[0], refs[1:]
    if first:
        tiles, refs = refs[:PAIR], refs[PAIR:]
        came, out, near, low, terms, acc, table, filled = refs
    else:
        near, low, terms, came, out, state, acc, table, filled = refs
    my_x, my_core, my_col = position()
    ids = source_rows[...]
    list_slots(dims, places, table, filled)
    if first:
        for r in range(n_col):
            blocks = [came[r * chips + chip, my_x] for chip in range(chips)]
            found = merge([(block[0], block[1]) for block in blocks])
            dist, count = settle(*found, is_source(dims, ids, my_x, r))
            near[r, 0] = own_first(dist, my_core)
            near[r, 1] = own_first(count, my_core)
        for at in range(chips):
            blocks = [came[my_col * chips + chip, at] for chip in range(chips)]
            found = merge([(block[0], block[1]) for block in blocks])
            dist, count = settle(*found, is_source(dims, ids, at, my_col))
            low[at, 0] = dist
            low[at, 1] = count
    else:
        other = came[(PAIR * my_x + 1 - my_core) * n_col + my_col]
        mine = jnp.concatenate([near[my_col, 0, :half, :], near[my_col, 1, :half, :]], axis=0)
        for core in range(PAIR):
            block = jnp.where(my_core == core, mine, other)
            dist = block[:half]
            rows = pl.ds(core * half, half)
            state[0, rows, :] = jnp.where(dist < 0.5 * far_value, dist, -1.0)
            state[1, rows, :] = block[half:]
    acc[...] = jnp.zeros(acc.shape, jnp.float32)

    def add_terms(k, r, s, part):
        acc[k * n_col + r, s] += jnp.sum(part.reshape(-1, SUB, LANES), axis=0)

    def select(chip, _):
        rows = PAIR * half
        count = low[chip, 1]
        share = jnp.where(count > 0.5, 1.0 / jnp.maximum(count, 1.0), 0.0)
        turned = jnp.concatenate([low[chip, 0], share], axis=0).T
        for at in range(rows):
            h, s = at // half, at % half
            dist = jnp.broadcast_to(turned[:, at : at + 1], (LANES, LANES))
            coef = jnp.broadcast_to(turned[:, rows + at : rows + at + 1], (LANES, LANES))

            def step(k, g, r, carry):
                hit = tiles[k][g] + near[r, 0, pl.ds(k * half + s, 1), :] == dist
                part = jnp.where(hit, coef, 0.0)
                terms[(k * slots + g) * half + s] = part
                add_terms(k, r, s, part)
                return carry

            over_slots(dims, places, table, filled, PAIR * chip + h, step, 0)
        return 0

    def scale(chip):
        line = (PAIR * chip + my_core) * n_col
        total = functools.reduce(jnp.add, [came[line + col] for col in range(n_col)])
        turned = (1.0 + low[chip, 1] * total).T
        for at in range(PAIR * half):
            c, s = PAIR * chip + at // half, at % half
            factor = jnp.broadcast_to(turned[:, at : at + 1], (LANES, LANES))

            def step(k, g, r, carry):
                add_terms(k, r, s, terms[(k * slots + g) * half + s] * factor)
                return carry

            over_slots(dims, places, table, filled, c, step, 0)

    if first:
        lax.fori_loop(0, chips, select, 0)
    else:
        for chip in range(chips):
            scale(chip)
    for r in range(n_col):
        if last:
            counted = jnp.where(is_source(dims, ids, my_x, r), 0.0, 1.0)
            weight = own_first(counted, my_core) * near[r, 1]
        for k in range(PAIR):
            if last:
                sums = jnp.sum(acc[k * n_col + r], axis=1)
                term = weight[k * half : k * half + half] * sums
                out[(my_core ^ k) * n_col + r] = jnp.sum(term, axis=0, keepdims=True)
            else:
                sums = jnp.sum(acc[(my_core ^ k) * n_col + r], axis=1)
                for chip in range(chips):
                    line = (PAIR * chip + my_core) * n_col
                    out[line + r, pl.ds(k * half, half), :] = sums
    if not last:
        give = jnp.concatenate([near[my_col, 0, half:, :], near[my_col, 1, half:, :]], axis=0)
        for chip in range(chips):
            for r in range(n_col):
                out[(PAIR * chip + 1 - my_core) * n_col + r] = give


def depend_level(dims, first, last, places, ids, tiles, bands, came):
    n_row, n_col, slots, half = dims
    if last:
        out_shape = [piece(PAIR * n_col, 1, LANES)]
    else:
        out_shape = [piece(n_row * n_col, PAIR * half, LANES)]
    if first:
        out_shape += [
            piece(n_col, 2, PAIR * half, LANES),
            piece(n_row // PAIR, 2, PAIR * half, LANES),
            piece(PAIR * slots * half, LANES, LANES),
        ]
    else:
        out_shape += [piece(2, PAIR * half, LANES)]
    vectors = [ids, *(tiles if first else []), *bands, came]
    return pl.pallas_call(
        functools.partial(depend_kernel, dims, first, last),
        out_shape=out_shape,
        in_specs=[in_smem()] * len(places) + [in_vmem()] * len(vectors),
        out_specs=[in_vmem()] * len(out_shape),
        scratch_shapes=[pltpu.VMEM((PAIR * n_col, half, SUB, LANES), jnp.float32)]
        + slot_scratch(dims),
        compiler_params=params(terms_limit),
        name="depend_level",
    )(*places, *vectors)


def result_kernel(rows, came, state, shown, paths, centrality):
    shown[...] = state[0]
    paths[...] = state[1]
    shares = [came[at] for at in range(came.shape[0])]
    centrality[...] = functools.reduce(jnp.add, shares) / rows


def results(dims, came, state):
    rows = PAIR * dims[3]
    return pl.pallas_call(
        functools.partial(result_kernel, rows),
        out_shape=[piece(rows, LANES)] * 2 + [piece(1, LANES)],
        in_specs=[in_vmem()] * 2,
        out_specs=[in_vmem()] * 3,
        compiler_params=params(small_limit),
        name="results",
    )(came, state)


def all_to_all(value, axes):
    return lax.all_to_all(value, axes, split_axis=0, concat_axis=0, tiled=True)


def swap_core(value):
    return lax.ppermute(value, "core", [(0, 1), (1, 0)])


def per_device(tiles, tile_index, tile_count, sources):
    slots = tiles.shape[0]
    rows = sources.shape[0]
    dims = (lax.axis_size("chip") * PAIR, lax.axis_size("col"), slots, rows // PAIR)
    own_places = tile_index.T
    line = ("col", "chip")

    everyone = ("chip", "core", "col")

    firsts, turned, ids = first_level(dims, own_places, sources, tiles)
    both = [turned, swap_core(turned)]
    places = [] if is_dense(dims) else [own_places, swap_core(own_places)]
    came = all_to_all(firsts, everyone)
    for level_no in range(1, LEVELS):
        whole = level_no == LEVELS - 1
        outs = relax_level(dims, level_no > 1, whole, places, ids, both, came)
        came = all_to_all(outs, line)
    sums, *bands = depend_level(dims, True, False, places, ids, both, [], came)
    for back_no in range(1, BACK):
        last = back_no == BACK - 1
        came = all_to_all(sums, everyone)
        sums, state = depend_level(dims, False, last, places, ids, both, bands, came)
    shown, paths, centrality = results(dims, all_to_all(sums, ("core", "col")), state)
    return shown, paths, centrality.reshape(LANES)


def solution(mesh):
    groups, rows, cols = mesh.devices.shape
    pairs = mesh.devices.reshape(groups, rows // PAIR, PAIR, cols)
    paired = jax.sharding.Mesh(pairs, ("groups", "chip", "core", "col"))
    vertices = ("chip", "core", "col")
    everywhere = ("groups",) + vertices
    in_specs = (P(everywhere, None, None), P(everywhere, None), P(everywhere), P("groups"))
    out_specs = (P("groups", vertices), P("groups", vertices), P(everywhere))
    return jax.shard_map(
        per_device, mesh=paired, in_specs=in_specs, out_specs=out_specs, check_vma=False
    )
```

```python
import functools

import jax
import jax.numpy as jnp
from jax import lax
from jax.experimental import pallas as pl
from jax.experimental.pallas import tpu as pltpu
from jax.sharding import PartitionSpec as P

LEVELS = 3
BACK = 2
LANES = 128
SUB = 8
PAIR = 2
SPAN = 32

far_value = 1000000.0
no_edge = 2000000.0
large_limit = 8 * 1024 * 1024
small_limit = 2 * 1024 * 1024
terms_limit = 20 * 1024 * 1024


def in_vmem():
    return pl.BlockSpec(memory_space=pltpu.VMEM)


def in_smem():
    return pl.BlockSpec(memory_space=pltpu.SMEM)


def in_hbm():
    return pl.BlockSpec(memory_space=pltpu.HBM)


def piece(*shape):
    return jax.ShapeDtypeStruct(shape, jnp.float32)


def params(limit):
    return pltpu.CompilerParams(vmem_limit_bytes=limit)


def is_dense(dims):
    return dims[2] == dims[0] * dims[1]


def position():
    return lax.axis_index("chip"), lax.axis_index("core"), lax.axis_index("col")


def source_ids(sources, first, half):
    row = lax.broadcasted_iota(jnp.int32, (PAIR * half, LANES), 0)
    ids = jnp.zeros((PAIR * half, LANES), jnp.int32)
    for s in range(half):
        ids = jnp.where(lax.rem(row, half) == s, sources[first + s], ids)
    return ids


def is_source(dims, ids, chip, col):
    n_row, n_col, slots, half = dims
    block = lax.broadcasted_iota(jnp.int32, ids.shape, 0) // half
    lane = lax.broadcasted_iota(jnp.int32, ids.shape, 1)
    return ids == ((PAIR * chip + block) * n_col + col) * LANES + lane


def own_first(rows, my_core):
    half = rows.shape[0] // PAIR
    return jnp.where(my_core == 0, rows, jnp.concatenate([rows[half:], rows[:half]], axis=0))


def settle(found_dist, found_count, at_source):
    dist = jnp.where(at_source, 0.0, jnp.minimum(found_dist, far_value))
    count = jnp.where(found_dist == dist, found_count, 0.0)
    return dist, jnp.where(at_source, 1.0, 0.0) + count


def merge(pairs):
    best = functools.reduce(jnp.minimum, [p[0] for p in pairs])
    total = functools.reduce(jnp.add, [jnp.where(p[0] == best, p[1], 0.0) for p in pairs])
    return best, total


def first_kernel(dims, *refs):
    n_row, n_col, slots, half = dims
    places_in, sources_in, tiles_in, out, turned, ids = refs[:6]
    places, sources, slot_of, tiles, sems = refs[6:]
    my_x, my_core, my_col = position()
    my_row = my_x * PAIR + my_core
    parts = sems.shape[0] - 2
    size = slots // parts
    given = [
        pltpu.make_async_copy(places_in, places, sems.at[parts]),
        pltpu.make_async_copy(sources_in, sources, sems.at[parts + 1]),
    ]
    fetch = []
    for part in range(parts):
        span = pl.ds(part * size, size)
        fetch.append(pltpu.make_async_copy(tiles_in.at[span], tiles.at[span], sems.at[part]))
    for copy in given + fetch:
        copy.start()

    def clear(at, _):
        slot_of[at] = -1
        return 0

    if not is_dense(dims):
        lax.fori_loop(0, n_row * n_col, clear, 0)
    for copy in given:
        copy.wait()
    for g in range(slots):
        slot_of[places[0, g] * n_row + places[1, g]] = g
    ids[...] = source_ids(sources, my_core * half, half)

    def turn(part):
        for g in range(part * size, part * size + size):
            at = places[0, g] * n_row + places[1, g] if is_dense(dims) else g
            raw = tiles[g]
            turned[at] = jnp.where(raw > 0, raw, no_edge).T

    for part in range(parts):
        fetch[part].wait()
        if part + 1 < parts:
            turn(part)
    row_at = lax.broadcasted_iota(jnp.int32, (PAIR * half, LANES), 0)
    lines = {}
    for c in range(n_row):
        for s in range(PAIR * half):
            vertex = sources[s]
            block, place = vertex // LANES, lax.rem(vertex, LANES)
            g = slot_of[lax.rem(block, n_col) * n_row + c]
            here = jnp.logical_and(block // n_col == my_row, g >= 0)
            row = tiles[jnp.maximum(g, 0), pl.ds(place, 1), :]
            to = jnp.where(here, c % PAIR * half + s % half, -1)
            line = lines.get((c // PAIR, s // half), jnp.zeros(row_at.shape, jnp.float32))
            lines[c // PAIR, s // half] = jnp.where(row_at == to, row, line)
    for (chip, core), line in lines.items():
        line = jnp.where(line > 0, line, far_value)
        for col in range(n_col):
            out[(chip * PAIR + core) * n_col + col] = line
    turn(parts - 1)


def first_level(dims, places, sources, tiles):
    n_row, n_col, slots, half = dims
    parts = 2 if slots % 2 == 0 else 1
    inputs = [pltpu.with_memory_space_constraint(x, pltpu.HBM) for x in (places, sources, tiles)]
    return pl.pallas_call(
        functools.partial(first_kernel, dims),
        out_shape=[
            piece(n_row * n_col, PAIR * half, LANES),
            piece(*tiles.shape),
            jax.ShapeDtypeStruct((PAIR * half, LANES), jnp.int32),
        ],
        in_specs=[in_hbm()] * 3,
        out_specs=[in_vmem()] * 3,
        scratch_shapes=[
            pltpu.SMEM(places.shape, jnp.int32),
            pltpu.SMEM(sources.shape, jnp.int32),
            pltpu.SMEM((n_row * n_col,), jnp.int32),
            pltpu.VMEM(tiles.shape, jnp.float32),
            pltpu.SemaphoreType.DMA((parts + 2,)),
        ],
        compiler_params=params(large_limit),
        name="first_level",
    )(*inputs)


def list_slots(dims, places, table, filled):
    n_row, n_col, slots, half = dims
    if is_dense(dims):
        return

    def clear(at, _):
        filled[at] = 0
        return 0

    lax.fori_loop(0, PAIR * n_row, clear, 0)
    for k in range(PAIR):

        def enter(g, _):
            at = k * n_row + places[k][1, g]
            table[at * n_col + filled[at]] = g
            filled[at] += 1
            return 0

        lax.fori_loop(0, slots, enter, 0)


def over_slots(dims, places, table, filled, c, step, carry):
    n_row, n_col, slots, half = dims
    for k in range(PAIR):
        if is_dense(dims):
            for r in range(n_col):
                carry = step(k, r * n_row + c, r, carry)
        else:
            at = k * n_row + c

            def entry(e, carry):
                g = table[at * n_col + e]
                return step(k, g, places[k][0, g], carry)

            carry = lax.fori_loop(0, filled[at], entry, carry)
    return carry


def slot_scratch(dims):
    n_row, n_col, slots, half = dims
    return [
        pltpu.SMEM((PAIR * n_row * n_col,), jnp.int32),
        pltpu.SMEM((PAIR * n_row,), jnp.int32),
    ]


def relax_kernel(dims, counted, whole, *refs):
    n_row, n_col, slots, half = dims
    chips = n_row // PAIR
    n_places = 0 if is_dense(dims) else PAIR
    places, refs = refs[:n_places], refs[n_places:]
    source_rows, tiles, refs = refs[0], refs[1 : 1 + PAIR], refs[1 + PAIR :]
    came, out, near, found, table, filled = refs
    my_x, my_core, my_col = position()
    ids = source_rows[...]
    list_slots(dims, places, table, filled)
    for r in range(n_col):
        if counted:
            blocks = [came[r * chips + chip, 0] for chip in range(chips)]
            reached, count = merge([(block[0], block[1]) for block in blocks])
        else:
            parts = [came[at * n_col + r] for at in range(n_row)]
            reached = functools.reduce(jnp.minimum, parts)
            count = jnp.where(reached < far_value, 1.0, 0.0)
        dist, count = settle(reached, count, is_source(dims, ids, my_x, r))
        near[r, 0] = own_first(dist, my_core)
        near[r, 1] = own_first(count, my_core)
    lane = lax.broadcasted_iota(jnp.int32, (SPAN, LANES), 1)

    spans = range(0, LANES, SPAN)
    items = [(h, q) for h in range(PAIR) for q in spans]

    def lowest(chip, at):
        h, q = items[at]

        def step(k, g, r, carry):
            weight = tiles[k][g, pl.ds(q, SPAN), :]
            rows = [near[r, 0, pl.ds(k * half + s, 1), :] for s in range(half)]
            return tuple(jnp.minimum(low, weight + row) for low, row in zip(carry, rows))

        start = (jnp.full((SPAN, LANES), far_value, jnp.float32),) * half
        reached = over_slots(dims, places, table, filled, PAIR * chip + h, step, start)
        return [jnp.min(low, axis=1, keepdims=True) for low in reached]

    def tally(chip, at, best):
        h, q = items[at]

        def step(k, g, r, carry):
            weight = tiles[k][g, pl.ds(q, SPAN), :]
            counts = []
            for s in range(half):
                row = pl.ds(k * half + s, 1)
                hit = weight + near[r, 0, row, :] == best[s]
                counts.append(carry[s] + jnp.where(hit, near[r, 1, row, :], 0.0))
            return tuple(counts)

        start = (jnp.zeros((SPAN, LANES), jnp.float32),) * half
        counts = over_slots(dims, places, table, filled, PAIR * chip + h, step, start)
        return [jnp.sum(count, axis=1, keepdims=True) for count in counts]

    def columns(chip, _):
        rows = PAIR * half
        turned = {q: jnp.zeros((SPAN, LANES), jnp.float32) for q in spans}
        best = lowest(chip, 0)
        for at, (h, q) in enumerate(items):
            later = lowest(chip, at + 1) if at + 1 < len(items) else None
            totals = tally(chip, at, best)
            for s in range(half):
                to = h * half + s
                with_total = jnp.where(lane == rows + to, totals[s], turned[q])
                turned[q] = jnp.where(lane == to, best[s], with_total)
            best = later
        both = jnp.concatenate([turned[q] for q in spans], axis=0).T
        found[chip, 0] = both[:rows]
        found[chip, 1] = both[rows : 2 * rows]
        return 0

    lax.fori_loop(0, chips, columns, 0)
    for chip in range(chips):
        for col in range(n_col):
            if whole:
                out[col * chips + chip] = found[...]
            else:
                out[col * chips + chip, 0] = found[chip]


def relax_level(dims, counted, whole, places, ids, tiles, came):
    n_row, n_col, slots, half = dims
    chips = n_row // PAIR
    return pl.pallas_call(
        functools.partial(relax_kernel, dims, counted, whole),
        out_shape=piece(chips * n_col, chips if whole else 1, 2, PAIR * half, LANES),
        in_specs=[in_smem()] * len(places) + [in_vmem()] * (PAIR + 2),
        out_specs=in_vmem(),
        scratch_shapes=[
            pltpu.VMEM((n_col, 2, PAIR * half, LANES), jnp.float32),
            pltpu.VMEM((chips, 2, PAIR * half, LANES), jnp.float32),
        ]
        + slot_scratch(dims),
        compiler_params=params(large_limit),
        name="relax_level",
    )(*places, ids, *tiles, came)


def depend_kernel(dims, first, last, *refs):
    n_row, n_col, slots, half = dims
    chips = n_row // PAIR
    n_places = 0 if is_dense(dims) else PAIR
    places, refs = refs[:n_places], refs[n_places:]
    source_rows, refs = refs[0], refs[1:]
    if first:
        tiles, refs = refs[:PAIR], refs[PAIR:]
        came, out, near, low, terms, acc, table, filled = refs
    else:
        near, low, terms, came, out, state, acc, table, filled = refs
    my_x, my_core, my_col = position()
    ids = source_rows[...]
    list_slots(dims, places, table, filled)
    if first:
        for r in range(n_col):
            blocks = [came[r * chips + chip, my_x] for chip in range(chips)]
            found = merge([(block[0], block[1]) for block in blocks])
            dist, count = settle(*found, is_source(dims, ids, my_x, r))
            near[r, 0] = own_first(dist, my_core)
            near[r, 1] = own_first(count, my_core)
        for at in range(chips):
            blocks = [came[my_col * chips + chip, at] for chip in range(chips)]
            found = merge([(block[0], block[1]) for block in blocks])
            dist, count = settle(*found, is_source(dims, ids, at, my_col))
            low[at, 0] = dist
            low[at, 1] = count
    else:
        other = came[(PAIR * my_x + 1 - my_core) * n_col + my_col]
        mine = jnp.concatenate([near[my_col, 0, :half, :], near[my_col, 1, :half, :]], axis=0)
        for core in range(PAIR):
            block = jnp.where(my_core == core, mine, other)
            dist = block[:half]
            rows = pl.ds(core * half, half)
            state[0, rows, :] = jnp.where(dist < 0.5 * far_value, dist, -1.0)
            state[1, rows, :] = block[half:]
    acc[...] = jnp.zeros(acc.shape, jnp.float32)

    def add_terms(k, r, s, part):
        acc[k * n_col + r, s] += jnp.sum(part.reshape(-1, SUB, LANES), axis=0)

    def select(chip, _):
        rows = PAIR * half
        count = low[chip, 1]
        share = jnp.where(count > 0.5, 1.0 / jnp.maximum(count, 1.0), 0.0)
        turned = jnp.concatenate([low[chip, 0], share], axis=0).T
        for at in range(rows):
            h, s = at // half, at % half
            dist = jnp.broadcast_to(turned[:, at : at + 1], (LANES, LANES))
            coef = jnp.broadcast_to(turned[:, rows + at : rows + at + 1], (LANES, LANES))

            def step(k, g, r, carry):
                hit = tiles[k][g] + near[r, 0, pl.ds(k * half + s, 1), :] == dist
                part = jnp.where(hit, coef, 0.0)
                terms[(k * slots + g) * half + s] = part
                add_terms(k, r, s, part)
                return carry

            over_slots(dims, places, table, filled, PAIR * chip + h, step, 0)
        return 0

    def scale(chip):
        line = (PAIR * chip + my_core) * n_col
        total = functools.reduce(jnp.add, [came[line + col] for col in range(n_col)])
        turned = (1.0 + low[chip, 1] * total).T
        for at in range(PAIR * half):
            c, s = PAIR * chip + at // half, at % half
            factor = jnp.broadcast_to(turned[:, at : at + 1], (LANES, LANES))

            def step(k, g, r, carry):
                add_terms(k, r, s, terms[(k * slots + g) * half + s] * factor)
                return carry

            over_slots(dims, places, table, filled, c, step, 0)

    if first:
        lax.fori_loop(0, chips, select, 0)
    else:
        for chip in range(chips):
            scale(chip)
    for r in range(n_col):
        if last:
            counted = jnp.where(is_source(dims, ids, my_x, r), 0.0, 1.0)
            weight = own_first(counted, my_core) * near[r, 1]
        for k in range(PAIR):
            if last:
                sums = jnp.sum(acc[k * n_col + r], axis=1)
                term = weight[k * half : k * half + half] * sums
                out[r * PAIR + (my_core ^ k)] = jnp.sum(term, axis=0, keepdims=True)
            else:
                sums = jnp.sum(acc[(my_core ^ k) * n_col + r], axis=1)
                for chip in range(chips):
                    line = (PAIR * chip + my_core) * n_col
                    out[line + r, pl.ds(k * half, half), :] = sums
    if not last:
        give = jnp.concatenate([near[my_col, 0, half:, :], near[my_col, 1, half:, :]], axis=0)
        for chip in range(chips):
            for r in range(n_col):
                out[(PAIR * chip + 1 - my_core) * n_col + r] = give


def depend_level(dims, first, last, places, ids, tiles, bands, came):
    n_row, n_col, slots, half = dims
    if last:
        out_shape = [piece(PAIR * n_col, 1, LANES)]
    else:
        out_shape = [piece(n_row * n_col, PAIR * half, LANES)]
    if first:
        out_shape += [
            piece(n_col, 2, PAIR * half, LANES),
            piece(n_row // PAIR, 2, PAIR * half, LANES),
            piece(PAIR * slots * half, LANES, LANES),
        ]
    else:
        out_shape += [piece(2, PAIR * half, LANES)]
    vectors = [ids, *(tiles if first else []), *bands, came]
    return pl.pallas_call(
        functools.partial(depend_kernel, dims, first, last),
        out_shape=out_shape,
        in_specs=[in_smem()] * len(places) + [in_vmem()] * len(vectors),
        out_specs=[in_vmem()] * len(out_shape),
        scratch_shapes=[pltpu.VMEM((PAIR * n_col, half, SUB, LANES), jnp.float32)]
        + slot_scratch(dims),
        compiler_params=params(terms_limit),
        name="depend_level",
    )(*places, *vectors)


def result_kernel(rows, came, state, shown, paths, centrality):
    shown[...] = state[0]
    paths[...] = state[1]
    shares = [came[at] for at in range(came.shape[0])]
    centrality[...] = functools.reduce(jnp.add, shares) / rows


def results(dims, came, state):
    rows = PAIR * dims[3]
    return pl.pallas_call(
        functools.partial(result_kernel, rows),
        out_shape=[piece(rows, LANES)] * 2 + [piece(1, LANES)],
        in_specs=[in_vmem()] * 2,
        out_specs=[in_vmem()] * 3,
        compiler_params=params(small_limit),
        name="results",
    )(came, state)


def all_to_all(value, axes):
    return lax.all_to_all(value, axes, split_axis=0, concat_axis=0, tiled=True)


def swap_core(value):
    return lax.ppermute(value, "core", [(0, 1), (1, 0)])


def per_device(tiles, tile_index, tile_count, sources):
    slots = tiles.shape[0]
    rows = sources.shape[0]
    dims = (lax.axis_size("chip") * PAIR, lax.axis_size("col"), slots, rows // PAIR)
    own_places = tile_index.T
    line = ("col", "chip")

    everyone = ("chip", "core", "col")

    firsts, turned, ids = first_level(dims, own_places, sources, tiles)
    both = [turned, swap_core(turned)]
    places = [] if is_dense(dims) else [own_places, swap_core(own_places)]
    came = all_to_all(firsts, everyone)
    for level_no in range(1, LEVELS):
        whole = level_no == LEVELS - 1
        outs = relax_level(dims, level_no > 1, whole, places, ids, both, came)
        came = all_to_all(outs, line)
    sums, *bands = depend_level(dims, True, False, places, ids, both, [], came)
    for back_no in range(1, BACK):
        last = back_no == BACK - 1
        came = all_to_all(sums, everyone)
        sums, state = depend_level(dims, False, last, places, ids, both, bands, came)
    shown, paths, centrality = results(dims, all_to_all(sums, ("col", "core")), state)
    return shown, paths, centrality.reshape(LANES)


def solution(mesh):
    groups, rows, cols = mesh.devices.shape
    pairs = mesh.devices.reshape(groups, rows // PAIR, PAIR, cols)
    paired = jax.sharding.Mesh(pairs, ("groups", "chip", "core", "col"))
    vertices = ("chip", "core", "col")
    everywhere = ("groups",) + vertices
    in_specs = (P(everywhere, None, None), P(everywhere, None), P(everywhere), P("groups"))
    out_specs = (P("groups", vertices), P("groups", vertices), P(everywhere))
    return jax.shard_map(
        per_device, mesh=paired, in_specs=in_specs, out_specs=out_specs, check_vma=False
    )
```
